32 devices in a mesh: outer: 2 (over y), inner: 16 (over z, x, core).
Axes of the slice: x: 2, y: 2, z: 4, core: 2. Of those that a mesh axis runs over, the one named last changes fastest.
Arguments:
- hidden: bfloat16 [32, 1024, 768], P(('outer', 'inner')), may hold values from -6 to 6
- cotangent: bfloat16 [32, 1024, 768], P(('outer', 'inner')), may hold values from -6 to 6
- capacity_class: int32 [32], P(('outer', 'inner')), may hold values from 0 to 2, as said below
- token_index: int32 [32, 512], P(('outer', 'inner')), may hold values from 0 to 1023, as said below
- gain_attn_a: bfloat16 [768], P(('outer', 'inner')), may hold values from 0.5 to 1.5
- qkv_weight_a: bfloat16 [768, 2304], P('inner', 'outer'), may hold values from -0.21875 to 0.21875
- out_weight_a: bfloat16 [768, 768], P('inner', 'outer'), may hold values from -0.625 to 0.625
- gain_mlp_a: bfloat16 [768], P(('outer', 'inner')), may hold values from 0.5 to 1.5
- up_weight_a: bfloat16 [768, 3072], P('inner', 'outer'), may hold values from -0.21875 to 0.21875
- down_weight_a: bfloat16 [3072, 768], P('inner', 'outer'), may hold values from -0.109375 to 0.109375
- router_weight: bfloat16 [768], P(('outer', 'inner')), may hold values from -0.21875 to 0.21875
- gain_attn_b: bfloat16 [768], P(('outer', 'inner')), may hold values from 0.5 to 1.5
- qkv_weight_b: bfloat16 [768, 2304], P('inner', 'outer'), may hold values from -0.21875 to 0.21875
- out_weight_b: bfloat16 [768, 768], P('inner', 'outer'), may hold values from -0.625 to 0.625
- gain_mlp_b: bfloat16 [768], P(('outer', 'inner')), may hold values from 0.5 to 1.5
- up_weight_b: bfloat16 [768, 3072], P('inner', 'outer'), may hold values from -0.21875 to 0.21875
- down_weight_b: bfloat16 [3072, 768], P('inner', 'outer'), may hold values from -0.109375 to 0.109375
Outputs:
- output: bfloat16 [32, 1024, 768], P(('outer', 'inner'))
- input_grad: float32 [32, 1024, 768], P(('outer', 'inner'))
- grad_gain_attn_a: float32 [768], P(('outer', 'inner'))
- grad_qkv_a: float32 [768, 2304], P('inner', 'outer')
- grad_out_a: float32 [768, 768], P('inner', 'outer')
- grad_gain_mlp_a: float32 [768], P(('outer', 'inner'))
- grad_up_a: float32 [768, 3072], P('inner', 'outer')
- grad_down_a: float32 [3072, 768], P('inner', 'outer')
- grad_router: float32 [768], P(('outer', 'inner'))
- grad_gain_attn_b: float32 [768], P(('outer', 'inner'))
- grad_qkv_b: float32 [768, 2304], P('inner', 'outer')
- grad_out_b: float32 [768, 768], P('inner', 'outer')
- grad_gain_mlp_b: float32 [768], P(('outer', 'inner'))
- grad_up_b: float32 [768, 3072], P('inner', 'outer')
- grad_down_b: float32 [3072, 768], P('inner', 'outer')
The draws below stay inside these ranges and needn't reach their ends.
Inputs may be any that keep to these rules, and one draw needn't show every extreme that they name: `capacity_class`: a sequence of class c has a buffer of 1024 / 8 * 2^c tokens; classes 0 and 2 both occur in every draw. `token_index`: row s holds, in its first 1024 / 8 * 2^capacity_class[s] entries, distinct positions of the sequence in increasing order; the remaining entries are 0 and are not used.
All inputs are finite; a program needn't handle non-finite values.
Results may differ from the reference program's by a relative error of at most 0.024.
Values may be sent and summed in bfloat16 or wider, within the bound.
A program may use at most 256 MiB of HBM per device.

```python
import jax
import jax.numpy as jnp
from jax import lax

D = 768
HEADS = 12
HEAD = 64
FF = 3072
LENGTH = 1024
SEQS = 32


def choose_classes(key):
    row_high = jax.random.randint(jax.random.fold_in(key, 21), (), 0, SEQS)
    row_low = (row_high + 1 + jax.random.randint(jax.random.fold_in(key, 22), (), 0, SEQS - 1)) % SEQS
    classes = jax.random.randint(jax.random.fold_in(key, 23), (SEQS,), 0, 3)
    classes = classes.at[row_high].set(2).at[row_low].set(0)
    return (classes, row_high)


def draw_capacity_class(key, part):
    classes, row_high = choose_classes(key)
    return classes.astype(jnp.int32)


def draw_token_index(key, part):
    classes, row_high = choose_classes(key)
    key = jax.random.fold_in(key, 7)
    limits = LENGTH // 8 * jnp.where(classes == 2, 4, 1 + classes)
    positions = jnp.broadcast_to(jnp.arange(LENGTH, dtype=jnp.int32)[None, :], (SEQS, LENGTH))
    priority = jax.random.randint(key, (SEQS, LENGTH), 0, 2 ** 20) * LENGTH + positions
    priority = priority.at[row_high, LENGTH - 1].set(-1)
    ranks = jnp.argsort(jnp.argsort(priority, axis=1), axis=1)
    chosen = jnp.where(ranks < limits[:, None], positions, LENGTH)
    ordered = jnp.sort(chosen, axis=1)[:, :LENGTH // 2]
    slots = jnp.arange(LENGTH // 2, dtype=jnp.int32)
    return jnp.where(slots[None, :] < limits[:, None], ordered, 0).astype(jnp.int32)


def levels(rng, shape, cuts, least, largest):
    gain, own = 1.0, jax.random.fold_in(rng, 6)
    for dim, blocks in cuts:
        steps = jnp.exp(jax.random.uniform(jax.random.fold_in(own, dim), (blocks,), jnp.float32, least / len(cuts), largest / len(cuts)))
        gain = gain * jnp.repeat(steps, shape[dim] // blocks).reshape([-1 if axis == dim else 1 for axis in range(len(shape))])
    return gain


def noise(stream_key, shape, scale, reach, cuts=(), kind=jnp.bfloat16):
    drawn = jax.random.normal(stream_key, shape, jnp.float32) * scale
    if len(cuts) > 0:
        drawn = levels(stream_key, shape, cuts, -0.22, 0.18) * drawn
    return jnp.clip(drawn, min=-reach, max=reach).astype(kind)


def setup_inputs(seed: int = 0) -> dict:
    key_of = jax.random.split(jax.random.key(seed), 18)
    hidden = noise(key_of[0], (SEQS, LENGTH, D), 1.0, 6.0, ((0, 32),))
    cotangent = noise(key_of[1], (SEQS, LENGTH, D), 1.0, 6.0, ((0, 32),))
    capacity_class = draw_capacity_class(jax.random.fold_in(key_of[17], 71), 0)
    token_index = draw_token_index(jax.random.fold_in(key_of[17], 71), 0)
    gain_attn_a = jnp.clip(1.0 + 0.1 * jax.random.normal(key_of[4], (D,), jnp.float32), 0.5, 1.5).astype(jnp.bfloat16)
    qkv_weight_a = noise(key_of[5], (D, 3 * D), D ** -0.5, 0.21875, ((0, 16), (1, 2)))
    out_weight_a = noise(key_of[6], (D, D), (D // 8) ** -0.5, 0.625, ((0, 16), (1, 2)))
    gain_mlp_a = jnp.clip(1.0 + 0.1 * jax.random.normal(key_of[7], (D,), jnp.float32), 0.5, 1.5).astype(jnp.bfloat16)
    up_weight_a = noise(key_of[8], (D, FF), D ** -0.5, 0.21875, ((0, 16), (1, 2)))
    down_weight_a = noise(key_of[9], (FF, D), FF ** -0.5, 0.109375, ((0, 16), (1, 2)))
    router_weight = noise(key_of[10], (D,), D ** -0.5, 0.21875, ((0, 32),))
    gain_attn_b = jnp.clip(1.0 + 0.1 * jax.random.normal(key_of[11], (D,), jnp.float32), 0.5, 1.5).astype(jnp.bfloat16)
    qkv_weight_b = noise(key_of[12], (D, 3 * D), D ** -0.5, 0.21875, ((0, 16), (1, 2)))
    out_weight_b = noise(key_of[13], (D, D), (D // 8) ** -0.5, 0.625, ((0, 16), (1, 2)))
    gain_mlp_b = jnp.clip(1.0 + 0.1 * jax.random.normal(key_of[14], (D,), jnp.float32), 0.5, 1.5).astype(jnp.bfloat16)
    up_weight_b = noise(key_of[15], (D, FF), D ** -0.5, 0.21875, ((0, 16), (1, 2)))
    down_weight_b = noise(key_of[16], (FF, D), FF ** -0.5, 0.109375, ((0, 16), (1, 2)))
    return dict(hidden=hidden, cotangent=cotangent, capacity_class=capacity_class, token_index=token_index, gain_attn_a=gain_attn_a, qkv_weight_a=qkv_weight_a, out_weight_a=out_weight_a, gain_mlp_a=gain_mlp_a, up_weight_a=up_weight_a, down_weight_a=down_weight_a, router_weight=router_weight, gain_attn_b=gain_attn_b, qkv_weight_b=qkv_weight_b, out_weight_b=out_weight_b, gain_mlp_b=gain_mlp_b, up_weight_b=up_weight_b, down_weight_b=down_weight_b)


@jax.custom_vjp
def low(v):
    return lax.optimization_barrier(v.astype(jnp.bfloat16)).astype(jnp.float32)

@jax.custom_vjp
def low_back(v):
    return v

def low_keep(v):
    return (low(v), None)

def low_pass(kept, grad):
    return (grad,)

def back_keep(v):
    return (v, None)

def back_low(kept, grad):
    return (low(grad),)
low.defvjp(low_keep, low_pass)
low_back.defvjp(back_keep, back_low)

def matmul(left, right):
    return jnp.dot(left, right, precision=lax.Precision.HIGHEST, preferred_element_type=jnp.float32)

def rms_norm(values, norm_gain):
    return values * lax.rsqrt(lax.optimization_barrier(jnp.mean(values * values, axis=-1, keepdims=True)) + 1e-06) * norm_gain

def head_attend(pieces):
    query_head, key_head, value_head = pieces
    scores = low_back(matmul(query_head, key_head.T)) * 0.125
    length = scores.shape[0]
    causal = lax.broadcasted_iota(jnp.int32, (length, length), 0) >= lax.broadcasted_iota(jnp.int32, (length, length), 1)
    scores = jnp.where(causal, scores, -1000000000.0)
    weights = low(jax.nn.softmax(scores, axis=-1))
    return low(low_back(matmul(weights, value_head)))

def residual_block(hidden, params):
    gain_attn, qkv_weight, out_weight, gain_mlp, up_weight, down_weight = params
    length = hidden.shape[0]
    normed = low(rms_norm(hidden, gain_attn))
    projected = low(low_back(matmul(normed, qkv_weight)))
    heads_split = projected.reshape(length, 3, HEADS, HEAD).transpose(1, 2, 0, 3)
    attended = lax.map(jax.checkpoint(head_attend), (heads_split[0], heads_split[1], heads_split[2]))
    merged = attended.transpose(1, 0, 2).reshape(length, HEADS * HEAD)
    branch = low_back(matmul(merged, out_weight))
    middle = hidden + branch
    normed_mlp = low(rms_norm(middle, gain_mlp))
    inner_pre = low_back(matmul(normed_mlp, up_weight))
    active = low(jax.nn.gelu(inner_pre, approximate=True))
    return branch + low_back(matmul(active, down_weight))

def routed(hidden, router, params, seq_class, seq_index):
    length = hidden.shape[0]

    def builder(buffer_size):

        def runner(hidden, router, params):
            picked_index = seq_index[:buffer_size]
            picked = hidden[picked_index]
            logits = lax.optimization_barrier(jnp.sum(picked * router, axis=-1))
            change = residual_block(picked, params)
            return hidden.at[picked_index].add(jax.nn.sigmoid(logits)[:, None] * change)
        return runner
    return lax.switch(seq_class, [builder(length // 8), builder(length // 4), builder(length // 2)], hidden, router, params)

def reference(hidden, cotangent, capacity_class, token_index, gain_attn_a, qkv_weight_a, out_weight_a, gain_mlp_a, up_weight_a, down_weight_a, router_weight, gain_attn_b, qkv_weight_b, out_weight_b, gain_mlp_b, up_weight_b, down_weight_b):
    first = tuple((weight_arr.astype(jnp.float32) for weight_arr in (gain_attn_a, qkv_weight_a, out_weight_a, gain_mlp_a, up_weight_a, down_weight_a)))
    second = tuple((weight_arr.astype(jnp.float32) for weight_arr in (gain_attn_b, qkv_weight_b, out_weight_b, gain_mlp_b, up_weight_b, down_weight_b)))
    router = router_weight.astype(jnp.float32)

    def sequence_step(totals, sliced):
        sequence, grad_rows, seq_class, seq_index = sliced

        def forward(sequence, router, first, second):
            middle = routed(sequence, router, first, seq_class, seq_index)
            return middle + residual_block(middle, second)
        result, pullback = jax.vjp(forward, sequence.astype(jnp.float32), router, first, second)
        gradients = pullback(grad_rows.astype(jnp.float32))
        totals = jax.tree.map(jnp.add, totals, gradients[1:])
        return (totals, (result.astype(jnp.bfloat16), gradients[0]))
    initial = jax.tree.map(jnp.zeros_like, (router, first, second))
    totals, outputs = lax.scan(sequence_step, initial, (hidden, cotangent, capacity_class, token_index))
    router_grad, first_grads, second_grads = totals
    return (outputs[0], outputs[1], first_grads[0], first_grads[1], first_grads[2], first_grads[3], first_grads[4], first_grads[5], router_grad, second_grads[0], second_grads[1], second_grads[2], second_grads[3], second_grads[4], second_grads[5])
```

```python
import functools

import jax
import jax.numpy as jnp
from jax import lax
from jax.experimental import pallas as pl
from jax.experimental.pallas import tpu as pltpu
from jax.sharding import PartitionSpec as P

HEADS = 12
HEAD = 64
MESH = pl.DeviceIdType.MESH


def place():
    o, i = lax.axis_index("outer"), lax.axis_index("inner")
    return o, i // 4, (i // 2) % 2, i % 2


def device(o, z, x, c):
    return (o, z * 4 + x * 2 + c)


def greet(o, z, x, c):
    barrier = pltpu.get_barrier_semaphore()
    signal = functools.partial(pl.semaphore_signal, barrier, inc=1, device_id_type=MESH)
    signal(device_id=device(1 - o, z, x, c))
    signal(device_id=device(o, z, 1 - x, c))
    signal(device_id=device(o, z, x, 1 - c))

    @pl.when(z > 0)
    def _():
        signal(device_id=device(o, z - 1, x, c))

    @pl.when(z < 3)
    def _():
        signal(device_id=device(o, z + 1, x, c))

    pl.semaphore_wait(barrier, 3 + jnp.where(z > 0, 1, 0) + jnp.where(z < 3, 1, 0))


def scatter_kernel(n, *refs):
    grads, outs = refs[:n], refs[n:2 * n]
    rest = refs[2 * n:]
    own, got_c, got_b, got_a, got_z = (rest[j * n:(j + 1) * n] for j in range(5))
    local_sem, send_sem, recv_sem = rest[5 * n:]
    o, z, x, c = place()
    greet(o, z, x, c)

    def block(p, s, cc):
        r, w = outs[p].shape
        bs, as_, k = s // 8, (s // 4) % 2, s % 4
        if p % 2 == 0:
            co, cx = jnp.where(bs == 1, o, 1 - o), jnp.where(as_ == 1, x, 1 - x)
        else:
            cx, co = jnp.where(bs == 1, x, 1 - x), jnp.where(as_ == 1, o, 1 - o)
        row = pl.multiple_of((k * 4 + cx * 2 + cc) * r, 16)
        col = pl.multiple_of(co * w, 128)
        return grads[p].at[pl.ds(row, r), pl.ds(col, w)]

    def a_dev(p):
        return device(o, z, 1 - x, c) if p % 2 == 0 else device(1 - o, z, x, c)

    def b_dev(p):
        return device(1 - o, z, x, c) if p % 2 == 0 else device(o, z, 1 - x, c)

    def send(p, src, dst, kind, rslot, target):
        return pltpu.make_async_remote_copy(
            src_ref=src, dst_ref=dst, send_sem=send_sem.at[p, kind], recv_sem=recv_sem.at[p, rslot],
            device_id=target, device_id_type=MESH)

    def wait(ref, sem):
        pltpu.make_async_copy(ref, ref, sem).wait()

    def loop(count, body):
        def step(s, carry):
            body(s)
            return carry
        lax.fori_loop(0, count, step, 0)

    def begin(p):
        def body(s):
            send(p, block(p, s, 1 - c), got_c[p].at[s], 0, s, device(o, z, x, 1 - c)).start()
            pltpu.make_async_copy(block(p, s, c), own[p].at[s], local_sem.at[p]).start()
        loop(16, body)

    def core_stage(p):
        wait(own[p], local_sem.at[p])

        def body(s):
            wait(got_c[p].at[s], recv_sem.at[p, s])
            own[p][s] = own[p][s] + got_c[p][s]

            @pl.when(s < 8)
            def _():
                send(p, own[p].at[s], got_b[p].at[s], 1, 16 + s, b_dev(p)).start()
        loop(16, body)

    def b_stage(p):
        def body(j):
            wait(got_b[p].at[j], recv_sem.at[p, 16 + j])
            own[p][8 + j] = own[p][8 + j] + got_b[p][j]

            @pl.when(j < 4)
            def _():
                send(p, own[p].at[8 + j], got_a[p].at[j], 2, 24 + j, a_dev(p)).start()
        loop(8, body)

    def send_z(p, k, step):
        t = z + step
        slot = jnp.where(k == t, jnp.where(step > 0, k, 4), k)
        send(p, own[p].at[12 + k], got_z[p].at[slot], 3, 28 + slot, device(o, t, x, c)).start()

    def a_stage(p):
        def body(k):
            wait(got_a[p].at[k], recv_sem.at[p, 24 + k])
            own[p][12 + k] = own[p][12 + k] + got_a[p][k]
        loop(4, body)

        @pl.when(z == 0)
        def _():
            for k in (3, 2, 1):
                send_z(p, k, 1)

        @pl.when(z == 3)
        def _():
            for k in (0, 1, 2):
                send_z(p, k, -1)

    def pass_on(p, k, step):
        wait(got_z[p].at[k], recv_sem.at[p, 28 + k])
        own[p][12 + k] = own[p][12 + k] + got_z[p][k]
        send_z(p, k, step)

    def z_stage(p, level):
        @pl.when(z == level)
        def _():
            for k in range(3, level, -1):
                pass_on(p, k, 1)

        @pl.when(z == 3 - level)
        def _():
            for k in range(0, 3 - level):
                pass_on(p, k, -1)

    def last(p):
        outs[p][...] = own[p][12 + z].astype(jnp.float32)

        @pl.when(z > 0)
        def _():
            wait(got_z[p].at[z], recv_sem.at[p, 28 + z])
            outs[p][...] += got_z[p][z].astype(jnp.float32)

        @pl.when(z < 3)
        def _():
            wait(got_z[p].at[4], recv_sem.at[p, 32])
            outs[p][...] += got_z[p][4].astype(jnp.float32)

        wait(own[p], send_sem.at[p, 0])
        wait(got_b[p], send_sem.at[p, 1])
        wait(got_a[p], send_sem.at[p, 2])
        wait(got_a[p].at[pl.ds(0, 3)], send_sem.at[p, 3])

    for p in range(n):
        begin(p)
    stages = [core_stage, b_stage, a_stage, lambda p: z_stage(p, 1), lambda p: z_stage(p, 2), last]
    for t in range(n + len(stages) - 1):
        for lag, stage in enumerate(stages):
            if 0 <= t - lag < n:
                stage(t - lag)


def scatter_all(grads, outer, inner, collective_id=1):
    n = len(grads)
    outs = [jax.ShapeDtypeStruct((g.shape[0] // inner, g.shape[1] // outer), jnp.float32) for g in grads]
    bufs = [pltpu.VMEM((m,) + s.shape, jnp.bfloat16) for m in (16, 16, 8, 4, 5) for s in outs]
    return pl.pallas_call(
        functools.partial(scatter_kernel, n),
        out_shape=outs,
        in_specs=[pl.BlockSpec(memory_space=pl.ANY)] * n,
        out_specs=[pl.BlockSpec(memory_space=pltpu.VMEM)] * n,
        scratch_shapes=bufs + [pltpu.SemaphoreType.DMA((n,)), pltpu.SemaphoreType.DMA((n, 4)), pltpu.SemaphoreType.DMA((n, 33))],
        compiler_params=pltpu.CompilerParams(collective_id=collective_id, has_side_effects=True, vmem_limit_bytes=60 * 2**20),
        name="scatter_gradients",
    )(*grads)


def gather_kernel(n, *refs):
    shards, outs = refs[:n], refs[n:2 * n]
    local_sem, send_sem, recv_sem = refs[2 * n:]
    o, z, x, c = place()

    greet(o, z, x, c)

    def block(p, co, cz, cx, cc):
        r, w = shards[p].shape
        row = pl.multiple_of((cz * 4 + cx * 2 + cc) * r, 16)
        col = pl.multiple_of(co * w, 128)
        return outs[p].at[pl.ds(row, r), pl.ds(col, w)]

    def send(p, src, dst, slot, rslot, target):
        return pltpu.make_async_remote_copy(
            src_ref=src, dst_ref=dst, send_sem=send_sem.at[p, slot], recv_sem=recv_sem.at[p, rslot],
            device_id=target, device_id_type=MESH)

    def up(p, k, src=None):
        b = block(p, o, k, x, c)
        return send(p, b if src is None else src, b, k, k, device(o, z + 1, x, c))

    def down(p, k, src=None):
        b = block(p, o, k, x, c)
        return send(p, b if src is None else src, b, 4 + k, k, device(o, z - 1, x, c))

    def first(p, k, src=None):
        b = block(p, o, k, x, c)
        t = device(o, z, 1 - x, c) if p % 2 == 0 else device(1 - o, z, x, c)
        return send(p, b if src is None else src, b, 8 + k, 4 + k, t)

    def second(p, k, a, src=None):
        if p % 2 == 0:
            b, t = block(p, o, k, a, c), device(1 - o, z, x, c)
        else:
            b, t = block(p, a, k, x, c), device(o, z, 1 - x, c)
        return send(p, b if src is None else src, b, 12 + 2 * k + a, 8 + 2 * k + a, t)

    def core(p, co, k, cx, src=None):
        b = block(p, co, k, cx, c)
        s = k * 4 + co * 2 + cx
        return send(p, b if src is None else src, b, 20 + s, 16 + s, device(o, z, x, 1 - c))

    def mine(p):
        return x if p % 2 == 0 else o

    def coords(p, k, a, b):
        return (b, k, a) if p % 2 == 0 else (a, k, b)

    def core_ab(p, k, a, b, src=None):
        co, ck, cx = coords(p, k, a, b)
        return core(p, co, ck, cx, src)

    def other(p):
        return o if p % 2 == 0 else x

    def own(p):
        s = shards[p]
        pltpu.make_async_copy(s, block(p, o, z, x, c), local_sem.at[p]).start()

        @pl.when(z < 3)
        def _():
            up(p, z, s).start()

        @pl.when(z > 0)
        def _():
            down(p, z, s).start()

        first(p, z, s).start()
        second(p, z, mine(p), s).start()
        core(p, o, z, x, s).start()

    def wait_block(p, rslot):
        b = block(p, o, z, x, c)
        pltpu.make_async_copy(shards[p], b, recv_sem.at[p, rslot]).wait()

    def z_phase(p):
        for d in range(1, 4):
            @pl.when(z >= d)
            def _():
                k = z - d
                wait_block(p, k)

                @pl.when(z < 3)
                def _():
                    up(p, k).start()

                first(p, k).start()
                second(p, k, mine(p)).start()
                core(p, o, k, x).start()

            @pl.when(z + d <= 3)
            def _():
                k = z + d
                wait_block(p, k)

                @pl.when(z > 0)
                def _():
                    down(p, k).start()

                first(p, k).start()
                second(p, k, mine(p)).start()
                core(p, o, k, x).start()

    def ks():
        return [(z + d) % 4 for d in range(4)]

    def a_phase(p):
        for k in ks():
            wait_block(p, 4 + k)
            a = 1 - mine(p)
            second(p, k, a).start()
            core_ab(p, k, a, other(p)).start()

    def b_phase(p):
        for k in ks():
            for a in (mine(p), 1 - mine(p)):
                wait_block(p, 8 + 2 * k + a)
                core_ab(p, k, a, 1 - other(p)).start()

    def c_phase(p):
        for s in range(16):
            wait_block(p, 16 + s)

    def ends(p):
        pltpu.make_async_copy(shards[p], block(p, o, z, x, c), local_sem.at[p]).wait()

        def done(slot):
            pltpu.make_async_copy(shards[p], block(p, o, z, x, c), send_sem.at[p, slot]).wait()

        for k in range(4):
            @pl.when(jnp.logical_and(z < 3, k <= z))
            def _():
                done(k)

            @pl.when(jnp.logical_and(z > 0, k >= z))
            def _():
                done(4 + k)
        for slot in range(8, 36):
            done(slot)

    own(0)
    for t in range(n + 3):
        if t + 1 < n:
            own(t + 1)
        if t < n:
            z_phase(t)
        if 0 <= t - 1 < n:
            a_phase(t - 1)
        if 0 <= t - 2 < n:
            b_phase(t - 2)
    for p in range(n):
        c_phase(p)
        ends(p)


def gather_all(shards, outer, inner, collective_id=0):
    n = len(shards)
    outs = [jax.ShapeDtypeStruct((s.shape[0] * inner, s.shape[1] * outer), s.dtype) for s in shards]
    return pl.pallas_call(
        functools.partial(gather_kernel, n),
        out_shape=outs,
        in_specs=[pl.BlockSpec(memory_space=pl.ANY)] * n,
        out_specs=[pl.BlockSpec(memory_space=pl.ANY)] * n,
        scratch_shapes=[pltpu.SemaphoreType.DMA((n,)), pltpu.SemaphoreType.DMA((n, 36)), pltpu.SemaphoreType.DMA((n, 32))],
        compiler_params=pltpu.CompilerParams(collective_id=collective_id, has_side_effects=True),
        name="gather_weights",
    )(*shards)


C = 0.125 * 1.4426950408889634
T = 256


def dg(a, b, ca, cb):
    return lax.dot_general(a, b, (((ca,), (cb,)), ((), ())), preferred_element_type=jnp.float32)


def split(x):
    lane = lax.broadcasted_iota(jnp.int32, x.shape, 1)
    z = jnp.zeros_like(x)
    return jnp.where(lane < 64, x, z), jnp.where(lane < 64, z, x)


def fwd_kernel(variant, q_ref, k_ref, v_ref, o_ref, lse_ref):
    L = q_ref.shape[0]
    lane = lax.broadcasted_iota(jnp.int32, (T, 128), 1)
    lane_t = lax.broadcasted_iota(jnp.int32, (128, T), 0)
    v0, v1 = split(v_ref[...])
    for i in range(L // T):
        n = (i + 1) * T
        q = q_ref[i * T:n, :]
        qs = split(q)
        k = k_ref[:n, :]
        acc = None
        for h in range(2):
            v = (v0, v1)[h][:n]
            if variant == 1:
                s = dg(qs[h], k, 1, 1)
                r = lax.broadcasted_iota(jnp.int32, (T, T), 0) >= lax.broadcasted_iota(jnp.int32, (T, T), 1)
                last = jnp.where(r, s[:, i * T:], -1e30)
                s = last if i == 0 else jnp.concatenate([s[:, :i * T], last], axis=1)
                m = jnp.max(s, axis=1, keepdims=True) * C
                p = jnp.exp2(s * C - m)
                l = jnp.sum(p, axis=1, keepdims=True)
                o = dg(p.astype(jnp.bfloat16), v, 1, 0) / l
                acc = o if acc is None else acc + o
                lse_ref[0, i * T:n, h:h + 1] = m + jnp.log2(l)
            else:
                s = dg(k, qs[h], 1, 1)
                r = lax.broadcasted_iota(jnp.int32, (T, T), 1) >= lax.broadcasted_iota(jnp.int32, (T, T), 0)
                last = jnp.where(r, s[i * T:], -1e30)
                s = last if i == 0 else jnp.concatenate([s[:i * T], last], axis=0)
                m = jnp.max(s, axis=0, keepdims=True) * C
                p = jnp.exp2(s * C - m)
                l = jnp.sum(p, axis=0, keepdims=True)
                lse_ref[0, h:h + 1, i * T:n] = m + jnp.log2(l)
                pb = p.astype(jnp.bfloat16)
                if variant == 2:
                    pb = (p * (1.0 / l)).astype(jnp.bfloat16)
                    o = dg(pb, v, 0, 0)
                else:
                    o = dg(v, pb, 0, 0) / l
                acc = o if acc is None else acc + o
        if variant == 3:
            acc = acc.T
        o_ref[i * T:n, :] = acc.astype(jnp.bfloat16)


def attend(projected, variant=2):
    L = projected.shape[0]
    lse_shape = (6, L, 8) if variant == 1 else (6, 8, L)
    return pl.pallas_call(
        functools.partial(fwd_kernel, variant),
        grid=(6,),
        in_specs=[pl.BlockSpec((L, 128), lambda h: (0, h)), pl.BlockSpec((L, 128), lambda h: (0, 6 + h)),
                  pl.BlockSpec((L, 128), lambda h: (0, 12 + h))],
        out_specs=[pl.BlockSpec((L, 128), lambda h: (0, h)), pl.BlockSpec((1,) + lse_shape[1:], lambda h: (h, 0, 0))],
        out_shape=[jax.ShapeDtypeStruct((L, 768), jnp.bfloat16), jax.ShapeDtypeStruct(lse_shape, jnp.float32)],
        compiler_params=pltpu.CompilerParams(vmem_limit_bytes=48 * 2**20),
        name="attend_forward",
    )(projected, projected, projected)


def bwd_kernel(variant, q_ref, k_ref, v_ref, o_ref, do_ref, lse_ref, dq_ref, dk_ref, dv_ref, dq_acc):
    L = q_ref.shape[0]
    q, do = q_ref[...], do_ref[...]
    qs, dos = split(q), split(do)
    dd = do.astype(jnp.float32) * o_ref[...].astype(jnp.float32)
    pick = lax.broadcasted_iota(jnp.int32, (8, 128), 0) == lax.broadcasted_iota(jnp.int32, (8, 128), 1) // 64
    delta = lax.dot_general(pick.astype(jnp.float32), dd, (((1,), (1,)), ((), ())), precision=lax.Precision.HIGHEST,
                            preferred_element_type=jnp.float32)
    for j in range(L // T):
        a = j * T
        ks, vs = split(k_ref[a:a + T, :]), split(v_ref[a:a + T, :])
        dk = dv = dq = None
        for h in range(2):
            s = dg(ks[h], q[a:], 1, 1)
            p = jnp.exp2(s * C - lse_ref[0, h:h + 1, a:])
            r = lax.broadcasted_iota(jnp.int32, (T, T), 1) >= lax.broadcasted_iota(jnp.int32, (T, T), 0)
            first = jnp.where(r, p[:, :T], 0.0)
            p = first if a + T == L else jnp.concatenate([first, p[:, T:]], axis=1)
            dp = dg(vs[h], do[a:], 1, 1)
            ds = (p * (dp - delta[h:h + 1, a:])).astype(jnp.bfloat16)
            dv_h = dg(p.astype(jnp.bfloat16), dos[h][a:], 1, 0)
            dk_h = dg(ds, qs[h][a:], 1, 0)
            if variant == 1:
                dq_h = dg(ds, ks[h], 0, 0)
            else:
                dq_h = dg(ks[h], ds, 0, 0)
            dk = dk_h if dk is None else dk + dk_h
            dv = dv_h if dv is None else dv + dv_h
            dq = dq_h if dq is None else dq + dq_h
        dk_ref[a:a + T, :] = (0.125 * dk).astype(jnp.bfloat16)
        dv_ref[a:a + T, :] = dv.astype(jnp.bfloat16)
        if variant == 1:
            if j == 0:
                dq_acc[...] = dq
            else:
                dq_acc[a:, :] += dq
        else:
            if j == 0:
                dq_acc[...] = dq
            else:
                dq_acc[:, a:] += dq
    res = dq_acc[...] if variant == 1 else dq_acc[...].T
    dq_ref[...] = (0.125 * res).astype(jnp.bfloat16)


def attend_back(projected, merged, grad_merged, lse, variant=2):
    L = projected.shape[0]
    b = lambda off: pl.BlockSpec((L, 128), lambda h: (0, off + h))
    return pl.pallas_call(
        functools.partial(bwd_kernel, variant),
        grid=(6,),
        in_specs=[b(0), b(6), b(12), b(0), b(0), pl.BlockSpec((1, 8, L), lambda h: (h, 0, 0))],
        out_specs=[b(0)] * 3,
        out_shape=[jax.ShapeDtypeStruct((L, 768), jnp.bfloat16)] * 3,
        scratch_shapes=[pltpu.VMEM((L, 128) if variant == 1 else (128, L), jnp.float32)],
        compiler_params=pltpu.CompilerParams(vmem_limit_bytes=48 * 2**20),
        name="attend_backward",
    )(projected, projected, projected, merged, grad_merged, lse)


def lowered(values):
    return values.astype(jnp.bfloat16)


def product(left, right, ca=1, cb=0):
    return lax.dot_general(left, right, (((ca,), (cb,)), ((), ())), preferred_element_type=jnp.float32)


def rms_scale(values):
    return lax.rsqrt(jnp.mean(values * values, axis=-1, keepdims=True) + 1e-06)


def rms_back(values, gain, grad):
    r = rms_scale(values)
    unit = values * r
    scaled = grad * gain
    back = r * (scaled - unit * jnp.mean(scaled * unit, axis=-1, keepdims=True))
    return back, jnp.sum(grad * unit, axis=0)


def gelu_and_slope(u):
    k = 0.7978845608028654
    t = jnp.tanh(k * (u + 0.044715 * u * u * u))
    half = 0.5 * (1.0 + t)
    return u * half, half + 0.5 * u * (1.0 - t * t) * k * (1.0 + 3 * 0.044715 * u * u)


def block_forward(hidden, params):
    gain_attn, qkv, out, gain_mlp, up, down = params
    normed = lowered(hidden * rms_scale(hidden) * gain_attn)
    projected = lowered(product(normed, qkv))
    merged, lse = attend(projected)
    branch = product(merged, out)
    middle = hidden + branch
    normed_mlp = lowered(middle * rms_scale(middle) * gain_mlp)
    inner_pre = product(normed_mlp, up)
    active = lowered(gelu_and_slope(inner_pre)[0])
    result = branch + product(active, down)
    return result, (hidden, normed, projected, merged, lse, middle, normed_mlp, inner_pre, active)


def block_backward(saved, params, grad_result):
    gain_attn, qkv, out, gain_mlp, up, down = params
    hidden, normed, projected, merged, lse, middle, normed_mlp, inner_pre, active = saved
    grad_low = lowered(grad_result)
    grad_active = product(grad_low, down, 1, 1)
    grad_down = lowered(product(active, grad_low, 0, 0))
    grad_inner = lowered(grad_active * gelu_and_slope(inner_pre)[1])
    grad_normed_mlp = product(grad_inner, up, 1, 1)
    grad_up = lowered(product(normed_mlp, grad_inner, 0, 0))
    grad_middle, grad_gain_mlp = rms_back(middle, gain_mlp, grad_normed_mlp)
    grad_branch = lowered(grad_result + grad_middle)
    grad_merged = lowered(product(grad_branch, out, 1, 1))
    grad_out = lowered(product(merged, grad_branch, 0, 0))
    grad_projected = jnp.concatenate(attend_back(projected, merged, grad_merged, lse), axis=1)
    grad_normed = product(grad_projected, qkv, 1, 1)
    grad_qkv = lowered(product(normed, grad_projected, 0, 0))
    grad_hidden, grad_gain_attn = rms_back(hidden, gain_attn, grad_normed)
    return grad_hidden + grad_middle, (grad_gain_attn, grad_qkv, grad_out, grad_gain_mlp, grad_up, grad_down)


def parts_of(values, count):
    pieces = []
    for _ in range(count):
        piece = lowered(values)
        pieces.append(piece)
        values = values - piece.astype(jnp.float32)
    return pieces


def pack_vectors(vectors):
    row = jnp.concatenate([v.astype(jnp.bfloat16) for v in vectors])
    return jnp.zeros((16, 128), jnp.bfloat16).at[0, : row.shape[0]].set(row)


def unpack_vectors(tiles, count, size, outer, inner):
    rows = tiles.reshape(inner, 16, outer, 128)[:, 0].transpose(1, 0, 2)
    each = size // (outer * inner)
    return [rows[:, :, j * each : (j + 1) * each].reshape(size) for j in range(count)]


def spread_vectors(vectors, outer, inner):
    each = [v.reshape(outer, inner, -1) for v in vectors]
    rows = lowered(jnp.concatenate(each, axis=2)).transpose(1, 0, 2)
    rows = jnp.pad(rows, ((0, 0), (0, 0), (0, 128 - rows.shape[2])))
    tiles = jnp.pad(rows[:, None], ((0, 0), (0, 15), (0, 0), (0, 0)))
    return tiles.reshape(inner * 16, outer * 128)


def fits(shards, outer, inner):
    return outer == 2 and inner == 16 and all(s[0] % 16 == 0 and s[1] % 128 == 0 for s in shards)


def per_device(outer, inner, *args):
    hidden, cotangent, capacity_class, token_index = args[:4]
    (gain_attn_a, qkv_a, out_a, gain_mlp_a, up_a, down_a, router_shard,
     gain_attn_b, qkv_b, out_b, gain_mlp_b, up_b, down_b) = args[4:]
    hidden, cotangent, seq_class, index = hidden[0], cotangent[0], capacity_class[0], token_index[0]
    length, width = hidden.shape
    vectors = (gain_attn_a, gain_mlp_a, router_shard, gain_attn_b, gain_mlp_b)
    shards = [qkv_a, out_a, up_a, down_a, pack_vectors(vectors), qkv_b, out_b, up_b, down_b]
    remote = fits([s.shape for s in shards], outer, inner)
    if remote:
        whole = gather_all(shards, outer, inner)
    else:
        whole = [lax.all_gather(lax.all_gather(s, "inner", axis=0, tiled=True), "outer", axis=1, tiled=True) for s in shards]
    gains = [v.astype(jnp.float32) for v in unpack_vectors(whole[4], 5, width, outer, inner)]
    params_a = (gains[0], whole[0], whole[1], gains[1], whole[2], whole[3])
    router = gains[2]
    params_b = (gains[3], whole[5], whole[6], gains[4], whole[7], whole[8])

    slots = index.shape[0]
    capacity = (length // 8) << seq_class
    spot = jnp.where(lax.iota(jnp.int32, slots) < capacity, index, -1)
    pick = lowered(spot[:, None] == lax.broadcasted_iota(jnp.int32, (slots, length), 1))

    def put(rows):
        return sum(product(pick, piece, 0, 0) for piece in parts_of(rows, 3))

    def take(rows):
        return sum(product(pick, piece) for piece in parts_of(rows, 3))

    sequence = hidden.astype(jnp.float32)
    picked = product(pick, hidden)
    gate = jax.nn.sigmoid(jnp.sum(picked * router, axis=-1))[:, None]
    change, saved_a = block_forward(picked, params_a)
    middle = sequence + put(gate * change)
    result, saved_b = block_forward(middle, params_b)
    output = lowered(middle + result)

    upstream = cotangent.astype(jnp.float32)
    grad_middle, grads_b = block_backward(saved_b, params_b, upstream)
    grad_middle = upstream + grad_middle
    grad_rows = take(grad_middle)
    grad_picked, grads_a = block_backward(saved_a, params_a, gate * grad_rows)
    grad_logits = jnp.sum(grad_rows * change, axis=-1, keepdims=True) * gate * (1.0 - gate)
    grad_router = jnp.sum(grad_logits * picked, axis=0)
    input_grad = grad_middle + put(grad_picked + grad_logits * router)

    spread = spread_vectors((grads_a[0], grads_a[3], grad_router, grads_b[0], grads_b[3]), outer, inner)
    sums = [grads_a[1], grads_a[2], grads_a[4], grads_a[5], spread, grads_b[1], grads_b[2], grads_b[4], grads_b[5]]
    if remote:
        done = scatter_all(sums, outer, inner)
    else:
        done = [
            lax.psum_scatter(
                lax.psum_scatter(s, "outer", scatter_dimension=1, tiled=True), "inner", scatter_dimension=0, tiled=True
            ).astype(jnp.float32)
            for s in sums
        ]
    each = gain_attn_a.shape[0]
    vec = [done[4][0, j * each : (j + 1) * each] for j in range(5)]
    return (output[None], input_grad[None], vec[0], done[0], done[1], vec[1], done[2], done[3], vec[2],
            vec[3], done[5], done[6], vec[4], done[7], done[8])


def solution(mesh):
    outer, inner = mesh.shape["outer"], mesh.shape["inner"]
    both = ("outer", "inner")
    rows, vector, matrix = P(both, None, None), P(both), P("inner", "outer")
    block = (vector, matrix, matrix, vector, matrix, matrix)
    return jax.shard_map(
        functools.partial(per_device, outer, inner),
        mesh=mesh,
        in_specs=(rows, rows, vector, P(both, None)) + block + (vector,) + block,
        out_specs=(rows, rows) + block + (vector,) + block,
        check_vma=False,
    )
```

```python
import functools

import jax
import jax.numpy as jnp
from jax import lax
from jax.experimental import pallas as pl
from jax.experimental.pallas import tpu as pltpu
from jax.sharding import PartitionSpec as P

MESH = pl.DeviceIdType.MESH


def place():
    o, i = lax.axis_index("outer"), lax.axis_index("inner")
    return o, i // 4, (i // 2) % 2, i % 2


def device(o, z, x, c):
    return (o, z * 4 + x * 2 + c)


def greet(o, z, x, c):
    barrier = pltpu.get_barrier_semaphore()
    signal = functools.partial(pl.semaphore_signal, barrier, inc=1, device_id_type=MESH)
    signal(device_id=device(1 - o, z, x, c))
    signal(device_id=device(o, z, 1 - x, c))
    signal(device_id=device(o, z, x, 1 - c))

    @pl.when(z > 0)
    def _():
        signal(device_id=device(o, z - 1, x, c))

    @pl.when(z < 3)
    def _():
        signal(device_id=device(o, z + 1, x, c))

    pl.semaphore_wait(barrier, 3 + jnp.where(z > 0, 1, 0) + jnp.where(z < 3, 1, 0))


def scatter_kernel(n, *refs):
    grads, outs = refs[:n], refs[n:2 * n]
    rest = refs[2 * n:]
    own, got_c, got_b, got_a, got_z = (rest[j * n:(j + 1) * n] for j in range(5))
    local_sem, send_sem, recv_sem = rest[5 * n:]
    o, z, x, c = place()
    greet(o, z, x, c)

    def block(p, s, cc):
        r, w = outs[p].shape
        bs, as_, k = s // 8, (s // 4) % 2, s % 4
        if p % 2 == 0:
            co, cx = jnp.where(bs == 1, o, 1 - o), jnp.where(as_ == 1, x, 1 - x)
        else:
            cx, co = jnp.where(bs == 1, x, 1 - x), jnp.where(as_ == 1, o, 1 - o)
        row = pl.multiple_of((k * 4 + cx * 2 + cc) * r, 16)
        col = pl.multiple_of(co * w, 128)
        return grads[p].at[pl.ds(row, r), pl.ds(col, w)]

    def a_dev(p):
        return device(o, z, 1 - x, c) if p % 2 == 0 else device(1 - o, z, x, c)

    def b_dev(p):
        return device(1 - o, z, x, c) if p % 2 == 0 else device(o, z, 1 - x, c)

    def send(p, src, dst, kind, rslot, target):
        return pltpu.make_async_remote_copy(
            src_ref=src, dst_ref=dst, send_sem=send_sem.at[p, kind], recv_sem=recv_sem.at[p, rslot],
            device_id=target, device_id_type=MESH)

    def wait(ref, sem):
        pltpu.make_async_copy(ref, ref, sem).wait()

    def loop(count, body):
        def step(s, carry):
            body(s)
            return carry
        lax.fori_loop(0, count, step, 0)

    def begin(p):
        def body(s):
            send(p, block(p, s, 1 - c), got_c[p].at[s], 0, s, device(o, z, x, 1 - c)).start()
            pltpu.make_async_copy(block(p, s, c), own[p].at[s], local_sem.at[p]).start()
        loop(16, body)

    def core_stage(p):
        wait(own[p], local_sem.at[p])

        def body(s):
            wait(got_c[p].at[s], recv_sem.at[p, s])
            own[p][s] = own[p][s] + got_c[p][s]

            @pl.when(s < 8)
            def _():
                send(p, own[p].at[s], got_b[p].at[s], 1, 16 + s, b_dev(p)).start()
        loop(16, body)

    def b_stage(p):
        def body(j):
            wait(got_b[p].at[j], recv_sem.at[p, 16 + j])
            own[p][8 + j] = own[p][8 + j] + got_b[p][j]

            @pl.when(j < 4)
            def _():
                send(p, own[p].at[8 + j], got_a[p].at[j], 2, 24 + j, a_dev(p)).start()
        loop(8, body)

    def send_z(p, k, step):
        t = z + step
        slot = jnp.where(k == t, jnp.where(step > 0, k, 4), k)
        send(p, own[p].at[12 + k], got_z[p].at[slot], 3, 28 + slot, device(o, t, x, c)).start()

    def a_stage(p):
        def body(k):
            wait(got_a[p].at[k], recv_sem.at[p, 24 + k])
            own[p][12 + k] = own[p][12 + k] + got_a[p][k]
        loop(4, body)

        @pl.when(z == 0)
        def _():
            for k in (3, 2, 1):
                send_z(p, k, 1)

        @pl.when(z == 3)
        def _():
            for k in (0, 1, 2):
                send_z(p, k, -1)

    def pass_on(p, k, step):
        wait(got_z[p].at[k], recv_sem.at[p, 28 + k])
        own[p][12 + k] = own[p][12 + k] + got_z[p][k]
        send_z(p, k, step)

    def z_stage(p, level):
        @pl.when(z == level)
        def _():
            for k in range(3, level, -1):
                pass_on(p, k, 1)

        @pl.when(z == 3 - level)
        def _():
            for k in range(0, 3 - level):
                pass_on(p, k, -1)

    def last(p):
        outs[p][...] = own[p][12 + z].astype(jnp.float32)

        @pl.when(z > 0)
        def _():
            wait(got_z[p].at[z], recv_sem.at[p, 28 + z])
            outs[p][...] += got_z[p][z].astype(jnp.float32)

        @pl.when(z < 3)
        def _():
            wait(got_z[p].at[4], recv_sem.at[p, 32])
            outs[p][...] += got_z[p][4].astype(jnp.float32)

        wait(own[p], send_sem.at[p, 0])
        wait(got_b[p], send_sem.at[p, 1])
        wait(got_a[p], send_sem.at[p, 2])
        wait(got_a[p].at[pl.ds(0, 3)], send_sem.at[p, 3])

    for p in range(n):
        begin(p)
    stages = [core_stage, b_stage, a_stage, lambda p: z_stage(p, 1), lambda p: z_stage(p, 2), last]
    for t in range(n + len(stages) - 1):
        for lag, stage in enumerate(stages):
            if 0 <= t - lag < n:
                stage(t - lag)


def scatter_all(grads, outer, inner, collective_id=1):
    n = len(grads)
    outs = [jax.ShapeDtypeStruct((g.shape[0] // inner, g.shape[1] // outer), jnp.float32) for g in grads]
    bufs = [pltpu.VMEM((m,) + s.shape, jnp.bfloat16) for m in (16, 16, 8, 4, 5) for s in outs]
    return pl.pallas_call(
        functools.partial(scatter_kernel, n),
        out_shape=outs,
        in_specs=[pl.BlockSpec(memory_space=pl.ANY)] * n,
        out_specs=[pl.BlockSpec(memory_space=pltpu.VMEM)] * n,
        scratch_shapes=bufs + [pltpu.SemaphoreType.DMA((n,)), pltpu.SemaphoreType.DMA((n, 4)), pltpu.SemaphoreType.DMA((n, 33))],
        compiler_params=pltpu.CompilerParams(collective_id=collective_id, has_side_effects=True, vmem_limit_bytes=60 * 2**20),
        name="scatter_gradients",
    )(*grads)


def gather_kernel(n, *refs):
    shards, outs = refs[:n], refs[n:2 * n]
    local_sem, send_sem, recv_sem = refs[2 * n:]
    o, z, x, c = place()

    greet(o, z, x, c)

    def block(p, co, cz, cx, cc):
        r, w = shards[p].shape
        row = pl.multiple_of((cz * 4 + cx * 2 + cc) * r, 16)
        col = pl.multiple_of(co * w, 128)
        return outs[p].at[pl.ds(row, r), pl.ds(col, w)]

    def send(p, src, dst, slot, rslot, target):
        return pltpu.make_async_remote_copy(
            src_ref=src, dst_ref=dst, send_sem=send_sem.at[p, slot], recv_sem=recv_sem.at[p, rslot],
            device_id=target, device_id_type=MESH)

    def up(p, k, src=None):
        b = block(p, o, k, x, c)
        return send(p, b if src is None else src, b, k, k, device(o, z + 1, x, c))

    def down(p, k, src=None):
        b = block(p, o, k, x, c)
        return send(p, b if src is None else src, b, 4 + k, k, device(o, z - 1, x, c))

    def first(p, k, src=None):
        b = block(p, o, k, x, c)
        t = device(o, z, 1 - x, c) if p % 2 == 0 else device(1 - o, z, x, c)
        return send(p, b if src is None else src, b, 8 + k, 4 + k, t)

    def second(p, k, a, src=None):
        if p % 2 == 0:
            b, t = block(p, o, k, a, c), device(1 - o, z, x, c)
        else:
            b, t = block(p, a, k, x, c), device(o, z, 1 - x, c)
        return send(p, b if src is None else src, b, 12 + 2 * k + a, 8 + 2 * k + a, t)

    def core(p, co, k, cx, src=None):
        b = block(p, co, k, cx, c)
        s = k * 4 + co * 2 + cx
        return send(p, b if src is None else src, b, 20 + s, 16 + s, device(o, z, x, 1 - c))

    def mine(p):
        return x if p % 2 == 0 else o

    def coords(p, k, a, b):
        return (b, k, a) if p % 2 == 0 else (a, k, b)

    def core_ab(p, k, a, b, src=None):
        co, ck, cx = coords(p, k, a, b)
        return core(p, co, ck, cx, src)

    def other(p):
        return o if p % 2 == 0 else x

    def own(p):
        s = shards[p]
        pltpu.make_async_copy(s, block(p, o, z, x, c), local_sem.at[p]).start()

        @pl.when(z < 3)
        def _():
            up(p, z, s).start()

        @pl.when(z > 0)
        def _():
            down(p, z, s).start()

        first(p, z, s).start()
        second(p, z, mine(p), s).start()
        core(p, o, z, x, s).start()

    def wait_block(p, rslot):
        b = block(p, o, z, x, c)
        pltpu.make_async_copy(shards[p], b, recv_sem.at[p, rslot]).wait()

    def z_phase(p):
        for d in range(1, 4):
            @pl.when(z >= d)
            def _():
                k = z - d
                wait_block(p, k)

                @pl.when(z < 3)
                def _():
                    up(p, k).start()

                first(p, k).start()
                second(p, k, mine(p)).start()
                core(p, o, k, x).start()

            @pl.when(z + d <= 3)
            def _():
                k = z + d
                wait_block(p, k)

                @pl.when(z > 0)
                def _():
                    down(p, k).start()

                first(p, k).start()
                second(p, k, mine(p)).start()
                core(p, o, k, x).start()

    def ks():
        return [(z + d) % 4 for d in range(4)]

    def a_phase(p):
        for k in ks():
            wait_block(p, 4 + k)
            a = 1 - mine(p)
            second(p, k, a).start()
            core_ab(p, k, a, other(p)).start()

    def b_phase(p):
        for k in ks():
            for a in (mine(p), 1 - mine(p)):
                wait_block(p, 8 + 2 * k + a)
                core_ab(p, k, a, 1 - other(p)).start()

    def c_phase(p):
        for s in range(16):
            wait_block(p, 16 + s)

    def ends(p):
        pltpu.make_async_copy(shards[p], block(p, o, z, x, c), local_sem.at[p]).wait()

        def done(slot):
            pltpu.make_async_copy(shards[p], block(p, o, z, x, c), send_sem.at[p, slot]).wait()

        for k in range(4):
            @pl.when(jnp.logical_and(z < 3, k <= z))
            def _():
                done(k)

            @pl.when(jnp.logical_and(z > 0, k >= z))
            def _():
                done(4 + k)
        for slot in range(8, 36):
            done(slot)

    own(0)
    for t in range(n + 3):
        if t + 1 < n:
            own(t + 1)
        if t < n:
            z_phase(t)
        if 0 <= t - 1 < n:
            a_phase(t - 1)
        if 0 <= t - 2 < n:
            b_phase(t - 2)
    for p in range(n):
        c_phase(p)
        ends(p)


def gather_all(shards, outer, inner, collective_id=0):
    n = len(shards)
    outs = [jax.ShapeDtypeStruct((s.shape[0] * inner, s.shape[1] * outer), s.dtype) for s in shards]
    return pl.pallas_call(
        functools.partial(gather_kernel, n),
        out_shape=outs,
        in_specs=[pl.BlockSpec(memory_space=pl.ANY)] * n,
        out_specs=[pl.BlockSpec(memory_space=pl.ANY)] * n,
        scratch_shapes=[pltpu.SemaphoreType.DMA((n,)), pltpu.SemaphoreType.DMA((n, 36)), pltpu.SemaphoreType.DMA((n, 32))],
        compiler_params=pltpu.CompilerParams(collective_id=collective_id, has_side_effects=True),
        name="gather_weights",
    )(*shards)


D = 768
SCALE = 0.125 * 1.4426950408889634
ROWS = 256
VMEM_BYTES = 63 * 2**20


def mul(a, b, ca=1, cb=0):
    return lax.dot_general(a, b, (((ca,), (cb,)), ((), ())), preferred_element_type=jnp.float32)


def low(v):
    return v.astype(jnp.bfloat16)


def cols(j):
    return pl.ds(pl.multiple_of(j * D, D), D)


def rms_scale(v):
    return lax.rsqrt(jnp.mean(v * v, axis=-1, keepdims=True) + 1e-06)


def rms_back(v, gain, grad):
    r = rms_scale(v)
    unit = v * r
    scaled = grad * gain
    back = r * (scaled - unit * jnp.mean(scaled * unit, axis=-1, keepdims=True))
    return back, jnp.sum((grad * unit).reshape(-1, 8, v.shape[-1]), axis=0)


def gelu_and_slope(u):
    k = 0.7978845608028654
    square = u * u
    t = jnp.tanh(u * (k + k * 0.044715 * square))
    half = 0.5 + 0.5 * t
    return u * half, half + u * (0.5 - 0.5 * t * t) * (k + 3 * 0.044715 * k * square)


def halves(v):
    lane = lax.broadcasted_iota(jnp.int32, v.shape, 1)
    zero = jnp.zeros_like(v)
    return jnp.where(lane < 64, v, zero), jnp.where(lane < 64, zero, v)


def two(v):
    first = low(v)
    return first, low(v - first.astype(jnp.float32))


class Block:
    def __init__(self, rows, refs):
        self.rows = rows
        self.__dict__.update(refs)

    @staticmethod
    def scratch(rows):
        f32, b16 = jnp.float32, jnp.bfloat16
        return dict(
            branch=((rows, D), f32), projected=((rows, 3 * D), b16), merged=((rows, D), b16), lse=((6, 8, rows), f32),
            active=((rows, 4 * D), b16), slope=((rows, 4 * D), b16), normed=((rows, D), b16), normed_mlp=((rows, D), b16))

    def tiles(self):
        return [slice(i, i + ROWS) for i in range(0, self.rows, ROWS)]

    def norm(self):
        for t in self.tiles():
            x = self.x[t]
            self.normed[t] = low(x * rms_scale(x) * self.gain_attn[...])

    def project(self, j):
        c = cols(j)
        self.projected[:, c] = low(mul(self.normed[...], self.qkv[:, c]))

    def pair(self, ref, part, pair, rows=slice(None)):
        return ref[rows, pl.ds(pl.multiple_of(part * D + pair * 128, 128), 128)]

    def attend(self, pair):
        v0, v1 = halves(self.pair(self.projected, 2, pair))
        causal = lax.broadcasted_iota(jnp.int32, (ROWS, ROWS), 1) >= lax.broadcasted_iota(jnp.int32, (ROWS, ROWS), 0)
        for t in self.tiles():
            n = t.stop
            qs = halves(self.pair(self.projected, 0, pair, t))
            k = self.pair(self.projected, 1, pair, slice(0, n))
            total = None
            for h in range(2):
                s = mul(k, qs[h], 1, 1)
                last = jnp.where(causal, s[t.start:], -1e30)
                s = last if t.start == 0 else jnp.concatenate([s[: t.start], last], axis=0)
                m = jnp.max(s, axis=0, keepdims=True) * SCALE
                p = jnp.exp2(s * SCALE - m)
                l = jnp.sum(p, axis=0, keepdims=True)
                self.lse[pair, h : h + 1, t] = m + jnp.log2(l)
                o = mul(low(p * (1.0 / l)), (v0, v1)[h][:n], 0, 0)
                total = o if total is None else total + o
            self.merged[t, pl.ds(pl.multiple_of(pair * 128, 128), 128)] = low(total)

    def join(self):
        for t in self.tiles():
            branch = mul(self.merged[t], self.out[...])
            self.branch[t] = branch
            middle = self.x[t] + branch
            self.normed_mlp[t] = low(middle * rms_scale(middle) * self.gain_mlp[...])

    def widen(self, j):
        c = cols(j)
        for t in self.tiles():
            active, slope = gelu_and_slope(mul(self.normed_mlp[t], self.up[:, c]))
            self.active[t, c] = low(active)
            self.slope[t, c] = low(slope)

    def narrow(self, t):
        return mul(self.active[t], self.down[...])

    def back_wide(self, j):
        c = cols(j)
        for t in self.tiles():
            grad = mul(self.grad_low[t], self.down[c, :], 1, 1)
            self.slope[t, c] = low(grad * self.slope[t, c].astype(jnp.float32))

    def grad_down(self, j):
        return low(mul(self.active[:, cols(j)], self.grad_low[...], 0, 0))

    def grad_up(self, j):
        return low(mul(self.normed_mlp[...], self.slope[:, cols(j)], 0, 0))

    def back_mlp(self, grad_of):
        total = jnp.zeros((8, D), jnp.float32)
        for t in self.tiles():
            grad = mul(self.slope[t], self.up[...], 1, 1)
            back, gain = rms_back(self.x[t] + self.branch[t], self.gain_mlp[...], grad)
            total = total + gain
            self.branch[t] = back
            self.normed_mlp[t] = low(grad_of(t) + back)
        return jnp.sum(total, axis=0, keepdims=True)

    def grad_out(self):
        return low(mul(self.merged[...], self.normed_mlp[...], 0, 0))

    def back_merged(self):
        self.active[:, :D] = low(mul(self.normed_mlp[...], self.out[...], 1, 1))

    def attend_back(self, pair, turned):
        rows = self.rows
        q, do = self.pair(self.projected, 0, pair), self.pair(self.active, 0, pair)
        qs, dos = halves(q), halves(do)
        dd = do.astype(jnp.float32) * self.pair(self.merged, 0, pair).astype(jnp.float32)
        pick = lax.broadcasted_iota(jnp.int32, (8, 128), 0) == lax.broadcasted_iota(jnp.int32, (8, 128), 1) // 64
        delta = lax.dot_general(pick.astype(jnp.float32), dd, (((1,), (1,)), ((), ())), precision=lax.Precision.HIGHEST,
                                preferred_element_type=jnp.float32)
        causal = lax.broadcasted_iota(jnp.int32, (ROWS, ROWS), 1) >= lax.broadcasted_iota(jnp.int32, (ROWS, ROWS), 0)
        for t in self.tiles():
            a = t.start
            ks, vs = halves(self.pair(self.projected, 1, pair, t)), halves(self.pair(self.projected, 2, pair, t))
            dk = dv = dq = 0.0
            for h in range(2):
                s = mul(ks[h], q[a:], 1, 1)
                p = jnp.exp2(s * SCALE - self.lse[pair, h : h + 1, a:])
                first = jnp.where(causal, p[:, :ROWS], 0.0)
                p = first if t.stop == rows else jnp.concatenate([first, p[:, ROWS:]], axis=1)
                dp = mul(vs[h], do[a:], 1, 1)
                ds = low(p * (dp - delta[h : h + 1, a:]))
                dv = dv + mul(low(p), dos[h][a:])
                dk = dk + mul(ds, qs[h][a:])
                dq = dq + mul(ks[h], ds, 0, 0)
            lanes = pl.multiple_of(pair * 128, 128)
            self.projected[t, pl.ds(D + lanes, 128)] = low(0.125 * dk)
            self.projected[t, pl.ds(2 * D + lanes, 128)] = low(dv)
            if a == 0:
                turned[:, :rows] = dq
            else:
                turned[:, a:rows] += dq
        self.projected[:, pl.ds(lanes, 128)] = low(0.125 * turned[:, :rows].T)

    def grad_qkv(self, j):
        return low(mul(self.normed[...], self.projected[:, cols(j)], 0, 0))

    def back_norm(self, finish):
        total = jnp.zeros((8, D), jnp.float32)
        for t in self.tiles():
            grad = mul(self.projected[t], self.qkv[...], 1, 1)
            back, gain = rms_back(self.x[t], self.gain_attn[...], grad)
            total = total + gain
            finish(t, back + self.branch[t])
        return jnp.sum(total, axis=0, keepdims=True)


SAVED = ("branch", "projected", "merged", "lse", "active", "slope", "normed", "normed_mlp")


def run(steps, hooks=None):
    at = 0
    for count, body in steps:
        if count == 0:
            body(0)
            continue
        after = [hooks[at + k] if hooks else [] for k in range(count)]
        at += count
        if count == 1:
            body(0)
            for f in after[0]:
                f()
            continue

        @pl.loop(0, count)
        def _(j):
            body(j)
            for k in range(count):
                if after[k]:
                    @pl.when(j == k)
                    def _():
                        for f in after[k]:
                            f()


class Loads:
    def __init__(self, pairs, sems):
        self.copies = {k: pltpu.make_async_copy(a, b, sems.at[j]) for j, (k, a, b) in enumerate(pairs)}
        for c in self.copies.values():
            c.start()

    def need(self, *names):
        for n in names:
            self.copies[n].wait()


class Ship:
    def __init__(self, stage, sems):
        self.stage, self.sems = stage, sems

    def wait(self, slot):
        pltpu.make_async_copy(self.stage.at[slot], self.stage.at[slot], self.sems.at[slot]).wait()

    def send(self, slot, value, target, busy):
        if busy is True:
            self.wait(slot)
        elif busy is not False:
            pl.when(busy)(lambda: self.wait(slot))
        self.stage[slot] = value
        pltpu.make_async_copy(self.stage.at[slot], target, self.sems.at[slot]).start()


def backward_steps(b, grad_of, ship, targets, vec, finish, turned):
    gqkv, gout, gup, gdown = targets

    def wide(j):
        b.back_wide(j)
        ship.send(0, b.grad_down(j), gdown.at[cols(j), :], j > 0)
        ship.send(1, b.grad_up(j), gup.at[:, cols(j)], j > 0)

    def mlp(_):
        vec(1, b.back_mlp(grad_of))

    def out(_):
        ship.send(0, b.grad_out(), gout, True)
        b.back_merged()

    def qkv(j):
        @pl.when(j == 0)
        def _():
            ship.wait(0)
        ship.send(1, b.grad_qkv(j), gqkv.at[:, cols(j)], True)

    def norm(_):
        vec(0, b.back_norm(finish))
        ship.wait(1)

    return [(4, wide), (1, mlp), (1, out), (6, lambda j: b.attend_back(j, turned)), (3, qkv), (1, norm)]


def dense_kernel(x_hbm, cot_hbm, vec_ref, qkv_hbm, out_hbm, up_hbm, down_hbm,
                 y_hbm, grad_hbm, gvec_ref, gqkv_hbm, gout_hbm, gup_hbm, gdown_hbm,
                 x, cot, qkv, out, up, down, y, turned, stage, load_sem, stage_sem, row_sem, *kept):
    loads = Loads((("x", x_hbm, x), ("qkv", qkv_hbm, qkv), ("out", out_hbm, out), ("up", up_hbm, up),
                   ("down", down_hbm, down), ("cot", cot_hbm, cot)), load_sem)
    b = Block(x.shape[0], dict(zip(SAVED, kept), x=x, grad_low=cot, qkv=qkv, out=out, up=up, down=down,
                               gain_attn=vec_ref.at[3:4], gain_mlp=vec_ref.at[4:5]))

    def norm(_):
        loads.need("x")
        b.norm()
        loads.need("qkv")

    def join(_):
        loads.need("out")
        b.join()
        loads.need("up")

    def narrow(_):
        loads.need("down", "cot")
        for t in b.tiles():
            y[t] = low(x[t] + b.branch[t] + b.narrow(t))
        pltpu.make_async_copy(y, y_hbm, row_sem.at[0]).start()

    def vec(j, value):
        gvec_ref[j : j + 1] = value

    def finish(t, grad):
        x[t] = grad + cot[t].astype(jnp.float32)
        pltpu.make_async_copy(x.at[t], grad_hbm.at[t], row_sem.at[1]).start()

    run([(1, norm), (3, b.project), (6, b.attend), (1, join), (4, b.widen), (1, narrow)]
        + backward_steps(b, lambda t: cot[t].astype(jnp.float32), Ship(stage, stage_sem),
                         (gqkv_hbm, gout_hbm, gup_hbm, gdown_hbm), vec, finish, turned))
    pltpu.make_async_copy(y, y_hbm, row_sem.at[0]).wait()
    pltpu.make_async_copy(x, grad_hbm, row_sem.at[1]).wait()


def shape(*dims, dtype=jnp.bfloat16):
    return jax.ShapeDtypeStruct(dims, dtype)


def any_specs(n):
    return [pl.BlockSpec(memory_space=pl.ANY)] * n


def vmem_specs(n):
    return [pl.BlockSpec(memory_space=pltpu.VMEM)] * n


WEIGHTS = [((D, 3 * D), jnp.bfloat16), ((D, D), jnp.bfloat16), ((D, 4 * D), jnp.bfloat16), ((4 * D, D), jnp.bfloat16)]


def buffers(*pairs):
    return [pltpu.VMEM(dims, dtype) for dims, dtype in pairs]


def kept_buffers(rows):
    s = Block.scratch(rows)
    return [s[k] for k in SAVED]


def dense_block(x, cot, vec, weights):
    rows = x.shape[0]
    f32, b16 = jnp.float32, jnp.bfloat16
    return pl.pallas_call(
        dense_kernel,
        in_specs=any_specs(2) + vmem_specs(1) + any_specs(4),
        out_specs=any_specs(2) + vmem_specs(1) + any_specs(4),
        out_shape=[shape(rows, D), shape(rows, D, dtype=f32), shape(2, D, dtype=f32)] + [shape(*s) for s, _ in WEIGHTS],
        scratch_shapes=buffers(((rows, D), f32), ((rows, D), b16), *WEIGHTS, ((rows, D), b16), ((128, rows), f32), ((2, D, D), b16))
        + [pltpu.SemaphoreType.DMA((6,)), pltpu.SemaphoreType.DMA((2,)), pltpu.SemaphoreType.DMA((2,))]
        + buffers(*kept_buffers(rows)),
        compiler_params=pltpu.CompilerParams(vmem_limit_bytes=VMEM_BYTES),
        name="dense_block",
    )(x, cot, vec, *weights)


def spots(length, spot_ref):
    at = lax.broadcasted_iota(jnp.int32, (length, spot_ref.shape[1]), 0)
    return low(jnp.where(at == spot_ref[...], 1.0, 0.0))


def lane_map(outer, inner):
    each = D // (outer * inner)
    d = jnp.arange(D, dtype=jnp.int32)
    return jnp.stack([d // each % inner, d // (each * inner) * 128 + d % each])


def spread_map(tiles_columns, map_ref):
    at = lax.broadcasted_iota(jnp.int32, (tiles_columns, D), 0)
    return low(jnp.where(at == map_ref[1:2], 1.0, 0.0))


def read_vectors(tiles, map_ref):
    rows, columns = tiles.shape
    every = mul(tiles[...], spread_map(columns, map_ref))
    inner = lax.broadcasted_iota(jnp.int32, (rows, D), 0) // 16
    return jnp.sum(jnp.where(inner == map_ref[0:1], every, 0.0).reshape(rows // 16, 16, D), axis=0)


def write_vectors(vectors, rows, columns, map_ref):
    every = jnp.broadcast_to(vectors[None], (rows // 16, 16, D)).reshape(rows, D)
    inner = lax.broadcasted_iota(jnp.int32, (rows, D), 0) // 16
    return low(mul(low(jnp.where(inner == map_ref[0:1], every, 0.0)), spread_map(columns, map_ref), 1, 1))


def gate_of(x, router):
    return jax.nn.sigmoid(jnp.sum(x * router, axis=-1, keepdims=True))


def routed_forward_steps(b, need, hidden, spot_ref, chosen, vec_ref, extra, middle_hbm, middle_sem, keep):
    length = hidden.shape[0]

    def pick(_):
        chosen[...] = spots(length, spot_ref)
        need("hidden")
        for t in b.tiles():
            b.x[t] = mul(chosen[:, t], hidden[...], 0, 0)
        need("vectors")
        b.norm()
        keep("x", "normed")
        need("qkv")

    def project(j):
        b.project(j)

    def join(_):
        keep("projected", "merged", "lse")
        need("out")
        b.join()
        keep("branch", "normed_mlp")
        need("up")

    def narrow(_):
        keep("active", "slope")
        need("down")
        for t in b.tiles():
            extra[t] = b.branch[t] + b.narrow(t)
        keep("change")

    def put(_):
        rows = [gate_of(b.x[t], vec_ref[2:3]) * extra[t] for t in b.tiles()]
        pieces = [two(r) for r in rows]
        for i in range(0, length, ROWS):
            t = slice(i, i + ROWS)
            total = hidden[t].astype(jnp.float32)
            for piece, s in zip(pieces, b.tiles()):
                for p in piece:
                    total = total + mul(chosen[t, s], p)
            b.middle[t] = total
            pltpu.make_async_copy(b.middle.at[t], middle_hbm.at[t], middle_sem).start()

    return [(1, pick), (3, project), (6, b.attend), (1, join), (4, b.widen), (1, narrow), (1, put)]


KEPT = ("x", "change") + SAVED


def routed_forward_kernel(hidden_hbm, spot_ref, map_ref, tiles_ref, qkv_hbm, out_hbm, up_hbm, down_hbm, *rest):
    n = len(KEPT)
    middle_hbm, vec_ref = rest[:2]
    kept_hbm = dict(zip(KEPT, rest[2 : 2 + n]))
    rest = rest[2 + n :]
    hidden, chosen, middle, qkv, out, up, down, load_sem, keep_sem, middle_sem = rest[:10]
    kept = dict(zip(KEPT, rest[10:]))
    loads = Loads((("hidden", hidden_hbm, hidden), ("qkv", qkv_hbm, qkv), ("out", out_hbm, out), ("up", up_hbm, up),
                   ("down", down_hbm, down)), load_sem)

    def need(name):
        if name == "vectors":
            vec_ref[...] = read_vectors(tiles_ref, map_ref)
        else:
            loads.need(name)

    saves = {k: pltpu.make_async_copy(kept[k], kept_hbm[k], keep_sem.at[j]) for j, k in enumerate(KEPT)}

    def keep(*names):
        for k in names:
            saves[k].start()

    b = Block(spot_ref.shape[1], dict(kept, middle=middle, qkv=qkv, out=out, up=up, down=down,
                                      gain_attn=vec_ref.at[0:1], gain_mlp=vec_ref.at[1:2]))
    run(routed_forward_steps(b, need, hidden, spot_ref, chosen, vec_ref, kept["change"], middle_hbm, middle_sem, keep))
    for k in KEPT:
        saves[k].wait()
    pltpu.make_async_copy(middle, middle_hbm, middle_sem).wait()


def kept_shapes(rows):
    return [((rows, D), jnp.float32)] * 2 + kept_buffers(rows)


def routed_forward(hidden, spot, place_map, tiles, weights):
    length, rows = hidden.shape[0], spot.shape[1]
    f32, b16 = jnp.float32, jnp.bfloat16
    kept = kept_shapes(rows)
    results = pl.pallas_call(
        routed_forward_kernel,
        in_specs=any_specs(1) + vmem_specs(3) + any_specs(4),
        out_specs=any_specs(1) + vmem_specs(1) + any_specs(len(kept)),
        out_shape=[shape(length, D, dtype=f32), shape(16, D, dtype=f32)] + [shape(*s, dtype=t) for s, t in kept],
        scratch_shapes=buffers(((length, D), b16), ((length, rows), b16), ((length, D), f32), *WEIGHTS)
        + [pltpu.SemaphoreType.DMA((5,)), pltpu.SemaphoreType.DMA((len(kept),)), pltpu.SemaphoreType.DMA]
        + buffers(*kept),
        compiler_params=pltpu.CompilerParams(vmem_limit_bytes=VMEM_BYTES),
        name="routed_forward",
    )(hidden, spot, place_map, tiles, *weights)
    return results[0], results[1], results[2:]


def routed_backward_steps(b, need, grad, spot_ref, chosen, vec_ref, change, grad_rows, gate, ship, targets, vec, turned,
                          grad_hbm, grad_sem):
    length = grad.shape[0]
    router = vec_ref.at[2:3]

    def take(_):
        chosen[...] = spots(length, spot_ref)
        need("grad")
        pieces = two(grad[...])
        need("x", "change")
        for t in b.tiles():
            rows = mul(chosen[:, t], pieces[0], 0, 0) + mul(chosen[:, t], pieces[1], 0, 0)
            g = gate_of(b.x[t], router[...])
            grad_rows[t] = g * rows
            b.grad_low[t] = low(g * rows)
            logits = jnp.sum(rows * change[t], axis=-1, keepdims=True) * g * (1.0 - g)
            gate[t] = jnp.broadcast_to(logits, (ROWS, 128))
        need("down", "active", "slope", "normed_mlp")

    def finish(t, g):
        change[t] = g + gate[t, 0:1] * router[...]

    def put(_):
        pieces = [two(change[t]) for t in b.tiles()]
        for i in range(0, length, ROWS):
            t = slice(i, i + ROWS)
            total = grad[t]
            for piece, s in zip(pieces, b.tiles()):
                for p in piece:
                    total = total + mul(chosen[t, s], p)
            grad[t] = total
            pltpu.make_async_copy(grad.at[t], grad_hbm.at[t], grad_sem).start()

    def route(_):
        total = jnp.zeros((8, D), jnp.float32)
        for t in b.tiles():
            total = total + jnp.sum((gate[t, 0:1] * b.x[t]).reshape(-1, 8, D), axis=0)
        vec(2, jnp.sum(total, axis=0, keepdims=True))

    back = backward_steps(b, lambda t: grad_rows[t], ship, targets, vec, finish, turned)
    waits = [None, ("up", "branch"), ("out", "merged"), ("projected", "lse"), ("normed",), ("qkv",)]
    steps = [(1, take)]
    for (count, body), names in zip(back, waits):
        if names is not None:
            steps.append((0, lambda _, names=names: need(*names)))
        steps.append((count, body))
    return steps + [(1, route), (1, put)]


def routed_backward_kernel(grad_hbm, spot_ref, vec_ref, qkv_hbm, out_hbm, up_hbm, down_hbm, *rest):
    n = len(KEPT)
    kept_hbm, rest = rest[:n], rest[n:]
    input_hbm, gvec_ref, gqkv_hbm, gout_hbm, gup_hbm, gdown_hbm = rest[:6]
    (grad, chosen, grad_low, grad_rows, gate, turned, stage, qkv, out, up, down, load_sem, stage_sem, row_sem) = rest[6:20]
    kept = rest[20:]
    order = ("grad", "x", "change", "down", "active", "slope", "normed_mlp", "up", "branch", "out", "merged", "projected",
             "lse", "normed", "qkv")
    where = dict(zip(KEPT, zip(kept_hbm, kept)), grad=(grad_hbm, grad), qkv=(qkv_hbm, qkv), out=(out_hbm, out),
                 up=(up_hbm, up), down=(down_hbm, down))
    loads = Loads([(k,) + where[k] for k in order], load_sem)
    named = dict(zip(KEPT, kept))
    b = Block(spot_ref.shape[1], dict(named, grad_low=grad_low, qkv=qkv, out=out, up=up, down=down,
                                      gain_attn=vec_ref.at[0:1], gain_mlp=vec_ref.at[1:2]))

    def vec(j, value):
        gvec_ref[j : j + 1] = value

    run(routed_backward_steps(b, loads.need, grad, spot_ref, chosen, vec_ref, named["change"], grad_rows, gate,
                              Ship(stage, stage_sem), (gqkv_hbm, gout_hbm, gup_hbm, gdown_hbm), vec, turned,
                              input_hbm, row_sem))
    pltpu.make_async_copy(grad, input_hbm, row_sem).wait()


def routed_backward(grad, spot, vec, weights, kept):
    length, rows = grad.shape[0], spot.shape[1]
    f32, b16 = jnp.float32, jnp.bfloat16
    return pl.pallas_call(
        routed_backward_kernel,
        in_specs=any_specs(1) + vmem_specs(2) + any_specs(4 + len(kept)),
        out_specs=any_specs(1) + vmem_specs(1) + any_specs(4),
        out_shape=[shape(length, D, dtype=f32), shape(3, D, dtype=f32)] + [shape(*s) for s, _ in WEIGHTS],
        scratch_shapes=buffers(((length, D), f32), ((length, rows), b16), ((rows, D), b16), ((rows, D), f32), ((rows, 128), f32),
                               ((128, rows), f32), ((2, D, D), b16), *WEIGHTS)
        + [pltpu.SemaphoreType.DMA((15,)), pltpu.SemaphoreType.DMA((2,)), pltpu.SemaphoreType.DMA]
        + buffers(*kept_shapes(rows)),
        compiler_params=pltpu.CompilerParams(vmem_limit_bytes=VMEM_BYTES),
        name="routed_backward",
    )(grad, spot, vec, *weights, *kept)


def pack_vectors(vectors):
    rows = jnp.stack([jnp.pad(v, (0, 128 - v.shape[0])) for v in vectors])
    return jnp.pad(rows, ((0, 16 - rows.shape[0]), (0, 0)))


def spread_vectors(vectors, outer, inner):
    rows = vectors.reshape(vectors.shape[0], outer, inner, -1).transpose(2, 0, 1, 3).astype(jnp.bfloat16)
    tiles = jnp.pad(rows, ((0, 0), (0, 16 - rows.shape[1]), (0, 0), (0, 128 - rows.shape[3])))
    return tiles.reshape(inner * 16, outer * 128)


def deliver_kernel(n, *refs):
    tile, sums, outs, vectors, sem = refs[0], refs[1 : n + 1], refs[n + 1 : 2 * n + 1], refs[2 * n + 1 : -1], refs[-1]
    copies = [pltpu.make_async_copy(a, b, sem.at[j]) for j, (a, b) in enumerate(zip(sums, outs))]
    for c in copies:
        c.start()
    for j, v in enumerate(vectors):
        v[...] = tile[j : j + 1, : v.shape[1]]
    for c in copies:
        c.wait()


def deliver(tile, sums, each, count):
    n = len(sums)
    return pl.pallas_call(
        functools.partial(deliver_kernel, n),
        in_specs=vmem_specs(1) + any_specs(n),
        out_specs=any_specs(n) + vmem_specs(count),
        out_shape=[shape(*s.shape, dtype=s.dtype) for s in sums] + [shape(1, each, dtype=jnp.float32)] * count,
        scratch_shapes=[pltpu.SemaphoreType.DMA((n,))],
        name="deliver",
    )(tile, *sums)


def fits(shards, outer, inner):
    return outer == 2 and inner == 16 and all(s.shape[0] % 16 == 0 and s.shape[1] % 128 == 0 for s in shards)


def per_device(outer, inner, *args):
    hidden, cotangent, capacity_class, token_index = args[:4]
    (gain_attn_a, qkv_a, out_a, gain_mlp_a, up_a, down_a, router_shard,
     gain_attn_b, qkv_b, out_b, gain_mlp_b, up_b, down_b) = args[4:]
    hidden, cotangent = hidden[0], cotangent[0]
    length = hidden.shape[0]
    tile = pack_vectors((gain_attn_a, gain_mlp_a, router_shard, gain_attn_b, gain_mlp_b))
    shards = [qkv_a, out_a, up_a, down_a, tile, qkv_b, out_b, up_b, down_b]
    remote = fits(shards, outer, inner)
    if remote:
        whole = gather_all(shards, outer, inner)
    else:
        whole = [lax.all_gather(lax.all_gather(s, "inner", axis=0, tiled=True), "outer", axis=1, tiled=True) for s in shards]
    weights_a, tiles, weights_b = whole[:4], whole[4], whole[5:]

    capacity = (length // 8) << capacity_class[0]
    slots = lax.broadcasted_iota(jnp.int32, token_index.shape, 1)
    spot = jnp.where(slots < capacity, token_index, -1)
    middle, vec, kept = routed_forward(hidden, spot, lane_map(outer, inner), tiles, weights_a)
    output, grad, gvec_b, *grads_b = dense_block(middle, cotangent, vec, weights_b)
    input_grad, gvec_a, *grads_a = routed_backward(grad, spot, vec, weights_a, kept)

    gtile = spread_vectors(jnp.concatenate([gvec_a, gvec_b]), outer, inner)
    sums = grads_a + [gtile] + grads_b
    if remote:
        done = scatter_all(sums, outer, inner)
    else:
        done = [
            lax.psum_scatter(
                lax.psum_scatter(s, "outer", scatter_dimension=1, tiled=True), "inner", scatter_dimension=0, tiled=True
            ).astype(jnp.float32)
            for s in sums
        ]
    each = gain_attn_a.shape[0]
    res = deliver(done[4], done[:4] + done[5:], each, 5)
    ga, gb, v = res[:4], res[4:8], [r[0] for r in res[8:]]
    return (output[None], input_grad[None], v[0], ga[0], ga[1], v[1], ga[2], ga[3], v[2], v[3], gb[0], gb[1], v[4], gb[2], gb[3])


def solution(mesh):
    outer, inner = mesh.shape["outer"], mesh.shape["inner"]
    both = ("outer", "inner")
    rows, vector, matrix = P(both, None, None), P(both), P("inner", "outer")
    block = (vector, matrix, matrix, vector, matrix, matrix)
    return jax.shard_map(
        functools.partial(per_device, outer, inner),
        mesh=mesh,
        in_specs=(rows, rows, vector, P(both, None)) + block + (vector,) + block,
        out_specs=(rows, rows) + block + (vector,) + block,
        check_vma=False,
    )
```

```python
import functools

import jax
import jax.numpy as jnp
from jax import lax
from jax.experimental import pallas as pl
from jax.experimental.pallas import tpu as pltpu
from jax.sharding import PartitionSpec as P

MESH = pl.DeviceIdType.MESH


def place():
    o, i = lax.axis_index("outer"), lax.axis_index("inner")
    return o, i // 4, (i // 2) % 2, i % 2


def device(o, z, x, c):
    return (o, z * 4 + x * 2 + c)


def greet(o, z, x, c):
    barrier = pltpu.get_barrier_semaphore()
    signal = functools.partial(pl.semaphore_signal, barrier, inc=1, device_id_type=MESH)
    signal(device_id=device(1 - o, z, x, c))
    signal(device_id=device(o, z, 1 - x, c))
    signal(device_id=device(o, z, x, 1 - c))

    @pl.when(z > 0)
    def _():
        signal(device_id=device(o, z - 1, x, c))

    @pl.when(z < 3)
    def _():
        signal(device_id=device(o, z + 1, x, c))

    pl.semaphore_wait(barrier, 3 + jnp.where(z > 0, 1, 0) + jnp.where(z < 3, 1, 0))


def scatter_kernel(n, *refs):
    grads, outs = refs[:n], refs[n:2 * n]
    rest = refs[2 * n:]
    own, got_c, got_b, got_a, got_z = (rest[j * n:(j + 1) * n] for j in range(5))
    local_sem, send_sem, recv_sem = rest[5 * n:]
    o, z, x, c = place()
    greet(o, z, x, c)

    def block(p, s, cc):
        r, w = outs[p].shape
        bs, as_, k = s // 8, (s // 4) % 2, s % 4
        if p % 2 == 0:
            co, cx = jnp.where(bs == 1, o, 1 - o), jnp.where(as_ == 1, x, 1 - x)
        else:
            cx, co = jnp.where(bs == 1, x, 1 - x), jnp.where(as_ == 1, o, 1 - o)
        row = pl.multiple_of((k * 4 + cx * 2 + cc) * r, 16)
        col = pl.multiple_of(co * w, 128)
        return grads[p].at[pl.ds(row, r), pl.ds(col, w)]

    def a_dev(p):
        return device(o, z, 1 - x, c) if p % 2 == 0 else device(1 - o, z, x, c)

    def b_dev(p):
        return device(1 - o, z, x, c) if p % 2 == 0 else device(o, z, 1 - x, c)

    def send(p, src, dst, kind, rslot, target):
        return pltpu.make_async_remote_copy(
            src_ref=src, dst_ref=dst, send_sem=send_sem.at[p, kind], recv_sem=recv_sem.at[p, rslot],
            device_id=target, device_id_type=MESH)

    def wait(ref, sem):
        pltpu.make_async_copy(ref, ref, sem).wait()

    def loop(count, body):
        def step(s, carry):
            body(s)
            return carry
        lax.fori_loop(0, count, step, 0)

    def begin(p):
        def body(s):
            send(p, block(p, s, 1 - c), got_c[p].at[s], 0, s, device(o, z, x, 1 - c)).start()
            pltpu.make_async_copy(block(p, s, c), own[p].at[s], local_sem.at[p]).start()
        loop(16, body)

    def core_stage(p):
        wait(own[p], local_sem.at[p])

        def body(s):
            wait(got_c[p].at[s], recv_sem.at[p, s])
            own[p][s] = own[p][s] + got_c[p][s]

            @pl.when(s < 8)
            def _():
                send(p, own[p].at[s], got_b[p].at[s], 1, 16 + s, b_dev(p)).start()
        loop(16, body)

    def b_stage(p):
        def body(j):
            wait(got_b[p].at[j], recv_sem.at[p, 16 + j])
            own[p][8 + j] = own[p][8 + j] + got_b[p][j]

            @pl.when(j < 4)
            def _():
                send(p, own[p].at[8 + j], got_a[p].at[j], 2, 24 + j, a_dev(p)).start()
        loop(8, body)

    def send_z(p, k, step):
        t = z + step
        slot = jnp.where(k == t, jnp.where(step > 0, k, 4), k)
        send(p, own[p].at[12 + k], got_z[p].at[slot], 3, 28 + slot, device(o, t, x, c)).start()

    def a_stage(p):
        def body(k):
            wait(got_a[p].at[k], recv_sem.at[p, 24 + k])
            own[p][12 + k] = own[p][12 + k] + got_a[p][k]
        loop(4, body)

        @pl.when(z == 0)
        def _():
            for k in (3, 2, 1):
                send_z(p, k, 1)

        @pl.when(z == 3)
        def _():
            for k in (0, 1, 2):
                send_z(p, k, -1)

    def pass_on(p, k, step):
        wait(got_z[p].at[k], recv_sem.at[p, 28 + k])
        own[p][12 + k] = own[p][12 + k] + got_z[p][k]
        send_z(p, k, step)

    def z_stage(p, level):
        @pl.when(z == level)
        def _():
            for k in range(3, level, -1):
                pass_on(p, k, 1)

        @pl.when(z == 3 - level)
        def _():
            for k in range(0, 3 - level):
                pass_on(p, k, -1)

    def last(p):
        outs[p][...] = own[p][12 + z].astype(jnp.float32)

        @pl.when(z > 0)
        def _():
            wait(got_z[p].at[z], recv_sem.at[p, 28 + z])
            outs[p][...] += got_z[p][z].astype(jnp.float32)

        @pl.when(z < 3)
        def _():
            wait(got_z[p].at[4], recv_sem.at[p, 32])
            outs[p][...] += got_z[p][4].astype(jnp.float32)

        wait(own[p], send_sem.at[p, 0])
        wait(got_b[p], send_sem.at[p, 1])
        wait(got_a[p], send_sem.at[p, 2])
        wait(got_a[p].at[pl.ds(0, 3)], send_sem.at[p, 3])

    for p in range(n):
        begin(p)
    stages = [core_stage, b_stage, a_stage, lambda p: z_stage(p, 1), lambda p: z_stage(p, 2), last]
    for t in range(n + len(stages) - 1):
        for lag, stage in enumerate(stages):
            if 0 <= t - lag < n:
                stage(t - lag)


def scatter_all(grads, outer, inner, collective_id=1):
    n = len(grads)
    outs = [jax.ShapeDtypeStruct((g.shape[0] // inner, g.shape[1] // outer), jnp.float32) for g in grads]
    bufs = [pltpu.VMEM((m,) + s.shape, jnp.bfloat16) for m in (16, 16, 8, 4, 5) for s in outs]
    return pl.pallas_call(
        functools.partial(scatter_kernel, n),
        out_shape=outs,
        in_specs=[pl.BlockSpec(memory_space=pl.ANY)] * n,
        out_specs=[pl.BlockSpec(memory_space=pltpu.VMEM)] * n,
        scratch_shapes=bufs + [pltpu.SemaphoreType.DMA((n,)), pltpu.SemaphoreType.DMA((n, 4)), pltpu.SemaphoreType.DMA((n, 33))],
        compiler_params=pltpu.CompilerParams(collective_id=collective_id, has_side_effects=True, vmem_limit_bytes=60 * 2**20),
        name="scatter_gradients",
    )(*grads)


FIRST_X = (True, True, False, True, False, False, True, True, False)


class Gather:
    @staticmethod
    def semaphores(n):
        return [pltpu.SemaphoreType.DMA((n,)), pltpu.SemaphoreType.DMA((n, 36)), pltpu.SemaphoreType.DMA((n, 32))]

    def __init__(self, shards, outs, local_sem, send_sem, recv_sem):
        o, z, x, c = place()
        n = len(shards)

        def block(p, co, cz, cx, cc):
            r, w = shards[p].shape
            row = pl.multiple_of((cz * 4 + cx * 2 + cc) * r, 16)
            col = pl.multiple_of(co * w, 128)
            return outs[p].at[pl.ds(row, r), pl.ds(col, w)]

        def send(p, src, dst, slot, rslot, target):
            return pltpu.make_async_remote_copy(
                src_ref=src, dst_ref=dst, send_sem=send_sem.at[p, slot], recv_sem=recv_sem.at[p, rslot],
                device_id=target, device_id_type=MESH)

        def up(p, k, src=None):
            b = block(p, o, k, x, c)
            return send(p, b if src is None else src, b, k, k, device(o, z + 1, x, c))

        def down(p, k, src=None):
            b = block(p, o, k, x, c)
            return send(p, b if src is None else src, b, 4 + k, k, device(o, z - 1, x, c))

        def first(p, k, src=None):
            b = block(p, o, k, x, c)
            t = device(o, z, 1 - x, c) if FIRST_X[p] else device(1 - o, z, x, c)
            return send(p, b if src is None else src, b, 8 + k, 4 + k, t)

        def second(p, k, a, src=None):
            if FIRST_X[p]:
                b, t = block(p, o, k, a, c), device(1 - o, z, x, c)
            else:
                b, t = block(p, a, k, x, c), device(o, z, 1 - x, c)
            return send(p, b if src is None else src, b, 12 + 2 * k + a, 8 + 2 * k + a, t)

        def core(p, co, k, cx, src=None):
            b = block(p, co, k, cx, c)
            s = k * 4 + co * 2 + cx
            return send(p, b if src is None else src, b, 20 + s, 16 + s, device(o, z, x, 1 - c))

        def mine(p):
            return x if FIRST_X[p] else o

        def coords(p, k, a, b):
            return (b, k, a) if FIRST_X[p] else (a, k, b)

        def core_ab(p, k, a, b, src=None):
            co, ck, cx = coords(p, k, a, b)
            return core(p, co, ck, cx, src)

        def other(p):
            return o if FIRST_X[p] else x

        def own(p):
            s = shards[p]
            pltpu.make_async_copy(s, block(p, o, z, x, c), local_sem.at[p]).start()

            @pl.when(z < 3)
            def _():
                up(p, z, s).start()

            @pl.when(z > 0)
            def _():
                down(p, z, s).start()

            first(p, z, s).start()
            second(p, z, mine(p), s).start()
            core(p, o, z, x, s).start()

        def wait_block(p, rslot):
            b = block(p, o, z, x, c)
            pltpu.make_async_copy(shards[p], b, recv_sem.at[p, rslot]).wait()

        def z_phase(p):
            for d in range(1, 4):
                @pl.when(z >= d)
                def _():
                    k = z - d
                    wait_block(p, k)

                    @pl.when(z < 3)
                    def _():
                        up(p, k).start()

                    first(p, k).start()
                    second(p, k, mine(p)).start()
                    core(p, o, k, x).start()

                @pl.when(z + d <= 3)
                def _():
                    k = z + d
                    wait_block(p, k)

                    @pl.when(z > 0)
                    def _():
                        down(p, k).start()

                    first(p, k).start()
                    second(p, k, mine(p)).start()
                    core(p, o, k, x).start()

        def ks():
            return [(z + d) % 4 for d in range(4)]

        def a_phase(p):
            for k in ks():
                wait_block(p, 4 + k)
                a = 1 - mine(p)
                second(p, k, a).start()
                core_ab(p, k, a, other(p)).start()

        def b_phase(p):
            for k in ks():
                for a in (mine(p), 1 - mine(p)):
                    wait_block(p, 8 + 2 * k + a)
                    core_ab(p, k, a, 1 - other(p)).start()

        def c_phase(p):
            for s in range(16):
                wait_block(p, 16 + s)

        def ends(p):
            def done(slot):
                pltpu.make_async_copy(shards[p], block(p, o, z, x, c), send_sem.at[p, slot]).wait()

            for k in range(4):
                @pl.when(jnp.logical_and(z < 3, k <= z))
                def _():
                    done(k)

                @pl.when(jnp.logical_and(z > 0, k >= z))
                def _():
                    done(4 + k)
            for slot in range(8, 36):
                done(slot)

        def only(f):
            return lambda p: f(p) if 0 <= p < n else None

        def begin():
            greet(o, z, x, c)
            own(0)

        def arrived(p):
            c_phase(p)
            pltpu.make_async_copy(shards[p], block(p, o, z, x, c), local_sem.at[p]).wait()

        def finish():
            for p in range(n):
                ends(p)

        self.begin, self.finish = begin, finish
        self.own, self.z_phase, self.a_phase, self.b_phase, self.arrived = map(only, (own, z_phase, a_phase, b_phase, arrived))


D = 768
SCALE = 0.125 * 1.4426950408889634
ROWS = 256
VMEM_BYTES = 63 * 2**20


def mul(a, b, ca=1, cb=0):
    return lax.dot_general(a, b, (((ca,), (cb,)), ((), ())), preferred_element_type=jnp.float32)


def low(v):
    return v.astype(jnp.bfloat16)


def cols(j):
    return pl.ds(pl.multiple_of(j * D, D), D)


def rms_scale(v):
    return lax.rsqrt(jnp.mean(v * v, axis=-1, keepdims=True) + 1e-06)


def rms_back(v, gain, grad):
    r = rms_scale(v)
    unit = v * r
    scaled = grad * gain
    back = r * (scaled - unit * jnp.mean(scaled * unit, axis=-1, keepdims=True))
    return back, jnp.sum((grad * unit).reshape(-1, 8, v.shape[-1]), axis=0)


def gelu_and_slope(u):
    k = 0.7978845608028654
    square = u * u
    t = jnp.tanh(u * (k + k * 0.044715 * square))
    half = 0.5 + 0.5 * t
    return u * half, half + u * (0.5 - 0.5 * t * t) * (k + 3 * 0.044715 * k * square)


def halves(v):
    lane = lax.broadcasted_iota(jnp.int32, v.shape, 1)
    zero = jnp.zeros_like(v)
    return jnp.where(lane < 64, v, zero), jnp.where(lane < 64, zero, v)


def two(v):
    first = low(v)
    return first, low(v - first.astype(jnp.float32))


class Block:
    def __init__(self, rows, refs):
        self.rows = rows
        self.__dict__.update(refs)

    @staticmethod
    def scratch(rows):
        f32, b16 = jnp.float32, jnp.bfloat16
        return dict(
            branch=((rows, D), f32), projected=((rows, 3 * D), b16), merged=((rows, D), b16), lse=((6, 8, rows), f32),
            active=((rows, 4 * D), b16), slope=((rows, 4 * D), b16), normed=((rows, D), b16), normed_mlp=((rows, D), b16))

    def tiles(self):
        return [slice(i, i + ROWS) for i in range(0, self.rows, ROWS)]

    def norm(self):
        for t in self.tiles():
            x = self.x[t]
            self.normed[t] = low(x * rms_scale(x) * self.gain_attn[...])

    def project(self, j):
        c = cols(j)
        self.projected[:, c] = low(mul(self.normed[...], self.qkv[:, c]))

    def pair(self, ref, part, pair, rows=slice(None)):
        return ref[rows, pl.ds(pl.multiple_of(part * D + pair * 128, 128), 128)]

    def attend(self, pair):
        v0, v1 = halves(self.pair(self.projected, 2, pair))
        causal = lax.broadcasted_iota(jnp.int32, (ROWS, ROWS), 1) >= lax.broadcasted_iota(jnp.int32, (ROWS, ROWS), 0)
        for t in self.tiles():
            n = t.stop
            qs = halves(self.pair(self.projected, 0, pair, t))
            k = self.pair(self.projected, 1, pair, slice(0, n))
            total = None
            for h in range(2):
                s = mul(k, qs[h], 1, 1)
                last = jnp.where(causal, s[t.start:], -1e30)
                s = last if t.start == 0 else jnp.concatenate([s[: t.start], last], axis=0)
                m = jnp.max(s, axis=0, keepdims=True) * SCALE
                p = jnp.exp2(s * SCALE - m)
                l = jnp.sum(p, axis=0, keepdims=True)
                self.lse[pair, h : h + 1, t] = m + jnp.log2(l)
                o = mul(low(p * (1.0 / l)), (v0, v1)[h][:n], 0, 0)
                total = o if total is None else total + o
            self.merged[t, pl.ds(pl.multiple_of(pair * 128, 128), 128)] = low(total)

    def join(self):
        for t in self.tiles():
            branch = mul(self.merged[t], self.out[...])
            self.branch[t] = branch
            middle = self.x[t] + branch
            self.normed_mlp[t] = low(middle * rms_scale(middle) * self.gain_mlp[...])

    def widen(self, j):
        c = cols(j)
        for t in self.tiles():
            active, slope = gelu_and_slope(mul(self.normed_mlp[t], self.up[:, c]))
            self.active[t, c] = low(active)
            self.slope[t, c] = low(slope)

    def narrow(self, t):
        return mul(self.active[t], self.down[...])

    def back_wide(self, j):
        c = cols(j)
        for t in self.tiles():
            grad = mul(self.grad_low[t], self.down[c, :], 1, 1)
            self.slope[t, c] = low(grad * self.slope[t, c].astype(jnp.float32))

    def grad_down(self, j):
        return low(mul(self.active[:, cols(j)], self.grad_low[...], 0, 0))

    def grad_up(self, j):
        return low(mul(self.normed_mlp[...], self.slope[:, cols(j)], 0, 0))

    def back_mlp(self, grad_of):
        total = jnp.zeros((8, D), jnp.float32)
        for t in self.tiles():
            grad = mul(self.slope[t], self.up[...], 1, 1)
            back, gain = rms_back(self.x[t] + self.branch[t], self.gain_mlp[...], grad)
            total = total + gain
            self.branch[t] = back
            self.normed_mlp[t] = low(grad_of(t) + back)
        return jnp.sum(total, axis=0, keepdims=True)

    def grad_out(self):
        return low(mul(self.merged[...], self.normed_mlp[...], 0, 0))

    def back_merged(self):
        self.active[:, :D] = low(mul(self.normed_mlp[...], self.out[...], 1, 1))

    def attend_back(self, pair, turned):
        rows = self.rows
        q, do = self.pair(self.projected, 0, pair), self.pair(self.active, 0, pair)
        qs, dos = halves(q), halves(do)
        dd = do.astype(jnp.float32) * self.pair(self.merged, 0, pair).astype(jnp.float32)
        pick = lax.broadcasted_iota(jnp.int32, (8, 128), 0) == lax.broadcasted_iota(jnp.int32, (8, 128), 1) // 64
        delta = lax.dot_general(pick.astype(jnp.float32), dd, (((1,), (1,)), ((), ())), precision=lax.Precision.HIGHEST,
                                preferred_element_type=jnp.float32)
        causal = lax.broadcasted_iota(jnp.int32, (ROWS, ROWS), 1) >= lax.broadcasted_iota(jnp.int32, (ROWS, ROWS), 0)
        for t in self.tiles():
            a = t.start
            ks, vs = halves(self.pair(self.projected, 1, pair, t)), halves(self.pair(self.projected, 2, pair, t))
            dk = dv = dq = 0.0
            for h in range(2):
                s = mul(ks[h], q[a:], 1, 1)
                p = jnp.exp2(s * SCALE - self.lse[pair, h : h + 1, a:])
                first = jnp.where(causal, p[:, :ROWS], 0.0)
                p = first if t.stop == rows else jnp.concatenate([first, p[:, ROWS:]], axis=1)
                dp = mul(vs[h], do[a:], 1, 1)
                ds = low(p * (dp - delta[h : h + 1, a:]))
                dv = dv + mul(low(p), dos[h][a:])
                dk = dk + mul(ds, qs[h][a:])
                dq = dq + mul(ks[h], ds, 0, 0)
            lanes = pl.multiple_of(pair * 128, 128)
            self.projected[t, pl.ds(D + lanes, 128)] = low(0.125 * dk)
            self.projected[t, pl.ds(2 * D + lanes, 128)] = low(dv)
            if a == 0:
                turned[:, :rows] = dq
            else:
                turned[:, a:rows] += dq
        self.projected[:, pl.ds(lanes, 128)] = low(0.125 * turned[:, :rows].T)

    def grad_qkv(self, j):
        return low(mul(self.normed[...], self.projected[:, cols(j)], 0, 0))

    def back_norm(self, finish):
        total = jnp.zeros((8, D), jnp.float32)
        for t in self.tiles():
            grad = mul(self.projected[t], self.qkv[...], 1, 1)
            back, gain = rms_back(self.x[t], self.gain_attn[...], grad)
            total = total + gain
            finish(t, back + self.branch[t])
        return jnp.sum(total, axis=0, keepdims=True)


SAVED = ("branch", "projected", "merged", "lse", "active", "slope", "normed", "normed_mlp")


def run(steps, hooks=None):
    at = 0
    for count, body in steps:
        if count == 0:
            body(0)
            continue
        after = [hooks[at + k] if hooks else [] for k in range(count)]
        at += count
        if count == 1:
            body(0)
            for f in after[0]:
                f()
            continue

        @pl.loop(0, count)
        def _(j):
            body(j)
            for k in range(count):
                if after[k]:
                    @pl.when(j == k)
                    def _():
                        for f in after[k]:
                            f()


class Loads:
    def __init__(self, pairs, sems):
        self.copies = {k: pltpu.make_async_copy(a, b, sems.at[j]) for j, (k, a, b) in enumerate(pairs)}
        for c in self.copies.values():
            c.start()

    def need(self, *names):
        for n in names:
            self.copies[n].wait()


class Ship:
    def __init__(self, stage, sems):
        self.stage, self.sems = stage, sems

    def wait(self, slot):
        pltpu.make_async_copy(self.stage.at[slot], self.stage.at[slot], self.sems.at[slot]).wait()

    def send(self, slot, value, target, busy):
        if busy is True:
            self.wait(slot)
        elif busy is not False:
            pl.when(busy)(lambda: self.wait(slot))
        self.stage[slot] = value
        pltpu.make_async_copy(self.stage.at[slot], target, self.sems.at[slot]).start()


def backward_steps(b, grad_of, ship, targets, vec, finish, turned):
    gqkv, gout, gup, gdown = targets

    def wide(j):
        b.back_wide(j)
        ship.send(0, b.grad_down(j), gdown.at[cols(j), :], j > 0)
        ship.send(1, b.grad_up(j), gup.at[:, cols(j)], j > 0)

    def mlp(_):
        vec(1, b.back_mlp(grad_of))

    def out(_):
        ship.send(0, b.grad_out(), gout, True)
        b.back_merged()

    def qkv(j):
        @pl.when(j == 0)
        def _():
            ship.wait(0)
        ship.send(1, b.grad_qkv(j), gqkv.at[:, cols(j)], True)

    def norm(_):
        vec(0, b.back_norm(finish))
        ship.wait(1)

    return [(4, wide), (1, mlp), (1, out), (6, lambda j: b.attend_back(j, turned)), (3, qkv), (1, norm)]


KEPT_DENSE = ("x", "branch", "projected", "merged", "lse", "normed_mlp")


def dense_kernel(cot_hbm, vec_ref, qkv_hbm, out_hbm, up_hbm, down_hbm, *rest):
    n = len(KEPT_DENSE)
    kept_hbm, rest = rest[:n], rest[n:]
    y_hbm, grad_hbm, gvec_ref, gqkv_hbm, gout_hbm, gup_hbm, gdown_hbm = rest[:7]
    cot, qkv, out, up, down, active, slope, normed, y, turned, stage, load_sem, stage_sem, row_sem = rest[7:21]
    kept = dict(zip(KEPT_DENSE, rest[21:]))
    where = dict(zip(KEPT_DENSE, zip(kept_hbm, rest[21:])), cot=(cot_hbm, cot), qkv=(qkv_hbm, qkv), out=(out_hbm, out),
                 up=(up_hbm, up), down=(down_hbm, down))
    order = ("normed_mlp", "up", "down", "x", "branch", "cot", "out", "merged", "projected", "lse", "qkv")
    loads = Loads([(k,) + where[k] for k in order], load_sem)
    b = Block(cot.shape[0], dict(kept, active=active, slope=slope, normed=normed, grad_low=cot, qkv=qkv, out=out, up=up, down=down,
                                 gain_attn=vec_ref.at[3:4], gain_mlp=vec_ref.at[4:5]))
    x = b.x

    def narrow(_):
        loads.need("x", "branch", "down")
        for t in b.tiles():
            y[t] = low(x[t] + b.branch[t] + b.narrow(t))
        pltpu.make_async_copy(y, y_hbm, row_sem.at[0]).start()
        loads.need("cot")

    def vec(j, value):
        gvec_ref[j : j + 1] = value

    def finish(t, grad):
        x[t] = grad + cot[t].astype(jnp.float32)
        pltpu.make_async_copy(x.at[t], grad_hbm.at[t], row_sem.at[1]).start()

    back = backward_steps(b, lambda t: cot[t].astype(jnp.float32), Ship(stage, stage_sem),
                          (gqkv_hbm, gout_hbm, gup_hbm, gdown_hbm), vec, finish, turned)
    run([(0, lambda _: loads.need("normed_mlp", "up")), (4, b.widen), (1, narrow)] + back[:2]
        + [(0, lambda _: loads.need("out", "merged"))] + back[2:3] + [(0, lambda _: loads.need("projected", "lse"))]
        + back[3:4] + [(0, lambda _: b.norm())] + back[4:5] + [(0, lambda _: loads.need("qkv"))] + back[5:])
    pltpu.make_async_copy(y, y_hbm, row_sem.at[0]).wait()
    pltpu.make_async_copy(x, grad_hbm, row_sem.at[1]).wait()


def shape(*dims, dtype=jnp.bfloat16):
    return jax.ShapeDtypeStruct(dims, dtype)


def any_specs(n):
    return [pl.BlockSpec(memory_space=pl.ANY)] * n


def vmem_specs(n):
    return [pl.BlockSpec(memory_space=pltpu.VMEM)] * n


WEIGHTS = [((D, 3 * D), jnp.bfloat16), ((D, D), jnp.bfloat16), ((D, 4 * D), jnp.bfloat16), ((4 * D, D), jnp.bfloat16)]


def buffers(*pairs):
    return [pltpu.VMEM(dims, dtype) for dims, dtype in pairs]


def kept_buffers(rows):
    s = Block.scratch(rows)
    return [s[k] for k in SAVED]


def dense_block(cot, vec, weights, kept):
    rows = cot.shape[0]
    f32, b16 = jnp.float32, jnp.bfloat16
    every = dict(Block.scratch(rows), x=((rows, D), f32))
    return pl.pallas_call(
        dense_kernel,
        in_specs=any_specs(1) + vmem_specs(1) + any_specs(4 + len(kept)),
        out_specs=any_specs(2) + vmem_specs(1) + any_specs(4),
        out_shape=[shape(rows, D), shape(rows, D, dtype=f32), shape(2, D, dtype=f32)] + [shape(*s) for s, _ in WEIGHTS],
        scratch_shapes=buffers(((rows, D), b16), *WEIGHTS, every["active"], every["slope"], every["normed"], ((rows, D), b16),
                               ((128, rows), f32), ((2, D, D), b16))
        + [pltpu.SemaphoreType.DMA((11,)), pltpu.SemaphoreType.DMA((2,)), pltpu.SemaphoreType.DMA((2,))]
        + buffers(*[every[k] for k in KEPT_DENSE]),
        compiler_params=pltpu.CompilerParams(vmem_limit_bytes=VMEM_BYTES),
        name="dense_block",
    )(cot, vec, *weights, *kept)


def spots(length, spot_ref):
    at = lax.broadcasted_iota(jnp.int32, (length, spot_ref.shape[1]), 0)
    return low(jnp.where(at == spot_ref[...], 1.0, 0.0))


def lane_map(outer, inner):
    each = D // (outer * inner)
    d = jnp.arange(D, dtype=jnp.int32)
    return jnp.stack([d // each % inner, d // (each * inner) * 128 + d % each])


def spread_map(tiles_columns, map_ref):
    at = lax.broadcasted_iota(jnp.int32, (tiles_columns, D), 0)
    return low(jnp.where(at == map_ref[1:2], 1.0, 0.0))


def read_vectors(tiles, map_ref):
    rows, columns = tiles.shape
    every = mul(tiles[...], spread_map(columns, map_ref))
    inner = lax.broadcasted_iota(jnp.int32, (rows, D), 0) // 16
    return jnp.sum(jnp.where(inner == map_ref[0:1], every, 0.0).reshape(rows // 16, 16, D), axis=0)


def write_vectors(vectors, rows, columns, map_ref):
    every = jnp.broadcast_to(vectors[None], (rows // 16, 16, D)).reshape(rows, D)
    inner = lax.broadcasted_iota(jnp.int32, (rows, D), 0) // 16
    return low(mul(low(jnp.where(inner == map_ref[0:1], every, 0.0)), spread_map(columns, map_ref), 1, 1))


def gate_of(x, router):
    return jax.nn.sigmoid(jnp.sum(x * router, axis=-1, keepdims=True))


def routed_forward_steps(b, need, hidden, spot_ref, chosen, vec_ref, extra, keep):
    length = hidden.shape[0]

    def pick(_):
        chosen[...] = spots(length, spot_ref)
        need("hidden")
        for t in b.tiles():
            b.x[t] = mul(chosen[:, t], hidden[...], 0, 0)
        need("vectors")
        b.norm()
        keep("x", "normed")
        need("qkv")

    def project(j):
        b.project(j)

    def join(_):
        keep("projected", "merged", "lse")
        need("out")
        b.join()
        keep("branch", "normed_mlp")
        need("up")

    def narrow(_):
        keep("active", "slope")
        need("down")
        for t in b.tiles():
            extra[t] = b.branch[t] + b.narrow(t)
        keep("change")

    def put(_):
        rows = [gate_of(b.x[t], vec_ref[2:3]) * extra[t] for t in b.tiles()]
        pieces = [two(r) for r in rows]
        for i in range(0, length, ROWS):
            t = slice(i, i + ROWS)
            total = hidden[t].astype(jnp.float32)
            for piece, s in zip(pieces, b.tiles()):
                for p in piece:
                    total = total + mul(chosen[t, s], p)
            b.middle[t] = total

    return [(1, pick), (3, project), (6, b.attend), (1, join), (4, b.widen), (1, narrow), (1, put)]


KEPT = ("x", "change") + SAVED


def kept_shapes(rows):
    return [((rows, D), jnp.float32)] * 2 + kept_buffers(rows)


def routed_backward_steps(b, need, grad, spot_ref, chosen, vec_ref, change, grad_rows, gate, ship, targets, vec, turned,
                          grad_hbm, grad_sem):
    length = grad.shape[0]
    router = vec_ref.at[2:3]

    def take(_):
        chosen[...] = spots(length, spot_ref)
        need("grad")
        pieces = two(grad[...])
        need("x", "change")
        for t in b.tiles():
            rows = mul(chosen[:, t], pieces[0], 0, 0) + mul(chosen[:, t], pieces[1], 0, 0)
            g = gate_of(b.x[t], router[...])
            grad_rows[t] = g * rows
            b.grad_low[t] = low(g * rows)
            logits = jnp.sum(rows * change[t], axis=-1, keepdims=True) * g * (1.0 - g)
            gate[t] = jnp.broadcast_to(logits, (ROWS, 128))
        need("down", "active", "slope", "normed_mlp")

    def finish(t, g):
        change[t] = g + gate[t, 0:1] * router[...]

    def put(_):
        pieces = [two(change[t]) for t in b.tiles()]
        for i in range(0, length, ROWS):
            t = slice(i, i + ROWS)
            total = grad[t]
            for piece, s in zip(pieces, b.tiles()):
                for p in piece:
                    total = total + mul(chosen[t, s], p)
            grad[t] = total
            pltpu.make_async_copy(grad.at[t], grad_hbm.at[t], grad_sem).start()

    def route(_):
        total = jnp.zeros((8, D), jnp.float32)
        for t in b.tiles():
            total = total + jnp.sum((gate[t, 0:1] * b.x[t]).reshape(-1, 8, D), axis=0)
        vec(2, jnp.sum(total, axis=0, keepdims=True))

    back = backward_steps(b, lambda t: grad_rows[t], ship, targets, vec, finish, turned)
    waits = [None, ("up", "branch"), ("out", "merged"), ("projected", "lse"), ("normed",), ("qkv",)]
    steps = [(1, take)]
    for (count, body), names in zip(back, waits):
        if names is not None:
            steps.append((0, lambda _, names=names: need(*names)))
        steps.append((count, body))
    return steps + [(1, route), (1, put)]


def routed_backward_kernel(grad_hbm, spot_ref, vec_ref, qkv_hbm, out_hbm, up_hbm, down_hbm, *rest):
    n = len(KEPT)
    kept_hbm, rest = rest[:n], rest[n:]
    input_hbm, gvec_ref, gqkv_hbm, gout_hbm, gup_hbm, gdown_hbm = rest[:6]
    (grad, chosen, grad_low, grad_rows, gate, turned, stage, qkv, out, up, down, load_sem, stage_sem, row_sem) = rest[6:20]
    kept = rest[20:]
    order = ("grad", "x", "change", "down", "active", "slope", "normed_mlp", "up", "branch", "out", "merged", "projected",
             "lse", "normed", "qkv")
    where = dict(zip(KEPT, zip(kept_hbm, kept)), grad=(grad_hbm, grad), qkv=(qkv_hbm, qkv), out=(out_hbm, out),
                 up=(up_hbm, up), down=(down_hbm, down))
    loads = Loads([(k,) + where[k] for k in order], load_sem)
    named = dict(zip(KEPT, kept))
    b = Block(spot_ref.shape[1], dict(named, grad_low=grad_low, qkv=qkv, out=out, up=up, down=down,
                                      gain_attn=vec_ref.at[0:1], gain_mlp=vec_ref.at[1:2]))

    def vec(j, value):
        gvec_ref[j : j + 1] = value

    run(routed_backward_steps(b, loads.need, grad, spot_ref, chosen, vec_ref, named["change"], grad_rows, gate,
                              Ship(stage, stage_sem), (gqkv_hbm, gout_hbm, gup_hbm, gdown_hbm), vec, turned,
                              input_hbm, row_sem))
    pltpu.make_async_copy(grad, input_hbm, row_sem).wait()


def routed_backward(grad, spot, vec, weights, kept):
    length, rows = grad.shape[0], spot.shape[1]
    f32, b16 = jnp.float32, jnp.bfloat16
    return pl.pallas_call(
        routed_backward_kernel,
        in_specs=any_specs(1) + vmem_specs(2) + any_specs(4 + len(kept)),
        out_specs=any_specs(1) + vmem_specs(1) + any_specs(4),
        out_shape=[shape(length, D, dtype=f32), shape(3, D, dtype=f32)] + [shape(*s) for s, _ in WEIGHTS],
        scratch_shapes=buffers(((length, D), f32), ((length, rows), b16), ((rows, D), b16), ((rows, D), f32), ((rows, 128), f32),
                               ((128, rows), f32), ((2, D, D), b16), *WEIGHTS)
        + [pltpu.SemaphoreType.DMA((15,)), pltpu.SemaphoreType.DMA((2,)), pltpu.SemaphoreType.DMA]
        + buffers(*kept_shapes(rows)),
        compiler_params=pltpu.CompilerParams(vmem_limit_bytes=VMEM_BYTES),
        name="routed_backward",
    )(grad, spot, vec, *weights, *kept)


def forward_kernel(remote, *refs):
    hidden_hbm, spot_ref, map_ref, *refs = refs
    given, refs = refs[:9], refs[9:]
    if remote:
        whole, refs = refs[:9], refs[9:]
    else:
        whole = given
    vec_ref, *refs = refs
    n, m = len(KEPT), len(KEPT_DENSE)
    kept_hbm, refs = dict(zip(KEPT, refs[:n])), refs[n:]
    dense_hbm, refs = dict(zip(KEPT_DENSE, refs[:m])), refs[m:]
    hidden, chosen, tiles, *refs = refs
    weights, refs = refs[:6], refs[6:]
    kept, refs = dict(zip(KEPT, refs[:n])), refs[n:]
    dense, refs = dict(zip(KEPT_DENSE, refs[:m])), refs[m:]
    normed, load_sem, keep_sem, dense_sem = refs[:4]
    names = ("vectors", "qkv", "out", "up", "down", "qkv_b", "out_b")
    first = pltpu.make_async_copy(hidden_hbm, hidden, load_sem.at[7])
    first.start()
    loads = {k: pltpu.make_async_copy(whole[j], dst, load_sem.at[j])
             for j, (k, dst) in enumerate(zip(names, [tiles] + weights))}
    flow = Gather(given, whole, *refs[4:]) if remote else None
    if not remote:
        for c in loads.values():
            c.start()

    def need(*wanted):
        for k in wanted:
            if k == "hidden":
                first.wait()
                continue
            loads[k].wait()
            if k == "vectors":
                vec_ref[...] = read_vectors(tiles, map_ref)

    saves = {k: pltpu.make_async_copy(kept[k], kept_hbm[k], keep_sem.at[j]) for j, k in enumerate(KEPT)}
    dense_saves = {k: pltpu.make_async_copy(dense[k], dense_hbm[k], dense_sem.at[j]) for j, k in enumerate(KEPT_DENSE)}

    def keep(*wanted):
        for k in wanted:
            saves[k].start()

    def keep_dense(*wanted):
        for k in wanted:
            dense_saves[k].start()

    qkv, out, up, down, qkv_b, out_b = weights
    b = Block(spot_ref.shape[1], dict(kept, middle=dense["x"], qkv=qkv, out=out, up=up, down=down,
                                      gain_attn=vec_ref.at[0:1], gain_mlp=vec_ref.at[1:2]))
    d = Block(hidden.shape[0], dict(dense, qkv=qkv_b, out=out_b, normed=normed,
                                    gain_attn=vec_ref.at[3:4], gain_mlp=vec_ref.at[4:5]))

    def norm(_):
        keep_dense("x")
        d.norm()
        need("qkv_b")

    def join(_):
        keep_dense("projected", "merged", "lse")
        need("out_b")
        d.join()
        keep_dense("branch", "normed_mlp")

    routed = routed_forward_steps(b, need, hidden, spot_ref, chosen, vec_ref, kept["change"], keep)
    steps = routed + [(1, norm), (3, d.project), (6, d.attend), (1, join)]
    if remote:
        def arrive(p):
            flow.arrived(p)
            if 0 <= p < len(names):
                loads[names[p]].start()

        flow.begin()
        slots = [[lambda t=t: flow.own(t + 1), lambda t=t: flow.z_phase(t), lambda t=t: flow.a_phase(t - 1),
                  lambda t=t: flow.b_phase(t - 2), lambda t=t: arrive(t - 3)] for t in range(12)]
        for t in range(6):
            for f in slots[t]:
                f()
        units = [[] for _ in range(sum(c for c, _ in steps))]
        plan = {6: (0, 2, 4, 5, 6), 7: (7, 8, 9, 9, 9), 8: (11, 12, 13, 14, 15), 9: (16, 16, 16, 16, 16), 10: (19, 20, 21, 22, 23), 11: (24, 25, 26, 26, 26)}
        for t, at in plan.items():
            for f, u in zip(slots[t], at):
                units[u].append(f)
        run(steps, units)
        flow.finish()
    else:
        run(steps)
    for c in list(saves.values()) + list(dense_saves.values()):
        c.wait()


def forward(remote, hidden, spot, place_map, weights, outer, inner):
    length, rows = hidden.shape[0], spot.shape[1]
    f32, b16 = jnp.float32, jnp.bfloat16
    kept = kept_shapes(rows)
    every = dict(Block.scratch(length), x=((length, D), f32))
    dense = [every[k] for k in KEPT_DENSE]
    whole = [shape(w.shape[0] * inner, w.shape[1] * outer) for w in weights] if remote else []
    tiles = (16 * inner, 128 * outer)
    scratch = (buffers(((length, D), b16), ((length, rows), b16), (tiles, b16), *WEIGHTS, *WEIGHTS[:2], *kept, *dense, ((length, D), b16))
               + [pltpu.SemaphoreType.DMA((k,)) for k in (8, len(kept), len(dense))])
    if remote:
        scratch += Gather.semaphores(len(weights))
    results = pl.pallas_call(
        functools.partial(forward_kernel, remote),
        in_specs=any_specs(1) + vmem_specs(2) + any_specs(9),
        out_specs=any_specs(len(whole)) + vmem_specs(1) + any_specs(len(kept) + len(dense)),
        out_shape=whole + [shape(16, D, dtype=f32)] + [shape(*s, dtype=t) for s, t in kept + dense],
        scratch_shapes=scratch,
        compiler_params=pltpu.CompilerParams(vmem_limit_bytes=VMEM_BYTES, **(dict(collective_id=0, has_side_effects=True) if remote else {})),
        name="forward",
    )(hidden, spot, place_map, *weights)
    if remote:
        weights, results = results[:9], results[9:]
    return weights, results[0], results[1 : 1 + len(kept)], results[1 + len(kept) :]


def pack_vectors(vectors):
    rows = jnp.stack([jnp.pad(v, (0, 128 - v.shape[0])) for v in vectors])
    return jnp.pad(rows, ((0, 16 - rows.shape[0]), (0, 0)))


def spread_vectors(vectors, outer, inner):
    rows = vectors.reshape(vectors.shape[0], outer, inner, -1).transpose(2, 0, 1, 3).astype(jnp.bfloat16)
    tiles = jnp.pad(rows, ((0, 0), (0, 16 - rows.shape[1]), (0, 0), (0, 128 - rows.shape[3])))
    return tiles.reshape(inner * 16, outer * 128)


def deliver_kernel(n, *refs):
    tile, sums, outs, vectors = refs[0], refs[1 : n + 1], refs[n + 1 : 2 * n + 1], refs[2 * n + 1 :]
    for a, b in zip(sums, outs):
        b[...] = a[...]
    for j, v in enumerate(vectors):
        v[...] = tile[j : j + 1, : v.shape[1]]


def deliver(tile, sums, each, count):
    n = len(sums)
    return pl.pallas_call(
        functools.partial(deliver_kernel, n),
        in_specs=vmem_specs(1 + n),
        out_specs=vmem_specs(n + count),
        out_shape=[shape(*s.shape, dtype=s.dtype) for s in sums] + [shape(1, each, dtype=jnp.float32)] * count,
        name="deliver",
    )(tile, *sums)


def fits(shards, outer, inner):
    return outer == 2 and inner == 16 and all(s.shape[0] % 16 == 0 and s.shape[1] % 128 == 0 for s in shards)


def per_device(outer, inner, *args):
    hidden, cotangent, capacity_class, token_index = args[:4]
    (gain_attn_a, qkv_a, out_a, gain_mlp_a, up_a, down_a, router_shard,
     gain_attn_b, qkv_b, out_b, gain_mlp_b, up_b, down_b) = args[4:]
    hidden, cotangent = hidden[0], cotangent[0]
    length = hidden.shape[0]
    tile = pack_vectors((gain_attn_a, gain_mlp_a, router_shard, gain_attn_b, gain_mlp_b))
    shards = [tile, qkv_a, out_a, up_a, down_a, qkv_b, out_b, up_b, down_b]
    remote = fits(shards, outer, inner)
    if not remote:
        shards = [lax.all_gather(lax.all_gather(s, "inner", axis=0, tiled=True), "outer", axis=1, tiled=True) for s in shards]

    capacity = (length // 8) << capacity_class[0]
    slots = lax.broadcasted_iota(jnp.int32, token_index.shape, 1)
    spot = jnp.where(slots < capacity, token_index, -1)
    whole, vec, kept, kept_dense = forward(remote, hidden, spot, lane_map(outer, inner), shards, outer, inner)
    output, grad, gvec_b, *grads_b = dense_block(cotangent, vec, whole[5:], kept_dense)
    input_grad, gvec_a, *grads_a = routed_backward(grad, spot, vec, whole[1:5], kept)

    gtile = spread_vectors(jnp.concatenate([gvec_a, gvec_b]), outer, inner)
    sums = grads_a + [gtile] + grads_b
    if remote:
        done = scatter_all(sums, outer, inner)
    else:
        done = [
            lax.psum_scatter(
                lax.psum_scatter(s, "outer", scatter_dimension=1, tiled=True), "inner", scatter_dimension=0, tiled=True
            ).astype(jnp.float32)
            for s in sums
        ]
    each = gain_attn_a.shape[0]
    res = deliver(done[4], done[:4] + done[5:], each, 5)
    ga, gb, v = res[:4], res[4:8], [r[0] for r in res[8:]]
    return (output[None], input_grad[None], v[0], ga[0], ga[1], v[1], ga[2], ga[3], v[2], v[3], gb[0], gb[1], v[4], gb[2], gb[3])


def solution(mesh):
    outer, inner = mesh.shape["outer"], mesh.shape["inner"]
    both = ("outer", "inner")
    rows, vector, matrix = P(both, None, None), P(both), P("inner", "outer")
    block = (vector, matrix, matrix, vector, matrix, matrix)
    return jax.shard_map(
        functools.partial(per_device, outer, inner),
        mesh=mesh,
        in_specs=(rows, rows, vector, P(both, None)) + block + (vector,) + block,
        out_specs=(rows, rows) + block + (vector,) + block,
        check_vma=False,
    )
```

```python
import functools

import jax
import jax.numpy as jnp
from jax import lax
from jax.experimental import pallas as pl
from jax.experimental.pallas import tpu as pltpu
from jax.sharding import PartitionSpec as P

MESH = pl.DeviceIdType.MESH


def place():
    o, i = lax.axis_index("outer"), lax.axis_index("inner")
    return o, i // 4, (i // 2) % 2, i % 2


def device(o, z, x, c):
    return (o, z * 4 + x * 2 + c)


def greet(o, z, x, c):
    barrier = pltpu.get_barrier_semaphore()
    signal = functools.partial(pl.semaphore_signal, barrier, inc=1, device_id_type=MESH)
    signal(device_id=device(1 - o, z, x, c))
    signal(device_id=device(o, z, 1 - x, c))
    signal(device_id=device(o, z, x, 1 - c))

    @pl.when(z > 0)
    def _():
        signal(device_id=device(o, z - 1, x, c))

    @pl.when(z < 3)
    def _():
        signal(device_id=device(o, z + 1, x, c))

    pl.semaphore_wait(barrier, 3 + jnp.where(z > 0, 1, 0) + jnp.where(z < 3, 1, 0))


GATHER_PARTS = (
        (0, 0, 16, 0, 128, False), (1, 0, 48, 0, 640, True), (1, 0, 48, 640, 512, False), (2, 0, 48, 0, 384, True), (3,
    0, 48, 0, 768, True), (3, 0, 48, 768, 768, False), (4, 0, 96, 0, 384, False), (4, 96, 96, 0, 384, True), (5, 0, 48,
    0, 640, False), (5, 0, 48, 640, 512, True), (6, 0, 48, 0, 384, False), (7, 0, 48, 0, 768, True), (7, 0, 48, 768,
    768, False), (8, 0, 96, 0, 384, False), (8, 96, 96, 0, 384, True))
GATHER_PLAN = (
        (0, 0, 0), (0, 0, 1), (0, 0, 2), (0, 1, 0), (0, 1, 1), (0, 1, 2), (0, 2, 0), (0, 2, 1), (0, 2, 2), (0, 3, 0),
    (0, 0, 3), (0, 3, 1), (0, 4, 0), (0, 3, 2), (0, 1, 3), (0, 0, 4), (0, 0, 5), (0, 2, 3), (0, 1, 4), (0, 4, 1), (0, 5,
    0), (0, 1, 5), (0, 3, 3), (0, 6, 0), (0, 2, 4), (0, 4, 2), (0, 2, 5), (0, 0, 6), (1, 5, 1), (1, 4, 3), (1, 3, 4),
    (1, 5, 2), (1, 6, 1), (1, 3, 5), (1, 1, 6), (1, 6, 2), (1, 0, 7), (1, 5, 3), (1, 0, 8), (1, 2, 6), (2, 6, 3), (2, 4,
    4), (2, 1, 7), (2, 1, 8), (3, 3, 6), (3, 2, 7), (3, 0, 9), (3, 2, 8), (5, 3, 7), (5, 4, 5), (5, 3, 8), (5, 1, 9),
    (5, 0, 10), (5, 0, 11), (6, 2, 9), (6, 1, 10), (6, 5, 4), (6, 1, 11), (6, 3, 9), (6, 2, 10), (6, 6, 4), (6, 4, 7),
    (6, 2, 11), (6, 3, 10), (6, 0, 12), (6, 4, 6), (6, 0, 13), (6, 3, 11), (6, 0, 14), (6, 5, 5), (6, 1, 12), (6, 1,
    13), (7, 6, 5), (7, 1, 14), (7, 2, 12), (8, 2, 13), (8, 2, 14), (8, 4, 8), (9, 4, 9), (9, 3, 12), (9, 3, 13), (9, 3,
    14), (14, 5, 6), (14, 5, 7), (15, 4, 10), (15, 6, 6), (15, 6, 7), (15, 4, 11), (17, 5, 8), (18, 5, 9), (18, 6, 8),
    (18, 6, 9), (20, 4, 12), (22, 4, 13), (24, 4, 14), (24, 5, 10), (25, 6, 10), (26, 5, 11), (26, 5, 12), (27, 6, 11),
    (27, 6, 12), (27, 5, 14), (27, 5, 13), (28, 6, 14), (28, 6, 13))


class Gather:
    @staticmethod
    def semaphores(n):
        return [pltpu.SemaphoreType.DMA(k) for k in ((n,), (n, 13), (n, 11))]

    def __init__(self, parts, shards, outs, local_sem, send_sem, recv_sem):
        o, z, x, c = place()
        n = len(parts)

        def shard(p):
            a, r0, r, c0, w, _ = parts[p]
            return shards[a].at[pl.ds(r0, r), pl.ds(c0, w)]

        def blocks(p, oo):
            a, r0, r, c0, w, _ = parts[p]
            rows, each = shards[a].shape
            view = outs[a].reshape(4, 2, 2, rows, 2 * each)
            return view, pl.ds(r0, r), pl.ds(pl.multiple_of(oo * each + c0, 128), w)

        def chunk(p, k):
            view, rows, columns = blocks(p, o)
            return view.at[k, x, c, rows, columns]

        def group(p, second, first):
            first_x = parts[p][5]
            px, po = (first, second) if first_x else (second, first)
            view, rows, columns = blocks(p, o if po else 1 - o)
            return view.at[:, x if px else 1 - x, c, rows, columns]

        def send(p, src, dst, slot, target):
            return pltpu.make_async_remote_copy(
                src_ref=src, dst_ref=dst, send_sem=send_sem.at[p, slot[0]], recv_sem=recv_sem.at[p, slot[1]],
                device_id=target, device_id_type=MESH)

        def wait(ref, sem):
            pltpu.make_async_copy(ref, ref, sem).wait()

        def up(p, k, hop, src=None):
            b = chunk(p, k)
            return send(p, b if src is None else src, b, (hop, k), device(o, z + 1, x, c))

        def down(p, k, hop, src=None):
            b = chunk(p, k)
            return send(p, b if src is None else src, b, (3 + hop, k), device(o, z - 1, x, c))

        def near(p, second):
            return device(o, z, 1 - x, c) if parts[p][5] != second else device(1 - o, z, x, c)

        def to_core(p, second, first):
            b = group(p, second, first)
            send(p, b, b, (9 + 2 * second + first, 7 + 2 * second + first), device(o, z, x, 1 - c)).start()

        def to_second(p, first):
            b = group(p, 1, first)
            send(p, b, b, (7 + first, 5 + first), near(p, True)).start()

        def local(p):
            return pltpu.make_async_copy(shard(p), chunk(p, z), local_sem.at[p])

        def own(p):
            @pl.when(z < 3)
            def _():
                up(p, z, 0, shard(p)).start()

            @pl.when(z > 0)
            def _():
                down(p, z, 0, shard(p)).start()

            local(p).start()

        def hop(d):
            def go(p):
                @pl.when(z >= d)
                def _():
                    wait(chunk(p, z - d), recv_sem.at[p, z - d])
                    if d < 3:
                        @pl.when(z < 3)
                        def _():
                            up(p, z - d, d).start()

                @pl.when(z + d <= 3)
                def _():
                    wait(chunk(p, z + d), recv_sem.at[p, z + d])
                    if d < 3:
                        @pl.when(z > 0)
                        def _():
                            down(p, z + d, d).start()
            return go

        third = hop(3)

        def first(p):
            third(p)
            local(p).wait()
            b = group(p, 1, 1)
            send(p, b, b, (6, 4), near(p, False)).start()
            to_second(p, 1)
            to_core(p, 1, 1)

        def second(p):
            wait(group(p, 1, 0), recv_sem.at[p, 4])
            to_second(p, 0)
            to_core(p, 1, 0)

        def cores(p):
            for f in (1, 0):
                wait(group(p, 0, f), recv_sem.at[p, 5 + f])
                to_core(p, 0, f)

        def arrived(p):
            for slot in range(4):
                wait(group(p, 1, 1), recv_sem.at[p, 7 + slot])

        def finish():
            for p in range(n):
                for d in range(3):
                    @pl.when(jnp.logical_and(z < 3, z >= d))
                    def _():
                        wait(chunk(p, z), send_sem.at[p, d])

                    @pl.when(jnp.logical_and(z > 0, z + d <= 3))
                    def _():
                        wait(chunk(p, z), send_sem.at[p, 3 + d])
                b = group(p, 1, 1)
                for slot in range(6, 13):
                    wait(b, send_sem.at[p, slot])

        self.finish = finish
        self.steps = (own, hop(1), hop(2), first, second, cores, arrived)

    def begin(self):
        greet(*place())


PARTS = (
        (2, 0, 48, 0, 768, True, 1), (3, 96, 96, 0, 384, False, 2), (3, 0, 96, 0, 384, False, 0), (2, 0, 48, 768, 768,
    True, 3), (1, 0, 48, 0, 384, False, 4), (0, 0, 48, 0, 640, True, 5), (0, 0, 48, 640, 512, False, 6), (6, 0, 48, 768,
    768, True, 3), (6, 0, 48, 0, 768, False, 1), (7, 96, 96, 0, 384, True, 2), (7, 0, 96, 0, 384, False, 0), (4, 0, 48,
    0, 640, True, 5), (4, 0, 48, 640, 512, False, 6), (5, 0, 48, 0, 384, True, 4), (8, 0, 16, 0, 128, False, 7))
BACK_PLAN = (
        (0, 0, 0), (0, 0, 1), (0, 0, 2), (0, 0, 3), (0, 0, 4), (1, 1, 0), (2, 2, 0), (2, 1, 1), (3, 2, 1), (3, 1, 2),
    (3, 1, 3), (4, 2, 2), (4, 2, 3), (5, 3, 0), (6, 4, 0), (6, 3, 1), (6, 1, 4), (7, 4, 1), (7, 2, 4), (10, 3, 3), (10,
    0, 5), (10, 0, 6), (11, 3, 2), (11, 4, 3), (12, 5, 1), (12, 4, 2), (12, 1, 5), (13, 5, 0), (13, 6, 1), (13, 2, 5),
    (14, 6, 0), (15, 7, 1), (15, 5, 2), (15, 3, 4), (16, 7, 0), (16, 6, 2), (16, 4, 4), (16, 1, 6), (16, 8, 1), (17, 5,
    3), (17, 2, 6), (18, 8, 0), (18, 9, 1), (18, 6, 3), (18, 7, 2), (18, 0, 9), (19, 3, 5), (20, 9, 0), (20, 8, 2), (20,
    5, 4), (20, 4, 5), (20, 7, 3), (20, 0, 8), (20, 1, 9), (21, 6, 4), (21, 2, 9), (21, 9, 2), (21, 3, 6), (21, 0, 10),
    (22, 8, 3), (22, 4, 6), (22, 1, 8), (22, 7, 4), (23, 2, 8), (23, 1, 10), (24, 9, 3), (24, 8, 4), (24, 5, 5), (24, 0,
    7), (24, 2, 10), (25, 6, 5), (26, 9, 4), (26, 0, 13), (27, 1, 7), (28, 7, 5), (29, 2, 7), (29, 3, 9), (29, 8, 5),
    (29, 0, 14), (29, 4, 9), (29, 5, 6), (29, 9, 5), (29, 0, 11), (29, 3, 8), (29, 6, 6), (29, 4, 8), (29, 7, 6), (29,
    8, 6), (29, 9, 6), (29, 0, 12), (29, 1, 11), (29, 2, 11), (29, 3, 7), (29, 3, 10), (29, 4, 7), (29, 4, 10), (29, 1,
    12), (29, 2, 12), (29, 5, 8), (29, 5, 9), (29, 6, 8), (29, 6, 9), (29, 7, 8), (29, 5, 7), (29, 6, 7), (29, 1, 13),
    (29, 8, 8), (29, 7, 9), (29, 2, 13), (29, 3, 11), (29, 4, 11), (29, 9, 8), (29, 8, 9), (29, 1, 14), (29, 7, 7), (29,
    2, 14), (29, 3, 12), (29, 4, 12), (29, 5, 10), (29, 9, 9), (29, 6, 10), (29, 8, 7), (29, 5, 11), (29, 3, 14), (29,
    6, 11), (29, 9, 7), (29, 4, 14), (29, 7, 10), (29, 3, 13), (29, 4, 13), (29, 8, 10), (29, 7, 11), (29, 5, 12), (29,
    6, 12), (29, 5, 14), (29, 6, 14), (29, 5, 13), (29, 9, 10), (29, 8, 11), (29, 6, 13), (29, 7, 12), (29, 9, 11), (29,
    7, 14), (29, 7, 13), (29, 8, 12), (29, 8, 14), (29, 8, 13), (29, 9, 12), (29, 9, 14), (29, 9, 13))


class Scatter:
    def __init__(self, parts, grads, outs, core_in, second_in, first_in, buffers, sems):
        o, z, x, c = place()
        acc, z_in, stage_own, stage_got, stage_second, stage_first, stage_out = buffers
        send_sem, recv_sem, own_sem, stage_sem, out_sem = sems
        n = len(parts)

        def kind(p):
            return 1 if parts[p][2] == 96 else 0

        def of(p):
            return parts[p][2], parts[p][4]

        def part(ref, p):
            r, w = of(p)
            return ref.at[:, pl.ds(0, r), pl.ds(0, w)]

        def group(p, second, first, core):
            g, r0, r, c0, w, first_x, _ = parts[p]
            px, po = (first, second) if first_x else (second, first)
            xx = x if px else 1 - x
            oo = o if po else 1 - o
            height, width = grads[g].shape
            each = width // 2
            return grads[g].reshape(4, 2, 2, height // 16, width).at[:, xx, core, pl.ds(r0, r), pl.ds(pl.multiple_of(oo * each + c0, 128), w)]

        def far(p, second):
            return device(o, z, 1 - x, c) if parts[p][5] != second else device(1 - o, z, x, c)

        def send(p, src, dst, kind_, slot, target):
            return pltpu.make_async_remote_copy(
                src_ref=src, dst_ref=dst, send_sem=send_sem.at[p, kind_], recv_sem=recv_sem.at[p, slot],
                device_id=target, device_id_type=MESH)

        def wait(ref, sem):
            pltpu.make_async_copy(ref, ref, sem).wait()

        slots, last_user = {}, {}
        turn = [0, 0]
        for p in range(n):
            k = kind(p)
            slots[p] = turn[k] % 2
            last_user[p] = next((q for q in range(p - 1, -1, -1) if kind(q) == k and slots[q] == slots[p]), None)
            turn[k] += 1

        def own_of(p):
            return part(stage_own[kind(p)].at[slots[p]], p)

        def total(p):
            return acc[parts[p][6]]

        def begin(p):
            for second in (0, 1):
                for first in (0, 1):
                    send(p, group(p, second, first, 1 - c), core_in[p].at[pl.ds(second * 8 + first * 4, 4)], 0, 0,
                         device(o, z, x, 1 - c)).start()
            for first in (0, 1):
                pltpu.make_async_copy(group(p, 1, first, c), total(p).at[pl.ds(first * 4, 4)], own_sem.at[p]).start()

        def core_fetch(p):
            k = kind(p)
            if last_user[p] is not None:
                q = last_user[p]
                wait(own_of(q), send_sem.at[q, 1])
            for first in (0, 1):
                pltpu.make_async_copy(group(p, 0, first, c), own_of(p).at[pl.ds(first * 4, 4)], stage_sem.at[kind(p), 0]).start()
            wait(core_in[p], recv_sem.at[p, 0])
            pltpu.make_async_copy(core_in[p].at[pl.ds(0, 8)], part(stage_got[k], p), stage_sem.at[kind(p), 1]).start()
            pltpu.make_async_copy(core_in[p].at[pl.ds(8, 8)], part(stage_second[k], p), stage_sem.at[kind(p), 2]).start()

        def core_add(p):
            own, got = own_of(p), part(stage_got[kind(p)], p)
            wait(own, stage_sem.at[kind(p), 0])
            wait(got, stage_sem.at[kind(p), 1])
            for first in (0, 1):
                s = pl.ds(first * 4, 4)
                own[s] = own[s] + got[s]
                send(p, own.at[s], second_in[p].at[s], 1, 1 + first, far(p, True)).start()
            mine = part(stage_second[kind(p)], p)
            wait(total(p), own_sem.at[p])
            wait(mine, stage_sem.at[kind(p), 2])
            total(p)[...] = total(p)[...] + mine[...]

        def second_fetch(p):
            got = part(stage_second[kind(p)], p)
            for first in (0, 1):
                s = pl.ds(first * 4, 4)
                wait(second_in[p].at[s], recv_sem.at[p, 1 + first])
            pltpu.make_async_copy(second_in[p], got, stage_sem.at[kind(p), 2]).start()

        def second_add(p):
            got = part(stage_second[kind(p)], p)
            wait(got, stage_sem.at[kind(p), 2])
            t = total(p)
            t[0:4] = t[0:4] + got[0:4]
            send(p, t.at[pl.ds(0, 4)], first_in[p], 2, 3, far(p, False)).start()
            t[4:8] = t[4:8] + got[4:8]

        def send_z(p, k, step):
            to = z + step
            slot = jnp.where(k == to, jnp.where(step > 0, k, 4), k)
            send(p, total(p).at[4 + k], z_in[p].at[slot], 3, 4 + slot, device(o, to, x, c)).start()

        def first_fetch(p):
            wait(first_in[p], recv_sem.at[p, 3])
            pltpu.make_async_copy(first_in[p], part(stage_first[kind(p)], p), stage_sem.at[kind(p), 3]).start()

        def first_add(p):
            got = part(stage_first[kind(p)], p)
            wait(got, stage_sem.at[kind(p), 3])
            t = total(p)
            t[4:8] = t[4:8] + got[...]

            @pl.when(z == 0)
            def _():
                for k in (3, 2, 1):
                    send_z(p, k, 1)

            @pl.when(z == 3)
            def _():
                for k in (0, 1, 2):
                    send_z(p, k, -1)

        def pass_on(p, k, step):
            wait(z_in[p].at[k], recv_sem.at[p, 4 + k])
            total(p)[4 + k] = total(p)[4 + k] + z_in[p][k]
            send_z(p, k, step)

        def along(level):
            def go(p):
                @pl.when(z == level)
                def _():
                    for k in range(3, level, -1):
                        pass_on(p, k, 1)

                @pl.when(z == 3 - level)
                def _():
                    for k in range(0, 3 - level):
                        pass_on(p, k, -1)
            return go

        out_user = [None, None]

        def copy_out(p):
            g, r0, r, c0, w, _, _ = parts[p]
            return pltpu.make_async_copy(stage_out[kind(p)].at[pl.ds(0, r), pl.ds(0, w)],
                                         outs[g].at[pl.ds(r0, r), pl.ds(c0, w)], out_sem.at[kind(p)])

        def finish():
            for p in out_user:
                copy_out(p).wait()

        def last(p):
            g, r0, r, c0, w, _, _ = parts[p]
            out = stage_out[kind(p)].at[pl.ds(0, r), pl.ds(0, w)]
            if out_user[kind(p)] is not None:
                copy_out(out_user[kind(p)]).wait()
            out_user[kind(p)] = p
            out[...] = total(p)[4 + z].astype(jnp.float32)

            @pl.when(z > 0)
            def _():
                wait(z_in[p].at[z], recv_sem.at[p, 4 + z])
                out[...] += z_in[p][z].astype(jnp.float32)

            @pl.when(z < 3)
            def _():
                wait(z_in[p].at[4], recv_sem.at[p, 8])
                out[...] += z_in[p][4].astype(jnp.float32)

            copy_out(p).start()
            wait(core_in[p], send_sem.at[p, 0])
            if all(last_user[q] != p for q in range(n)):
                wait(own_of(p), send_sem.at[p, 1])
            wait(first_in[p], send_sem.at[p, 2])
            wait(first_in[p].at[pl.ds(0, 3)], send_sem.at[p, 3])

        self.finish = finish
        self.steps = (begin, core_fetch, core_add, second_fetch, second_add, first_fetch, first_add, along(1), along(2), last)

    @staticmethod
    def shapes(parts):
        return [shape(m, s[2], s[4]) for m in (16, 8, 4) for s in parts]

    @staticmethod
    def scratch(parts):
        b16 = jnp.bfloat16
        sizes = {s[6]: (8, s[2], s[4]) for s in parts}
        acc = [(sizes[k], b16) for k in sorted(sizes)]
        lands = [((m, s[2], s[4]), b16) for m in (5,) for s in parts]
        stages = [((m, 48, 768), b16) if k == 0 else ((m, 96, 384), b16) for m in (8, 8, 4) for k in (0, 1)]
        stages = [((2, 8, 48, 768), b16), ((2, 8, 96, 384), b16)] + stages
        stages += [((48, 768), jnp.float32), ((96, 384), jnp.float32)]
        n = len(parts)
        return buffers(*acc, *lands, *stages) + [pltpu.SemaphoreType.DMA(k) for k in ((n, 4), (n, 9), (n,), (2, 4), (2,))]

    @staticmethod
    def unpack(parts, refs):
        n, m = len(parts), len({s[6] for s in parts})
        acc, refs = refs[:m], refs[m:]
        z_in, refs = refs[:n], refs[n:]
        return (acc, z_in, refs[0:2], refs[2:4], refs[4:6], refs[6:8], refs[8:10]), refs[10:15]


D = 768
SCALE = 0.125 * 1.4426950408889634
ROWS = 256
VMEM_BYTES = 127 * 2**19


def mul(a, b, ca=1, cb=0):
    return lax.dot_general(a, b, (((ca,), (cb,)), ((), ())), preferred_element_type=jnp.float32)


def low(v):
    return v.astype(jnp.bfloat16)


def cols(j):
    return pl.ds(pl.multiple_of(j * D, D), D)


def rms_scale(v):
    return lax.rsqrt(jnp.mean(v * v, axis=-1, keepdims=True) + 1e-06)


def rms_back(v, gain, grad):
    r = rms_scale(v)
    unit = v * r
    scaled = grad * gain
    back = r * (scaled - unit * jnp.mean(scaled * unit, axis=-1, keepdims=True))
    return back, jnp.sum((grad * unit).reshape(-1, 8, v.shape[-1]), axis=0)


def gelu_and_slope(u):
    k = 0.7978845608028654
    square = u * u
    t = jnp.tanh(u * (k + k * 0.044715 * square))
    half = 0.5 + 0.5 * t
    return u * half, half + u * (0.5 - 0.5 * t * t) * (k + 3 * 0.044715 * k * square)


def halves(v):
    lane = lax.broadcasted_iota(jnp.int32, v.shape, 1)
    zero = jnp.zeros_like(v)
    return jnp.where(lane < 64, v, zero), jnp.where(lane < 64, zero, v)


def two(v):
    first = low(v)
    return first, low(v - first.astype(jnp.float32))


class Block:
    def __init__(self, rows, refs):
        self.rows = rows
        self.__dict__.update(refs)

    @staticmethod
    def scratch(rows):
        f32, b16 = jnp.float32, jnp.bfloat16
        return dict(
            branch=((rows, D), f32), projected=((rows, 3 * D), b16), merged=((rows, D), b16), lse=((6, 8, rows), f32),
            active=((rows, 4 * D), b16), slope=((rows, 4 * D), b16), normed=((rows, D), b16), normed_mlp=((rows, D), b16))

    def rows_of(self, t):
        return self.x[t].astype(jnp.float32)

    def tiles(self):
        return [slice(i, i + ROWS) for i in range(0, self.rows, ROWS)]

    def norm(self):
        for t in self.tiles():
            x = self.rows_of(t)
            self.normed[t] = low(x * rms_scale(x) * self.gain_attn[...])

    def project(self, j):
        c = cols(j)
        self.projected[:, c] = low(mul(self.normed[...], self.qkv[:, c]))

    def pair(self, ref, part, pair, rows=slice(None)):
        return ref[rows, pl.ds(pl.multiple_of(part * D + pair * 128, 128), 128)]

    def attend(self, pair):
        v0, v1 = halves(self.pair(self.projected, 2, pair))
        causal = lax.broadcasted_iota(jnp.int32, (ROWS, ROWS), 1) >= lax.broadcasted_iota(jnp.int32, (ROWS, ROWS), 0)
        for t in self.tiles():
            n = t.stop
            qs = halves(self.pair(self.projected, 0, pair, t))
            k = self.pair(self.projected, 1, pair, slice(0, n))
            total = None
            for h in range(2):
                s = mul(k, qs[h], 1, 1)
                last = jnp.where(causal, s[t.start:], -1e30)
                s = last if t.start == 0 else jnp.concatenate([s[: t.start], last], axis=0)
                m = jnp.max(s, axis=0, keepdims=True) * SCALE
                p = jnp.exp2(s * SCALE - m)
                l = jnp.sum(p, axis=0, keepdims=True)
                self.lse[pair, h : h + 1, t] = m + jnp.log2(l)
                o = mul(low(p * (1.0 / l)), (v0, v1)[h][:n], 0, 0)
                total = o if total is None else total + o
            self.merged[t, pl.ds(pl.multiple_of(pair * 128, 128), 128)] = low(total)

    def join(self):
        for t in self.tiles():
            branch = mul(self.merged[t], self.out[...])
            self.branch[t] = branch
            middle = self.rows_of(t) + branch
            self.normed_mlp[t] = low(middle * rms_scale(middle) * self.gain_mlp[...])

    def widen(self, j):
        c = cols(j)
        for t in self.tiles():
            active, slope = gelu_and_slope(mul(self.normed_mlp[t], self.up[:, c]))
            self.active[t, c] = low(active)
            self.slope[t, c] = low(slope)

    def narrow(self, t):
        return mul(self.active[t], self.down[...])

    def back_wide(self, j):
        c = cols(j)
        for t in self.tiles():
            grad = mul(self.grad_low[t], self.down[c, :], 1, 1)
            self.slope[t, c] = low(grad * self.slope[t, c].astype(jnp.float32))

    def grad_down(self, j):
        return low(mul(self.active[:, cols(j)], self.grad_low[...], 0, 0))

    def grad_up(self, j):
        return low(mul(self.normed_mlp[...], self.slope[:, cols(j)], 0, 0))

    def back_mlp(self, grad_of):
        total = jnp.zeros((8, D), jnp.float32)
        for t in self.tiles():
            grad = mul(self.slope[t], self.up[...], 1, 1)
            back, gain = rms_back(self.rows_of(t) + self.branch[t], self.gain_mlp[...], grad)
            total = total + gain
            self.branch[t] = back
            self.normed_mlp[t] = low(grad_of(t) + back)
        return jnp.sum(total, axis=0, keepdims=True)

    def grad_out(self):
        return low(mul(self.merged[...], self.normed_mlp[...], 0, 0))

    def back_merged(self):
        self.active[:, :D] = low(mul(self.normed_mlp[...], self.out[...], 1, 1))

    def attend_back(self, pair, turned):
        rows = self.rows
        q, do = self.pair(self.projected, 0, pair), self.pair(self.active, 0, pair)
        qs, dos = halves(q), halves(do)
        dd = do.astype(jnp.float32) * self.pair(self.merged, 0, pair).astype(jnp.float32)
        pick = lax.broadcasted_iota(jnp.int32, (8, 128), 0) == lax.broadcasted_iota(jnp.int32, (8, 128), 1) // 64
        delta = lax.dot_general(pick.astype(jnp.float32), dd, (((1,), (1,)), ((), ())), precision=lax.Precision.HIGHEST,
                                preferred_element_type=jnp.float32)
        causal = lax.broadcasted_iota(jnp.int32, (ROWS, ROWS), 1) >= lax.broadcasted_iota(jnp.int32, (ROWS, ROWS), 0)
        for t in self.tiles():
            a = t.start
            ks, vs = halves(self.pair(self.projected, 1, pair, t)), halves(self.pair(self.projected, 2, pair, t))
            dk = dv = dq = 0.0
            for h in range(2):
                s = mul(ks[h], q[a:], 1, 1)
                p = jnp.exp2(s * SCALE - self.lse[pair, h : h + 1, a:])
                first = jnp.where(causal, p[:, :ROWS], 0.0)
                p = first if t.stop == rows else jnp.concatenate([first, p[:, ROWS:]], axis=1)
                dp = mul(vs[h], do[a:], 1, 1)
                ds = low(p * (dp - delta[h : h + 1, a:]))
                dv = dv + mul(low(p), dos[h][a:])
                dk = dk + mul(ds, qs[h][a:])
                dq = dq + mul(ks[h], ds, 0, 0)
            lanes = pl.multiple_of(pair * 128, 128)
            self.projected[t, pl.ds(D + lanes, 128)] = low(0.125 * dk)
            self.projected[t, pl.ds(2 * D + lanes, 128)] = low(dv)
            if a == 0:
                turned[:, :rows] = dq
            else:
                turned[:, a:rows] += dq
        self.projected[:, pl.ds(lanes, 128)] = low(0.125 * turned[:, :rows].T)

    def grad_qkv(self, j):
        return low(mul(self.normed[...], self.projected[:, cols(j)], 0, 0))

    def back_norm(self, finish):
        total = jnp.zeros((8, D), jnp.float32)
        for t in self.tiles():
            grad = mul(self.projected[t], self.qkv[...], 1, 1)
            back, gain = rms_back(self.rows_of(t), self.gain_attn[...], grad)
            total = total + gain
            finish(t, back + self.branch[t])
        return jnp.sum(total, axis=0, keepdims=True)


SAVED = ("branch", "projected", "merged", "lse", "active", "slope", "normed", "normed_mlp")


def run(steps, hooks=None):
    at = 0
    waits = []
    for count, body in steps:
        if count == 0:
            waits.append(body)
            continue
        before = [list(hooks[at + k]) if hooks else [] for k in range(count)]
        at += count
        for f in before[0]:
            f()
        for f in waits:
            f(0)
        waits = []
        if count == 1:
            body(0)
            continue

        @pl.loop(0, count)
        def _(j):
            for k in range(1, count):
                if before[k]:
                    @pl.when(j == k)
                    def _():
                        for f in before[k]:
                            f()
            body(j)


class Loads:
    def __init__(self, pairs, sems):
        self.copies = {k: pltpu.make_async_copy(a, b, sems.at[j]) for j, (k, a, b) in enumerate(pairs)}
        for c in self.copies.values():
            c.start()

    def need(self, *names):
        for n in names:
            self.copies[n].wait()


class Ship:
    def __init__(self, stages, sems):
        self.stages, self.sems, self.single = stages, sems, len(stages) == 1

    def wait(self, slot):
        slot = min(slot, len(self.stages) - 1)
        pltpu.make_async_copy(self.stages[slot], self.stages[slot], self.sems.at[slot]).wait()

    def send(self, slot, value, target, busy):
        slot = min(slot, len(self.stages) - 1)
        if busy is True:
            self.wait(slot)
        elif busy is not False:
            pl.when(busy)(lambda: self.wait(slot))
        self.stages[slot][...] = value()
        pltpu.make_async_copy(self.stages[slot], target, self.sems.at[slot]).start()


def wide_steps(b, grad_of, ship, targets, vec):
    gout, gup, gdown = targets

    def wide(j):
        b.back_wide(j)
        ship.send(0, lambda: b.grad_down(j), gdown.at[cols(j), :], j > 0)
        ship.send(1, lambda: b.grad_up(j), gup.at[:, cols(j)], ship.single or j > 0)

    def mlp(_):
        ship.wait(0)
        if not ship.single:
            ship.wait(1)
        vec(b.back_mlp(grad_of))

    def out(_):
        ship.send(1, b.grad_out, gout, False)
        b.back_merged()

    return [(4, wide), (1, mlp), (1, out)]


def attend_steps(b, ship, gqkv, vec, finish, turned, busy):
    def qkv(j):
        ship.send(1, lambda: b.grad_qkv(j), gqkv.at[:, cols(j)], True if busy else j > 0)

    def norm(_):
        vec(b.back_norm(finish))
        ship.wait(1)

    return [(6, lambda j: b.attend_back(j, turned)), (3, qkv), (1, norm)]


KEPT_DENSE = ("x", "branch", "projected", "merged", "lse", "normed_mlp")


MIDDLE_IN = ("x", "branch", "merged", "normed_mlp")


def middle_kernel(cot_hbm, vec_ref, out_hbm, up_hbm, down_hbm, *rest):
    n = len(MIDDLE_IN)
    kept_hbm, rest = rest[:n], rest[n:]
    y_hbm, grad_hbm, gmerged_hbm, gvec_ref, gout_hbm, gup_hbm, gdown_hbm = rest[:7]
    cot, out, up, down, active, slope, y, stage_0, stage_1, load_sem, stage_sem, row_sem = rest[7:19]
    kept = dict(zip(MIDDLE_IN, rest[19:]))
    where = dict(zip(MIDDLE_IN, zip(kept_hbm, rest[19:])), cot=(cot_hbm, cot), out=(out_hbm, out), up=(up_hbm, up), down=(down_hbm, down))
    order = ("normed_mlp", "up", "down", "x", "branch", "cot", "out", "merged")
    loads = Loads([(k,) + where[k] for k in order], load_sem)
    b = Block(cot.shape[0], dict(kept, active=active, slope=slope, grad_low=cot, out=out, up=up, down=down,
                                 gain_mlp=vec_ref.at[4:5]))

    def narrow(_):
        loads.need("x", "branch", "down")
        for t in b.tiles():
            y[t] = low(b.x[t] + b.branch[t] + b.narrow(t))
        pltpu.make_async_copy(y, y_hbm, row_sem.at[0]).start()
        loads.need("cot")

    def vec(value):
        gvec_ref[...] = value

    def cot_of(t):
        return cot[t].astype(jnp.float32)

    def grad(_):
        for t in b.tiles():
            b.branch[t] += cot_of(t)
        pltpu.make_async_copy(b.branch, grad_hbm, row_sem.at[1]).start()
        loads.need("out", "merged")

    ship = Ship((stage_0, stage_1), stage_sem)
    wide, mlp, last = wide_steps(b, cot_of, ship, (gout_hbm, gup_hbm, gdown_hbm), vec)
    run([(0, lambda _: loads.need("normed_mlp", "up")), (4, b.widen), (1, narrow), wide, mlp, (0, grad), last])
    pltpu.make_async_copy(active.at[:, pl.ds(0, D)], gmerged_hbm, row_sem.at[2]).start()
    ship.wait(1)
    for src, dst, j in ((y, y_hbm, 0), (b.branch, grad_hbm, 1), (active.at[:, pl.ds(0, D)], gmerged_hbm, 2)):
        pltpu.make_async_copy(src, dst, row_sem.at[j]).wait()


def shape(*dims, dtype=jnp.bfloat16):
    return jax.ShapeDtypeStruct(dims, dtype)


def any_specs(n):
    return [pl.BlockSpec(memory_space=pl.ANY)] * n


def vmem_specs(n):
    return [pl.BlockSpec(memory_space=pltpu.VMEM)] * n


WEIGHTS = [((D, 3 * D), jnp.bfloat16), ((D, D), jnp.bfloat16), ((D, 4 * D), jnp.bfloat16), ((4 * D, D), jnp.bfloat16)]


def buffers(*pairs):
    return [pltpu.VMEM(dims, dtype) for dims, dtype in pairs]


def kept_buffers(rows):
    s = Block.scratch(rows)
    return [s[k] for k in SAVED]


def dense_middle(cot, vec, weights, kept):
    rows = cot.shape[0]
    f32, b16 = jnp.float32, jnp.bfloat16
    every = dict(Block.scratch(rows), x=((rows, D), f32))
    return pl.pallas_call(
        middle_kernel,
        in_specs=any_specs(1) + vmem_specs(1) + any_specs(3 + len(kept)),
        out_specs=any_specs(3) + vmem_specs(1) + any_specs(3),
        out_shape=[shape(rows, D), shape(rows, D, dtype=f32), shape(rows, D), shape(1, D, dtype=f32)]
        + [shape(*s) for s, _ in WEIGHTS[1:]],
        scratch_shapes=buffers(((rows, D), b16), *WEIGHTS[1:], every["active"], every["slope"], ((rows, D), b16),
                               ((D, D), b16), ((D, D), b16))
        + [pltpu.SemaphoreType.DMA((8,)), pltpu.SemaphoreType.DMA((2,)), pltpu.SemaphoreType.DMA((3,))]
        + buffers(*[every[k] for k in MIDDLE_IN]),
        compiler_params=pltpu.CompilerParams(vmem_limit_bytes=VMEM_BYTES),
        name="dense_middle",
    )(cot, vec, *weights, *kept)


def spots(start, count, spot):
    at = lax.broadcasted_iota(jnp.int32, (count, spot.shape[1]), 0) + start
    return low(jnp.where(at == spot, 1.0, 0.0))


def lane_map(outer, inner):
    each = D // (outer * inner)
    d = jnp.arange(D, dtype=jnp.int32)
    return jnp.stack([d // each % inner, d // (each * inner) * 128 + d % each])


def spread_map(tiles_columns, map_ref):
    at = lax.broadcasted_iota(jnp.int32, (tiles_columns, D), 0)
    return low(jnp.where(at == map_ref[1:2], 1.0, 0.0))


def read_vectors(tiles, map_ref):
    rows, columns = tiles.shape
    every = mul(tiles[...], spread_map(columns, map_ref))
    inner = lax.broadcasted_iota(jnp.int32, (rows, D), 0) // 16
    return jnp.sum(jnp.where(inner == map_ref[0:1], every, 0.0).reshape(rows // 16, 16, D), axis=0)


def write_vectors(vectors, rows, columns, map_ref):
    every = jnp.broadcast_to(vectors[None], (rows // 16, 16, D)).reshape(rows, D)
    inner = lax.broadcasted_iota(jnp.int32, (rows, D), 0) // 16
    return low(mul(low(jnp.where(inner == map_ref[0:1], every, 0.0)), spread_map(columns, map_ref), 1, 1))


def gate_of(x, router):
    return jax.nn.sigmoid(jnp.sum(x * router, axis=-1, keepdims=True))


def routed_forward_steps(b, need, hidden, spot_ref, chosen, vec_ref, extra, keep):
    length = hidden.shape[0]

    def pick(_):
        chosen[...] = spots(0, length, spot_ref[...])
        need("hidden")
        for t in b.tiles():
            b.x[t] = low(mul(chosen[:, t], hidden[...], 0, 0))
        need("vectors")
        b.norm()
        keep("x", "normed")

    def join(_):
        keep("projected", "merged", "lse")
        need("out")
        b.join()
        keep("branch", "normed_mlp")

    def narrow(_):
        keep("active", "slope")
        need("down")
        for t in b.tiles():
            extra[t] = b.branch[t] + b.narrow(t)
        keep("change")

    def put(_):
        rows = [gate_of(b.rows_of(t), vec_ref[2:3]) * extra[t] for t in b.tiles()]
        pieces = [two(r) for r in rows]
        for i in range(0, length, ROWS):
            t = slice(i, i + ROWS)
            total = hidden[t].astype(jnp.float32)
            for piece, s in zip(pieces, b.tiles()):
                for p in piece:
                    total = total + mul(chosen[t, s], p)
            b.middle[t] = total

    return [(1, pick), (0, lambda _: need("qkv")), (3, b.project), (6, b.attend), (1, join), (0, lambda _: need("up")), (4, b.widen),
            (1, narrow), (1, put)]


KEPT = ("x", "change") + SAVED


def kept_shapes(rows):
    return [((rows, D), jnp.bfloat16), ((rows, D), jnp.float32)] + kept_buffers(rows)


def routed_backward_steps(b, need, grad, spot_ref, vec_ref, change, grad_rows, gate, ship, targets, vec, turned,
                          grad_hbm, grad_sem):
    length = grad.shape[0]
    router = vec_ref.at[2:3]
    gqkv, *others = targets

    def take(_):
        pieces = two(grad[...])
        need("x", "change")
        for t in b.tiles():
            chosen = spots(0, length, spot_ref[:, t])
            rows = mul(chosen, pieces[0], 0, 0) + mul(chosen, pieces[1], 0, 0)
            g = gate_of(b.rows_of(t), router[...])
            b.grad_low[t], grad_rows[t] = two(g * rows)
            logits = jnp.sum(rows * change[t], axis=-1, keepdims=True) * g * (1.0 - g)
            gate[t] = jnp.broadcast_to(logits, (ROWS, 128))
        need("down", "active", "slope", "normed_mlp")

    def finish(t, g):
        change[t] = g + gate[t, 0:1] * router[...]

    def put(_):
        pieces = [two(change[t]) for t in b.tiles()]
        for i in range(0, length, ROWS):
            t = slice(i, i + ROWS)
            total = grad[t]
            for piece, s in zip(pieces, b.tiles()):
                chosen = spots(i, ROWS, spot_ref[:, s])
                for p in piece:
                    total = total + mul(chosen, p)
            grad[t] = total
            pltpu.make_async_copy(grad.at[t], grad_hbm.at[t], grad_sem).start()

    def route(_):
        total = jnp.zeros((8, D), jnp.float32)
        for t in b.tiles():
            total = total + jnp.sum((gate[t, 0:1] * b.rows_of(t)).reshape(-1, 8, D), axis=0)
        vec(2, jnp.sum(total, axis=0, keepdims=True))

    wide, mlp, out = wide_steps(b, lambda t: b.grad_low[t].astype(jnp.float32) + grad_rows[t].astype(jnp.float32), ship, others, lambda v: vec(1, v))
    attend, qkv, norm = attend_steps(b, ship, gqkv, lambda v: vec(0, v), finish, turned, True)

    def wants(*names):
        return (0, lambda _: need(*names))

    return [(1, take), wide, wants("up", "branch"), mlp, wants("out", "merged"), out, wants("projected", "lse"), attend,
            wants("normed"), qkv, wants("qkv"), norm, (1, route), (1, put)]


def forward_kernel(remote, *refs):
    hidden_hbm, spot_ref, map_ref, *refs = refs
    given, refs = refs[:9], refs[9:]
    if remote:
        whole, refs = refs[:9], refs[9:]
    else:
        whole = given
    vec_ref, *refs = refs
    n, m = len(KEPT), len(KEPT_DENSE)
    kept_hbm, refs = dict(zip(KEPT, refs[:n])), refs[n:]
    dense_hbm, refs = dict(zip(KEPT_DENSE, refs[:m])), refs[m:]
    hidden, chosen, tiles, *refs = refs
    weights, refs = refs[:6], refs[6:]
    kept, refs = dict(zip(KEPT, refs[:n])), refs[n:]
    dense, refs = dict(zip(KEPT_DENSE, refs[:m])), refs[m:]
    normed, load_sem, keep_sem, dense_sem = refs[:4]
    names = ("vectors", "qkv", "out", "up", "down", "qkv_b", "out_b")
    first = pltpu.make_async_copy(hidden_hbm, hidden, load_sem.at[7])
    first.start()
    loads = {k: pltpu.make_async_copy(whole[j], dst, load_sem.at[j])
             for j, (k, dst) in enumerate(zip(names, [tiles] + weights))}
    flow = Gather(GATHER_PARTS, given, whole, *refs[4:]) if remote else None
    if not remote:
        for c in loads.values():
            c.start()

    def need(*wanted):
        for k in wanted:
            if k == "hidden":
                first.wait()
                continue
            loads[k].wait()
            if k == "vectors":
                vec_ref[...] = read_vectors(tiles, map_ref)

    saves = {k: pltpu.make_async_copy(kept[k], kept_hbm[k], keep_sem.at[j]) for j, k in enumerate(KEPT)}
    dense_saves = {k: pltpu.make_async_copy(dense[k], dense_hbm[k], dense_sem.at[j]) for j, k in enumerate(KEPT_DENSE)}

    def keep(*wanted):
        for k in wanted:
            saves[k].start()

    def keep_dense(*wanted):
        for k in wanted:
            dense_saves[k].start()

    qkv, out, up, down, qkv_b, out_b = weights
    b = Block(spot_ref.shape[1], dict(kept, middle=dense["x"], qkv=qkv, out=out, up=up, down=down,
                                      gain_attn=vec_ref.at[0:1], gain_mlp=vec_ref.at[1:2]))
    d = Block(hidden.shape[0], dict(dense, qkv=qkv_b, out=out_b, normed=normed,
                                    gain_attn=vec_ref.at[3:4], gain_mlp=vec_ref.at[4:5]))

    def norm(_):
        keep_dense("x")
        d.norm()

    def join(_):
        keep_dense("projected", "merged", "lse")
        need("out_b")
        d.join()
        keep_dense("branch", "normed_mlp")

    routed = routed_forward_steps(b, need, hidden, spot_ref, chosen, vec_ref, kept["change"], keep)
    steps = routed + [(1, norm), (0, lambda _: need("qkv_b")), (3, d.project), (6, d.attend), (1, join)]
    if remote:
        last = {part[0]: p for p, part in enumerate(GATHER_PARTS)}

        def take(step, p):
            flow.steps[step](p)
            a = GATHER_PARTS[p][0]
            if step == 6 and p == last[a] and a < len(names):
                loads[names[a]].start()

        units = [[] for _ in range(sum(c for c, _ in steps) + 1)]
        for unit, step, p in GATHER_PLAN:
            units[unit].append(functools.partial(take, step, p))
        flow.begin()
        run(steps, units)
        for f in units[-1]:
            f()
        flow.finish()
    else:
        run(steps)
    for c in list(saves.values()) + list(dense_saves.values()):
        c.wait()


def forward(remote, hidden, spot, place_map, weights, outer, inner):
    length, rows = hidden.shape[0], spot.shape[1]
    f32, b16 = jnp.float32, jnp.bfloat16
    kept = kept_shapes(rows)
    every = dict(Block.scratch(length), x=((length, D), f32))
    dense = [every[k] for k in KEPT_DENSE]
    whole = [shape(w.shape[0] * inner, w.shape[1] * outer) for w in weights] if remote else []
    tiles = (16 * inner, 128 * outer)
    scratch = (buffers(((length, D), b16), ((length, rows), b16), (tiles, b16), *WEIGHTS, *WEIGHTS[:2], *kept, *dense, ((length, D), b16))
               + [pltpu.SemaphoreType.DMA((k,)) for k in (8, len(kept), len(dense))])
    if remote:
        scratch += Gather.semaphores(len(GATHER_PARTS))
    results = pl.pallas_call(
        functools.partial(forward_kernel, remote),
        in_specs=any_specs(1) + vmem_specs(2) + any_specs(9),
        out_specs=any_specs(len(whole)) + vmem_specs(1) + any_specs(len(kept) + len(dense)),
        out_shape=whole + [shape(16, D, dtype=f32)] + [shape(*s, dtype=t) for s, t in kept + dense],
        scratch_shapes=scratch,
        compiler_params=pltpu.CompilerParams(vmem_limit_bytes=VMEM_BYTES, **(dict(collective_id=0, has_side_effects=True) if remote else {})),
        name="forward",
    )(hidden, spot, place_map, *weights)
    if remote:
        weights, results = results[:9], results[9:]
    return weights, results[0], results[1 : 1 + len(kept)], results[1 + len(kept) :]


DENSE_IN = ("x", "projected", "merged", "lse", "grad_merged", "plus")


def backward_kernel(remote, *refs):
    spot_ref, map_ref, vec_ref, gmlp_ref, *refs = refs
    weights_hbm, refs = refs[:5], refs[5:]
    n, m = len(KEPT), len(DENSE_IN)
    dense_hbm, refs = dict(zip(DENSE_IN, refs[:m])), refs[m:]
    kept_hbm, refs = dict(zip(KEPT, refs[:n])), refs[n:]
    given, refs = refs[:3], refs[3:]
    input_hbm, *refs = refs
    if remote:
        outs, refs = refs[:9], refs[9:]
    else:
        gvec_ref, *refs = refs
    made, refs = refs[:5], refs[5:]
    if remote:
        k = len(PARTS)
        core_in, second_in, first_in, refs = refs[:k], refs[k : 2 * k], refs[2 * k : 3 * k], refs[3 * k :]
    (x, plus, projected, merged, grad_merged, lse, normed, qkv, turned, grad_rows, gate, out, up, down, x_a, active, slope,
     stage, load_sem, stage_sem, row_sem, *refs) = refs
    half = spot_ref.shape[1]
    top, rest = pl.ds(0, half), pl.ds(half, half)
    a_refs = dict(x=x_a, change=plus.at[rest], branch=plus.at[top], projected=projected.at[top], merged=merged.at[top],
                  lse=lse.at[:, :, top], active=active, slope=slope, normed=normed.at[top], normed_mlp=normed.at[rest])
    copies = dict(zip(("d_qkv", "qkv", "out", "up", "down"), zip(weights_hbm, (qkv, qkv, out, up, down))))
    copies.update({"d_" + k: (dense_hbm[k], r) for k, r in zip(DENSE_IN, (x, projected, merged, lse, grad_merged, plus))})
    copies.update({k: (kept_hbm[k], a_refs[k]) for k in KEPT})
    copies = {k: pltpu.make_async_copy(*v, load_sem.at[j]) for j, (k, v) in enumerate(copies.items())}
    late = ("change", "normed_mlp", "branch", "merged", "projected", "lse", "normed", "qkv")
    for k in ("d_projected", "d_merged", "d_grad_merged", "d_lse", "d_x", "d_qkv", "d_plus", "x", "down", "active", "slope", "up", "out"):
        copies[k].start()

    def need(*names):
        for k in names:
            copies[k].wait()

    d = Block(x.shape[0], dict(x=x, branch=plus, projected=projected, merged=merged, lse=lse, active=grad_merged, normed=normed,
                               qkv=qkv, gain_attn=vec_ref.at[3:4]))
    b = Block(half, dict(a_refs, grad_low=grad_merged.at[rest], qkv=qkv, out=out, up=up, down=down,
                         gain_attn=vec_ref.at[0:1], gain_mlp=vec_ref.at[1:2]))
    if remote:
        gvec_ref, tile, *refs = refs
    gvec_ref[...] = jnp.zeros_like(gvec_ref)
    gvec_ref[4:5] = gmlp_ref[...]

    def vec(j, value):
        gvec_ref[j : j + 1] = value

    ship = Ship((stage,), stage_sem)
    gqkv_b, gqkv_a, gout_a, gup_a, gdown_a = made

    def finish(t, g):
        x[t] = g

    attend, qkv_step, norm_step = attend_steps(d, ship, gqkv_b, lambda v: vec(3, v), finish, turned, False)

    def norm(_):
        norm_step[1](0)
        for k in late:
            copies[k].start()

    steps = [(0, lambda _: need("d_projected", "d_merged", "d_grad_merged", "d_lse")), attend,
             (0, lambda _: need("d_x")), (0, lambda _: d.norm()), qkv_step, (0, lambda _: need("d_qkv", "d_plus")), (1, norm)]
    steps += routed_backward_steps(b, need, x, spot_ref, vec_ref, a_refs["change"], grad_rows, gate, ship,
                                   (gqkv_a, gout_a, gup_a, gdown_a), vec, turned, input_hbm, row_sem.at[0])
    if not remote:
        run(steps)
    else:
        grads = (gqkv_b, *given, gqkv_a, gout_a, gup_a, gdown_a, tile)
        sums = Scatter(PARTS, grads, outs, core_in, second_in, first_in, *Scatter.unpack(PARTS, refs))

        hooks = [[] for _ in range(sum(c for c, _ in steps) + 1)]
        for unit, step, p in BACK_PLAN:
            hooks[unit].append(functools.partial(sums.steps[step], p))
        greet(*place())
        run(steps, hooks)
        tile[...] = write_vectors(gvec_ref[...], *tile.shape, map_ref)
        for g in hooks[-1]:
            g()
        sums.finish()
    pltpu.make_async_copy(x, input_hbm, row_sem.at[0]).wait()


def backward(remote, spot, place_map, vec, gmlp, weights, dense, kept, given, outer, inner):
    length, rows = dense[0].shape[0], spot.shape[1]
    f32, b16 = jnp.float32, jnp.bfloat16
    made = [shape(*WEIGHTS[j][0]) for j in (0, 0, 1, 2, 3)]
    results = [shape(length, D, dtype=f32)]
    specs = any_specs(1)
    if remote:
        shards = [shape(s[0] // inner, s[1] // outer, dtype=f32) for s, _ in WEIGHTS]
        results += shards + shards + [shape(16, 128, dtype=f32)]
        specs += any_specs(9)
        lands = Scatter.shapes(PARTS)
    else:
        results += [shape(16, D, dtype=f32)]
        specs += vmem_specs(1)
        lands = []
    every = dict(Block.scratch(length), x=((length, D), f32))
    short = Block.scratch(rows)
    scratch = buffers(*[every[k] for k in ("x", "x", "projected", "merged", "merged", "lse", "normed")], WEIGHTS[0],
                      ((128, length), f32), ((rows, D), b16), ((rows, 128), f32), *WEIGHTS[1:],
                      ((rows, D), b16), short["active"], short["slope"], ((D, D), b16))
    scratch += [pltpu.SemaphoreType.DMA((k,)) for k in (5 + len(DENSE_IN) + len(kept), 2, 1)]
    if remote:
        scratch += buffers(((16, D), f32), ((16 * inner, 128 * outer), b16)) + Scatter.scratch(PARTS)
    return pl.pallas_call(
        functools.partial(backward_kernel, remote),
        in_specs=vmem_specs(4) + any_specs(5 + len(dense) + len(kept) + len(given)),
        out_specs=specs + any_specs(len(made) + len(lands)),
        out_shape=results + made + lands,
        scratch_shapes=scratch,
        compiler_params=pltpu.CompilerParams(vmem_limit_bytes=VMEM_BYTES, **(dict(collective_id=1, has_side_effects=True) if remote else {})),
        name="backward",
    )(spot, place_map, vec, gmlp, *weights, *dense, *kept, *given)


def pack_vectors(vectors):
    rows = jnp.stack([jnp.pad(v, (0, 128 - v.shape[0])) for v in vectors])
    return jnp.pad(rows, ((0, 16 - rows.shape[0]), (0, 0)))


def spread_vectors(vectors, outer, inner):
    rows = vectors.reshape(vectors.shape[0], outer, inner, -1).transpose(2, 0, 1, 3).astype(jnp.bfloat16)
    tiles = jnp.pad(rows, ((0, 0), (0, 16 - rows.shape[1]), (0, 0), (0, 128 - rows.shape[3])))
    return tiles.reshape(inner * 16, outer * 128)


def deliver_kernel(n, *refs):
    tile, sums, outs, vectors = refs[0], refs[1 : n + 1], refs[n + 1 : 2 * n + 1], refs[2 * n + 1 :]
    for a, b in zip(sums, outs):
        b[...] = a[...]
    for j, v in enumerate(vectors):
        v[...] = tile[j : j + 1, : v.shape[1]]


def deliver(tile, sums, each, count):
    n = len(sums)
    return pl.pallas_call(
        functools.partial(deliver_kernel, n),
        in_specs=vmem_specs(1 + n),
        out_specs=vmem_specs(n + count),
        out_shape=[shape(*s.shape, dtype=s.dtype) for s in sums] + [shape(1, each, dtype=jnp.float32)] * count,
        name="deliver",
    )(tile, *sums)


def fits(shards, outer, inner):
    return outer == 2 and inner == 16 and all(s.shape[0] % 16 == 0 and s.shape[1] % 128 == 0 for s in shards)


def per_device(outer, inner, *args):
    hidden, cotangent, capacity_class, token_index = args[:4]
    (gain_attn_a, qkv_a, out_a, gain_mlp_a, up_a, down_a, router_shard,
     gain_attn_b, qkv_b, out_b, gain_mlp_b, up_b, down_b) = args[4:]
    hidden, cotangent = hidden[0], cotangent[0]
    length = hidden.shape[0]
    tile = pack_vectors((gain_attn_a, gain_mlp_a, router_shard, gain_attn_b, gain_mlp_b))
    shards = [tile, qkv_a, out_a, up_a, down_a, qkv_b, out_b, up_b, down_b]
    remote = fits(shards, outer, inner)
    if not remote:
        shards = [lax.all_gather(lax.all_gather(s, "inner", axis=0, tiled=True), "outer", axis=1, tiled=True) for s in shards]

    capacity = (length // 8) << capacity_class[0]
    slots = lax.broadcasted_iota(jnp.int32, token_index.shape, 1)
    spot = jnp.where(slots < capacity, token_index, -1)
    whole, vec, kept, kept_dense = forward(remote, hidden, spot, lane_map(outer, inner), shards, outer, inner)
    saved = dict(zip(KEPT_DENSE, kept_dense))
    output, plus, grad_merged, gmlp, *given = dense_middle(
        cotangent, vec, whole[6:], [saved[k] for k in MIDDLE_IN])
    dense = [saved[k] for k in DENSE_IN[:4]] + [grad_merged, plus]
    input_grad, *res = backward(remote, spot, lane_map(outer, inner), vec, gmlp, (whole[5], *whole[1:5]), dense, kept, given, outer, inner)
    if remote:
        done, gtile = res[:8], res[8]
    else:
        gvec, gqkv_b, *grads_a = res
        done = [
            lax.psum_scatter(
                lax.psum_scatter(s, "outer", scatter_dimension=1, tiled=True), "inner", scatter_dimension=0, tiled=True
            ).astype(jnp.float32)
            for s in [gqkv_b, *given, *grads_a, spread_vectors(gvec[:5], outer, inner)]
        ]
        done, gtile = done[:8], done[8]
    each = gain_attn_a.shape[0]
    res = deliver(gtile, done, each, 5)
    gb, ga, v = res[:4], res[4:8], [r[0] for r in res[8:]]
    return (output[None], input_grad[None], v[0], ga[0], ga[1], v[1], ga[2], ga[3], v[2], v[3], gb[0], gb[1], v[4], gb[2], gb[3])


def solution(mesh):
    outer, inner = mesh.shape["outer"], mesh.shape["inner"]
    both = ("outer", "inner")
    rows, vector, matrix = P(both, None, None), P(both), P("inner", "outer")
    block = (vector, matrix, matrix, vector, matrix, matrix)
    return jax.shard_map(
        functools.partial(per_device, outer, inner),
        mesh=mesh,
        in_specs=(rows, rows, vector, P(both, None)) + block + (vector,) + block,
        out_specs=(rows, rows) + block + (vector,) + block,
        check_vma=False,
    )
```

```python
import functools

import jax
import jax.numpy as jnp
from jax import lax
from jax.experimental import pallas as pl
from jax.experimental.pallas import tpu as pltpu
from jax.sharding import PartitionSpec as P

MESH = pl.DeviceIdType.MESH


def place():
    o, i = lax.axis_index("outer"), lax.axis_index("inner")
    return o, i // 4, (i // 2) % 2, i % 2


def device(o, z, x, c):
    return (o, z * 4 + x * 2 + c)


def greet(o, z, x, c):
    barrier = pltpu.get_barrier_semaphore()
    signal = functools.partial(pl.semaphore_signal, barrier, inc=1, device_id_type=MESH)
    signal(device_id=device(1 - o, z, x, c))
    signal(device_id=device(o, z, 1 - x, c))
    signal(device_id=device(o, z, x, 1 - c))

    @pl.when(z > 0)
    def _():
        signal(device_id=device(o, z - 1, x, c))

    @pl.when(z < 3)
    def _():
        signal(device_id=device(o, z + 1, x, c))

    pl.semaphore_wait(barrier, 3 + jnp.where(z > 0, 1, 0) + jnp.where(z < 3, 1, 0))


GATHER_PARTS = (
        (0, 0, 16, 0, 128, False, False), (1, 0, 48, 0, 384, True, False), (2, 0, 48, 0, 384, True, False), (5, 0, 48,
    0, 384, False, False), (4, 0, 96, 0, 384, False, True), (1, 0, 48, 768, 384, True, False), (1, 0, 48, 384, 384,
    False, False), (3, 0, 48, 0, 768, False, False), (3, 0, 48, 768, 768, True, False), (5, 0, 48, 768, 384, True,
    True), (4, 96, 96, 0, 384, False, False), (5, 0, 48, 384, 384, True, False), (7, 0, 48, 768, 768, False, False), (7,
    0, 48, 0, 768, False, False), (6, 0, 48, 0, 384, True, True), (8, 0, 96, 0, 384, True, False), (8, 96, 96, 0, 384,
    True, True))
GATHER_PLAN = (
        (0, 0, 0), (0, 0, 1), (0, 0, 2), (0, 0, 3), (0, 1, 0), (0, 1, 1), (0, 1, 2), (0, 1, 3), (0, 2, 0), (0, 2, 1),
    (0, 2, 2), (0, 2, 3), (0, 3, 0), (0, 0, 4), (0, 3, 1), (0, 0, 5), (0, 3, 2), (0, 0, 6), (0, 4, 0), (0, 3, 3), (0, 0,
    7), (0, 1, 5), (0, 1, 4), (0, 1, 6), (0, 1, 7), (0, 2, 5), (0, 4, 1), (0, 2, 6), (0, 2, 7), (0, 3, 5), (0, 0, 8),
    (0, 4, 2), (0, 5, 0), (0, 3, 6), (0, 0, 9), (0, 6, 0), (0, 3, 7), (0, 0, 10), (0, 4, 3), (0, 1, 8), (1, 5, 1), (1,
    2, 4), (1, 4, 5), (1, 2, 8), (1, 1, 10), (1, 6, 1), (1, 1, 9), (1, 5, 2), (1, 6, 2), (1, 4, 6), (1, 3, 4), (1, 0,
    11), (1, 3, 8), (1, 0, 12), (1, 2, 10), (1, 5, 3), (1, 4, 7), (1, 6, 3), (1, 5, 6), (1, 4, 4), (1, 5, 5), (1, 1,
    11), (1, 2, 9), (1, 6, 6), (1, 1, 12), (1, 6, 5), (1, 3, 10), (1, 0, 13), (2, 4, 8), (7, 5, 4), (7, 2, 11), (8, 5,
    7), (9, 6, 4), (9, 3, 9), (9, 4, 10), (9, 0, 14), (10, 6, 7), (10, 2, 12), (11, 1, 13), (11, 3, 11), (11, 0, 15),
    (11, 5, 8), (11, 4, 9), (11, 3, 12), (11, 0, 16), (11, 6, 8), (11, 2, 13), (11, 5, 10), (11, 1, 14), (12, 1, 15),
    (13, 6, 10), (13, 4, 11), (14, 5, 9), (15, 4, 12), (15, 3, 13), (16, 6, 9), (16, 2, 14), (16, 2, 15), (18, 5, 11),
    (18, 1, 16), (18, 3, 14), (18, 6, 11), (18, 3, 15), (19, 5, 12), (19, 4, 13), (19, 4, 14), (20, 2, 16), (21, 6, 12),
    (22, 5, 14), (23, 6, 14), (24, 4, 15), (24, 3, 16), (26, 5, 13), (27, 6, 13), (27, 5, 15), (27, 4, 16), (29, 6, 15),
    (30, 5, 16), (31, 6, 16))


class Gather:
    @staticmethod
    def semaphores(n):
        return [pltpu.SemaphoreType.DMA(k) for k in ((n,), (n, 23), (n, 19))]

    def __init__(self, parts, shards, outs, local_sem, send_sem, recv_sem):
        o, z, x, c = place()
        n = len(parts)

        def shard(p):
            a, r0, r, c0, w, _, _ = parts[p]
            return shards[a].at[pl.ds(r0, r), pl.ds(c0, w)]

        def blocks(p, oo):
            a, r0, r, c0, w, _, _ = parts[p]
            rows, each = shards[a].shape
            view = outs[a].reshape(4, 2, 2, rows, 2 * each)
            return view, pl.ds(r0, r), pl.ds(pl.multiple_of(oo * each + c0, 128), w)

        def chunk(p, k):
            view, rows, columns = blocks(p, o)
            return view.at[k, x, c, rows, columns]

        def group(p, second, first):
            first_x = parts[p][5]
            px, po = (first, second) if first_x else (second, first)
            view, rows, columns = blocks(p, o if po else 1 - o)
            return view.at[:, x if px else 1 - x, c, rows, columns]

        def send(p, src, dst, slot, target):
            return pltpu.make_async_remote_copy(
                src_ref=src, dst_ref=dst, send_sem=send_sem.at[p, slot[0]], recv_sem=recv_sem.at[p, slot[1]],
                device_id=target, device_id_type=MESH)

        def wait(ref, sem):
            pltpu.make_async_copy(ref, ref, sem).wait()

        def up(p, k, hop, src=None):
            b = chunk(p, k)
            return send(p, b if src is None else src, b, (hop, k), device(o, z + 1, x, c))

        def down(p, k, hop, src=None):
            b = chunk(p, k)
            return send(p, b if src is None else src, b, (3 + hop, k), device(o, z - 1, x, c))

        def near(p, second):
            return device(o, z, 1 - x, c) if parts[p][5] != second else device(1 - o, z, x, c)

        def to_core(p, second, first):
            b = group(p, second, first)
            send(p, b, b, (9 + 2 * second + first, 7 + 2 * second + first), device(o, z, x, 1 - c)).start()

        def to_second(p, first):
            b = group(p, 1, first)
            send(p, b, b, (7 + first, 5 + first), near(p, True)).start()

        def local(p):
            return pltpu.make_async_copy(shard(p), chunk(p, z), local_sem.at[p])

        def own(p):
            @pl.when(z < 3)
            def _():
                up(p, z, 0, shard(p)).start()

            @pl.when(z > 0)
            def _():
                down(p, z, 0, shard(p)).start()

            local(p).start()

        def hop(d):
            def go(p):
                @pl.when(z >= d)
                def _():
                    wait(chunk(p, z - d), recv_sem.at[p, z - d])
                    if d < 3:
                        @pl.when(z < 3)
                        def _():
                            up(p, z - d, d).start()

                @pl.when(z + d <= 3)
                def _():
                    wait(chunk(p, z + d), recv_sem.at[p, z + d])
                    if d < 3:
                        @pl.when(z > 0)
                        def _():
                            down(p, z + d, d).start()
            return go

        third = hop(3)

        def first(p):
            third(p)
            local(p).wait()
            b = group(p, 1, 1)
            send(p, b, b, (6, 4), near(p, False)).start()
            to_second(p, 1)
            to_core(p, 1, 1)

        def second(p):
            wait(group(p, 1, 0), recv_sem.at[p, 4])
            to_second(p, 0)
            to_core(p, 1, 0)

        def cores(p):
            for f in (1, 0):
                wait(group(p, 0, f), recv_sem.at[p, 5 + f])
                to_core(p, 0, f)

        def arrived(p):
            for slot in range(4):
                wait(group(p, 1, 1), recv_sem.at[p, 7 + slot])

        def plane(p, second, first):
            first_x = parts[p][5]
            px, po = (first, second) if first_x else (second, first)
            view, rows, columns = blocks(p, o if po else 1 - o)
            return view.at[z, x if px else 1 - x, c, rows, columns]

        def layer(p, k, oo):
            view, rows, columns = blocks(p, oo)
            return view.at[k, :, c, rows, columns]

        def late_own(p):
            s, b = shard(p), plane(p, 1, 1)
            send(p, s, b, (12, 8), near(p, False)).start()
            send(p, s, b, (13, 9), near(p, True)).start()
            local(p).start()

        def late_first(p):
            b = plane(p, 1, 0)
            wait(b, recv_sem.at[p, 8])
            send(p, b, b, (14, 10), near(p, True)).start()

        def spread(p, k, hop, rise, fall):
            for oo in (0, 1):
                b = layer(p, k, oo)
                if rise:
                    @pl.when(z < 3)
                    def _():
                        send(p, b, b, (2 * hop + oo, 2 * k + oo), device(o, z + 1, x, c)).start()
                if fall:
                    @pl.when(z > 0)
                    def _():
                        send(p, b, b, (6 + 2 * hop + oo, 2 * k + oo), device(o, z - 1, x, c)).start()
                send(p, b, b, (15 + 2 * k + oo, 11 + 2 * k + oo), device(o, z, x, 1 - c)).start()

        def late_second(p):
            wait(plane(p, 0, 1), recv_sem.at[p, 9])
            wait(plane(p, 0, 0), recv_sem.at[p, 10])
            local(p).wait()
            spread(p, z, 0, True, True)

        def late_hop(d):
            def go(p):
                for k, there, rise in ((z - d, z >= d, True), (z + d, z + d <= 3, False)):
                    @pl.when(there)
                    def _():
                        for oo in (0, 1):
                            wait(layer(p, k, oo), recv_sem.at[p, 2 * k + oo])
                        spread(p, k, d, rise and d < 3, not rise and d < 3)
            return go

        def late_arrived(p):
            for slot in range(8):
                wait(layer(p, 0, 0), recv_sem.at[p, 11 + slot])

        def late_finish(p):
            for oo in (0, 1):
                for d in range(3):
                    @pl.when(jnp.logical_and(z < 3, z >= d))
                    def _():
                        wait(layer(p, 0, 0), send_sem.at[p, 2 * d + oo])

                    @pl.when(jnp.logical_and(z > 0, z + d <= 3))
                    def _():
                        wait(layer(p, 0, 0), send_sem.at[p, 6 + 2 * d + oo])
            for slot in (12, 13, 14):
                wait(plane(p, 1, 1), send_sem.at[p, slot])
            for slot in range(15, 23):
                wait(layer(p, 0, 0), send_sem.at[p, slot])

        def early_finish(p):
            for d in range(3):
                @pl.when(jnp.logical_and(z < 3, z >= d))
                def _():
                    wait(chunk(p, z), send_sem.at[p, d])

                @pl.when(jnp.logical_and(z > 0, z + d <= 3))
                def _():
                    wait(chunk(p, z), send_sem.at[p, 3 + d])
            for slot in range(6, 13):
                wait(group(p, 1, 1), send_sem.at[p, slot])

        early = (own, hop(1), hop(2), first, second, cores, arrived)
        late = (late_own, late_first, late_second, late_hop(1), late_hop(2), late_hop(3), late_arrived)

        def finish():
            for p in range(n):
                (late_finish if parts[p][6] else early_finish)(p)

        self.finish = finish
        self.take = lambda step, p: (late if parts[p][6] else early)[step](p)

    def begin(self):
        greet(*place())


PARTS = (
        (2, 0, 48, 0, 768, True, 1), (3, 96, 96, 0, 384, False, 2), (3, 0, 96, 0, 384, False, 0), (2, 0, 48, 768, 768,
    True, 3), (1, 0, 48, 0, 384, False, 4), (0, 0, 48, 0, 640, True, 5), (0, 0, 48, 640, 512, False, 6), (6, 0, 48, 768,
    768, True, 3), (6, 0, 48, 0, 768, False, 1), (7, 96, 96, 0, 384, True, 2), (7, 0, 96, 0, 384, False, 0), (4, 0, 48,
    0, 640, True, 5), (4, 0, 48, 640, 512, False, 6), (5, 0, 48, 0, 384, True, 4), (8, 0, 16, 0, 128, False, 7))
BACK_PLAN = (
        (0, 0, 0), (0, 0, 1), (0, 0, 2), (0, 0, 3), (0, 0, 4), (1, 1, 0), (2, 2, 0), (2, 1, 1), (3, 2, 1), (3, 1, 2),
    (3, 1, 3), (4, 2, 2), (4, 2, 3), (5, 3, 0), (6, 4, 0), (6, 3, 1), (6, 1, 4), (7, 4, 1), (7, 2, 4), (10, 3, 3), (10,
    0, 5), (10, 0, 6), (11, 3, 2), (11, 4, 3), (12, 5, 1), (12, 4, 2), (12, 1, 5), (13, 5, 0), (13, 6, 1), (13, 2, 5),
    (14, 6, 0), (15, 7, 1), (15, 5, 2), (15, 3, 4), (16, 7, 0), (16, 6, 2), (16, 4, 4), (16, 1, 6), (16, 8, 1), (17, 5,
    3), (17, 2, 6), (18, 8, 0), (18, 9, 1), (18, 6, 3), (18, 7, 2), (18, 0, 9), (19, 3, 5), (20, 9, 0), (20, 8, 2), (20,
    5, 4), (20, 4, 5), (20, 7, 3), (20, 0, 8), (20, 1, 9), (21, 6, 4), (21, 2, 9), (21, 9, 2), (21, 3, 6), (21, 0, 10),
    (22, 8, 3), (22, 4, 6), (22, 1, 8), (22, 7, 4), (23, 2, 8), (23, 1, 10), (24, 9, 3), (24, 8, 4), (24, 5, 5), (24, 0,
    7), (24, 2, 10), (25, 6, 5), (26, 9, 4), (26, 0, 13), (27, 1, 7), (28, 7, 5), (29, 2, 7), (29, 3, 9), (29, 8, 5),
    (29, 0, 14), (29, 4, 9), (29, 5, 6), (29, 9, 5), (29, 0, 11), (29, 3, 8), (29, 6, 6), (29, 4, 8), (29, 7, 6), (29,
    8, 6), (29, 9, 6), (29, 0, 12), (29, 1, 11), (29, 2, 11), (29, 3, 7), (29, 3, 10), (29, 4, 7), (29, 4, 10), (29, 1,
    12), (29, 2, 12), (29, 5, 8), (29, 5, 9), (29, 6, 8), (29, 6, 9), (29, 7, 8), (29, 5, 7), (29, 6, 7), (29, 1, 13),
    (29, 8, 8), (29, 7, 9), (29, 2, 13), (29, 3, 11), (29, 4, 11), (29, 9, 8), (29, 8, 9), (29, 1, 14), (29, 7, 7), (29,
    2, 14), (29, 3, 12), (29, 4, 12), (29, 5, 10), (29, 9, 9), (29, 6, 10), (29, 8, 7), (29, 5, 11), (29, 3, 14), (29,
    6, 11), (29, 9, 7), (29, 4, 14), (29, 7, 10), (29, 3, 13), (29, 4, 13), (29, 8, 10), (29, 7, 11), (29, 5, 12), (29,
    6, 12), (29, 5, 14), (29, 6, 14), (29, 5, 13), (29, 9, 10), (29, 8, 11), (29, 6, 13), (29, 7, 12), (29, 9, 11), (29,
    7, 14), (29, 7, 13), (29, 8, 12), (29, 8, 14), (29, 8, 13), (29, 9, 12), (29, 9, 14), (29, 9, 13))


class Scatter:
    def __init__(self, parts, grads, outs, core_in, second_in, first_in, buffers, sems):
        o, z, x, c = place()
        acc, z_in, stage_own, stage_got, stage_second, stage_first, stage_out = buffers
        send_sem, recv_sem, own_sem, stage_sem, out_sem = sems
        n = len(parts)

        def kind(p):
            return 1 if parts[p][2] == 96 else 0

        def of(p):
            return parts[p][2], parts[p][4]

        def part(ref, p):
            r, w = of(p)
            return ref.at[:, pl.ds(0, r), pl.ds(0, w)]

        def group(p, second, first, core):
            g, r0, r, c0, w, first_x, _ = parts[p]
            px, po = (first, second) if first_x else (second, first)
            xx = x if px else 1 - x
            oo = o if po else 1 - o
            height, width = grads[g].shape
            each = width // 2
            return grads[g].reshape(4, 2, 2, height // 16, width).at[:, xx, core, pl.ds(r0, r), pl.ds(pl.multiple_of(oo * each + c0, 128), w)]

        def far(p, second):
            return device(o, z, 1 - x, c) if parts[p][5] != second else device(1 - o, z, x, c)

        def send(p, src, dst, kind_, slot, target):
            return pltpu.make_async_remote_copy(
                src_ref=src, dst_ref=dst, send_sem=send_sem.at[p, kind_], recv_sem=recv_sem.at[p, slot],
                device_id=target, device_id_type=MESH)

        def wait(ref, sem):
            pltpu.make_async_copy(ref, ref, sem).wait()

        slots, last_user = {}, {}
        turn = [0, 0]
        for p in range(n):
            k = kind(p)
            slots[p] = turn[k] % 2
            last_user[p] = next((q for q in range(p - 1, -1, -1) if kind(q) == k and slots[q] == slots[p]), None)
            turn[k] += 1

        def own_of(p):
            return part(stage_own[kind(p)].at[slots[p]], p)

        def total(p):
            return acc[parts[p][6]]

        def begin(p):
            for second in (0, 1):
                for first in (0, 1):
                    send(p, group(p, second, first, 1 - c), core_in[p].at[pl.ds(second * 8 + first * 4, 4)], 0, 0,
                         device(o, z, x, 1 - c)).start()
            for first in (0, 1):
                pltpu.make_async_copy(group(p, 1, first, c), total(p).at[pl.ds(first * 4, 4)], own_sem.at[p]).start()

        def core_fetch(p):
            k = kind(p)
            if last_user[p] is not None:
                q = last_user[p]
                wait(own_of(q), send_sem.at[q, 1])
            for first in (0, 1):
                pltpu.make_async_copy(group(p, 0, first, c), own_of(p).at[pl.ds(first * 4, 4)], stage_sem.at[kind(p), 0]).start()
            wait(core_in[p], recv_sem.at[p, 0])
            pltpu.make_async_copy(core_in[p].at[pl.ds(0, 8)], part(stage_got[k], p), stage_sem.at[kind(p), 1]).start()
            pltpu.make_async_copy(core_in[p].at[pl.ds(8, 8)], part(stage_second[k], p), stage_sem.at[kind(p), 2]).start()

        def core_add(p):
            own, got = own_of(p), part(stage_got[kind(p)], p)
            wait(own, stage_sem.at[kind(p), 0])
            wait(got, stage_sem.at[kind(p), 1])
            for first in (0, 1):
                s = pl.ds(first * 4, 4)
                own[s] = own[s] + got[s]
                send(p, own.at[s], second_in[p].at[s], 1, 1 + first, far(p, True)).start()
            mine = part(stage_second[kind(p)], p)
            wait(total(p), own_sem.at[p])
            wait(mine, stage_sem.at[kind(p), 2])
            total(p)[...] = total(p)[...] + mine[...]

        def second_fetch(p):
            got = part(stage_second[kind(p)], p)
            for first in (0, 1):
                s = pl.ds(first * 4, 4)
                wait(second_in[p].at[s], recv_sem.at[p, 1 + first])
            pltpu.make_async_copy(second_in[p], got, stage_sem.at[kind(p), 2]).start()

        def second_add(p):
            got = part(stage_second[kind(p)], p)
            wait(got, stage_sem.at[kind(p), 2])
            t = total(p)
            t[0:4] = t[0:4] + got[0:4]
            send(p, t.at[pl.ds(0, 4)], first_in[p], 2, 3, far(p, False)).start()
            t[4:8] = t[4:8] + got[4:8]

        def send_z(p, k, step):
            to = z + step
            slot = jnp.where(k == to, jnp.where(step > 0, k, 4), k)
            send(p, total(p).at[4 + k], z_in[p].at[slot], 3, 4 + slot, device(o, to, x, c)).start()

        def first_fetch(p):
            wait(first_in[p], recv_sem.at[p, 3])
            pltpu.make_async_copy(first_in[p], part(stage_first[kind(p)], p), stage_sem.at[kind(p), 3]).start()

        def first_add(p):
            got = part(stage_first[kind(p)], p)
            wait(got, stage_sem.at[kind(p), 3])
            t = total(p)
            t[4:8] = t[4:8] + got[...]

            @pl.when(z == 0)
            def _():
                for k in (3, 2, 1):
                    send_z(p, k, 1)

            @pl.when(z == 3)
            def _():
                for k in (0, 1, 2):
                    send_z(p, k, -1)

        def pass_on(p, k, step):
            wait(z_in[p].at[k], recv_sem.at[p, 4 + k])
            total(p)[4 + k] = total(p)[4 + k] + z_in[p][k]
            send_z(p, k, step)

        def along(level):
            def go(p):
                @pl.when(z == level)
                def _():
                    for k in range(3, level, -1):
                        pass_on(p, k, 1)

                @pl.when(z == 3 - level)
                def _():
                    for k in range(0, 3 - level):
                        pass_on(p, k, -1)
            return go

        out_user = [None, None]

        def copy_out(p):
            g, r0, r, c0, w, _, _ = parts[p]
            return pltpu.make_async_copy(stage_out[kind(p)].at[pl.ds(0, r), pl.ds(0, w)],
                                         outs[g].at[pl.ds(r0, r), pl.ds(c0, w)], out_sem.at[kind(p)])

        def finish():
            for p in out_user:
                copy_out(p).wait()

        def last(p):
            g, r0, r, c0, w, _, _ = parts[p]
            out = stage_out[kind(p)].at[pl.ds(0, r), pl.ds(0, w)]
            if out_user[kind(p)] is not None:
                copy_out(out_user[kind(p)]).wait()
            out_user[kind(p)] = p
            out[...] = total(p)[4 + z].astype(jnp.float32)

            @pl.when(z > 0)
            def _():
                wait(z_in[p].at[z], recv_sem.at[p, 4 + z])
                out[...] += z_in[p][z].astype(jnp.float32)

            @pl.when(z < 3)
            def _():
                wait(z_in[p].at[4], recv_sem.at[p, 8])
                out[...] += z_in[p][4].astype(jnp.float32)

            copy_out(p).start()
            wait(core_in[p], send_sem.at[p, 0])
            if all(last_user[q] != p for q in range(n)):
                wait(own_of(p), send_sem.at[p, 1])
            wait(first_in[p], send_sem.at[p, 2])
            wait(first_in[p].at[pl.ds(0, 3)], send_sem.at[p, 3])

        self.finish = finish
        self.steps = (begin, core_fetch, core_add, second_fetch, second_add, first_fetch, first_add, along(1), along(2), last)

    @staticmethod
    def shapes(parts):
        return [shape(m, s[2], s[4]) for m in (16, 8, 4) for s in parts]

    @staticmethod
    def scratch(parts):
        b16 = jnp.bfloat16
        sizes = {s[6]: (8, s[2], s[4]) for s in parts}
        acc = [(sizes[k], b16) for k in sorted(sizes)]
        lands = [((m, s[2], s[4]), b16) for m in (5,) for s in parts]
        stages = [((m, 48, 768), b16) if k == 0 else ((m, 96, 384), b16) for m in (8, 8, 4) for k in (0, 1)]
        stages = [((2, 8, 48, 768), b16), ((2, 8, 96, 384), b16)] + stages
        stages += [((48, 768), jnp.float32), ((96, 384), jnp.float32)]
        n = len(parts)
        return buffers(*acc, *lands, *stages) + [pltpu.SemaphoreType.DMA(k) for k in ((n, 4), (n, 9), (n,), (2, 4), (2,))]

    @staticmethod
    def unpack(parts, refs):
        n, m = len(parts), len({s[6] for s in parts})
        acc, refs = refs[:m], refs[m:]
        z_in, refs = refs[:n], refs[n:]
        return (acc, z_in, refs[0:2], refs[2:4], refs[4:6], refs[6:8], refs[8:10]), refs[10:15]


D = 768
SCALE = 0.125 * 1.4426950408889634
ROWS = 256
VMEM_BYTES = 127 * 2**19


def mul(a, b, ca=1, cb=0):
    return lax.dot_general(a, b, (((ca,), (cb,)), ((), ())), preferred_element_type=jnp.float32)


def low(v):
    return v.astype(jnp.bfloat16)


def cols(j):
    return pl.ds(pl.multiple_of(j * D, D), D)


def rms_scale(v):
    return lax.rsqrt(jnp.mean(v * v, axis=-1, keepdims=True) + 1e-06)


def rms_back(v, gain, grad):
    r = rms_scale(v)
    unit = v * r
    scaled = grad * gain
    back = r * (scaled - unit * jnp.mean(scaled * unit, axis=-1, keepdims=True))
    return back, jnp.sum((grad * unit).reshape(-1, 8, v.shape[-1]), axis=0)


def gelu_and_slope(u):
    k = 0.7978845608028654
    square = u * u
    t = jnp.tanh(u * (k + k * 0.044715 * square))
    half = 0.5 + 0.5 * t
    return u * half, half + u * (0.5 - 0.5 * t * t) * (k + 3 * 0.044715 * k * square)


def halves(v):
    lane = lax.broadcasted_iota(jnp.int32, v.shape, 1)
    zero = jnp.zeros_like(v)
    return jnp.where(lane < 64, v, zero), jnp.where(lane < 64, zero, v)


def two(v):
    first = low(v)
    return first, low(v - first.astype(jnp.float32))


class Block:
    def __init__(self, rows, refs):
        self.rows = rows
        self.__dict__.update(refs)

    @staticmethod
    def scratch(rows):
        f32, b16 = jnp.float32, jnp.bfloat16
        return dict(
            branch=((rows, D), f32), projected=((rows, 3 * D), b16), merged=((rows, D), b16), lse=((6, 8, rows), f32),
            active=((rows, 4 * D), b16), slope=((rows, 4 * D), b16), normed=((rows, D), b16), normed_mlp=((rows, D), b16))

    def rows_of(self, t):
        return self.x[t].astype(jnp.float32)

    def tiles(self):
        return [slice(i, i + ROWS) for i in range(0, self.rows, ROWS)]

    def norm(self):
        for t in self.tiles():
            x = self.rows_of(t)
            self.normed[t] = low(x * rms_scale(x) * self.gain_attn[...])

    def project(self, j):
        c = cols(j)
        self.projected[:, c] = low(mul(self.normed[...], self.qkv[:, c]))

    def pair(self, ref, part, pair, rows=slice(None)):
        return ref[rows, pl.ds(pl.multiple_of(part * D + pair * 128, 128), 128)]

    def attend(self, pair):
        v0, v1 = halves(self.pair(self.projected, 2, pair))
        causal = lax.broadcasted_iota(jnp.int32, (ROWS, ROWS), 1) >= lax.broadcasted_iota(jnp.int32, (ROWS, ROWS), 0)
        for t in self.tiles():
            n = t.stop
            qs = halves(self.pair(self.projected, 0, pair, t))
            k = self.pair(self.projected, 1, pair, slice(0, n))
            total = None
            for h in range(2):
                s = mul(k, qs[h], 1, 1)
                last = jnp.where(causal, s[t.start:], -1e30)
                s = last if t.start == 0 else jnp.concatenate([s[: t.start], last], axis=0)
                m = jnp.max(s, axis=0, keepdims=True) * SCALE
                p = jnp.exp2(s * SCALE - m)
                l = jnp.sum(p, axis=0, keepdims=True)
                self.lse[pair, h : h + 1, t] = m + jnp.log2(l)
                o = mul(low(p * (1.0 / l)), (v0, v1)[h][:n], 0, 0)
                total = o if total is None else total + o
            self.merged[t, pl.ds(pl.multiple_of(pair * 128, 128), 128)] = low(total)

    def join(self):
        for t in self.tiles():
            branch = mul(self.merged[t], self.out[...])
            self.branch[t] = branch
            middle = self.rows_of(t) + branch
            self.normed_mlp[t] = low(middle * rms_scale(middle) * self.gain_mlp[...])

    def widen(self, j):
        c = cols(j)
        for t in self.tiles():
            active, slope = gelu_and_slope(mul(self.normed_mlp[t], self.up[:, c]))
            self.active[t, c] = low(active)
            self.slope[t, c] = low(slope)

    def narrow(self, t):
        return mul(self.active[t], self.down[...])

    def back_wide(self, j):
        c = cols(j)
        for t in self.tiles():
            grad = mul(self.grad_low[t], self.down[c, :], 1, 1)
            self.slope[t, c] = low(grad * self.slope[t, c].astype(jnp.float32))

    def grad_down(self, j):
        return low(mul(self.active[:, cols(j)], self.grad_low[...], 0, 0))

    def grad_up(self, j):
        return low(mul(self.normed_mlp[...], self.slope[:, cols(j)], 0, 0))

    def back_mlp(self, grad_of):
        total = jnp.zeros((8, D), jnp.float32)
        for t in self.tiles():
            grad = mul(self.slope[t], self.up[...], 1, 1)
            back, gain = rms_back(self.rows_of(t) + self.branch[t], self.gain_mlp[...], grad)
            total = total + gain
            self.branch[t] = back
            self.normed_mlp[t] = low(grad_of(t) + back)
        return jnp.sum(total, axis=0, keepdims=True)

    def grad_out(self):
        return low(mul(self.merged[...], self.normed_mlp[...], 0, 0))

    def back_merged(self):
        self.active[:, :D] = low(mul(self.normed_mlp[...], self.out[...], 1, 1))

    def attend_back(self, pair, turned):
        rows = self.rows
        q, do = self.pair(self.projected, 0, pair), self.pair(self.active, 0, pair)
        qs, dos = halves(q), halves(do)
        dd = do.astype(jnp.float32) * self.pair(self.merged, 0, pair).astype(jnp.float32)
        pick = lax.broadcasted_iota(jnp.int32, (8, 128), 0) == lax.broadcasted_iota(jnp.int32, (8, 128), 1) // 64
        delta = lax.dot_general(pick.astype(jnp.float32), dd, (((1,), (1,)), ((), ())), precision=lax.Precision.HIGHEST,
                                preferred_element_type=jnp.float32)
        causal = lax.broadcasted_iota(jnp.int32, (ROWS, ROWS), 1) >= lax.broadcasted_iota(jnp.int32, (ROWS, ROWS), 0)
        for t in self.tiles():
            a = t.start
            ks, vs = halves(self.pair(self.projected, 1, pair, t)), halves(self.pair(self.projected, 2, pair, t))
            dk = dv = dq = 0.0
            for h in range(2):
                s = mul(ks[h], q[a:], 1, 1)
                p = jnp.exp2(s * SCALE - self.lse[pair, h : h + 1, a:])
                first = jnp.where(causal, p[:, :ROWS], 0.0)
                p = first if t.stop == rows else jnp.concatenate([first, p[:, ROWS:]], axis=1)
                dp = mul(vs[h], do[a:], 1, 1)
                ds = low(p * (dp - delta[h : h + 1, a:]))
                dv = dv + mul(low(p), dos[h][a:])
                dk = dk + mul(ds, qs[h][a:])
                dq = dq + mul(ks[h], ds, 0, 0)
            lanes = pl.multiple_of(pair * 128, 128)
            self.projected[t, pl.ds(D + lanes, 128)] = low(0.125 * dk)
            self.projected[t, pl.ds(2 * D + lanes, 128)] = low(dv)
            if a == 0:
                turned[:, :rows] = dq
            else:
                turned[:, a:rows] += dq
        self.projected[:, pl.ds(lanes, 128)] = low(0.125 * turned[:, :rows].T)

    def grad_qkv(self, j):
        return low(mul(self.normed[...], self.projected[:, cols(j)], 0, 0))

    def back_norm(self, finish):
        total = jnp.zeros((8, D), jnp.float32)
        for t in self.tiles():
            grad = mul(self.projected[t], self.qkv[...], 1, 1)
            back, gain = rms_back(self.rows_of(t), self.gain_attn[...], grad)
            total = total + gain
            finish(t, back + self.branch[t])
        return jnp.sum(total, axis=0, keepdims=True)


SAVED = ("branch", "projected", "merged", "lse", "active", "slope", "normed", "normed_mlp")


def run(steps, hooks=None):
    at = 0
    waits = []
    for count, body in steps:
        if count == 0:
            waits.append(body)
            continue
        before = [list(hooks[at + k]) if hooks else [] for k in range(count)]
        at += count
        for f in before[0]:
            f()
        for f in waits:
            f(0)
        waits = []
        if count == 1:
            body(0)
            continue

        @pl.loop(0, count)
        def _(j):
            for k in range(1, count):
                if before[k]:
                    @pl.when(j == k)
                    def _():
                        for f in before[k]:
                            f()
            body(j)


class Loads:
    def __init__(self, pairs, sems):
        self.copies = {k: pltpu.make_async_copy(a, b, sems.at[j]) for j, (k, a, b) in enumerate(pairs)}
        for c in self.copies.values():
            c.start()

    def need(self, *names):
        for n in names:
            self.copies[n].wait()


class Ship:
    def __init__(self, stages, sems):
        self.stages, self.sems, self.single = stages, sems, len(stages) == 1

    def wait(self, slot):
        slot = min(slot, len(self.stages) - 1)
        pltpu.make_async_copy(self.stages[slot], self.stages[slot], self.sems.at[slot]).wait()

    def send(self, slot, value, target, busy):
        slot = min(slot, len(self.stages) - 1)
        if busy is True:
            self.wait(slot)
        elif busy is not False:
            pl.when(busy)(lambda: self.wait(slot))
        self.stages[slot][...] = value()
        pltpu.make_async_copy(self.stages[slot], target, self.sems.at[slot]).start()


def wide_steps(b, grad_of, ship, targets, vec):
    gout, gup, gdown = targets

    def wide(j):
        b.back_wide(j)
        ship.send(0, lambda: b.grad_down(j), gdown.at[cols(j), :], j > 0)
        ship.send(1, lambda: b.grad_up(j), gup.at[:, cols(j)], ship.single or j > 0)

    def mlp(_):
        ship.wait(0)
        if not ship.single:
            ship.wait(1)
        vec(b.back_mlp(grad_of))

    def out(_):
        ship.send(1, b.grad_out, gout, False)
        b.back_merged()

    return [(4, wide), (1, mlp), (1, out)]


def attend_steps(b, ship, gqkv, vec, finish, turned, busy):
    def qkv(j):
        ship.send(1, lambda: b.grad_qkv(j), gqkv.at[:, cols(j)], True if busy else j > 0)

    def norm(_):
        vec(b.back_norm(finish))
        ship.wait(1)

    return [(6, lambda j: b.attend_back(j, turned)), (3, qkv), (1, norm)]


def shape(*dims, dtype=jnp.bfloat16):
    return jax.ShapeDtypeStruct(dims, dtype)


def any_specs(n):
    return [pl.BlockSpec(memory_space=pl.ANY)] * n


def vmem_specs(n):
    return [pl.BlockSpec(memory_space=pltpu.VMEM)] * n


WEIGHTS = [((D, 3 * D), jnp.bfloat16), ((D, D), jnp.bfloat16), ((D, 4 * D), jnp.bfloat16), ((4 * D, D), jnp.bfloat16)]


def buffers(*pairs):
    return [pltpu.VMEM(dims, dtype) for dims, dtype in pairs]


def kept_buffers(rows):
    s = Block.scratch(rows)
    return [s[k] for k in SAVED]


def spots(start, count, spot):
    at = lax.broadcasted_iota(jnp.int32, (count, spot.shape[1]), 0) + start
    return low(jnp.where(at == spot, 1.0, 0.0))


def lane_map(outer, inner):
    each = D // (outer * inner)
    d = jnp.arange(D, dtype=jnp.int32)
    return jnp.stack([d // each % inner, d // (each * inner) * 128 + d % each])


def spread_map(tiles_columns, map_ref):
    at = lax.broadcasted_iota(jnp.int32, (tiles_columns, D), 0)
    return low(jnp.where(at == map_ref[1:2], 1.0, 0.0))


def read_vectors(tiles, map_ref):
    rows, columns = tiles.shape
    every = mul(tiles[...], spread_map(columns, map_ref))
    inner = lax.broadcasted_iota(jnp.int32, (rows, D), 0) // 16
    return jnp.sum(jnp.where(inner == map_ref[0:1], every, 0.0).reshape(rows // 16, 16, D), axis=0)


def write_vectors(vectors, rows, columns, map_ref):
    every = jnp.broadcast_to(vectors[None], (rows // 16, 16, D)).reshape(rows, D)
    inner = lax.broadcasted_iota(jnp.int32, (rows, D), 0) // 16
    return low(mul(low(jnp.where(inner == map_ref[0:1], every, 0.0)), spread_map(columns, map_ref), 1, 1))


def gate_of(x, router):
    return jax.nn.sigmoid(jnp.sum(x * router, axis=-1, keepdims=True))


def routed_forward_steps(b, need, hidden, spot_ref, chosen, vec_ref, extra, keep):
    length = hidden.shape[0]

    def pick(_):
        chosen[...] = spots(0, length, spot_ref[...])
        need("hidden")
        for t in b.tiles():
            b.x[t] = low(mul(chosen[:, t], hidden[...], 0, 0))
        need("vectors")
        b.norm()
        keep("x", "normed")

    def join(_):
        keep("projected", "merged", "lse")
        need("out")
        b.join()
        keep("branch", "normed_mlp")

    def narrow(_):
        keep("active", "slope")
        need("down")
        for t in b.tiles():
            extra[t] = b.branch[t] + b.narrow(t)
        keep("change")

    def put(_):
        rows = [gate_of(b.rows_of(t), vec_ref[2:3]) * extra[t] for t in b.tiles()]
        pieces = [two(r) for r in rows]
        for i in range(0, length, ROWS):
            t = slice(i, i + ROWS)
            total = hidden[t].astype(jnp.float32)
            for piece, s in zip(pieces, b.tiles()):
                for p in piece:
                    total = total + mul(chosen[t, s], p)
            b.middle[t] = total

    return [(1, pick), (0, lambda _: need("qkv")), (3, b.project), (6, b.attend), (1, join), (0, lambda _: need("up")), (4, b.widen),
            (1, narrow), (1, put)]


KEPT = ("x", "change") + SAVED


def kept_shapes(rows):
    return [((rows, D), jnp.bfloat16), ((rows, D), jnp.float32)] + kept_buffers(rows)


def routed_backward_steps(b, need, grad, spot_ref, vec_ref, change, grad_rows, gate, ship, targets, vec, turned,
                          grad_hbm, grad_sem):
    length = grad.shape[0]
    router = vec_ref.at[2:3]
    gqkv, *others = targets

    def take(_):
        pieces = two(grad[...])
        need("x", "change")
        for t in b.tiles():
            chosen = spots(0, length, spot_ref[:, t])
            rows = mul(chosen, pieces[0], 0, 0) + mul(chosen, pieces[1], 0, 0)
            g = gate_of(b.rows_of(t), router[...])
            b.grad_low[t], grad_rows[t] = two(g * rows)
            logits = jnp.sum(rows * change[t], axis=-1, keepdims=True) * g * (1.0 - g)
            gate[t] = jnp.broadcast_to(logits, (ROWS, 128))
        need("down", "active", "slope", "normed_mlp")

    def finish(t, g):
        change[t] = g + gate[t, 0:1] * router[...]

    def put(_):
        pieces = [two(change[t]) for t in b.tiles()]
        for i in range(0, length, ROWS):
            t = slice(i, i + ROWS)
            total = grad[t]
            for piece, s in zip(pieces, b.tiles()):
                chosen = spots(i, ROWS, spot_ref[:, s])
                for p in piece:
                    total = total + mul(chosen, p)
            grad[t] = total
            pltpu.make_async_copy(grad.at[t], grad_hbm.at[t], grad_sem).start()

    def route(_):
        total = jnp.zeros((8, D), jnp.float32)
        for t in b.tiles():
            total = total + jnp.sum((gate[t, 0:1] * b.rows_of(t)).reshape(-1, 8, D), axis=0)
        vec(2, jnp.sum(total, axis=0, keepdims=True))

    wide, mlp, out = wide_steps(b, lambda t: b.grad_low[t].astype(jnp.float32) + grad_rows[t].astype(jnp.float32), ship, others, lambda v: vec(1, v))
    attend, qkv, norm = attend_steps(b, ship, gqkv, lambda v: vec(0, v), finish, turned, True)

    def wants(*names):
        return (0, lambda _: need(*names))

    return [(1, take), wide, wants("up", "branch"), mlp, wants("out", "merged"), out, wants("projected", "lse"), attend,
            wants("normed"), qkv, wants("qkv"), norm, (1, route), (1, put)]


KEPT_DENSE = ("x", "projected", "merged", "lse")


def forward_kernel(remote, *refs):
    hidden_hbm, cot_hbm, spot_ref, map_ref, *refs = refs
    given, refs = refs[:9], refs[9:]
    if remote:
        whole, refs = refs[:9], refs[9:]
    else:
        whole = given
    vec_ref, gvec_ref, y_hbm, plus_hbm, gmerged_hbm, gout_hbm, gup_hbm, gdown_hbm, *refs = refs
    n, m = len(KEPT), len(KEPT_DENSE)
    kept_hbm, refs = dict(zip(KEPT, refs[:n])), refs[n:]
    dense_hbm, refs = dict(zip(KEPT_DENSE, refs[:m])), refs[m:]
    hidden, cot, chosen, tiles, qkv, out, up, down, qkv_b, out_b, *refs = refs
    change, branch_a, lse_a, active, slope, x, branch, projected, merged, lse, normed, normed_mlp, stage, *refs = refs
    load_sem, keep_sem, dense_sem, stage_sem, row_sem, *refs = refs
    length, half = hidden.shape[0], spot_ref.shape[1]
    top, rest = pl.ds(0, half), pl.ds(half, half)
    kept = dict(x=active.at[rest, cols(0)], change=change, branch=branch_a, projected=active.at[top, pl.ds(0, 3 * D)],
                merged=active.at[rest, cols(1)], lse=lse_a, active=slope.at[top], slope=slope.at[rest],
                normed=active.at[rest, cols(2)], normed_mlp=active.at[rest, cols(3)])
    into = (tiles, qkv, out, up, down, qkv_b, out_b, up, down)
    loads = [pltpu.make_async_copy(src, dst, load_sem.at[j]) for j, (src, dst) in enumerate(zip(whole, into))]
    loads += [pltpu.make_async_copy(src, dst, load_sem.at[9 + j]) for j, (src, dst) in enumerate(((hidden_hbm, hidden), (cot_hbm, cot)))]
    where = dict(vectors=0, qkv=1, out=2, up=3, down=4, hidden=9)
    loads[9].start()
    loads[10].start()

    def need(name):
        loads[where[name]].wait()
        if name == "vectors":
            vec_ref[...] = read_vectors(tiles, map_ref)

    saves = {k: pltpu.make_async_copy(kept[k], kept_hbm[k], keep_sem.at[j]) for j, k in enumerate(KEPT)}
    dense = dict(x=x, projected=projected, merged=merged, lse=lse)
    dense_saves = {k: pltpu.make_async_copy(dense[k], dense_hbm[k], dense_sem.at[j]) for j, k in enumerate(KEPT_DENSE)}

    def keep(*wanted):
        for k in wanted:
            saves[k].start()

    b = Block(half, dict(kept, middle=x, qkv=qkv, out=out, up=up, down=down,
                         gain_attn=vec_ref.at[0:1], gain_mlp=vec_ref.at[1:2]))
    d = Block(length, dict(dense, branch=branch, normed=normed, normed_mlp=normed_mlp, active=active, slope=slope, grad_low=cot,
                           qkv=qkv_b, out=out_b, up=up, down=down, gain_attn=vec_ref.at[3:4], gain_mlp=vec_ref.at[4:5]))

    def norm(_):
        dense_saves["x"].start()
        d.norm()

    def join(_):
        for k in KEPT_DENSE[1:]:
            dense_saves[k].start()
        loads[6].wait()
        d.join()

    def before_widen(_):
        for c in saves.values():
            c.wait()
        loads[7].wait()

    def narrow(_):
        loads[8].wait()
        for t in d.tiles():
            hidden[t] = low(x[t] + branch[t] + d.narrow(t))
        pltpu.make_async_copy(hidden, y_hbm, row_sem.at[0]).start()
        loads[10].wait()

    def cot_of(t):
        return cot[t].astype(jnp.float32)

    def vec(value):
        gvec_ref[...] = value

    def grad(_):
        for t in d.tiles():
            branch[t] += cot_of(t)
        pltpu.make_async_copy(branch, plus_hbm, row_sem.at[1]).start()

    ship = Ship((stage.at[0], stage.at[1]), stage_sem)
    wide, mlp, last = wide_steps(d, cot_of, ship, (gout_hbm, gup_hbm, gdown_hbm), vec)
    steps = routed_forward_steps(b, need, hidden, spot_ref, chosen, vec_ref, change, keep)
    steps += [(1, norm), (0, lambda _: loads[5].wait()), (3, d.project), (6, d.attend), (1, join), (0, before_widen), (4, d.widen),
              (1, narrow), wide, mlp, (0, grad), last]
    late = 17
    if remote:
        flow = Gather(GATHER_PARTS, given, whole, *refs)
        ends = {}
        for _, step, p in GATHER_PLAN:
            if step == 6:
                ends[GATHER_PARTS[p][0]] = p
        units = [[] for _ in range(sum(c for c, _ in steps) + 1)]
        for unit, step, p in GATHER_PLAN:
            units[unit].append(functools.partial(flow.take, step, p))
            a = GATHER_PARTS[p][0]
            if step == 6 and p == ends[a]:
                units[max(unit, late) if a > 6 else unit].append(loads[a].start)
        flow.begin()
    else:
        for c in loads[:7]:
            c.start()
        units = [[] for _ in range(sum(c for c, _ in steps) + 1)]
        units[late] = [loads[7].start, loads[8].start]
    run(steps, units)
    for f in units[-1]:
        f()
    gmerged = pltpu.make_async_copy(active.at[:, pl.ds(0, D)], gmerged_hbm, row_sem.at[2])
    gmerged.start()
    ship.wait(1)
    if remote:
        flow.finish()
    for c in dense_saves.values():
        c.wait()
    gmerged.wait()
    pltpu.make_async_copy(hidden, y_hbm, row_sem.at[0]).wait()
    pltpu.make_async_copy(branch, plus_hbm, row_sem.at[1]).wait()


def forward(remote, hidden, cot, spot, place_map, weights, outer, inner):
    length, rows = hidden.shape[0], spot.shape[1]
    f32, b16 = jnp.float32, jnp.bfloat16
    kept, short, every = kept_shapes(rows), Block.scratch(rows), Block.scratch(length)
    every["x"] = every["branch"]
    dense = [every[k] for k in KEPT_DENSE]
    whole = [shape(w.shape[0] * inner, w.shape[1] * outer) for w in weights] if remote else []
    scratch = buffers(((length, D), b16), ((length, D), b16), ((length, rows), b16), ((16 * inner, 128 * outer), b16), *WEIGHTS,
                      *WEIGHTS[:2], ((rows, D), f32), short["branch"], short["lse"],
                      *[every[k] for k in ("active", "slope", "x", "branch", "projected", "merged", "lse", "normed", "normed_mlp")],
                      ((2, D, D), b16))
    scratch += [pltpu.SemaphoreType.DMA((k,)) for k in (11, len(kept), len(dense), 2, 3)]
    if remote:
        scratch += Gather.semaphores(len(GATHER_PARTS))
    results = pl.pallas_call(
        functools.partial(forward_kernel, remote),
        in_specs=any_specs(2) + vmem_specs(2) + any_specs(9),
        out_specs=any_specs(len(whole)) + vmem_specs(2) + any_specs(6 + len(kept) + len(dense)),
        out_shape=whole + [shape(16, D, dtype=f32), shape(1, D, dtype=f32), shape(length, D), shape(length, D, dtype=f32),
                           shape(length, D)] + [shape(*s) for s, _ in WEIGHTS[1:]] + [shape(*s, dtype=t) for s, t in kept + dense],
        scratch_shapes=scratch,
        compiler_params=pltpu.CompilerParams(vmem_limit_bytes=VMEM_BYTES, **(dict(collective_id=0, has_side_effects=True) if remote else {})),
        name="forward",
    )(hidden, cot, spot, place_map, *weights)
    if remote:
        weights, results = results[:9], results[9:]
    return weights, results[:8], results[8 : 8 + len(kept)], results[8 + len(kept) :]


DENSE_IN = ("x", "projected", "merged", "lse", "grad_merged", "plus")


def backward_kernel(remote, *refs):
    spot_ref, map_ref, vec_ref, gmlp_ref, *refs = refs
    weights_hbm, refs = refs[:5], refs[5:]
    n, m = len(KEPT), len(DENSE_IN)
    dense_hbm, refs = dict(zip(DENSE_IN, refs[:m])), refs[m:]
    kept_hbm, refs = dict(zip(KEPT, refs[:n])), refs[n:]
    given, refs = refs[:3], refs[3:]
    input_hbm, *refs = refs
    if remote:
        outs, refs = refs[:9], refs[9:]
    else:
        gvec_ref, *refs = refs
    made, refs = refs[:5], refs[5:]
    if remote:
        k = len(PARTS)
        core_in, second_in, first_in, refs = refs[:k], refs[k : 2 * k], refs[2 * k : 3 * k], refs[3 * k :]
    (x, plus, projected, merged, grad_merged, lse, normed, qkv, turned, grad_rows, gate, out, up, down, x_a, active, slope,
     stage, load_sem, stage_sem, row_sem, *refs) = refs
    half = spot_ref.shape[1]
    top, rest = pl.ds(0, half), pl.ds(half, half)
    a_refs = dict(x=x_a, change=plus.at[rest], branch=plus.at[top], projected=projected.at[top], merged=merged.at[top],
                  lse=lse.at[:, :, top], active=active, slope=slope, normed=normed.at[top], normed_mlp=normed.at[rest])
    copies = dict(zip(("d_qkv", "qkv", "out", "up", "down"), zip(weights_hbm, (qkv, qkv, out, up, down))))
    copies.update({"d_" + k: (dense_hbm[k], r) for k, r in zip(DENSE_IN, (x, projected, merged, lse, grad_merged, plus))})
    copies.update({k: (kept_hbm[k], a_refs[k]) for k in KEPT})
    copies = {k: pltpu.make_async_copy(*v, load_sem.at[j]) for j, (k, v) in enumerate(copies.items())}
    late = ("change", "normed_mlp", "branch", "merged", "projected", "lse", "normed", "qkv")
    for k in ("d_projected", "d_merged", "d_grad_merged", "d_lse", "d_x", "d_qkv", "d_plus", "x", "down", "active", "slope", "up", "out"):
        copies[k].start()

    def need(*names):
        for k in names:
            copies[k].wait()

    d = Block(x.shape[0], dict(x=x, branch=plus, projected=projected, merged=merged, lse=lse, active=grad_merged, normed=normed,
                               qkv=qkv, gain_attn=vec_ref.at[3:4]))
    b = Block(half, dict(a_refs, grad_low=grad_merged.at[rest], qkv=qkv, out=out, up=up, down=down,
                         gain_attn=vec_ref.at[0:1], gain_mlp=vec_ref.at[1:2]))
    if remote:
        gvec_ref, tile, *refs = refs
    gvec_ref[...] = jnp.zeros_like(gvec_ref)
    gvec_ref[4:5] = gmlp_ref[...]

    def vec(j, value):
        gvec_ref[j : j + 1] = value

    ship = Ship((stage,), stage_sem)
    gqkv_b, gqkv_a, gout_a, gup_a, gdown_a = made

    def finish(t, g):
        x[t] = g

    attend, qkv_step, norm_step = attend_steps(d, ship, gqkv_b, lambda v: vec(3, v), finish, turned, False)

    def norm(_):
        norm_step[1](0)
        for k in late:
            copies[k].start()

    steps = [(0, lambda _: need("d_projected", "d_merged", "d_grad_merged", "d_lse")), attend,
             (0, lambda _: need("d_x")), (0, lambda _: d.norm()), qkv_step, (0, lambda _: need("d_qkv", "d_plus")), (1, norm)]
    steps += routed_backward_steps(b, need, x, spot_ref, vec_ref, a_refs["change"], grad_rows, gate, ship,
                                   (gqkv_a, gout_a, gup_a, gdown_a), vec, turned, input_hbm, row_sem.at[0])
    if not remote:
        run(steps)
    else:
        grads = (gqkv_b, *given, gqkv_a, gout_a, gup_a, gdown_a, tile)
        sums = Scatter(PARTS, grads, outs, core_in, second_in, first_in, *Scatter.unpack(PARTS, refs))

        hooks = [[] for _ in range(sum(c for c, _ in steps) + 1)]
        for unit, step, p in BACK_PLAN:
            hooks[unit].append(functools.partial(sums.steps[step], p))
        greet(*place())
        run(steps, hooks)
        tile[...] = write_vectors(gvec_ref[...], *tile.shape, map_ref)
        for g in hooks[-1]:
            g()
        sums.finish()
    pltpu.make_async_copy(x, input_hbm, row_sem.at[0]).wait()


def backward(remote, spot, place_map, vec, gmlp, weights, dense, kept, given, outer, inner):
    length, rows = dense[0].shape[0], spot.shape[1]
    f32, b16 = jnp.float32, jnp.bfloat16
    made = [shape(*WEIGHTS[j][0]) for j in (0, 0, 1, 2, 3)]
    results = [shape(length, D, dtype=f32)]
    specs = any_specs(1)
    if remote:
        shards = [shape(s[0] // inner, s[1] // outer, dtype=f32) for s, _ in WEIGHTS]
        results += shards + shards + [shape(16, 128, dtype=f32)]
        specs += any_specs(9)
        lands = Scatter.shapes(PARTS)
    else:
        results += [shape(16, D, dtype=f32)]
        specs += vmem_specs(1)
        lands = []
    every = dict(Block.scratch(length), x=((length, D), f32))
    short = Block.scratch(rows)
    scratch = buffers(*[every[k] for k in ("x", "x", "projected", "merged", "merged", "lse", "normed")], WEIGHTS[0],
                      ((128, length), f32), ((rows, D), b16), ((rows, 128), f32), *WEIGHTS[1:],
                      ((rows, D), b16), short["active"], short["slope"], ((D, D), b16))
    scratch += [pltpu.SemaphoreType.DMA((k,)) for k in (5 + len(DENSE_IN) + len(kept), 2, 1)]
    if remote:
        scratch += buffers(((16, D), f32), ((16 * inner, 128 * outer), b16)) + Scatter.scratch(PARTS)
    return pl.pallas_call(
        functools.partial(backward_kernel, remote),
        in_specs=vmem_specs(4) + any_specs(5 + len(dense) + len(kept) + len(given)),
        out_specs=specs + any_specs(len(made) + len(lands)),
        out_shape=results + made + lands,
        scratch_shapes=scratch,
        compiler_params=pltpu.CompilerParams(vmem_limit_bytes=VMEM_BYTES, **(dict(collective_id=1, has_side_effects=True) if remote else {})),
        name="backward",
    )(spot, place_map, vec, gmlp, *weights, *dense, *kept, *given)


def pack_vectors(vectors):
    rows = jnp.stack([jnp.pad(v, (0, 128 - v.shape[0])) for v in vectors])
    return jnp.pad(rows, ((0, 16 - rows.shape[0]), (0, 0)))


def spread_vectors(vectors, outer, inner):
    rows = vectors.reshape(vectors.shape[0], outer, inner, -1).transpose(2, 0, 1, 3).astype(jnp.bfloat16)
    tiles = jnp.pad(rows, ((0, 0), (0, 16 - rows.shape[1]), (0, 0), (0, 128 - rows.shape[3])))
    return tiles.reshape(inner * 16, outer * 128)


def deliver_kernel(n, *refs):
    tile, sums, outs, vectors = refs[0], refs[1 : n + 1], refs[n + 1 : 2 * n + 1], refs[2 * n + 1 :]
    for a, b in zip(sums, outs):
        b[...] = a[...]
    for j, v in enumerate(vectors):
        v[...] = tile[j : j + 1, : v.shape[1]]


def deliver(tile, sums, each, count):
    n = len(sums)
    return pl.pallas_call(
        functools.partial(deliver_kernel, n),
        in_specs=vmem_specs(1 + n),
        out_specs=vmem_specs(n + count),
        out_shape=[shape(*s.shape, dtype=s.dtype) for s in sums] + [shape(1, each, dtype=jnp.float32)] * count,
        name="deliver",
    )(tile, *sums)


def fits(shards, outer, inner):
    return outer == 2 and inner == 16 and all(s.shape[0] % 16 == 0 and s.shape[1] % 128 == 0 for s in shards)


def per_device(outer, inner, *args):
    hidden, cotangent, capacity_class, token_index = args[:4]
    (gain_attn_a, qkv_a, out_a, gain_mlp_a, up_a, down_a, router_shard,
     gain_attn_b, qkv_b, out_b, gain_mlp_b, up_b, down_b) = args[4:]
    hidden, cotangent = hidden[0], cotangent[0]
    length = hidden.shape[0]
    tile = pack_vectors((gain_attn_a, gain_mlp_a, router_shard, gain_attn_b, gain_mlp_b))
    shards = [tile, qkv_a, out_a, up_a, down_a, qkv_b, out_b, up_b, down_b]
    remote = fits(shards, outer, inner)
    if not remote:
        shards = [lax.all_gather(lax.all_gather(s, "inner", axis=0, tiled=True), "outer", axis=1, tiled=True) for s in shards]

    capacity = (length // 8) << capacity_class[0]
    slots = lax.broadcasted_iota(jnp.int32, token_index.shape, 1)
    spot = jnp.where(slots < capacity, token_index, -1)
    whole, made, kept, dense = forward(remote, hidden, cotangent, spot, lane_map(outer, inner), shards, outer, inner)
    vec, gmlp, output, plus, grad_merged, *given = made
    input_grad, *res = backward(
        remote, spot, lane_map(outer, inner), vec, gmlp, (whole[5], *whole[1:5]), [*dense, grad_merged, plus], kept, given, outer, inner)
    if remote:
        done, gtile = res[:8], res[8]
    else:
        gvec, gqkv_b, *grads_a = res
        done = [
            lax.psum_scatter(
                lax.psum_scatter(s, "outer", scatter_dimension=1, tiled=True), "inner", scatter_dimension=0, tiled=True
            ).astype(jnp.float32)
            for s in [gqkv_b, *given, *grads_a, spread_vectors(gvec[:5], outer, inner)]
        ]
        done, gtile = done[:8], done[8]
    each = gain_attn_a.shape[0]
    res = deliver(gtile, done, each, 5)
    gb, ga, v = res[:4], res[4:8], [r[0] for r in res[8:]]
    return (output[None], input_grad[None], v[0], ga[0], ga[1], v[1], ga[2], ga[3], v[2], v[3], gb[0], gb[1], v[4], gb[2], gb[3])


def solution(mesh):
    outer, inner = mesh.shape["outer"], mesh.shape["inner"]
    both = ("outer", "inner")
    rows, vector, matrix = P(both, None, None), P(both), P("inner", "outer")
    block = (vector, matrix, matrix, vector, matrix, matrix)
    return jax.shard_map(
        functools.partial(per_device, outer, inner),
        mesh=mesh,
        in_specs=(rows, rows, vector, P(both, None)) + block + (vector,) + block,
        out_specs=(rows, rows) + block + (vector,) + block,
        check_vma=False,
    )
```

```python
import functools

import jax
import jax.numpy as jnp
from jax import lax
from jax.experimental import pallas as pl
from jax.experimental.pallas import tpu as pltpu
from jax.sharding import PartitionSpec as P

MESH = pl.DeviceIdType.MESH


def place():
    o, i = lax.axis_index("outer"), lax.axis_index("inner")
    return o, i // 4, (i // 2) % 2, i % 2


def device(o, z, x, c):
    return (o, z * 4 + x * 2 + c)


def greet(o, z, x, c):
    barrier = pltpu.get_barrier_semaphore()
    signal = functools.partial(pl.semaphore_signal, barrier, inc=1, device_id_type=MESH)
    signal(device_id=device(1 - o, z, x, c))
    signal(device_id=device(o, z, 1 - x, c))
    signal(device_id=device(o, z, x, 1 - c))

    @pl.when(z > 0)
    def _():
        signal(device_id=device(o, z - 1, x, c))

    @pl.when(z < 3)
    def _():
        signal(device_id=device(o, z + 1, x, c))

    pl.semaphore_wait(barrier, 3 + jnp.where(z > 0, 1, 0) + jnp.where(z < 3, 1, 0))


GATHER_PARTS = (
        (0, 0, 16, 0, 128, False, False), (1, 0, 48, 0, 384, True, False), (2, 0, 48, 0, 384, True, False), (5, 0, 48,
    0, 384, False, False), (4, 0, 96, 0, 384, False, True), (1, 0, 48, 768, 384, True, False), (1, 0, 48, 384, 384,
    False, False), (3, 0, 48, 0, 768, False, False), (3, 0, 48, 768, 768, True, False), (5, 0, 48, 768, 384, True,
    True), (4, 96, 96, 0, 384, False, False), (5, 0, 48, 384, 384, True, False), (7, 0, 48, 768, 768, False, False), (7,
    0, 48, 0, 768, False, False), (6, 0, 48, 0, 384, True, True), (8, 0, 96, 0, 384, True, False), (8, 96, 96, 0, 384,
    True, True))
GATHER_PLAN = (
        (0, 0, 0), (0, 0, 1), (0, 0, 2), (0, 0, 3), (0, 1, 0), (0, 1, 1), (0, 1, 2), (0, 1, 3), (0, 2, 0), (0, 2, 1),
    (0, 2, 2), (0, 2, 3), (0, 3, 0), (0, 0, 4), (0, 3, 1), (0, 0, 5), (0, 3, 2), (0, 0, 6), (0, 4, 0), (0, 3, 3), (0, 0,
    7), (0, 1, 5), (0, 1, 4), (0, 1, 6), (0, 1, 7), (0, 2, 5), (0, 4, 1), (0, 2, 6), (0, 2, 7), (0, 3, 5), (0, 0, 8),
    (0, 4, 2), (0, 5, 0), (0, 3, 6), (0, 0, 9), (0, 6, 0), (0, 3, 7), (0, 0, 10), (0, 4, 3), (0, 1, 8), (1, 5, 1), (1,
    2, 4), (1, 4, 5), (1, 2, 8), (1, 1, 10), (1, 6, 1), (1, 1, 9), (1, 5, 2), (1, 6, 2), (1, 4, 6), (1, 3, 4), (1, 0,
    11), (1, 3, 8), (1, 0, 12), (1, 2, 10), (1, 5, 3), (1, 4, 7), (1, 6, 3), (1, 5, 6), (1, 4, 4), (1, 5, 5), (1, 1,
    11), (1, 2, 9), (1, 6, 6), (1, 1, 12), (1, 6, 5), (1, 3, 10), (1, 0, 13), (2, 4, 8), (7, 5, 4), (7, 2, 11), (8, 5,
    7), (9, 6, 4), (9, 3, 9), (9, 4, 10), (9, 0, 14), (10, 6, 7), (10, 2, 12), (11, 1, 13), (11, 3, 11), (11, 0, 15),
    (11, 5, 8), (11, 4, 9), (11, 3, 12), (11, 0, 16), (11, 6, 8), (11, 2, 13), (11, 5, 10), (11, 1, 14), (12, 1, 15),
    (13, 6, 10), (13, 4, 11), (14, 5, 9), (15, 4, 12), (15, 3, 13), (16, 6, 9), (16, 2, 14), (16, 2, 15), (18, 5, 11),
    (18, 1, 16), (18, 3, 14), (18, 6, 11), (18, 3, 15), (19, 5, 12), (19, 4, 13), (19, 4, 14), (20, 2, 16), (21, 6, 12),
    (22, 5, 14), (23, 6, 14), (24, 4, 15), (24, 3, 16), (26, 5, 13), (27, 6, 13), (27, 5, 15), (27, 4, 16), (29, 6, 15),
    (30, 5, 16), (31, 6, 16))


class Gather:
    @staticmethod
    def semaphores(n):
        return [pltpu.SemaphoreType.DMA(k) for k in ((n,), (n, 23), (n, 19))]

    def __init__(self, parts, shards, outs, local_sem, send_sem, recv_sem):
        o, z, x, c = place()
        n = len(parts)

        def shard(p):
            a, r0, r, c0, w, _, _ = parts[p]
            return shards[a].at[pl.ds(r0, r), pl.ds(c0, w)]

        def blocks(p, oo):
            a, r0, r, c0, w, _, _ = parts[p]
            rows, each = shards[a].shape
            view = outs[a].reshape(4, 2, 2, rows, 2 * each)
            return view, pl.ds(r0, r), pl.ds(pl.multiple_of(oo * each + c0, 128), w)

        def chunk(p, k):
            view, rows, columns = blocks(p, o)
            return view.at[k, x, c, rows, columns]

        def group(p, second, first):
            first_x = parts[p][5]
            px, po = (first, second) if first_x else (second, first)
            view, rows, columns = blocks(p, o if po else 1 - o)
            return view.at[:, x if px else 1 - x, c, rows, columns]

        def send(p, src, dst, slot, target):
            return pltpu.make_async_remote_copy(
                src_ref=src, dst_ref=dst, send_sem=send_sem.at[p, slot[0]], recv_sem=recv_sem.at[p, slot[1]],
                device_id=target, device_id_type=MESH)

        def wait(ref, sem):
            pltpu.make_async_copy(ref, ref, sem).wait()

        def up(p, k, hop, src=None):
            b = chunk(p, k)
            return send(p, b if src is None else src, b, (hop, k), device(o, z + 1, x, c))

        def down(p, k, hop, src=None):
            b = chunk(p, k)
            return send(p, b if src is None else src, b, (3 + hop, k), device(o, z - 1, x, c))

        def near(p, second):
            return device(o, z, 1 - x, c) if parts[p][5] != second else device(1 - o, z, x, c)

        def to_core(p, second, first):
            b = group(p, second, first)
            send(p, b, b, (9 + 2 * second + first, 7 + 2 * second + first), device(o, z, x, 1 - c)).start()

        def to_second(p, first):
            b = group(p, 1, first)
            send(p, b, b, (7 + first, 5 + first), near(p, True)).start()

        def local(p):
            return pltpu.make_async_copy(shard(p), chunk(p, z), local_sem.at[p])

        def own(p):
            @pl.when(z < 3)
            def _():
                up(p, z, 0, shard(p)).start()

            @pl.when(z > 0)
            def _():
                down(p, z, 0, shard(p)).start()

            local(p).start()

        def hop(d):
            def go(p):
                @pl.when(z >= d)
                def _():
                    wait(chunk(p, z - d), recv_sem.at[p, z - d])
                    if d < 3:
                        @pl.when(z < 3)
                        def _():
                            up(p, z - d, d).start()

                @pl.when(z + d <= 3)
                def _():
                    wait(chunk(p, z + d), recv_sem.at[p, z + d])
                    if d < 3:
                        @pl.when(z > 0)
                        def _():
                            down(p, z + d, d).start()
            return go

        third = hop(3)

        def first(p):
            third(p)
            local(p).wait()
            b = group(p, 1, 1)
            send(p, b, b, (6, 4), near(p, False)).start()
            to_second(p, 1)
            to_core(p, 1, 1)

        def second(p):
            wait(group(p, 1, 0), recv_sem.at[p, 4])
            to_second(p, 0)
            to_core(p, 1, 0)

        def cores(p):
            for f in (1, 0):
                wait(group(p, 0, f), recv_sem.at[p, 5 + f])
                to_core(p, 0, f)

        def arrived(p):
            for slot in range(4):
                wait(group(p, 1, 1), recv_sem.at[p, 7 + slot])

        def plane(p, second, first):
            first_x = parts[p][5]
            px, po = (first, second) if first_x else (second, first)
            view, rows, columns = blocks(p, o if po else 1 - o)
            return view.at[z, x if px else 1 - x, c, rows, columns]

        def layer(p, k, oo):
            view, rows, columns = blocks(p, oo)
            return view.at[k, :, c, rows, columns]

        def late_own(p):
            s, b = shard(p), plane(p, 1, 1)
            send(p, s, b, (12, 8), near(p, False)).start()
            send(p, s, b, (13, 9), near(p, True)).start()
            local(p).start()

        def late_first(p):
            b = plane(p, 1, 0)
            wait(b, recv_sem.at[p, 8])
            send(p, b, b, (14, 10), near(p, True)).start()

        def spread(p, k, hop, rise, fall):
            for oo in (0, 1):
                b = layer(p, k, oo)
                if rise:
                    @pl.when(z < 3)
                    def _():
                        send(p, b, b, (2 * hop + oo, 2 * k + oo), device(o, z + 1, x, c)).start()
                if fall:
                    @pl.when(z > 0)
                    def _():
                        send(p, b, b, (6 + 2 * hop + oo, 2 * k + oo), device(o, z - 1, x, c)).start()
                send(p, b, b, (15 + 2 * k + oo, 11 + 2 * k + oo), device(o, z, x, 1 - c)).start()

        def late_second(p):
            wait(plane(p, 0, 1), recv_sem.at[p, 9])
            wait(plane(p, 0, 0), recv_sem.at[p, 10])
            local(p).wait()
            spread(p, z, 0, True, True)

        def late_hop(d):
            def go(p):
                for k, there, rise in ((z - d, z >= d, True), (z + d, z + d <= 3, False)):
                    @pl.when(there)
                    def _():
                        for oo in (0, 1):
                            wait(layer(p, k, oo), recv_sem.at[p, 2 * k + oo])
                        spread(p, k, d, rise and d < 3, not rise and d < 3)
            return go

        def late_arrived(p):
            for slot in range(8):
                wait(layer(p, 0, 0), recv_sem.at[p, 11 + slot])

        def late_finish(p):
            for oo in (0, 1):
                for d in range(3):
                    @pl.when(jnp.logical_and(z < 3, z >= d))
                    def _():
                        wait(layer(p, 0, 0), send_sem.at[p, 2 * d + oo])

                    @pl.when(jnp.logical_and(z > 0, z + d <= 3))
                    def _():
                        wait(layer(p, 0, 0), send_sem.at[p, 6 + 2 * d + oo])
            for slot in (12, 13, 14):
                wait(plane(p, 1, 1), send_sem.at[p, slot])
            for slot in range(15, 23):
                wait(layer(p, 0, 0), send_sem.at[p, slot])

        def early_finish(p):
            for d in range(3):
                @pl.when(jnp.logical_and(z < 3, z >= d))
                def _():
                    wait(chunk(p, z), send_sem.at[p, d])

                @pl.when(jnp.logical_and(z > 0, z + d <= 3))
                def _():
                    wait(chunk(p, z), send_sem.at[p, 3 + d])
            for slot in range(6, 13):
                wait(group(p, 1, 1), send_sem.at[p, slot])

        early = (own, hop(1), hop(2), first, second, cores, arrived)
        late = (late_own, late_first, late_second, late_hop(1), late_hop(2), late_hop(3), late_arrived)

        def finish():
            for p in range(n):
                (late_finish if parts[p][6] else early_finish)(p)

        self.finish = finish
        self.take = lambda step, p: (late if parts[p][6] else early)[step](p)

    def begin(self):
        greet(*place())


PARTS = (
        (3, 96, 96, 0, 384, False, 2, False), (2, 0, 48, 0, 768, True, 1, False), (2, 0, 48, 768, 768, True, 3, True),
    (3, 0, 96, 0, 384, True, 0, False), (1, 0, 48, 0, 384, True, 4, False), (0, 0, 48, 640, 512, False, 6, False), (7,
    96, 96, 0, 384, False, 2, False), (0, 0, 48, 0, 640, True, 5, False), (6, 0, 48, 768, 768, True, 3, True), (6, 0,
    48, 0, 768, True, 1, False), (4, 0, 48, 640, 512, False, 6, False), (4, 0, 48, 0, 640, True, 5, False), (5, 0, 48,
    0, 384, False, 4, False), (7, 0, 96, 0, 384, True, 0, False), (8, 0, 16, 0, 128, True, 7, False))
BACK_PLAN = (
        (0, 0, 3), (0, 0, 2), (0, 0, 0), (0, 0, 1), (0, 0, 4), (1, 1, 3), (2, 2, 3), (2, 1, 2), (2, 1, 0), (3, 2, 2),
    (3, 2, 0), (3, 1, 1), (4, 2, 1), (4, 1, 4), (5, 3, 3), (5, 2, 4), (6, 4, 3), (6, 3, 2), (6, 3, 0), (7, 4, 0), (10,
    5, 3), (10, 0, 7), (10, 0, 5), (10, 4, 2), (10, 6, 3), (10, 3, 1), (11, 4, 1), (11, 1, 7), (12, 7, 3), (12, 2, 7),
    (12, 1, 5), (12, 5, 0), (13, 8, 3), (13, 2, 5), (13, 5, 2), (13, 6, 0), (13, 5, 1), (13, 3, 4), (14, 9, 3), (14, 6,
    1), (14, 4, 4), (15, 3, 7), (15, 7, 0), (16, 0, 13), (16, 4, 7), (16, 3, 5), (16, 6, 2), (16, 8, 0), (16, 7, 1),
    (16, 5, 4), (17, 4, 5), (17, 6, 4), (18, 1, 13), (18, 9, 0), (18, 0, 6), (18, 8, 1), (19, 2, 13), (19, 5, 7), (19,
    7, 4), (20, 1, 6), (20, 6, 7), (20, 5, 5), (20, 7, 2), (20, 0, 8), (20, 9, 1), (20, 0, 9), (20, 8, 4), (20, 6, 5),
    (20, 2, 6), (21, 9, 4), (22, 1, 8), (22, 7, 7), (23, 2, 8), (23, 1, 9), (23, 7, 5), (24, 8, 7), (24, 0, 12), (24, 2,
    9), (26, 3, 13), (26, 8, 5), (27, 4, 13), (27, 9, 7), (27, 9, 5), (27, 0, 10), (27, 0, 11), (27, 3, 6), (29, 1, 10),
    (29, 4, 6), (29, 0, 14), (29, 2, 10), (29, 3, 8), (29, 5, 13), (29, 1, 11), (29, 6, 13), (29, 2, 11), (29, 3, 9),
    (29, 4, 9), (29, 1, 12), (29, 5, 6), (29, 2, 12), (29, 3, 10), (29, 6, 6), (29, 7, 13), (29, 4, 10), (29, 4, 8),
    (29, 7, 6), (29, 5, 9), (29, 6, 9), (29, 1, 14), (29, 8, 13), (29, 2, 14), (29, 3, 11), (29, 4, 11), (29, 5, 8),
    (29, 9, 13), (29, 7, 9), (29, 8, 6), (29, 3, 12), (29, 4, 12), (29, 5, 10), (29, 3, 14), (29, 6, 10), (29, 4, 14),
    (29, 9, 6), (29, 8, 9), (29, 5, 11), (29, 6, 8), (29, 7, 10), (29, 6, 11), (29, 5, 14), (29, 9, 9), (29, 6, 14),
    (29, 5, 12), (29, 7, 8), (29, 8, 10), (29, 6, 12), (29, 7, 11), (29, 9, 10), (29, 7, 14), (29, 7, 12), (29, 8, 11),
    (29, 8, 14), (29, 8, 12), (29, 9, 11), (29, 9, 14), (29, 9, 12))


class Scatter:
    def __init__(self, parts, grads, outs, core_in, second_in, first_in, buffers, sems):
        o, z, x, c = place()
        acc, z_in, stage_own, stage_got, stage_second, stage_first, stage_out = buffers
        send_sem, recv_sem, own_sem, stage_sem, out_sem = sems
        n = len(parts)

        def kind(p):
            return 1 if parts[p][2] == 96 else 0

        def of(p):
            return parts[p][2], parts[p][4]

        def part(ref, p):
            r, w = of(p)
            return ref.at[:, pl.ds(0, r), pl.ds(0, w)]

        def group(p, second, first, core):
            g, r0, r, c0, w, first_x, _, _ = parts[p]
            px, po = (first, second) if first_x else (second, first)
            xx = x if px else 1 - x
            oo = o if po else 1 - o
            height, width = grads[g].shape
            each = width // 2
            return grads[g].reshape(4, 2, 2, height // 16, width).at[:, xx, core, pl.ds(r0, r), pl.ds(pl.multiple_of(oo * each + c0, 128), w)]

        def far(p, second):
            return device(o, z, 1 - x, c) if parts[p][5] != second else device(1 - o, z, x, c)

        def send(p, src, dst, kind_, slot, target):
            return pltpu.make_async_remote_copy(
                src_ref=src, dst_ref=dst, send_sem=send_sem.at[p, kind_], recv_sem=recv_sem.at[p, slot],
                device_id=target, device_id_type=MESH)

        def wait(ref, sem):
            pltpu.make_async_copy(ref, ref, sem).wait()

        slots, last_user = {}, {}
        turn = [0, 0]
        for p in range(n):
            k = kind(p)
            if parts[p][7]:
                slots[p], last_user[p] = None, None
                continue
            slots[p] = turn[k] % 2
            last_user[p] = next((q for q in range(p - 1, -1, -1) if kind(q) == k and slots[q] == slots[p]), None)
            turn[k] += 1

        def own_of(p):
            return part(stage_own[kind(p)].at[slots[p]], p)

        def total(p):
            return acc[parts[p][6]]

        def begin(p):
            for second in (0, 1):
                for first in (0, 1):
                    send(p, group(p, second, first, 1 - c), core_in[p].at[pl.ds(second * 8 + first * 4, 4)], 0, 0,
                         device(o, z, x, 1 - c)).start()
            for second in (0, 1) if parts[p][7] else (1,):
                for first in (0, 1):
                    at = second * 8 + first * 4 if parts[p][7] else first * 4
                    pltpu.make_async_copy(group(p, second, first, c), total(p).at[pl.ds(at, 4)], own_sem.at[p]).start()

        def core_fetch(p):
            k = kind(p)
            if last_user[p] is not None:
                q = last_user[p]
                wait(own_of(q), send_sem.at[q, 1])
            for first in () if parts[p][7] else (0, 1):
                pltpu.make_async_copy(group(p, 0, first, c), own_of(p).at[pl.ds(first * 4, 4)], stage_sem.at[kind(p), 0]).start()
            wait(core_in[p], recv_sem.at[p, 0])
            pltpu.make_async_copy(core_in[p].at[pl.ds(0, 8)], part(stage_got[k], p), stage_sem.at[kind(p), 1]).start()
            pltpu.make_async_copy(core_in[p].at[pl.ds(8, 8)], part(stage_second[k], p), stage_sem.at[kind(p), 2]).start()

        def core_add(p):
            own, got = own_of(p), part(stage_got[kind(p)], p)
            wait(own, stage_sem.at[kind(p), 0])
            wait(got, stage_sem.at[kind(p), 1])
            for first in (0, 1):
                s = pl.ds(first * 4, 4)
                own[s] = own[s] + got[s]
                send(p, own.at[s], second_in[p].at[s], 1, 1 + first, far(p, True)).start()
            mine = part(stage_second[kind(p)], p)
            wait(total(p), own_sem.at[p])
            wait(mine, stage_sem.at[kind(p), 2])
            total(p)[...] = total(p)[...] + mine[...]

        def second_fetch(p):
            got = part(stage_second[kind(p)], p)
            for first in (0, 1):
                s = pl.ds(first * 4, 4)
                wait(second_in[p].at[s], recv_sem.at[p, 1 + first])
            pltpu.make_async_copy(second_in[p], got, stage_sem.at[kind(p), 2]).start()

        def second_add(p):
            got = part(stage_second[kind(p)], p)
            wait(got, stage_sem.at[kind(p), 2])
            t = total(p)
            t[0:4] = t[0:4] + got[0:4]
            send(p, t.at[pl.ds(0, 4)], first_in[p], 2, 3, far(p, False)).start()
            t[4:8] = t[4:8] + got[4:8]

        def send_z(p, k, step):
            to = z + step
            slot = jnp.where(k == to, jnp.where(step > 0, k, 4), k)
            send(p, total(p).at[4 + k], z_in[p].at[slot], 3, 4 + slot, device(o, to, x, c)).start()

        def first_fetch(p):
            wait(first_in[p], recv_sem.at[p, 3])
            pltpu.make_async_copy(first_in[p], part(stage_first[kind(p)], p), stage_sem.at[kind(p), 3]).start()

        def first_add(p):
            got = part(stage_first[kind(p)], p)
            wait(got, stage_sem.at[kind(p), 3])
            t = total(p)
            t[4:8] = t[4:8] + got[...]

            @pl.when(z == 0)
            def _():
                for k in (3, 2, 1):
                    send_z(p, k, 1)

            @pl.when(z == 3)
            def _():
                for k in (0, 1, 2):
                    send_z(p, k, -1)

        def pass_on(p, k, step):
            wait(z_in[p].at[k], recv_sem.at[p, 4 + k])
            total(p)[4 + k] = total(p)[4 + k] + z_in[p][k]
            send_z(p, k, step)

        def along(level):
            def go(p):
                @pl.when(z == level)
                def _():
                    for k in range(3, level, -1):
                        pass_on(p, k, 1)

                @pl.when(z == 3 - level)
                def _():
                    for k in range(0, 3 - level):
                        pass_on(p, k, -1)
            return go

        out_user = [None, None]

        def copy_out(p):
            g, r0, r, c0, w, _, _, _ = parts[p]
            return pltpu.make_async_copy(stage_out[kind(p)].at[pl.ds(0, r), pl.ds(0, w)],
                                         outs[g].at[pl.ds(r0, r), pl.ds(c0, w)], out_sem.at[kind(p)])

        def finish():
            for p in out_user:
                copy_out(p).wait()

        def last(p):
            g, r0, r, c0, w, _, _, _ = parts[p]
            out = stage_out[kind(p)].at[pl.ds(0, r), pl.ds(0, w)]
            if out_user[kind(p)] is not None:
                copy_out(out_user[kind(p)]).wait()
            out_user[kind(p)] = p
            out[...] = total(p)[4 + z].astype(jnp.float32)

            @pl.when(z > 0)
            def _():
                wait(z_in[p].at[z], recv_sem.at[p, 4 + z])
                out[...] += z_in[p][z].astype(jnp.float32)

            @pl.when(z < 3)
            def _():
                wait(z_in[p].at[4], recv_sem.at[p, 8])
                out[...] += z_in[p][4].astype(jnp.float32)

            copy_out(p).start()
            wait(core_in[p], send_sem.at[p, 0])
            if all(last_user[q] != p for q in range(n)):
                wait(own_of(p), send_sem.at[p, 1])
            wait(first_in[p], send_sem.at[p, 2])
            wait(first_in[p].at[pl.ds(0, 3)], send_sem.at[p, 3])

        def planes(p):
            r, w = of(p)
            return total(p).reshape(4, 4, r, w)

        def send_plane(p, k, step):
            to = z + step
            slot = jnp.where(k == to, jnp.where(step > 0, k, 4), k)
            send(p, planes(p).at[:, k], second_in[p].at[pl.ds(slot * 4, 4)], 3, 4 + slot, device(o, to, x, c)).start()

        def early_add(p):
            k = kind(p)
            got, more = part(stage_got[k], p), part(stage_second[k], p)
            t = total(p)
            wait(t, own_sem.at[p])
            wait(got, stage_sem.at[k, 1])
            wait(more, stage_sem.at[k, 2])
            t[0:8] = t[0:8] + got[...]
            t[8:16] = t[8:16] + more[...]

            @pl.when(z == 0)
            def _():
                for j in (3, 2, 1):
                    send_plane(p, j, 1)

            @pl.when(z == 3)
            def _():
                for j in (0, 1, 2):
                    send_plane(p, j, -1)

        def take_planes(p, taken):
            stage = part(stage_second[kind(p)], p)
            copies = []
            for j, (slot, _) in enumerate(taken):
                wait(second_in[p].at[pl.ds(0, 4)], recv_sem.at[p, 4 + slot])
                copies.append(pltpu.make_async_copy(second_in[p].at[pl.ds(slot * 4, 4)], stage.at[pl.ds(j * 4, 4)],
                                                    stage_sem.at[kind(p), 2]))
                copies[-1].start()
            wait(stage.at[pl.ds(0, 4 * len(taken))], stage_sem.at[kind(p), 2])
            for j, (_, k) in enumerate(taken):
                v = planes(p).at[:, k]
                v[...] = v[...] + stage[j * 4 : j * 4 + 4]

        def early_along(level):
            def go(p):
                @pl.when(z == level)
                def _():
                    ks = range(3, level, -1)
                    take_planes(p, [(k, k) for k in ks])
                    for k in ks:
                        send_plane(p, k, 1)

                @pl.when(z == 3 - level)
                def _():
                    ks = range(0, 3 - level)
                    take_planes(p, [(k, k) for k in ks])
                    for k in ks:
                        send_plane(p, k, -1)
            return go

        def early_end(p):
            @pl.when(z == 0)
            def _():
                take_planes(p, [(4, 0)])

            @pl.when(z == 3)
            def _():
                take_planes(p, [(3, 3)])

            for k in (1, 2):
                @pl.when(z == k)
                def _():
                    take_planes(p, [(k, k), (4, k)])
            send(p, planes(p).at[pl.ds(0, 2), z], z_in[p].at[pl.ds(0, 2)], 1, 1, far(p, True)).start()

        def early_second(p):
            wait(z_in[p].at[pl.ds(0, 2)], recv_sem.at[p, 1])
            for f in (0, 1):
                v = planes(p).at[2 + f, z]
                v[...] = v[...] + z_in[p][f]
            send(p, planes(p).at[2, z], z_in[p].at[2], 2, 3, far(p, False)).start()

        def early_last(p):
            g, r0, r, c0, w, _, _, _ = parts[p]
            out = stage_out[kind(p)].at[pl.ds(0, r), pl.ds(0, w)]
            if out_user[kind(p)] is not None:
                copy_out(out_user[kind(p)]).wait()
            out_user[kind(p)] = p
            wait(z_in[p].at[2], recv_sem.at[p, 3])
            out[...] = planes(p)[3, z].astype(jnp.float32) + z_in[p][2].astype(jnp.float32)
            copy_out(p).start()
            wait(core_in[p], send_sem.at[p, 0])
            wait(total(p).at[pl.ds(0, 12)], send_sem.at[p, 3])
            wait(z_in[p].at[pl.ds(0, 2)], send_sem.at[p, 1])
            wait(z_in[p].at[2], send_sem.at[p, 2])

        self.finish = finish
        late = (begin, core_fetch, core_add, second_fetch, second_add, first_fetch, first_add, along(1), along(2), last)
        early = (begin, core_fetch, early_add, early_along(1), early_along(2), early_end, early_second, early_last)
        self.take = lambda step, p: (early if parts[p][7] else late)[step](p)

    @staticmethod
    def shapes(parts):
        return [shape(20 if m == 8 and s[7] else m, s[2], s[4]) for m in (16, 8, 4) for s in parts]

    @staticmethod
    def scratch(parts):
        b16 = jnp.bfloat16
        sizes = {s[6]: (16 if s[7] else 8, s[2], s[4]) for s in parts}
        acc = [(sizes[k], b16) for k in sorted(sizes)]
        lands = [((3 if s[7] else 5, s[2], s[4]), b16) for s in parts]
        stages = [((m, 48, 768), b16) if k == 0 else ((m, 96, 384), b16) for m in (8, 8, 4) for k in (0, 1)]
        stages = [((2, 8, 48, 768), b16), ((2, 8, 96, 384), b16)] + stages
        stages += [((48, 768), jnp.float32), ((96, 384), jnp.float32)]
        n = len(parts)
        return buffers(*acc, *lands, *stages) + [pltpu.SemaphoreType.DMA(k) for k in ((n, 4), (n, 9), (n,), (2, 4), (2,))]

    @staticmethod
    def unpack(parts, refs):
        n, m = len(parts), len({s[6] for s in parts})
        acc, refs = refs[:m], refs[m:]
        z_in, refs = refs[:n], refs[n:]
        return (acc, z_in, refs[0:2], refs[2:4], refs[4:6], refs[6:8], refs[8:10]), refs[10:15]


D = 768
SCALE = 0.125 * 1.4426950408889634
ROWS = 256
VMEM_BYTES = 127 * 2**19


def mul(a, b, ca=1, cb=0):
    return lax.dot_general(a, b, (((ca,), (cb,)), ((), ())), preferred_element_type=jnp.float32)


def low(v):
    return v.astype(jnp.bfloat16)


def cols(j):
    return pl.ds(pl.multiple_of(j * D, D), D)


def rms_scale(v):
    return lax.rsqrt(jnp.mean(v * v, axis=-1, keepdims=True) + 1e-06)


def rms_back(v, gain, grad):
    r = rms_scale(v)
    unit = v * r
    scaled = grad * gain
    back = r * (scaled - unit * jnp.mean(scaled * unit, axis=-1, keepdims=True))
    return back, jnp.sum((grad * unit).reshape(-1, 8, v.shape[-1]), axis=0)


def gelu_and_slope(u):
    k = 0.7978845608028654
    inner = u * (k + k * 0.044715 * (u * u))
    half = 0.5 + 0.5 * jnp.tanh(inner)
    return u * half, half * (1.0 + (1.0 - half) * (6.0 * inner - 4.0 * k * u))


def halves(v):
    lane = lax.broadcasted_iota(jnp.int32, v.shape, 1)
    zero = jnp.zeros_like(v)
    return jnp.where(lane < 64, v, zero), jnp.where(lane < 64, zero, v)


def two(v):
    first = low(v)
    return first, low(v - first.astype(jnp.float32))


def staggered(tiles, product, finish):
    held = product(tiles[0])
    for t, later in zip(tiles, tiles[1:] + [None]):
        coming = product(later) if later is not None else None
        finish(t, held)
        held = coming


class Block:
    def __init__(self, rows, refs):
        self.rows = rows
        self.__dict__.update(refs)

    @staticmethod
    def scratch(rows):
        f32, b16 = jnp.float32, jnp.bfloat16
        return dict(
            branch=((rows, D), f32), projected=((rows, 3 * D), b16), merged=((rows, D), b16), lse=((6, 8, rows), f32),
            active=((rows, 4 * D), b16), slope=((rows, 4 * D), b16), normed=((rows, D), b16), normed_mlp=((rows, D), b16))

    def rows_of(self, t):
        return self.x[t].astype(jnp.float32)

    def tiles(self):
        return [slice(i, i + ROWS) for i in range(0, self.rows, ROWS)]

    def norm(self):
        for t in self.tiles():
            x = self.rows_of(t)
            self.normed[t] = low(x * rms_scale(x) * self.gain_attn[...])

    def project(self, j):
        c = cols(j)
        self.projected[:, c] = low(mul(self.normed[...], self.qkv[:, c]))

    def pair(self, ref, part, pair, rows=slice(None)):
        return ref[rows, pl.ds(pl.multiple_of(part * D + pair * 128, 128), 128)]

    def attend(self, pair):
        v0, v1 = halves(self.pair(self.projected, 2, pair))
        causal = lax.broadcasted_iota(jnp.int32, (ROWS, ROWS), 1) >= lax.broadcasted_iota(jnp.int32, (ROWS, ROWS), 0)
        for t in self.tiles():
            n = t.stop
            qs = halves(self.pair(self.projected, 0, pair, t))
            k = self.pair(self.projected, 1, pair, slice(0, n))
            total = None
            scores = [mul(k, qs[h], 1, 1) for h in range(2)]
            for h in range(2):
                s = scores[h]
                last = jnp.where(causal, s[t.start:], -1e30)
                s = last if t.start == 0 else jnp.concatenate([s[: t.start], last], axis=0)
                m = jnp.max(s, axis=0, keepdims=True) * SCALE
                p = jnp.exp2(s * SCALE - m)
                l = jnp.sum(p, axis=0, keepdims=True)
                self.lse[pair, h : h + 1, t] = m + jnp.log2(l)
                o = mul(low(p * (1.0 / l)), (v0, v1)[h][:n], 0, 0)
                total = o if total is None else total + o
            self.merged[t, pl.ds(pl.multiple_of(pair * 128, 128), 128)] = low(total)

    def join(self):
        for t in self.tiles():
            branch = mul(self.merged[t], self.out[...])
            self.branch[t] = branch
            middle = self.rows_of(t) + branch
            self.normed_mlp[t] = low(middle * rms_scale(middle) * self.gain_mlp[...])

    def widen(self, j):
        c = cols(j)

        def finish(t, pre):
            active, slope = gelu_and_slope(pre)
            self.active[t, c] = low(active)
            self.slope[t, c] = low(slope)

        staggered(self.tiles(), lambda t: mul(self.normed_mlp[t], self.up[:, c]), finish)

    def narrow(self, t):
        return mul(self.active[t], self.down[...])

    def back_wide(self, j):
        c = cols(j)

        def finish(t, grad):
            self.slope[t, c] = low(grad * self.slope[t, c].astype(jnp.float32))

        staggered(self.tiles(), lambda t: mul(self.grad_low[t], self.down[c, :], 1, 1), finish)

    def grad_down(self, j):
        return low(mul(self.active[:, cols(j)], self.grad_low[...], 0, 0))

    def grad_up(self, j):
        return low(mul(self.normed_mlp[...], self.slope[:, cols(j)], 0, 0))

    def back_mlp(self, grad_of):
        total = jnp.zeros((8, D), jnp.float32)
        for t in self.tiles():
            grad = mul(self.slope[t], self.up[...], 1, 1)
            back, gain = rms_back(self.rows_of(t) + self.branch[t], self.gain_mlp[...], grad)
            total = total + gain
            self.branch[t] = back
            self.normed_mlp[t] = low(grad_of(t) + back)
        return jnp.sum(total, axis=0, keepdims=True)

    def grad_out(self):
        return low(mul(self.merged[...], self.normed_mlp[...], 0, 0))

    def back_merged(self):
        self.active[:, :D] = low(mul(self.normed_mlp[...], self.out[...], 1, 1))

    def attend_back(self, pair, turned):
        rows = self.rows
        q, do = self.pair(self.projected, 0, pair), self.pair(self.active, 0, pair)
        qs, dos = halves(q), halves(do)
        dd = do.astype(jnp.float32) * self.pair(self.merged, 0, pair).astype(jnp.float32)
        pick = lax.broadcasted_iota(jnp.int32, (8, 128), 0) == lax.broadcasted_iota(jnp.int32, (8, 128), 1) // 64
        delta = lax.dot_general(pick.astype(jnp.float32), dd, (((1,), (1,)), ((), ())), precision=lax.Precision.HIGHEST,
                                preferred_element_type=jnp.float32)
        causal = lax.broadcasted_iota(jnp.int32, (ROWS, ROWS), 1) >= lax.broadcasted_iota(jnp.int32, (ROWS, ROWS), 0)
        for t in self.tiles():
            a = t.start
            ks, vs = halves(self.pair(self.projected, 1, pair, t)), halves(self.pair(self.projected, 2, pair, t))
            dk = dv = dq = 0.0
            scores = [mul(ks[h], q[a:], 1, 1) for h in range(2)]
            dps = [mul(vs[h], do[a:], 1, 1) for h in range(2)]
            for h in range(2):
                s, dp = scores[h], dps[h]
                p = jnp.exp2(s * SCALE - self.lse[pair, h : h + 1, a:])
                first = jnp.where(causal, p[:, :ROWS], 0.0)
                p = first if t.stop == rows else jnp.concatenate([first, p[:, ROWS:]], axis=1)
                ds = low(p * (dp - delta[h : h + 1, a:]))
                dv = dv + mul(low(p), dos[h][a:])
                dk = dk + mul(ds, qs[h][a:])
                dq = dq + mul(ks[h], ds, 0, 0)
            lanes = pl.multiple_of(pair * 128, 128)
            self.projected[t, pl.ds(D + lanes, 128)] = low(0.125 * dk)
            self.projected[t, pl.ds(2 * D + lanes, 128)] = low(dv)
            if a == 0:
                turned[:, :rows] = dq
            else:
                turned[:, a:rows] += dq
        self.projected[:, pl.ds(lanes, 128)] = low(0.125 * turned[:, :rows].T)

    def grad_qkv(self, j):
        return low(mul(self.normed[...], self.projected[:, cols(j)], 0, 0))

    def back_norm(self, finish):
        total = jnp.zeros((8, D), jnp.float32)
        for t in self.tiles():
            grad = mul(self.projected[t], self.qkv[...], 1, 1)
            back, gain = rms_back(self.rows_of(t), self.gain_attn[...], grad)
            total = total + gain
            finish(t, back + self.branch[t])
        return jnp.sum(total, axis=0, keepdims=True)


SAVED = ("branch", "projected", "merged", "lse", "active", "slope", "normed", "normed_mlp")


def run(steps, hooks=None):
    at = 0
    waits = []
    for count, body in steps:
        if count == 0:
            waits.append(body)
            continue
        before = [list(hooks[at + k]) if hooks else [] for k in range(count)]
        at += count
        for f in before[0]:
            f()
        for f in waits:
            f(0)
        waits = []
        if count == 1:
            body(0)
            continue

        @pl.loop(0, count)
        def _(j):
            for k in range(1, count):
                if before[k]:
                    @pl.when(j == k)
                    def _():
                        for f in before[k]:
                            f()
            body(j)


class Loads:
    def __init__(self, pairs, sems):
        self.copies = {k: pltpu.make_async_copy(a, b, sems.at[j]) for j, (k, a, b) in enumerate(pairs)}
        for c in self.copies.values():
            c.start()

    def need(self, *names):
        for n in names:
            self.copies[n].wait()


class Ship:
    def __init__(self, stages, sems):
        self.stages, self.sems, self.single = stages, sems, len(stages) == 1

    def wait(self, slot):
        slot = min(slot, len(self.stages) - 1)
        pltpu.make_async_copy(self.stages[slot], self.stages[slot], self.sems.at[slot]).wait()

    def send(self, slot, value, target, busy):
        slot = min(slot, len(self.stages) - 1)
        if busy is True:
            self.wait(slot)
        elif busy is not False:
            pl.when(busy)(lambda: self.wait(slot))
        self.stages[slot][...] = value()
        pltpu.make_async_copy(self.stages[slot], target, self.sems.at[slot]).start()


def wide_steps(b, grad_of, ship, targets, vec):
    gout, gup, gdown = targets

    def wide(j):
        b.back_wide(j)
        ship.send(0, lambda: b.grad_down(j), gdown.at[cols(j), :], j > 0)
        ship.send(1, lambda: b.grad_up(j), gup.at[:, cols(j)], ship.single or j > 0)

    def mlp(_):
        ship.wait(0)
        if not ship.single:
            ship.wait(1)
        vec(b.back_mlp(grad_of))

    def out(_):
        ship.send(1, b.grad_out, gout, False)
        b.back_merged()

    return [(4, wide), (1, mlp), (1, out)]


def attend_steps(b, ship, gqkv, vec, finish, turned, busy):
    def qkv(j):
        ship.send(1, lambda: b.grad_qkv(j), gqkv.at[:, cols(j)], True if busy else j > 0)

    def norm(_):
        vec(b.back_norm(finish))
        ship.wait(1)

    return [(6, lambda j: b.attend_back(j, turned)), (3, qkv), (1, norm)]


def shape(*dims, dtype=jnp.bfloat16):
    return jax.ShapeDtypeStruct(dims, dtype)


def any_specs(n):
    return [pl.BlockSpec(memory_space=pl.ANY)] * n


def vmem_specs(n):
    return [pl.BlockSpec(memory_space=pltpu.VMEM)] * n


WEIGHTS = [((D, 3 * D), jnp.bfloat16), ((D, D), jnp.bfloat16), ((D, 4 * D), jnp.bfloat16), ((4 * D, D), jnp.bfloat16)]


def buffers(*pairs):
    return [pltpu.VMEM(dims, dtype) for dims, dtype in pairs]


def kept_buffers(rows):
    s = Block.scratch(rows)
    return [s[k] for k in SAVED]


def spots(start, count, spot):
    at = lax.broadcasted_iota(jnp.int32, (count, spot.shape[1]), 0) + start
    return low(jnp.where(at == spot, 1.0, 0.0))


def lane_map(outer, inner):
    each = D // (outer * inner)
    d = jnp.arange(D, dtype=jnp.int32)
    return jnp.stack([d // each % inner, d // (each * inner) * 128 + d % each])


def spread_map(tiles_columns, map_ref):
    at = lax.broadcasted_iota(jnp.int32, (tiles_columns, D), 0)
    return low(jnp.where(at == map_ref[1:2], 1.0, 0.0))


def read_vectors(tiles, map_ref):
    rows, columns = tiles.shape
    every = mul(tiles[...], spread_map(columns, map_ref))
    inner = lax.broadcasted_iota(jnp.int32, (rows, D), 0) // 16
    return jnp.sum(jnp.where(inner == map_ref[0:1], every, 0.0).reshape(rows // 16, 16, D), axis=0)


def write_vectors(vectors, rows, columns, map_ref):
    every = jnp.broadcast_to(vectors[None], (rows // 16, 16, D)).reshape(rows, D)
    inner = lax.broadcasted_iota(jnp.int32, (rows, D), 0) // 16
    return low(mul(low(jnp.where(inner == map_ref[0:1], every, 0.0)), spread_map(columns, map_ref), 1, 1))


def gate_of(x, router):
    return jax.nn.sigmoid(jnp.sum(x * router, axis=-1, keepdims=True))


def routed_forward_steps(b, need, hidden, spot_ref, chosen, vec_ref, extra, keep):
    length = hidden.shape[0]

    def pick(_):
        chosen[...] = spots(0, length, spot_ref[...])
        need("hidden")
        for t in b.tiles():
            b.x[t] = low(mul(chosen[:, t], hidden[...], 0, 0))
        need("vectors")
        b.norm()
        keep("x", "normed")

    def join(_):
        keep("projected", "merged", "lse")
        need("out")
        b.join()
        keep("branch", "normed_mlp")

    def narrow(_):
        keep("active", "slope")
        need("down")
        for t in b.tiles():
            extra[t] = b.branch[t] + b.narrow(t)
        keep("change")

    def put(_):
        rows = [gate_of(b.rows_of(t), vec_ref[2:3]) * extra[t] for t in b.tiles()]
        pieces = [two(r) for r in rows]
        for i in range(0, length, ROWS):
            t = slice(i, i + ROWS)
            total = hidden[t].astype(jnp.float32)
            for piece, s in zip(pieces, b.tiles()):
                for p in piece:
                    total = total + mul(chosen[t, s], p)
            b.middle[t] = total

    return [(1, pick), (0, lambda _: need("qkv")), (3, b.project), (6, b.attend), (1, join), (0, lambda _: need("up")), (4, b.widen),
            (1, narrow), (1, put)]


KEPT = ("x", "change") + SAVED


def kept_shapes(rows):
    return [((rows, D), jnp.bfloat16), ((rows, D), jnp.float32)] + kept_buffers(rows)


def routed_backward_steps(b, need, grad, spot_ref, vec_ref, change, grad_rows, gate, ship, targets, vec, turned,
                          grad_hbm, grad_sem):
    length = grad.shape[0]
    router = vec_ref.at[2:3]
    gqkv, *others = targets

    def take(_):
        pieces = two(grad[...])
        need("x", "change")
        for t in b.tiles():
            chosen = spots(0, length, spot_ref[:, t])
            rows = mul(chosen, pieces[0], 0, 0) + mul(chosen, pieces[1], 0, 0)
            g = gate_of(b.rows_of(t), router[...])
            b.grad_low[t], grad_rows[t] = two(g * rows)
            logits = jnp.sum(rows * change[t], axis=-1, keepdims=True) * g * (1.0 - g)
            gate[t] = jnp.broadcast_to(logits, (ROWS, 128))
        need("down", "active", "slope", "normed_mlp")

    def finish(t, g):
        change[t] = g + gate[t, 0:1] * router[...]

    def put(_):
        pieces = [two(change[t]) for t in b.tiles()]
        for i in range(0, length, ROWS):
            t = slice(i, i + ROWS)
            total = grad[t]
            for piece, s in zip(pieces, b.tiles()):
                chosen = spots(i, ROWS, spot_ref[:, s])
                for p in piece:
                    total = total + mul(chosen, p)
            grad[t] = total
            pltpu.make_async_copy(grad.at[t], grad_hbm.at[t], grad_sem).start()

    def route(_):
        total = jnp.zeros((8, D), jnp.float32)
        for t in b.tiles():
            total = total + jnp.sum((gate[t, 0:1] * b.rows_of(t)).reshape(-1, 8, D), axis=0)
        vec(2, jnp.sum(total, axis=0, keepdims=True))

    wide, mlp, out = wide_steps(b, lambda t: b.grad_low[t].astype(jnp.float32) + grad_rows[t].astype(jnp.float32), ship, others, lambda v: vec(1, v))
    attend, qkv, norm = attend_steps(b, ship, gqkv, lambda v: vec(0, v), finish, turned, True)

    def wants(*names):
        return (0, lambda _: need(*names))

    return [(1, take), wide, wants("up", "branch"), mlp, wants("out", "merged"), out, wants("projected", "lse"), attend,
            wants("normed"), qkv, wants("qkv"), norm, (1, route), (1, put)]


KEPT_DENSE = ("x", "projected", "merged", "lse")


def forward_kernel(remote, *refs):
    hidden_hbm, cot_hbm, spot_ref, map_ref, *refs = refs
    given, refs = refs[:9], refs[9:]
    if remote:
        whole, refs = refs[:9], refs[9:]
    else:
        whole = given
    vec_ref, gvec_ref, y_hbm, plus_hbm, gmerged_hbm, gout_hbm, gup_hbm, gdown_hbm, *refs = refs
    n, m = len(KEPT), len(KEPT_DENSE)
    kept_hbm, refs = dict(zip(KEPT, refs[:n])), refs[n:]
    dense_hbm, refs = dict(zip(KEPT_DENSE, refs[:m])), refs[m:]
    hidden, cot, chosen, tiles, qkv, out, up, down, qkv_b, out_b, *refs = refs
    change, branch_a, lse_a, active, slope, x, branch, projected, merged, lse, normed, normed_mlp, stage, *refs = refs
    load_sem, keep_sem, dense_sem, stage_sem, row_sem, *refs = refs
    length, half = hidden.shape[0], spot_ref.shape[1]
    top, rest = pl.ds(0, half), pl.ds(half, half)
    kept = dict(x=active.at[rest, cols(0)], change=change, branch=branch_a, projected=active.at[top, pl.ds(0, 3 * D)],
                merged=active.at[rest, cols(1)], lse=lse_a, active=slope.at[top], slope=slope.at[rest],
                normed=active.at[rest, cols(2)], normed_mlp=active.at[rest, cols(3)])
    into = (tiles, qkv, out, up, down, qkv_b, out_b, up, down)
    loads = [pltpu.make_async_copy(src, dst, load_sem.at[j]) for j, (src, dst) in enumerate(zip(whole, into))]
    loads += [pltpu.make_async_copy(src, dst, load_sem.at[9 + j]) for j, (src, dst) in enumerate(((hidden_hbm, hidden), (cot_hbm, cot)))]
    where = dict(vectors=0, qkv=1, out=2, up=3, down=4, hidden=9)
    loads[9].start()
    loads[10].start()

    def need(name):
        loads[where[name]].wait()
        if name == "vectors":
            vec_ref[...] = read_vectors(tiles, map_ref)

    saves = {k: pltpu.make_async_copy(kept[k], kept_hbm[k], keep_sem.at[j]) for j, k in enumerate(KEPT)}
    dense = dict(x=x, projected=projected, merged=merged, lse=lse)
    dense_saves = {k: pltpu.make_async_copy(dense[k], dense_hbm[k], dense_sem.at[j]) for j, k in enumerate(KEPT_DENSE)}

    def keep(*wanted):
        for k in wanted:
            saves[k].start()

    b = Block(half, dict(kept, middle=x, qkv=qkv, out=out, up=up, down=down,
                         gain_attn=vec_ref.at[0:1], gain_mlp=vec_ref.at[1:2]))
    d = Block(length, dict(dense, branch=branch, normed=normed, normed_mlp=normed_mlp, active=active, slope=slope, grad_low=cot,
                           qkv=qkv_b, out=out_b, up=up, down=down, gain_attn=vec_ref.at[3:4], gain_mlp=vec_ref.at[4:5]))

    def norm(_):
        dense_saves["x"].start()
        d.norm()

    def join(_):
        for k in KEPT_DENSE[1:]:
            dense_saves[k].start()
        loads[6].wait()
        d.join()

    def before_widen(_):
        for c in saves.values():
            c.wait()
        loads[7].wait()

    def narrow(_):
        loads[8].wait()
        for t in d.tiles():
            hidden[t] = low(x[t] + branch[t] + d.narrow(t))
        pltpu.make_async_copy(hidden, y_hbm, row_sem.at[0]).start()
        loads[10].wait()

    def cot_of(t):
        return cot[t].astype(jnp.float32)

    def vec(value):
        gvec_ref[...] = value

    def grad(_):
        for t in d.tiles():
            branch[t] += cot_of(t)
        pltpu.make_async_copy(branch, plus_hbm, row_sem.at[1]).start()

    ship = Ship((stage.at[0], stage.at[1]), stage_sem)
    wide, mlp, last = wide_steps(d, cot_of, ship, (gout_hbm, gup_hbm, gdown_hbm), vec)
    steps = routed_forward_steps(b, need, hidden, spot_ref, chosen, vec_ref, change, keep)
    steps += [(1, norm), (0, lambda _: loads[5].wait()), (3, d.project), (6, d.attend), (1, join), (0, before_widen), (4, d.widen),
              (1, narrow), wide, mlp, (0, grad), last]
    late = 17
    if remote:
        flow = Gather(GATHER_PARTS, given, whole, *refs)
        ends = {}
        for _, step, p in GATHER_PLAN:
            if step == 6:
                ends[GATHER_PARTS[p][0]] = p
        units = [[] for _ in range(sum(c for c, _ in steps) + 1)]
        for unit, step, p in GATHER_PLAN:
            units[unit].append(functools.partial(flow.take, step, p))
            a = GATHER_PARTS[p][0]
            if step == 6 and p == ends[a]:
                units[max(unit, late) if a > 6 else unit].append(loads[a].start)
        flow.begin()
    else:
        for c in loads[:7]:
            c.start()
        units = [[] for _ in range(sum(c for c, _ in steps) + 1)]
        units[late] = [loads[7].start, loads[8].start]
    run(steps, units)
    for f in units[-1]:
        f()
    gmerged = pltpu.make_async_copy(active.at[:, pl.ds(0, D)], gmerged_hbm, row_sem.at[2])
    gmerged.start()
    ship.wait(1)
    if remote:
        flow.finish()
    for c in dense_saves.values():
        c.wait()
    gmerged.wait()
    pltpu.make_async_copy(hidden, y_hbm, row_sem.at[0]).wait()
    pltpu.make_async_copy(branch, plus_hbm, row_sem.at[1]).wait()


def forward(remote, hidden, cot, spot, place_map, weights, outer, inner):
    length, rows = hidden.shape[0], spot.shape[1]
    f32, b16 = jnp.float32, jnp.bfloat16
    kept, short, every = kept_shapes(rows), Block.scratch(rows), Block.scratch(length)
    every["x"] = every["branch"]
    dense = [every[k] for k in KEPT_DENSE]
    whole = [shape(w.shape[0] * inner, w.shape[1] * outer) for w in weights] if remote else []
    scratch = buffers(((length, D), b16), ((length, D), b16), ((length, rows), b16), ((16 * inner, 128 * outer), b16), *WEIGHTS,
                      *WEIGHTS[:2], ((rows, D), f32), short["branch"], short["lse"],
                      *[every[k] for k in ("active", "slope", "x", "branch", "projected", "merged", "lse", "normed", "normed_mlp")],
                      ((2, D, D), b16))
    scratch += [pltpu.SemaphoreType.DMA((k,)) for k in (11, len(kept), len(dense), 2, 3)]
    if remote:
        scratch += Gather.semaphores(len(GATHER_PARTS))
    results = pl.pallas_call(
        functools.partial(forward_kernel, remote),
        in_specs=any_specs(2) + vmem_specs(2) + any_specs(9),
        out_specs=any_specs(len(whole)) + vmem_specs(2) + any_specs(6 + len(kept) + len(dense)),
        out_shape=whole + [shape(16, D, dtype=f32), shape(1, D, dtype=f32), shape(length, D), shape(length, D, dtype=f32),
                           shape(length, D)] + [shape(*s) for s, _ in WEIGHTS[1:]] + [shape(*s, dtype=t) for s, t in kept + dense],
        scratch_shapes=scratch,
        compiler_params=pltpu.CompilerParams(vmem_limit_bytes=VMEM_BYTES, **(dict(collective_id=0, has_side_effects=True) if remote else {})),
        name="forward",
    )(hidden, cot, spot, place_map, *weights)
    if remote:
        weights, results = results[:9], results[9:]
    return weights, results[:8], results[8 : 8 + len(kept)], results[8 + len(kept) :]


DENSE_IN = ("x", "projected", "merged", "lse", "grad_merged", "plus")


def backward_kernel(remote, *refs):
    spot_ref, map_ref, vec_ref, gmlp_ref, *refs = refs
    weights_hbm, refs = refs[:5], refs[5:]
    n, m = len(KEPT), len(DENSE_IN)
    dense_hbm, refs = dict(zip(DENSE_IN, refs[:m])), refs[m:]
    kept_hbm, refs = dict(zip(KEPT, refs[:n])), refs[n:]
    given, refs = refs[:3], refs[3:]
    input_hbm, *refs = refs
    if remote:
        outs, refs = refs[:9], refs[9:]
    else:
        gvec_ref, *refs = refs
    made, refs = refs[:5], refs[5:]
    if remote:
        k = len(PARTS)
        core_in, second_in, first_in, refs = refs[:k], refs[k : 2 * k], refs[2 * k : 3 * k], refs[3 * k :]
    (x, plus, projected, merged, grad_merged, lse, normed, qkv, turned, grad_rows, gate, out, up, down, x_a, active, slope,
     stage, load_sem, stage_sem, row_sem, *refs) = refs
    half = spot_ref.shape[1]
    top, rest = pl.ds(0, half), pl.ds(half, half)
    a_refs = dict(x=x_a, change=plus.at[rest], branch=plus.at[top], projected=projected.at[top], merged=merged.at[top],
                  lse=lse.at[:, :, top], active=active, slope=slope, normed=normed.at[top], normed_mlp=normed.at[rest])
    copies = dict(zip(("d_qkv", "qkv", "out", "up", "down"), zip(weights_hbm, (qkv, qkv, out, up, down))))
    copies.update({"d_" + k: (dense_hbm[k], r) for k, r in zip(DENSE_IN, (x, projected, merged, lse, grad_merged, plus))})
    copies.update({k: (kept_hbm[k], a_refs[k]) for k in KEPT})
    copies = {k: pltpu.make_async_copy(*v, load_sem.at[j]) for j, (k, v) in enumerate(copies.items())}
    late = ("change", "normed_mlp", "branch", "merged", "projected", "lse", "normed", "qkv")
    for k in ("d_projected", "d_merged", "d_grad_merged", "d_lse", "d_x", "d_qkv", "d_plus", "x", "down", "active", "slope", "up", "out"):
        copies[k].start()

    def need(*names):
        for k in names:
            copies[k].wait()

    d = Block(x.shape[0], dict(x=x, branch=plus, projected=projected, merged=merged, lse=lse, active=grad_merged, normed=normed,
                               qkv=qkv, gain_attn=vec_ref.at[3:4]))
    b = Block(half, dict(a_refs, grad_low=grad_merged.at[rest], qkv=qkv, out=out, up=up, down=down,
                         gain_attn=vec_ref.at[0:1], gain_mlp=vec_ref.at[1:2]))
    if remote:
        gvec_ref, tile, *refs = refs
    gvec_ref[...] = jnp.zeros_like(gvec_ref)
    gvec_ref[4:5] = gmlp_ref[...]

    def vec(j, value):
        gvec_ref[j : j + 1] = value

    ship = Ship((stage,), stage_sem)
    gqkv_b, gqkv_a, gout_a, gup_a, gdown_a = made

    def finish(t, g):
        x[t] = g

    attend, qkv_step, norm_step = attend_steps(d, ship, gqkv_b, lambda v: vec(3, v), finish, turned, False)

    def norm(_):
        norm_step[1](0)
        for k in late:
            copies[k].start()

    steps = [(0, lambda _: need("d_projected", "d_merged", "d_grad_merged", "d_lse")), attend,
             (0, lambda _: need("d_x")), (0, lambda _: d.norm()), qkv_step, (0, lambda _: need("d_qkv", "d_plus")), (1, norm)]
    steps += routed_backward_steps(b, need, x, spot_ref, vec_ref, a_refs["change"], grad_rows, gate, ship,
                                   (gqkv_a, gout_a, gup_a, gdown_a), vec, turned, input_hbm, row_sem.at[0])
    if not remote:
        run(steps)
    else:
        grads = (gqkv_b, *given, gqkv_a, gout_a, gup_a, gdown_a, tile)
        sums = Scatter(PARTS, grads, outs, core_in, second_in, first_in, *Scatter.unpack(PARTS, refs))

        hooks = [[] for _ in range(sum(c for c, _ in steps) + 1)]
        for unit, step, p in BACK_PLAN:
            hooks[unit].append(functools.partial(sums.take, step, p))
        greet(*place())
        run(steps, hooks)
        tile[...] = write_vectors(gvec_ref[...], *tile.shape, map_ref)
        for g in hooks[-1]:
            g()
        sums.finish()
    pltpu.make_async_copy(x, input_hbm, row_sem.at[0]).wait()


def backward(remote, spot, place_map, vec, gmlp, weights, dense, kept, given, outer, inner):
    length, rows = dense[0].shape[0], spot.shape[1]
    f32, b16 = jnp.float32, jnp.bfloat16
    made = [shape(*WEIGHTS[j][0]) for j in (0, 0, 1, 2, 3)]
    results = [shape(length, D, dtype=f32)]
    specs = any_specs(1)
    if remote:
        shards = [shape(s[0] // inner, s[1] // outer, dtype=f32) for s, _ in WEIGHTS]
        results += shards + shards + [shape(16, 128, dtype=f32)]
        specs += any_specs(9)
        lands = Scatter.shapes(PARTS)
    else:
        results += [shape(16, D, dtype=f32)]
        specs += vmem_specs(1)
        lands = []
    every = dict(Block.scratch(length), x=((length, D), f32))
    short = Block.scratch(rows)
    scratch = buffers(*[every[k] for k in ("x", "x", "projected", "merged", "merged", "lse", "normed")], WEIGHTS[0],
                      ((128, length), f32), ((rows, D), b16), ((rows, 128), f32), *WEIGHTS[1:],
                      ((rows, D), b16), short["active"], short["slope"], ((D, D), b16))
    scratch += [pltpu.SemaphoreType.DMA((k,)) for k in (5 + len(DENSE_IN) + len(kept), 2, 1)]
    if remote:
        scratch += buffers(((16, D), f32), ((16 * inner, 128 * outer), b16)) + Scatter.scratch(PARTS)
    return pl.pallas_call(
        functools.partial(backward_kernel, remote),
        in_specs=vmem_specs(4) + any_specs(5 + len(dense) + len(kept) + len(given)),
        out_specs=specs + any_specs(len(made) + len(lands)),
        out_shape=results + made + lands,
        scratch_shapes=scratch,
        compiler_params=pltpu.CompilerParams(vmem_limit_bytes=VMEM_BYTES, **(dict(collective_id=1, has_side_effects=True) if remote else {})),
        name="backward",
    )(spot, place_map, vec, gmlp, *weights, *dense, *kept, *given)


def pack_vectors(vectors):
    rows = jnp.stack([jnp.pad(v, (0, 128 - v.shape[0])) for v in vectors])
    return jnp.pad(rows, ((0, 16 - rows.shape[0]), (0, 0)))


def spread_vectors(vectors, outer, inner):
    rows = vectors.reshape(vectors.shape[0], outer, inner, -1).transpose(2, 0, 1, 3).astype(jnp.bfloat16)
    tiles = jnp.pad(rows, ((0, 0), (0, 16 - rows.shape[1]), (0, 0), (0, 128 - rows.shape[3])))
    return tiles.reshape(inner * 16, outer * 128)


def deliver_kernel(n, *refs):
    tile, sums, outs, vectors = refs[0], refs[1 : n + 1], refs[n + 1 : 2 * n + 1], refs[2 * n + 1 :]
    for a, b in zip(sums, outs):
        b[...] = a[...]
    for j, v in enumerate(vectors):
        v[...] = tile[j : j + 1, : v.shape[1]]


def deliver(tile, sums, each, count):
    n = len(sums)
    return pl.pallas_call(
        functools.partial(deliver_kernel, n),
        in_specs=vmem_specs(1 + n),
        out_specs=vmem_specs(n + count),
        out_shape=[shape(*s.shape, dtype=s.dtype) for s in sums] + [shape(1, each, dtype=jnp.float32)] * count,
        name="deliver",
    )(tile, *sums)


def fits(shards, outer, inner):
    return outer == 2 and inner == 16 and all(s.shape[0] % 16 == 0 and s.shape[1] % 128 == 0 for s in shards)


def per_device(outer, inner, *args):
    hidden, cotangent, capacity_class, token_index = args[:4]
    (gain_attn_a, qkv_a, out_a, gain_mlp_a, up_a, down_a, router_shard,
     gain_attn_b, qkv_b, out_b, gain_mlp_b, up_b, down_b) = args[4:]
    hidden, cotangent = hidden[0], cotangent[0]
    length = hidden.shape[0]
    tile = pack_vectors((gain_attn_a, gain_mlp_a, router_shard, gain_attn_b, gain_mlp_b))
    shards = [tile, qkv_a, out_a, up_a, down_a, qkv_b, out_b, up_b, down_b]
    remote = fits(shards, outer, inner)
    if not remote:
        shards = [lax.all_gather(lax.all_gather(s, "inner", axis=0, tiled=True), "outer", axis=1, tiled=True) for s in shards]

    capacity = (length // 8) << capacity_class[0]
    slots = lax.broadcasted_iota(jnp.int32, token_index.shape, 1)
    spot = jnp.where(slots < capacity, token_index, -1)
    whole, made, kept, dense = forward(remote, hidden, cotangent, spot, lane_map(outer, inner), shards, outer, inner)
    vec, gmlp, output, plus, grad_merged, *given = made
    input_grad, *res = backward(
        remote, spot, lane_map(outer, inner), vec, gmlp, (whole[5], *whole[1:5]), [*dense, grad_merged, plus], kept, given, outer, inner)
    if remote:
        done, gtile = res[:8], res[8]
    else:
        gvec, gqkv_b, *grads_a = res
        done = [
            lax.psum_scatter(
                lax.psum_scatter(s, "outer", scatter_dimension=1, tiled=True), "inner", scatter_dimension=0, tiled=True
            ).astype(jnp.float32)
            for s in [gqkv_b, *given, *grads_a, spread_vectors(gvec[:5], outer, inner)]
        ]
        done, gtile = done[:8], done[8]
    each = gain_attn_a.shape[0]
    res = deliver(gtile, done, each, 5)
    gb, ga, v = res[:4], res[4:8], [r[0] for r in res[8:]]
    return (output[None], input_grad[None], v[0], ga[0], ga[1], v[1], ga[2], ga[3], v[2], v[3], gb[0], gb[1], v[4], gb[2], gb[3])


def solution(mesh):
    outer, inner = mesh.shape["outer"], mesh.shape["inner"]
    both = ("outer", "inner")
    rows, vector, matrix = P(both, None, None), P(both), P("inner", "outer")
    block = (vector, matrix, matrix, vector, matrix, matrix)
    return jax.shard_map(
        functools.partial(per_device, outer, inner),
        mesh=mesh,
        in_specs=(rows, rows, vector, P(both, None)) + block + (vector,) + block,
        out_specs=(rows, rows) + block + (vector,) + block,
        check_vma=False,
    )
```

```python
import functools

import jax
import jax.numpy as jnp
import numpy as np
from jax import lax
from jax.experimental import pallas as pl
from jax.experimental.pallas import tpu as pltpu
from jax.sharding import PartitionSpec as P

MESH = pl.DeviceIdType.MESH


def place():
    o, i = lax.axis_index("outer"), lax.axis_index("inner")
    return o, i // 4, (i // 2) % 2, i % 2


def device(o, z, x, c):
    return (o, z * 4 + x * 2 + c)


def greet(o, z, x, c):
    barrier = pltpu.get_barrier_semaphore()
    signal = functools.partial(pl.semaphore_signal, barrier, inc=1, device_id_type=MESH)
    signal(device_id=device(1 - o, z, x, c))
    signal(device_id=device(o, z, 1 - x, c))
    signal(device_id=device(o, z, x, 1 - c))

    @pl.when(z > 0)
    def _():
        signal(device_id=device(o, z - 1, x, c))

    @pl.when(z < 3)
    def _():
        signal(device_id=device(o, z + 1, x, c))

    pl.semaphore_wait(barrier, 3 + jnp.where(z > 0, 1, 0) + jnp.where(z < 3, 1, 0))


GATHER_PARTS = (
        (0, 0, 16, 0, 128, True, False), (1, 0, 48, 384, 384, True, False), (1, 0, 48, 768, 384, False, False), (1, 0,
    48, 0, 384, True, False), (2, 0, 48, 0, 384, True, False), (3, 0, 48, 768, 768, True, False), (5, 0, 48, 768, 384,
    True, True), (4, 96, 96, 0, 384, False, True), (3, 0, 48, 0, 768, False, False), (4, 0, 96, 0, 384, False, False),
    (6, 0, 48, 0, 384, True, True), (5, 0, 48, 384, 384, False, False), (5, 0, 48, 0, 384, True, False), (7, 0, 48, 0,
    768, False, False), (7, 0, 48, 768, 768, True, False), (8, 0, 96, 0, 384, True, False), (8, 96, 96, 0, 384, False,
    True))
GATHER_PLAN = (
        (0, 0, 0), (0, 0, 1), (0, 0, 2), (0, 0, 3), (0, 0, 4), (0, 1, 0), (0, 1, 1), (0, 1, 2), (0, 1, 3), (0, 1, 4),
    (0, 2, 0), (0, 2, 1), (0, 2, 2), (0, 2, 3), (0, 2, 4), (0, 3, 0), (0, 0, 5), (0, 3, 1), (0, 0, 6), (0, 3, 2), (0, 0,
    7), (0, 4, 0), (0, 3, 3), (0, 0, 8), (0, 3, 4), (0, 0, 9), (0, 1, 5), (0, 4, 1), (0, 1, 6), (0, 1, 8), (0, 1, 9),
    (0, 4, 2), (0, 2, 5), (0, 1, 7), (0, 2, 8), (0, 5, 0), (0, 2, 9), (0, 6, 0), (0, 4, 3), (0, 3, 5), (0, 0, 10), (0,
    3, 8), (0, 0, 11), (1, 4, 4), (1, 3, 9), (1, 1, 11), (1, 0, 12), (1, 5, 2), (1, 5, 1), (1, 2, 6), (1, 2, 7), (1, 2,
    11), (1, 6, 2), (1, 1, 12), (1, 6, 1), (1, 5, 3), (1, 3, 6), (1, 0, 13), (1, 6, 3), (1, 4, 5), (1, 1, 10), (5, 3,
    7), (5, 3, 11), (5, 0, 14), (5, 0, 15), (6, 2, 12), (8, 4, 6), (8, 4, 8), (9, 1, 13), (10, 5, 4), (10, 6, 4), (10,
    4, 7), (10, 1, 14), (11, 4, 9), (11, 1, 15), (11, 3, 12), (11, 0, 16), (11, 5, 8), (11, 5, 6), (11, 5, 5), (11, 2,
    13), (11, 6, 8), (11, 6, 6), (11, 2, 10), (11, 6, 5), (11, 5, 9), (11, 4, 11), (12, 5, 7), (12, 6, 9), (12, 4, 12),
    (13, 2, 14), (13, 1, 16), (14, 6, 7), (14, 2, 15), (14, 3, 13), (15, 5, 11), (15, 5, 12), (15, 2, 16), (16, 3, 10),
    (16, 6, 11), (16, 6, 12), (16, 3, 14), (17, 4, 13), (17, 3, 15), (21, 3, 16), (22, 4, 10), (22, 4, 14), (24, 5, 13),
    (24, 4, 16), (25, 5, 10), (25, 6, 13), (25, 5, 14), (26, 6, 10), (26, 6, 14), (26, 4, 15), (27, 5, 16), (28, 6, 16),
    (29, 5, 15), (30, 6, 15))


class Gather:
    @staticmethod
    def semaphores(n):
        return [pltpu.SemaphoreType.DMA(k) for k in ((n,), (n, 23), (n, 19))]

    def __init__(self, parts, shards, outs, local_sem, send_sem, recv_sem):
        o, z, x, c = place()
        n = len(parts)

        def shard(p):
            a, r0, r, c0, w, _, _ = parts[p]
            return shards[a].at[pl.ds(r0, r), pl.ds(c0, w)]

        def blocks(p, oo):
            a, r0, r, c0, w, _, _ = parts[p]
            rows, each = shards[a].shape
            view = outs[a].reshape(4, 2, 2, rows, 2 * each)
            return view, pl.ds(r0, r), pl.ds(pl.multiple_of(oo * each + c0, 128), w)

        def chunk(p, k):
            view, rows, columns = blocks(p, o)
            return view.at[k, x, c, rows, columns]

        def group(p, second, first):
            first_x = parts[p][5]
            px, po = (first, second) if first_x else (second, first)
            view, rows, columns = blocks(p, o if po else 1 - o)
            return view.at[:, x if px else 1 - x, c, rows, columns]

        def send(p, src, dst, slot, target):
            return pltpu.make_async_remote_copy(
                src_ref=src, dst_ref=dst, send_sem=send_sem.at[p, slot[0]], recv_sem=recv_sem.at[p, slot[1]],
                device_id=target, device_id_type=MESH)

        def wait(ref, sem):
            pltpu.make_async_copy(ref, ref, sem).wait()

        def up(p, k, hop, src=None):
            b = chunk(p, k)
            return send(p, b if src is None else src, b, (hop, k), device(o, z + 1, x, c))

        def down(p, k, hop, src=None):
            b = chunk(p, k)
            return send(p, b if src is None else src, b, (3 + hop, k), device(o, z - 1, x, c))

        def near(p, second):
            return device(o, z, 1 - x, c) if parts[p][5] != second else device(1 - o, z, x, c)

        def to_core(p, second, first):
            b = group(p, second, first)
            send(p, b, b, (9 + 2 * second + first, 7 + 2 * second + first), device(o, z, x, 1 - c)).start()

        def to_second(p, first):
            b = group(p, 1, first)
            send(p, b, b, (7 + first, 5 + first), near(p, True)).start()

        def local(p):
            return pltpu.make_async_copy(shard(p), chunk(p, z), local_sem.at[p])

        def own(p):
            @pl.when(z < 3)
            def _():
                up(p, z, 0, shard(p)).start()

            @pl.when(z > 0)
            def _():
                down(p, z, 0, shard(p)).start()

            local(p).start()

        def hop(d):
            def go(p):
                @pl.when(z >= d)
                def _():
                    wait(chunk(p, z - d), recv_sem.at[p, z - d])
                    if d < 3:
                        @pl.when(z < 3)
                        def _():
                            up(p, z - d, d).start()

                @pl.when(z + d <= 3)
                def _():
                    wait(chunk(p, z + d), recv_sem.at[p, z + d])
                    if d < 3:
                        @pl.when(z > 0)
                        def _():
                            down(p, z + d, d).start()
            return go

        third = hop(3)

        def first(p):
            third(p)
            local(p).wait()
            b = group(p, 1, 1)
            send(p, b, b, (6, 4), near(p, False)).start()
            to_second(p, 1)
            to_core(p, 1, 1)

        def second(p):
            wait(group(p, 1, 0), recv_sem.at[p, 4])
            to_second(p, 0)
            to_core(p, 1, 0)

        def cores(p):
            for f in (1, 0):
                wait(group(p, 0, f), recv_sem.at[p, 5 + f])
                to_core(p, 0, f)

        def arrived(p):
            for slot in range(4):
                wait(group(p, 1, 1), recv_sem.at[p, 7 + slot])

        def plane(p, second, first):
            first_x = parts[p][5]
            px, po = (first, second) if first_x else (second, first)
            view, rows, columns = blocks(p, o if po else 1 - o)
            return view.at[z, x if px else 1 - x, c, rows, columns]

        def layer(p, k, oo):
            view, rows, columns = blocks(p, oo)
            return view.at[k, :, c, rows, columns]

        def late_own(p):
            s, b = shard(p), plane(p, 1, 1)
            send(p, s, b, (12, 8), near(p, False)).start()
            send(p, s, b, (13, 9), near(p, True)).start()
            local(p).start()

        def late_first(p):
            b = plane(p, 1, 0)
            wait(b, recv_sem.at[p, 8])
            send(p, b, b, (14, 10), near(p, True)).start()

        def spread(p, k, hop, rise, fall):
            for oo in (0, 1):
                b = layer(p, k, oo)
                if rise:
                    @pl.when(z < 3)
                    def _():
                        send(p, b, b, (2 * hop + oo, 2 * k + oo), device(o, z + 1, x, c)).start()
                if fall:
                    @pl.when(z > 0)
                    def _():
                        send(p, b, b, (6 + 2 * hop + oo, 2 * k + oo), device(o, z - 1, x, c)).start()
                send(p, b, b, (15 + 2 * k + oo, 11 + 2 * k + oo), device(o, z, x, 1 - c)).start()

        def late_second(p):
            wait(plane(p, 0, 1), recv_sem.at[p, 9])
            wait(plane(p, 0, 0), recv_sem.at[p, 10])
            local(p).wait()
            spread(p, z, 0, True, True)

        def late_hop(d):
            def go(p):
                for k, there, rise in ((z - d, z >= d, True), (z + d, z + d <= 3, False)):
                    @pl.when(there)
                    def _():
                        for oo in (0, 1):
                            wait(layer(p, k, oo), recv_sem.at[p, 2 * k + oo])
                        spread(p, k, d, rise and d < 3, not rise and d < 3)
            return go

        def late_arrived(p):
            for slot in range(8):
                wait(layer(p, 0, 0), recv_sem.at[p, 11 + slot])

        def late_finish(p):
            for oo in (0, 1):
                for d in range(3):
                    @pl.when(jnp.logical_and(z < 3, z >= d))
                    def _():
                        wait(layer(p, 0, 0), send_sem.at[p, 2 * d + oo])

                    @pl.when(jnp.logical_and(z > 0, z + d <= 3))
                    def _():
                        wait(layer(p, 0, 0), send_sem.at[p, 6 + 2 * d + oo])
            for slot in (12, 13, 14):
                wait(plane(p, 1, 1), send_sem.at[p, slot])
            for slot in range(15, 23):
                wait(layer(p, 0, 0), send_sem.at[p, slot])

        def early_finish(p):
            for d in range(3):
                @pl.when(jnp.logical_and(z < 3, z >= d))
                def _():
                    wait(chunk(p, z), send_sem.at[p, d])

                @pl.when(jnp.logical_and(z > 0, z + d <= 3))
                def _():
                    wait(chunk(p, z), send_sem.at[p, 3 + d])
            for slot in range(6, 13):
                wait(group(p, 1, 1), send_sem.at[p, slot])

        early = (own, hop(1), hop(2), first, second, cores, arrived)
        late = (late_own, late_first, late_second, late_hop(1), late_hop(2), late_hop(3), late_arrived)

        def finish():
            for p in range(n):
                (late_finish if parts[p][6] else early_finish)(p)

        self.finish = finish
        self.take = lambda step, p: (late if parts[p][6] else early)[step](p)

    def begin(self):
        greet(*place())


PARTS = (
        (3, 96, 96, 0, 384, False, 2, False), (2, 0, 48, 0, 768, True, 1, False), (2, 0, 48, 768, 768, True, 3, True),
    (3, 0, 96, 0, 384, True, 0, False), (1, 0, 48, 0, 384, True, 4, False), (0, 0, 48, 640, 512, False, 6, False), (7,
    96, 96, 0, 384, False, 2, False), (0, 0, 48, 0, 640, True, 5, False), (6, 0, 48, 768, 768, True, 3, True), (6, 0,
    48, 0, 768, True, 1, False), (4, 0, 48, 640, 512, False, 6, False), (4, 0, 48, 0, 640, True, 5, False), (5, 0, 48,
    0, 384, False, 4, False), (7, 0, 96, 0, 384, True, 0, False), (8, 0, 16, 0, 128, True, 7, False))
BACK_PLAN = (
        (0, 0, 3), (0, 0, 2), (0, 0, 0), (0, 0, 1), (0, 0, 4), (1, 1, 3), (2, 2, 3), (2, 1, 2), (2, 1, 0), (3, 2, 2),
    (3, 2, 0), (3, 1, 1), (4, 2, 1), (4, 1, 4), (5, 3, 3), (5, 2, 4), (6, 4, 3), (6, 3, 2), (6, 3, 0), (7, 4, 0), (10,
    5, 3), (10, 0, 7), (10, 0, 5), (10, 4, 2), (10, 6, 3), (10, 3, 1), (11, 4, 1), (11, 1, 7), (12, 7, 3), (12, 2, 7),
    (12, 1, 5), (12, 5, 0), (13, 8, 3), (13, 2, 5), (13, 5, 2), (13, 6, 0), (13, 5, 1), (13, 3, 4), (14, 9, 3), (14, 6,
    1), (14, 4, 4), (15, 3, 7), (15, 7, 0), (16, 0, 13), (16, 4, 7), (16, 3, 5), (16, 6, 2), (16, 8, 0), (16, 7, 1),
    (16, 5, 4), (17, 4, 5), (17, 6, 4), (18, 1, 13), (18, 9, 0), (18, 0, 6), (18, 8, 1), (19, 2, 13), (19, 5, 7), (19,
    7, 4), (20, 1, 6), (20, 6, 7), (20, 5, 5), (20, 7, 2), (20, 0, 8), (20, 9, 1), (20, 0, 9), (20, 8, 4), (20, 6, 5),
    (20, 2, 6), (21, 9, 4), (22, 1, 8), (22, 7, 7), (23, 2, 8), (23, 1, 9), (23, 7, 5), (24, 8, 7), (24, 0, 12), (24, 2,
    9), (26, 3, 13), (26, 8, 5), (27, 4, 13), (27, 9, 7), (27, 9, 5), (27, 0, 10), (27, 0, 11), (27, 3, 6), (29, 1, 10),
    (29, 4, 6), (29, 0, 14), (29, 2, 10), (29, 3, 8), (29, 5, 13), (29, 1, 11), (29, 6, 13), (29, 2, 11), (29, 3, 9),
    (29, 4, 9), (29, 1, 12), (29, 5, 6), (29, 2, 12), (29, 3, 10), (29, 6, 6), (29, 7, 13), (29, 4, 10), (29, 4, 8),
    (29, 7, 6), (29, 5, 9), (29, 6, 9), (29, 1, 14), (29, 8, 13), (29, 2, 14), (29, 3, 11), (29, 4, 11), (29, 5, 8),
    (29, 9, 13), (29, 7, 9), (29, 8, 6), (29, 3, 12), (29, 4, 12), (29, 5, 10), (29, 3, 14), (29, 6, 10), (29, 4, 14),
    (29, 9, 6), (29, 8, 9), (29, 5, 11), (29, 6, 8), (29, 7, 10), (29, 6, 11), (29, 5, 14), (29, 9, 9), (29, 6, 14),
    (29, 5, 12), (29, 7, 8), (29, 8, 10), (29, 6, 12), (29, 7, 11), (29, 9, 10), (29, 7, 14), (29, 7, 12), (29, 8, 11),
    (29, 8, 14), (29, 8, 12), (29, 9, 11), (29, 9, 14), (29, 9, 12))


class Scatter:
    def __init__(self, parts, grads, outs, core_in, second_in, first_in, buffers, sems):
        o, z, x, c = place()
        acc, z_in, stage_own, stage_got, stage_second, stage_first, stage_out = buffers
        send_sem, recv_sem, own_sem, stage_sem, out_sem = sems
        n = len(parts)

        def kind(p):
            return 1 if parts[p][2] == 96 else 0

        def of(p):
            return parts[p][2], parts[p][4]

        def part(ref, p):
            r, w = of(p)
            return ref.at[:, pl.ds(0, r), pl.ds(0, w)]

        def group(p, second, first, core):
            g, r0, r, c0, w, first_x, _, _ = parts[p]
            px, po = (first, second) if first_x else (second, first)
            xx = x if px else 1 - x
            oo = o if po else 1 - o
            height, width = grads[g].shape
            each = width // 2
            return grads[g].reshape(4, 2, 2, height // 16, width).at[:, xx, core, pl.ds(r0, r), pl.ds(pl.multiple_of(oo * each + c0, 128), w)]

        def far(p, second):
            return device(o, z, 1 - x, c) if parts[p][5] != second else device(1 - o, z, x, c)

        def send(p, src, dst, kind_, slot, target):
            return pltpu.make_async_remote_copy(
                src_ref=src, dst_ref=dst, send_sem=send_sem.at[p, kind_], recv_sem=recv_sem.at[p, slot],
                device_id=target, device_id_type=MESH)

        def wait(ref, sem):
            pltpu.make_async_copy(ref, ref, sem).wait()

        slots, last_user = {}, {}
        turn = [0, 0]
        for p in range(n):
            k = kind(p)
            if parts[p][7]:
                slots[p], last_user[p] = None, None
                continue
            slots[p] = turn[k] % 2
            last_user[p] = next((q for q in range(p - 1, -1, -1) if kind(q) == k and slots[q] == slots[p]), None)
            turn[k] += 1

        def own_of(p):
            return part(stage_own[kind(p)].at[slots[p]], p)

        def total(p):
            return acc[parts[p][6]]

        def begin(p):
            for second in (0, 1):
                for first in (0, 1):
                    send(p, group(p, second, first, 1 - c), core_in[p].at[pl.ds(second * 8 + first * 4, 4)], 0, 0,
                         device(o, z, x, 1 - c)).start()
            for second in (0, 1) if parts[p][7] else (1,):
                for first in (0, 1):
                    at = second * 8 + first * 4 if parts[p][7] else first * 4
                    pltpu.make_async_copy(group(p, second, first, c), total(p).at[pl.ds(at, 4)], own_sem.at[p]).start()

        def core_fetch(p):
            k = kind(p)
            if last_user[p] is not None:
                q = last_user[p]
                wait(own_of(q), send_sem.at[q, 1])
            for first in () if parts[p][7] else (0, 1):
                pltpu.make_async_copy(group(p, 0, first, c), own_of(p).at[pl.ds(first * 4, 4)], stage_sem.at[kind(p), 0]).start()
            wait(core_in[p], recv_sem.at[p, 0])
            pltpu.make_async_copy(core_in[p].at[pl.ds(0, 8)], part(stage_got[k], p), stage_sem.at[kind(p), 1]).start()
            pltpu.make_async_copy(core_in[p].at[pl.ds(8, 8)], part(stage_second[k], p), stage_sem.at[kind(p), 2]).start()

        def core_add(p):
            own, got = own_of(p), part(stage_got[kind(p)], p)
            wait(own, stage_sem.at[kind(p), 0])
            wait(got, stage_sem.at[kind(p), 1])
            for first in (0, 1):
                s = pl.ds(first * 4, 4)
                own[s] = own[s] + got[s]
                send(p, own.at[s], second_in[p].at[s], 1, 1 + first, far(p, True)).start()
            mine = part(stage_second[kind(p)], p)
            wait(total(p), own_sem.at[p])
            wait(mine, stage_sem.at[kind(p), 2])
            total(p)[...] = total(p)[...] + mine[...]

        def second_fetch(p):
            got = part(stage_second[kind(p)], p)
            for first in (0, 1):
                s = pl.ds(first * 4, 4)
                wait(second_in[p].at[s], recv_sem.at[p, 1 + first])
            pltpu.make_async_copy(second_in[p], got, stage_sem.at[kind(p), 2]).start()

        def second_add(p):
            got = part(stage_second[kind(p)], p)
            wait(got, stage_sem.at[kind(p), 2])
            t = total(p)
            t[0:4] = t[0:4] + got[0:4]
            send(p, t.at[pl.ds(0, 4)], first_in[p], 2, 3, far(p, False)).start()
            t[4:8] = t[4:8] + got[4:8]

        def send_z(p, k, step):
            to = z + step
            slot = jnp.where(k == to, jnp.where(step > 0, k, 4), k)
            send(p, total(p).at[4 + k], z_in[p].at[slot], 3, 4 + slot, device(o, to, x, c)).start()

        def first_fetch(p):
            wait(first_in[p], recv_sem.at[p, 3])
            pltpu.make_async_copy(first_in[p], part(stage_first[kind(p)], p), stage_sem.at[kind(p), 3]).start()

        def first_add(p):
            got = part(stage_first[kind(p)], p)
            wait(got, stage_sem.at[kind(p), 3])
            t = total(p)
            t[4:8] = t[4:8] + got[...]

            @pl.when(z == 0)
            def _():
                for k in (3, 2, 1):
                    send_z(p, k, 1)

            @pl.when(z == 3)
            def _():
                for k in (0, 1, 2):
                    send_z(p, k, -1)

        def pass_on(p, k, step):
            wait(z_in[p].at[k], recv_sem.at[p, 4 + k])
            total(p)[4 + k] = total(p)[4 + k] + z_in[p][k]
            send_z(p, k, step)

        def along(level):
            def go(p):
                @pl.when(z == level)
                def _():
                    for k in range(3, level, -1):
                        pass_on(p, k, 1)

                @pl.when(z == 3 - level)
                def _():
                    for k in range(0, 3 - level):
                        pass_on(p, k, -1)
            return go

        out_user = [None, None]

        def copy_out(p):
            g, r0, r, c0, w, _, _, _ = parts[p]
            return pltpu.make_async_copy(stage_out[kind(p)].at[pl.ds(0, r), pl.ds(0, w)],
                                         outs[g].at[pl.ds(r0, r), pl.ds(c0, w)], out_sem.at[kind(p)])

        def finish():
            for p in out_user:
                copy_out(p).wait()

        def last(p):
            g, r0, r, c0, w, _, _, _ = parts[p]
            out = stage_out[kind(p)].at[pl.ds(0, r), pl.ds(0, w)]
            if out_user[kind(p)] is not None:
                copy_out(out_user[kind(p)]).wait()
            out_user[kind(p)] = p
            out[...] = total(p)[4 + z].astype(jnp.float32)

            @pl.when(z > 0)
            def _():
                wait(z_in[p].at[z], recv_sem.at[p, 4 + z])
                out[...] += z_in[p][z].astype(jnp.float32)

            @pl.when(z < 3)
            def _():
                wait(z_in[p].at[4], recv_sem.at[p, 8])
                out[...] += z_in[p][4].astype(jnp.float32)

            copy_out(p).start()
            wait(core_in[p], send_sem.at[p, 0])
            if all(last_user[q] != p for q in range(n)):
                wait(own_of(p), send_sem.at[p, 1])
            wait(first_in[p], send_sem.at[p, 2])
            wait(first_in[p].at[pl.ds(0, 3)], send_sem.at[p, 3])

        def planes(p):
            r, w = of(p)
            return total(p).reshape(4, 4, r, w)

        def send_plane(p, k, step):
            to = z + step
            slot = jnp.where(k == to, jnp.where(step > 0, k, 4), k)
            send(p, planes(p).at[:, k], second_in[p].at[pl.ds(slot * 4, 4)], 3, 4 + slot, device(o, to, x, c)).start()

        def early_add(p):
            k = kind(p)
            got, more = part(stage_got[k], p), part(stage_second[k], p)
            t = total(p)
            wait(t, own_sem.at[p])
            wait(got, stage_sem.at[k, 1])
            wait(more, stage_sem.at[k, 2])
            t[0:8] = t[0:8] + got[...]
            t[8:16] = t[8:16] + more[...]

            @pl.when(z == 0)
            def _():
                for j in (3, 2, 1):
                    send_plane(p, j, 1)

            @pl.when(z == 3)
            def _():
                for j in (0, 1, 2):
                    send_plane(p, j, -1)

        def take_planes(p, taken):
            stage = part(stage_second[kind(p)], p)
            copies = []
            for j, (slot, _) in enumerate(taken):
                wait(second_in[p].at[pl.ds(0, 4)], recv_sem.at[p, 4 + slot])
                copies.append(pltpu.make_async_copy(second_in[p].at[pl.ds(slot * 4, 4)], stage.at[pl.ds(j * 4, 4)],
                                                    stage_sem.at[kind(p), 2]))
                copies[-1].start()
            wait(stage.at[pl.ds(0, 4 * len(taken))], stage_sem.at[kind(p), 2])
            for j, (_, k) in enumerate(taken):
                v = planes(p).at[:, k]
                v[...] = v[...] + stage[j * 4 : j * 4 + 4]

        def early_along(level):
            def go(p):
                @pl.when(z == level)
                def _():
                    ks = range(3, level, -1)
                    take_planes(p, [(k, k) for k in ks])
                    for k in ks:
                        send_plane(p, k, 1)

                @pl.when(z == 3 - level)
                def _():
                    ks = range(0, 3 - level)
                    take_planes(p, [(k, k) for k in ks])
                    for k in ks:
                        send_plane(p, k, -1)
            return go

        def early_end(p):
            @pl.when(z == 0)
            def _():
                take_planes(p, [(4, 0)])

            @pl.when(z == 3)
            def _():
                take_planes(p, [(3, 3)])

            for k in (1, 2):
                @pl.when(z == k)
                def _():
                    take_planes(p, [(k, k), (4, k)])
            send(p, planes(p).at[pl.ds(0, 2), z], z_in[p].at[pl.ds(0, 2)], 1, 1, far(p, True)).start()

        def early_second(p):
            wait(z_in[p].at[pl.ds(0, 2)], recv_sem.at[p, 1])
            for f in (0, 1):
                v = planes(p).at[2 + f, z]
                v[...] = v[...] + z_in[p][f]
            send(p, planes(p).at[2, z], z_in[p].at[2], 2, 3, far(p, False)).start()

        def early_last(p):
            g, r0, r, c0, w, _, _, _ = parts[p]
            out = stage_out[kind(p)].at[pl.ds(0, r), pl.ds(0, w)]
            if out_user[kind(p)] is not None:
                copy_out(out_user[kind(p)]).wait()
            out_user[kind(p)] = p
            wait(z_in[p].at[2], recv_sem.at[p, 3])
            out[...] = planes(p)[3, z].astype(jnp.float32) + z_in[p][2].astype(jnp.float32)
            copy_out(p).start()
            wait(core_in[p], send_sem.at[p, 0])
            wait(total(p).at[pl.ds(0, 12)], send_sem.at[p, 3])
            wait(z_in[p].at[pl.ds(0, 2)], send_sem.at[p, 1])
            wait(z_in[p].at[2], send_sem.at[p, 2])

        self.finish = finish
        late = (begin, core_fetch, core_add, second_fetch, second_add, first_fetch, first_add, along(1), along(2), last)
        early = (begin, core_fetch, early_add, early_along(1), early_along(2), early_end, early_second, early_last)
        self.take = lambda step, p: (early if parts[p][7] else late)[step](p)

    @staticmethod
    def shapes(parts):
        return [shape(20 if m == 8 and s[7] else m, s[2], s[4]) for m in (16, 8, 4) for s in parts]

    @staticmethod
    def scratch(parts):
        b16 = jnp.bfloat16
        sizes = {s[6]: (16 if s[7] else 8, s[2], s[4]) for s in parts}
        acc = [(sizes[k], b16) for k in sorted(sizes)]
        lands = [((3 if s[7] else 5, s[2], s[4]), b16) for s in parts]
        stages = [((m, 48, 768), b16) if k == 0 else ((m, 96, 384), b16) for m in (8, 8, 4) for k in (0, 1)]
        stages = [((2, 8, 48, 768), b16), ((2, 8, 96, 384), b16)] + stages
        stages += [((48, 768), jnp.float32), ((96, 384), jnp.float32)]
        n = len(parts)
        return buffers(*acc, *lands, *stages) + [pltpu.SemaphoreType.DMA(k) for k in ((n, 4), (n, 9), (n,), (2, 4), (2,))]

    @staticmethod
    def unpack(parts, refs):
        n, m = len(parts), len({s[6] for s in parts})
        acc, refs = refs[:m], refs[m:]
        z_in, refs = refs[:n], refs[n:]
        return (acc, z_in, refs[0:2], refs[2:4], refs[4:6], refs[6:8], refs[8:10]), refs[10:15]


D = 768
SCALE = 0.125 * 1.4426950408889634
ROWS = 256
VMEM_BYTES = 127 * 2**19


def mul(a, b, ca=1, cb=0):
    return lax.dot_general(a, b, (((ca,), (cb,)), ((), ())), preferred_element_type=jnp.float32)


def low(v):
    return v.astype(jnp.bfloat16)


def cols(j):
    return pl.ds(pl.multiple_of(j * D, D), D)


def rms_scale(v):
    return lax.rsqrt(jnp.mean(v * v, axis=-1, keepdims=True) + 1e-06)


def rms_back(v, gain, grad):
    r = rms_scale(v)
    unit = v * r
    scaled = grad * gain
    back = r * (scaled - unit * jnp.mean(scaled * unit, axis=-1, keepdims=True))
    return back, jnp.sum((grad * unit).reshape(-1, 8, v.shape[-1]), axis=0)


def gelu_and_slope(u):
    k = 0.7978845608028654
    inner = u * (k + k * 0.044715 * (u * u))
    half = 0.5 + 0.5 * jnp.tanh(inner)
    return u * half, half * (1.0 + (1.0 - half) * (6.0 * inner - 4.0 * k * u))


def halves(v):
    lane = lax.broadcasted_iota(jnp.int32, v.shape, 1)
    zero = jnp.zeros_like(v)
    return jnp.where(lane < 64, v, zero), jnp.where(lane < 64, zero, v)


def two(v):
    first = low(v)
    return first, low(v - first.astype(jnp.float32))


def staggered(tiles, product, finish):
    held = product(tiles[0])
    for t, later in zip(tiles, tiles[1:] + [None]):
        coming = product(later) if later is not None else None
        finish(t, held)
        held = coming


class Block:
    def __init__(self, rows, refs):
        self.rows = rows
        self.__dict__.update(refs)

    @staticmethod
    def scratch(rows):
        f32, b16 = jnp.float32, jnp.bfloat16
        return dict(
            branch=((rows, D), f32), projected=((rows, 3 * D), b16), merged=((rows, D), b16), lse=((6, 8, rows), f32),
            active=((rows, 4 * D), b16), slope=((rows, 4 * D), b16), normed=((rows, D), b16), normed_mlp=((rows, D), b16))

    def rows_of(self, t):
        return self.x[t].astype(jnp.float32)

    def tiles(self):
        return [slice(i, i + ROWS) for i in range(0, self.rows, ROWS)]

    def norm(self):
        for t in self.tiles():
            x = self.rows_of(t)
            self.normed[t] = low(x * rms_scale(x) * self.gain_attn[...])

    def project(self, j):
        c = cols(j)
        self.projected[:, c] = low(mul(self.normed[...], self.qkv[:, c]))

    def pair(self, ref, part, pair, rows=slice(None)):
        return ref[rows, pl.ds(pl.multiple_of(part * D + pair * 128, 128), 128)]

    def attend(self, pair):
        v0, v1 = halves(self.pair(self.projected, 2, pair))
        causal = lax.broadcasted_iota(jnp.int32, (ROWS, ROWS), 1) >= lax.broadcasted_iota(jnp.int32, (ROWS, ROWS), 0)
        for t in self.tiles():
            n = t.stop
            qs = halves(self.pair(self.projected, 0, pair, t))
            k = self.pair(self.projected, 1, pair, slice(0, n))
            total = None
            scores = [mul(k, qs[h], 1, 1) for h in range(2)]
            for h in range(2):
                s = scores[h]
                last = jnp.where(causal, s[t.start:], -1e30)
                s = last if t.start == 0 else jnp.concatenate([s[: t.start], last], axis=0)
                m = jnp.max(s, axis=0, keepdims=True) * SCALE
                p = jnp.exp2(s * SCALE - m)
                l = jnp.sum(p, axis=0, keepdims=True)
                self.lse[pair, h : h + 1, t] = m + jnp.log2(l)
                o = mul(low(p * (1.0 / l)), (v0, v1)[h][:n], 0, 0)
                total = o if total is None else total + o
            self.merged[t, pl.ds(pl.multiple_of(pair * 128, 128), 128)] = low(total)

    def join(self):
        for t in self.tiles():
            branch = mul(self.merged[t], self.out[...])
            self.branch[t] = branch
            middle = self.rows_of(t) + branch
            self.normed_mlp[t] = low(middle * rms_scale(middle) * self.gain_mlp[...])

    def widen(self, j):
        c = cols(j)

        def finish(t, pre):
            active, slope = gelu_and_slope(pre)
            self.active[t, c] = low(active)
            self.slope[t, c] = low(slope)

        staggered(self.tiles(), lambda t: mul(self.normed_mlp[t], self.up[:, c]), finish)

    def narrow(self, t):
        return mul(self.active[t], self.down[...])

    def back_wide(self, j):
        c = cols(j)

        def finish(t, grad):
            self.slope[t, c] = low(grad * self.slope[t, c].astype(jnp.float32))

        staggered(self.tiles(), lambda t: mul(self.grad_low[t], self.down[c, :], 1, 1), finish)

    def grad_down(self, j):
        return low(mul(self.active[:, cols(j)], self.grad_low[...], 0, 0))

    def grad_up(self, j):
        return low(mul(self.normed_mlp[...], self.slope[:, cols(j)], 0, 0))

    def back_mlp(self, grad_of):
        total = jnp.zeros((8, D), jnp.float32)
        for t in self.tiles():
            grad = mul(self.slope[t], self.up[...], 1, 1)
            back, gain = rms_back(self.rows_of(t) + self.branch[t], self.gain_mlp[...], grad)
            total = total + gain
            self.branch[t] = back
            self.normed_mlp[t] = low(grad_of(t) + back)
        return jnp.sum(total, axis=0, keepdims=True)

    def grad_out(self):
        return low(mul(self.merged[...], self.normed_mlp[...], 0, 0))

    def back_merged(self):
        self.active[:, :D] = low(mul(self.normed_mlp[...], self.out[...], 1, 1))

    def attend_back(self, pair, turned):
        rows = self.rows
        q, do = self.pair(self.projected, 0, pair), self.pair(self.active, 0, pair)
        qs, dos = halves(q), halves(do)
        dd = do.astype(jnp.float32) * self.pair(self.merged, 0, pair).astype(jnp.float32)
        pick = lax.broadcasted_iota(jnp.int32, (8, 128), 0) == lax.broadcasted_iota(jnp.int32, (8, 128), 1) // 64
        delta = lax.dot_general(pick.astype(jnp.float32), dd, (((1,), (1,)), ((), ())), precision=lax.Precision.HIGHEST,
                                preferred_element_type=jnp.float32)
        causal = lax.broadcasted_iota(jnp.int32, (ROWS, ROWS), 1) >= lax.broadcasted_iota(jnp.int32, (ROWS, ROWS), 0)
        for t in self.tiles():
            a = t.start
            ks, vs = halves(self.pair(self.projected, 1, pair, t)), halves(self.pair(self.projected, 2, pair, t))
            dk = dv = dq = 0.0
            scores = [mul(ks[h], q[a:], 1, 1) for h in range(2)]
            dps = [mul(vs[h], do[a:], 1, 1) for h in range(2)]
            for h in range(2):
                s, dp = scores[h], dps[h]
                p = jnp.exp2(s * SCALE - self.lse[pair, h : h + 1, a:])
                first = jnp.where(causal, p[:, :ROWS], 0.0)
                p = first if t.stop == rows else jnp.concatenate([first, p[:, ROWS:]], axis=1)
                ds = low(p * (dp - delta[h : h + 1, a:]))
                dv = dv + mul(low(p), dos[h][a:])
                dk = dk + mul(ds, qs[h][a:])
                dq = dq + mul(ks[h], ds, 0, 0)
            lanes = pl.multiple_of(pair * 128, 128)
            self.projected[t, pl.ds(D + lanes, 128)] = low(0.125 * dk)
            self.projected[t, pl.ds(2 * D + lanes, 128)] = low(dv)
            if a == 0:
                turned[:, :rows] = dq
            else:
                turned[:, a:rows] += dq
        self.projected[:, pl.ds(lanes, 128)] = low(0.125 * turned[:, :rows].T)

    def grad_qkv(self, j):
        return low(mul(self.normed[...], self.projected[:, cols(j)], 0, 0))

    def back_norm(self, finish):
        total = jnp.zeros((8, D), jnp.float32)
        for t in self.tiles():
            grad = mul(self.projected[t], self.qkv[...], 1, 1)
            back, gain = rms_back(self.rows_of(t), self.gain_attn[...], grad)
            total = total + gain
            finish(t, back + self.branch[t])
        return jnp.sum(total, axis=0, keepdims=True)


SAVED = ("branch", "projected", "merged", "lse", "active", "slope", "normed", "normed_mlp")


def run(steps, hooks=None):
    at = 0
    waits = []
    for count, body in steps:
        if count == 0:
            waits.append(body)
            continue
        before = [list(hooks[at + k]) if hooks else [] for k in range(count)]
        at += count
        for f in before[0]:
            f()
        for f in waits:
            f(0)
        waits = []
        if count == 1:
            body(0)
            continue

        @pl.loop(0, count)
        def _(j):
            for k in range(1, count):
                if before[k]:
                    @pl.when(j == k)
                    def _():
                        for f in before[k]:
                            f()
            body(j)


class Loads:
    def __init__(self, pairs, sems):
        self.copies = {k: pltpu.make_async_copy(a, b, sems.at[j]) for j, (k, a, b) in enumerate(pairs)}
        for c in self.copies.values():
            c.start()

    def need(self, *names):
        for n in names:
            self.copies[n].wait()


class Ship:
    def __init__(self, stages, sems):
        self.stages, self.sems, self.single = stages, sems, len(stages) == 1

    def wait(self, slot):
        slot = min(slot, len(self.stages) - 1)
        pltpu.make_async_copy(self.stages[slot], self.stages[slot], self.sems.at[slot]).wait()

    def send(self, slot, value, target, busy):
        slot = min(slot, len(self.stages) - 1)
        if busy is True:
            self.wait(slot)
        elif busy is not False:
            pl.when(busy)(lambda: self.wait(slot))
        self.stages[slot][...] = value()
        pltpu.make_async_copy(self.stages[slot], target, self.sems.at[slot]).start()


def wide_steps(b, grad_of, ship, targets, vec):
    gout, gup, gdown = targets

    def wide(j):
        b.back_wide(j)
        ship.send(0, lambda: b.grad_down(j), gdown.at[cols(j), :], j > 0)
        ship.send(1, lambda: b.grad_up(j), gup.at[:, cols(j)], ship.single or j > 0)

    def mlp(_):
        ship.wait(0)
        if not ship.single:
            ship.wait(1)
        vec(b.back_mlp(grad_of))

    def out(_):
        ship.send(1, b.grad_out, gout, False)
        b.back_merged()

    return [(4, wide), (1, mlp), (1, out)]


def attend_steps(b, ship, gqkv, vec, finish, turned, busy):
    def qkv(j):
        ship.send(1, lambda: b.grad_qkv(j), gqkv.at[:, cols(j)], True if busy else j > 0)

    def norm(_):
        vec(b.back_norm(finish))
        ship.wait(1)

    return [(6, lambda j: b.attend_back(j, turned)), (3, qkv), (1, norm)]


def shape(*dims, dtype=jnp.bfloat16):
    return jax.ShapeDtypeStruct(dims, dtype)


def any_specs(n):
    return [pl.BlockSpec(memory_space=pl.ANY)] * n


def vmem_specs(n):
    return [pl.BlockSpec(memory_space=pltpu.VMEM)] * n


WEIGHTS = [((D, 3 * D), jnp.bfloat16), ((D, D), jnp.bfloat16), ((D, 4 * D), jnp.bfloat16), ((4 * D, D), jnp.bfloat16)]


def buffers(*pairs):
    return [pltpu.VMEM(dims, dtype) for dims, dtype in pairs]


def kept_buffers(rows):
    s = Block.scratch(rows)
    return [s[k] for k in SAVED]


def spots(start, count, spot):
    at = lax.broadcasted_iota(jnp.int32, (count, spot.shape[1]), 0) + start
    return low(jnp.where(at == spot, 1.0, 0.0))


def spots_of(index_ref, class_ref, length):
    slot = lax.broadcasted_iota(jnp.int32, index_ref.shape, 1)
    return jnp.where(slot < lax.shift_left(length // 8, class_ref[...]), index_ref[...], -1)


def lane_map(outer, inner):
    each = D // (outer * inner)
    d = np.arange(D, dtype=np.int32)
    return np.stack([d // each % inner, d // (each * inner) * 128 + d % each])


def spread_map(tiles_columns, map_ref):
    at = lax.broadcasted_iota(jnp.int32, (tiles_columns, D), 0)
    return low(jnp.where(at == map_ref[1:2], 1.0, 0.0))


def read_vectors(tiles, map_ref):
    rows, columns = tiles.shape
    every = mul(tiles[...], spread_map(columns, map_ref))
    inner = lax.broadcasted_iota(jnp.int32, (rows, D), 0) // 16
    return jnp.sum(jnp.where(inner == map_ref[0:1], every, 0.0).reshape(rows // 16, 16, D), axis=0)


def write_vectors(vectors, rows, columns, map_ref):
    every = jnp.broadcast_to(vectors[None], (rows // 16, 16, D)).reshape(rows, D)
    inner = lax.broadcasted_iota(jnp.int32, (rows, D), 0) // 16
    return low(mul(low(jnp.where(inner == map_ref[0:1], every, 0.0)), spread_map(columns, map_ref), 1, 1))


def gate_of(x, router):
    return jax.nn.sigmoid(jnp.sum(x * router, axis=-1, keepdims=True))


def routed_forward_steps(b, need, hidden, spot_ref, chosen, vec_ref, extra, keep):
    length = hidden.shape[0]

    def pick(_):
        chosen[...] = spots(0, length, spot_ref[...])
        need("hidden")
        for t in b.tiles():
            b.x[t] = low(mul(chosen[:, t], hidden[...], 0, 0))
        need("vectors")
        b.norm()
        keep("x", "normed")

    def join(_):
        keep("projected", "merged", "lse")
        need("out")
        b.join()
        keep("branch", "normed_mlp")

    def narrow(_):
        keep("active", "slope")
        need("down")
        for t in b.tiles():
            extra[t] = b.branch[t] + b.narrow(t)
        keep("change")

    def put(_):
        rows = [gate_of(b.rows_of(t), vec_ref[2:3]) * extra[t] for t in b.tiles()]
        pieces = [two(r) for r in rows]
        for i in range(0, length, ROWS):
            t = slice(i, i + ROWS)
            total = hidden[t].astype(jnp.float32)
            for piece, s in zip(pieces, b.tiles()):
                for p in piece:
                    total = total + mul(chosen[t, s], p)
            b.middle[t] = total

    return [(1, pick), (0, lambda _: need("qkv")), (3, b.project), (6, b.attend), (1, join), (0, lambda _: need("up")), (4, b.widen),
            (1, narrow), (1, put)]


KEPT = ("x", "change") + SAVED


def kept_shapes(rows):
    return [((rows, D), jnp.bfloat16), ((rows, D), jnp.float32)] + kept_buffers(rows)


def routed_backward_steps(b, need, grad, spot_ref, vec_ref, change, grad_rows, gate, ship, targets, vec, turned,
                          grad_hbm, grad_sem):
    length = grad.shape[0]
    router = vec_ref.at[2:3]
    gqkv, *others = targets

    def take(_):
        pieces = two(grad[...])
        need("x", "change")
        for t in b.tiles():
            chosen = spots(0, length, spot_ref[:, t])
            rows = mul(chosen, pieces[0], 0, 0) + mul(chosen, pieces[1], 0, 0)
            g = gate_of(b.rows_of(t), router[...])
            b.grad_low[t], grad_rows[t] = two(g * rows)
            logits = jnp.sum(rows * change[t], axis=-1, keepdims=True) * g * (1.0 - g)
            gate[t] = jnp.broadcast_to(logits, (ROWS, 128))
        need("down", "active", "slope", "normed_mlp")

    def finish(t, g):
        change[t] = g + gate[t, 0:1] * router[...]

    def put(_):
        pieces = [two(change[t]) for t in b.tiles()]
        for i in range(0, length, ROWS):
            t = slice(i, i + ROWS)
            total = grad[t]
            for piece, s in zip(pieces, b.tiles()):
                chosen = spots(i, ROWS, spot_ref[:, s])
                for p in piece:
                    total = total + mul(chosen, p)
            grad[t] = total
            pltpu.make_async_copy(grad.at[t], grad_hbm.at[t], grad_sem).start()

    def route(_):
        total = jnp.zeros((8, D), jnp.float32)
        for t in b.tiles():
            total = total + jnp.sum((gate[t, 0:1] * b.rows_of(t)).reshape(-1, 8, D), axis=0)
        vec(2, jnp.sum(total, axis=0, keepdims=True))

    wide, mlp, out = wide_steps(b, lambda t: b.grad_low[t].astype(jnp.float32) + grad_rows[t].astype(jnp.float32), ship, others, lambda v: vec(1, v))
    attend, qkv, norm = attend_steps(b, ship, gqkv, lambda v: vec(0, v), finish, turned, True)

    def wants(*names):
        return (0, lambda _: need(*names))

    return [(1, take), wide, wants("up", "branch"), mlp, wants("out", "merged"), out, wants("projected", "lse"), attend,
            wants("normed"), qkv, wants("qkv"), norm, (1, route), (1, put)]


KEPT_DENSE = ("x", "projected", "merged", "lse")


def forward_kernel(remote, *refs):
    hidden_hbm, cot_hbm, index_ref, class_ref, map_ref, first_ref, *refs = refs
    given, refs = refs[:8], refs[8:]
    if remote:
        whole, refs = refs[:9], refs[9:]
    else:
        whole = [first_ref, *given]
    vec_ref, gvec_ref, y_hbm, plus_hbm, gmerged_hbm, gout_hbm, gup_hbm, gdown_hbm, *refs = refs
    n, m = len(KEPT), len(KEPT_DENSE)
    kept_hbm, refs = dict(zip(KEPT, refs[:n])), refs[n:]
    dense_hbm, refs = dict(zip(KEPT_DENSE, refs[:m])), refs[m:]
    hidden, cot, chosen, tiles, qkv, out, up, down, qkv_b, out_b, *refs = refs
    change, branch_a, lse_a, active, slope, x, branch, projected, merged, lse, normed, normed_mlp, stage, *refs = refs
    load_sem, keep_sem, dense_sem, stage_sem, row_sem, *refs = refs
    length, half = hidden.shape[0], index_ref.shape[1]
    spot_ref = spots_of(index_ref, class_ref, length)
    top, rest = pl.ds(0, half), pl.ds(half, half)
    kept = dict(x=active.at[rest, cols(0)], change=change, branch=branch_a, projected=active.at[top, pl.ds(0, 3 * D)],
                merged=active.at[rest, cols(1)], lse=lse_a, active=slope.at[top], slope=slope.at[rest],
                normed=active.at[rest, cols(2)], normed_mlp=active.at[rest, cols(3)])
    into = (tiles, qkv, out, up, down, qkv_b, out_b, up, down)
    loads = [pltpu.make_async_copy(src, dst, load_sem.at[j]) for j, (src, dst) in enumerate(zip(whole, into))]
    loads += [pltpu.make_async_copy(src, dst, load_sem.at[9 + j]) for j, (src, dst) in enumerate(((hidden_hbm, hidden), (cot_hbm, cot)))]
    where = dict(vectors=0, qkv=1, out=2, up=3, down=4, hidden=9)
    loads[9].start()
    loads[10].start()

    def need(name):
        loads[where[name]].wait()
        if name == "vectors":
            vec_ref[...] = read_vectors(tiles, map_ref)

    saves = {k: pltpu.make_async_copy(kept[k], kept_hbm[k], keep_sem.at[j]) for j, k in enumerate(KEPT)}
    dense = dict(x=x, projected=projected, merged=merged, lse=lse)
    dense_saves = {k: pltpu.make_async_copy(dense[k], dense_hbm[k], dense_sem.at[j]) for j, k in enumerate(KEPT_DENSE)}

    def keep(*wanted):
        for k in wanted:
            saves[k].start()

    b = Block(half, dict(kept, middle=x, qkv=qkv, out=out, up=up, down=down,
                         gain_attn=vec_ref.at[0:1], gain_mlp=vec_ref.at[1:2]))
    d = Block(length, dict(dense, branch=branch, normed=normed, normed_mlp=normed_mlp, active=active, slope=slope, grad_low=cot,
                           qkv=qkv_b, out=out_b, up=up, down=down, gain_attn=vec_ref.at[3:4], gain_mlp=vec_ref.at[4:5]))

    def norm(_):
        dense_saves["x"].start()
        d.norm()

    def join(_):
        for k in KEPT_DENSE[1:]:
            dense_saves[k].start()
        loads[6].wait()
        d.join()

    def before_widen(_):
        for c in saves.values():
            c.wait()
        loads[7].wait()

    def narrow(_):
        loads[8].wait()
        for t in d.tiles():
            hidden[t] = low(x[t] + branch[t] + d.narrow(t))
        pltpu.make_async_copy(hidden, y_hbm, row_sem.at[0]).start()
        loads[10].wait()

    def cot_of(t):
        return cot[t].astype(jnp.float32)

    def vec(value):
        gvec_ref[...] = value

    def grad(_):
        for t in d.tiles():
            branch[t] += cot_of(t)
        pltpu.make_async_copy(branch, plus_hbm, row_sem.at[1]).start()

    ship = Ship((stage.at[0], stage.at[1]), stage_sem)
    wide, mlp, last = wide_steps(d, cot_of, ship, (gout_hbm, gup_hbm, gdown_hbm), vec)
    steps = routed_forward_steps(b, need, hidden, spot_ref, chosen, vec_ref, change, keep)
    steps += [(1, norm), (0, lambda _: loads[5].wait()), (3, d.project), (6, d.attend), (1, join), (0, before_widen), (4, d.widen),
              (1, narrow), wide, mlp, (0, grad), last]
    late = 17
    if remote:
        tile, *refs = refs
        tile[...] = jnp.zeros_like(tile)
        tile[: first_ref.shape[0], : first_ref.shape[1]] = first_ref[...]
        flow = Gather(GATHER_PARTS, [tile, *given], whole, *refs)
        ends = {}
        for _, step, p in GATHER_PLAN:
            if step == 6:
                ends[GATHER_PARTS[p][0]] = p
        units = [[] for _ in range(sum(c for c, _ in steps) + 1)]
        for unit, step, p in GATHER_PLAN:
            units[unit].append(functools.partial(flow.take, step, p))
            a = GATHER_PARTS[p][0]
            if step == 6 and p == ends[a]:
                units[max(unit, late) if a > 6 else unit].append(loads[a].start)
        flow.begin()
    else:
        for c in loads[:7]:
            c.start()
        units = [[] for _ in range(sum(c for c, _ in steps) + 1)]
        units[late] = [loads[7].start, loads[8].start]
    run(steps, units)
    for f in units[-1]:
        f()
    gmerged = pltpu.make_async_copy(active.at[:, pl.ds(0, D)], gmerged_hbm, row_sem.at[2])
    gmerged.start()
    ship.wait(1)
    if remote:
        flow.finish()
    for c in dense_saves.values():
        c.wait()
    gmerged.wait()
    pltpu.make_async_copy(hidden, y_hbm, row_sem.at[0]).wait()
    pltpu.make_async_copy(branch, plus_hbm, row_sem.at[1]).wait()


def forward(remote, hidden, cot, index, capacity_class, place_map, vectors, weights, outer, inner):
    length, rows = hidden.shape[0], index.shape[1]
    f32, b16 = jnp.float32, jnp.bfloat16
    kept, short, every = kept_shapes(rows), Block.scratch(rows), Block.scratch(length)
    every["x"] = every["branch"]
    dense = [every[k] for k in KEPT_DENSE]
    whole = [shape(16 * inner, 128 * outer)] + [shape(w.shape[0] * inner, w.shape[1] * outer) for w in weights] if remote else []
    scratch = buffers(((length, D), b16), ((length, D), b16), ((length, rows), b16), ((16 * inner, 128 * outer), b16), *WEIGHTS,
                      *WEIGHTS[:2], ((rows, D), f32), short["branch"], short["lse"],
                      *[every[k] for k in ("active", "slope", "x", "branch", "projected", "merged", "lse", "normed", "normed_mlp")],
                      ((2, D, D), b16))
    scratch += [pltpu.SemaphoreType.DMA((k,)) for k in (11, len(kept), len(dense), 2, 3)]
    if remote:
        scratch += buffers(((16, 128), b16)) + Gather.semaphores(len(GATHER_PARTS))
    results = pl.pallas_call(
        functools.partial(forward_kernel, remote),
        in_specs=any_specs(2) + vmem_specs(3 + remote) + any_specs(9 - remote),
        out_specs=any_specs(len(whole)) + vmem_specs(2) + any_specs(6 + len(kept) + len(dense)),
        out_shape=whole + [shape(16, D, dtype=f32), shape(1, D, dtype=f32), shape(length, D), shape(length, D, dtype=f32),
                           shape(length, D)] + [shape(*s) for s, _ in WEIGHTS[1:]] + [shape(*s, dtype=t) for s, t in kept + dense],
        scratch_shapes=scratch,
        compiler_params=pltpu.CompilerParams(vmem_limit_bytes=VMEM_BYTES, **(dict(collective_id=0, has_side_effects=True) if remote else {})),
        name="forward",
    )(hidden, cot, index, capacity_class, place_map, vectors, *weights)
    if remote:
        weights, results = results[1:9], results[9:]
    return weights, results[:8], results[8 : 8 + len(kept)], results[8 + len(kept) :]


DENSE_IN = ("x", "projected", "merged", "lse", "grad_merged", "plus")


def backward_kernel(remote, *refs):
    index_ref, class_ref, map_ref, vec_ref, gmlp_ref, *refs = refs
    weights_hbm, refs = refs[:5], refs[5:]
    n, m = len(KEPT), len(DENSE_IN)
    dense_hbm, refs = dict(zip(DENSE_IN, refs[:m])), refs[m:]
    kept_hbm, refs = dict(zip(KEPT, refs[:n])), refs[n:]
    given, refs = refs[:3], refs[3:]
    input_hbm, *refs = refs
    if remote:
        outs, refs = refs[:9], refs[9:]
    else:
        gvec_ref, *refs = refs
    made, refs = refs[:5], refs[5:]
    if remote:
        k = len(PARTS)
        core_in, second_in, first_in, refs = refs[:k], refs[k : 2 * k], refs[2 * k : 3 * k], refs[3 * k :]
    (x, plus, projected, merged, grad_merged, lse, normed, qkv, turned, grad_rows, gate, out, up, down, x_a, active, slope,
     stage, load_sem, stage_sem, row_sem, *refs) = refs
    half = index_ref.shape[1]
    spot_ref = spots_of(index_ref, class_ref, dense_hbm["x"].shape[0])
    top, rest = pl.ds(0, half), pl.ds(half, half)
    a_refs = dict(x=x_a, change=plus.at[rest], branch=plus.at[top], projected=projected.at[top], merged=merged.at[top],
                  lse=lse.at[:, :, top], active=active, slope=slope, normed=normed.at[top], normed_mlp=normed.at[rest])
    copies = dict(zip(("d_qkv", "qkv", "out", "up", "down"), zip(weights_hbm, (qkv, qkv, out, up, down))))
    copies.update({"d_" + k: (dense_hbm[k], r) for k, r in zip(DENSE_IN, (x, projected, merged, lse, grad_merged, plus))})
    copies.update({k: (kept_hbm[k], a_refs[k]) for k in KEPT})
    copies = {k: pltpu.make_async_copy(*v, load_sem.at[j]) for j, (k, v) in enumerate(copies.items())}
    late = ("change", "normed_mlp", "branch", "merged", "projected", "lse", "normed", "qkv")
    for k in ("d_projected", "d_merged", "d_grad_merged", "d_lse"):
        copies[k].start()

    def need(*names):
        for k in names:
            copies[k].wait()

    d = Block(x.shape[0], dict(x=x, branch=plus, projected=projected, merged=merged, lse=lse, active=grad_merged, normed=normed,
                               qkv=qkv, gain_attn=vec_ref.at[3:4]))
    b = Block(half, dict(a_refs, grad_low=grad_merged.at[rest], qkv=qkv, out=out, up=up, down=down,
                         gain_attn=vec_ref.at[0:1], gain_mlp=vec_ref.at[1:2]))
    if remote:
        gvec_ref, tile, *refs = refs
    gvec_ref[...] = jnp.zeros_like(gvec_ref)
    gvec_ref[4:5] = gmlp_ref[...]

    def vec(j, value):
        gvec_ref[j : j + 1] = value

    ship = Ship((stage,), stage_sem)
    gqkv_b, gqkv_a, gout_a, gup_a, gdown_a = made

    def finish(t, g):
        x[t] = g

    attend, qkv_step, norm_step = attend_steps(d, ship, gqkv_b, lambda v: vec(3, v), finish, turned, False)

    def norm(_):
        norm_step[1](0)
        for k in late:
            copies[k].start()

    def enter(_):
        need("d_projected", "d_merged", "d_grad_merged", "d_lse")
        for k in ("d_x", "d_qkv", "d_plus", "x", "down", "active", "slope", "up", "out"):
            copies[k].start()

    steps = [(0, enter), attend,
             (0, lambda _: need("d_x")), (0, lambda _: d.norm()), qkv_step, (0, lambda _: need("d_qkv", "d_plus")), (1, norm)]
    steps += routed_backward_steps(b, need, x, spot_ref, vec_ref, a_refs["change"], grad_rows, gate, ship,
                                   (gqkv_a, gout_a, gup_a, gdown_a), vec, turned, input_hbm, row_sem.at[0])
    if not remote:
        run(steps)
    else:
        grads = (gqkv_b, *given, gqkv_a, gout_a, gup_a, gdown_a, tile)
        sums = Scatter(PARTS, grads, outs, core_in, second_in, first_in, *Scatter.unpack(PARTS, refs))

        hooks = [[] for _ in range(sum(c for c, _ in steps) + 1)]
        for unit, step, p in BACK_PLAN:
            hooks[unit].append(functools.partial(sums.take, step, p))
        greet(*place())
        run(steps, hooks)
        tile[...] = write_vectors(gvec_ref[...], *tile.shape, map_ref)
        for g in hooks[-1]:
            g()
        sums.finish()
    pltpu.make_async_copy(x, input_hbm, row_sem.at[0]).wait()


def backward(remote, index, capacity_class, place_map, vec, gmlp, weights, dense, kept, given, outer, inner):
    length, rows = dense[0].shape[0], index.shape[1]
    f32, b16 = jnp.float32, jnp.bfloat16
    made = [shape(*WEIGHTS[j][0]) for j in (0, 0, 1, 2, 3)]
    results = [shape(length, D, dtype=f32)]
    specs = any_specs(1)
    if remote:
        shards = [shape(s[0] // inner, s[1] // outer, dtype=f32) for s, _ in WEIGHTS]
        results += shards + shards + [shape(16, 128, dtype=f32)]
        specs += any_specs(9)
        lands = Scatter.shapes(PARTS)
    else:
        results += [shape(16, D, dtype=f32)]
        specs += vmem_specs(1)
        lands = []
    every = dict(Block.scratch(length), x=((length, D), f32))
    short = Block.scratch(rows)
    scratch = buffers(*[every[k] for k in ("x", "x", "projected", "merged", "merged", "lse", "normed")], WEIGHTS[0],
                      ((128, length), f32), ((rows, D), b16), ((rows, 128), f32), *WEIGHTS[1:],
                      ((rows, D), b16), short["active"], short["slope"], ((D, D), b16))
    scratch += [pltpu.SemaphoreType.DMA((k,)) for k in (5 + len(DENSE_IN) + len(kept), 2, 1)]
    if remote:
        scratch += buffers(((16, D), f32), ((16 * inner, 128 * outer), b16)) + Scatter.scratch(PARTS)
    return pl.pallas_call(
        functools.partial(backward_kernel, remote),
        in_specs=vmem_specs(5) + any_specs(5 + len(dense) + len(kept) + len(given)),
        out_specs=specs + any_specs(len(made) + len(lands)),
        out_shape=results + made + lands,
        scratch_shapes=scratch,
        compiler_params=pltpu.CompilerParams(vmem_limit_bytes=VMEM_BYTES, **(dict(collective_id=1, has_side_effects=True) if remote else {})),
        name="backward",
    )(index, capacity_class, place_map, vec, gmlp, *weights, *dense, *kept, *given)


def spread_vectors(vectors, outer, inner):
    rows = vectors.reshape(vectors.shape[0], outer, inner, -1).transpose(2, 0, 1, 3).astype(jnp.bfloat16)
    tiles = jnp.pad(rows, ((0, 0), (0, 16 - rows.shape[1]), (0, 0), (0, 128 - rows.shape[3])))
    return tiles.reshape(inner * 16, outer * 128)


def deliver_kernel(n, *refs):
    tile, sums, outs, vectors = refs[0], refs[1 : n + 1], refs[n + 1 : 2 * n + 1], refs[2 * n + 1 :]
    for a, b in zip(sums, outs):
        b[...] = a[...]
    for j, v in enumerate(vectors):
        v[...] = tile[j : j + 1, : v.shape[1]]


def deliver(tile, sums, each, count):
    n = len(sums)
    return pl.pallas_call(
        functools.partial(deliver_kernel, n),
        in_specs=vmem_specs(1 + n),
        out_specs=vmem_specs(n + count),
        out_shape=[shape(*s.shape, dtype=s.dtype) for s in sums] + [shape(1, each, dtype=jnp.float32)] * count,
        name="deliver",
    )(tile, *sums)


def fits(shards, outer, inner):
    return outer == 2 and inner == 16 and all(s.shape[0] % 16 == 0 and s.shape[1] % 128 == 0 for s in shards)


def per_device(outer, inner, *args):
    hidden, cotangent, capacity_class, token_index = args[:4]
    (gain_attn_a, qkv_a, out_a, gain_mlp_a, up_a, down_a, router_shard,
     gain_attn_b, qkv_b, out_b, gain_mlp_b, up_b, down_b) = args[4:]
    hidden, cotangent = hidden[0], cotangent[0]
    length = hidden.shape[0]
    vectors = jnp.stack((gain_attn_a, gain_mlp_a, router_shard, gain_attn_b, gain_mlp_b))
    shards = [qkv_a, out_a, up_a, down_a, qkv_b, out_b, up_b, down_b]
    remote = fits(shards, outer, inner)
    if not remote:
        tile = jnp.pad(vectors, ((0, 16 - vectors.shape[0]), (0, 128 - vectors.shape[1])))
        vectors, *shards = [
            lax.all_gather(lax.all_gather(s, "inner", axis=0, tiled=True), "outer", axis=1, tiled=True) for s in (tile, *shards)
        ]
    spot = (token_index, capacity_class.reshape(1, 1), lane_map(outer, inner))
    whole, made, kept, dense = forward(remote, hidden, cotangent, *spot, vectors, shards, outer, inner)
    vec, gmlp, output, plus, grad_merged, *given = made
    input_grad, *res = backward(
        remote, *spot, vec, gmlp, (whole[4], *whole[:4]), [*dense, grad_merged, plus], kept, given, outer, inner)
    if remote:
        done, gtile = res[:8], res[8]
    else:
        gvec, gqkv_b, *grads_a = res
        done = [
            lax.psum_scatter(
                lax.psum_scatter(s, "outer", scatter_dimension=1, tiled=True), "inner", scatter_dimension=0, tiled=True
            ).astype(jnp.float32)
            for s in [gqkv_b, *given, *grads_a, spread_vectors(gvec[:5], outer, inner)]
        ]
        done, gtile = done[:8], done[8]
    each = gain_attn_a.shape[0]
    res = deliver(gtile, done, each, 5)
    gb, ga, v = res[:4], res[4:8], [r[0] for r in res[8:]]
    return (output[None], input_grad[None], v[0], ga[0], ga[1], v[1], ga[2], ga[3], v[2], v[3], gb[0], gb[1], v[4], gb[2], gb[3])


def solution(mesh):
    outer, inner = mesh.shape["outer"], mesh.shape["inner"]
    both = ("outer", "inner")
    rows, vector, matrix = P(both, None, None), P(both), P("inner", "outer")
    block = (vector, matrix, matrix, vector, matrix, matrix)
    return jax.shard_map(
        functools.partial(per_device, outer, inner),
        mesh=mesh,
        in_specs=(rows, rows, vector, P(both, None)) + block + (vector,) + block,
        out_specs=(rows, rows) + block + (vector,) + block,
        check_vma=False,
    )
```

```python
import functools

import jax
import jax.numpy as jnp
import numpy as np
from jax import lax
from jax.experimental import pallas as pl
from jax.experimental.pallas import tpu as pltpu
from jax.sharding import PartitionSpec as P

MESH = pl.DeviceIdType.MESH


def place():
    o, i = lax.axis_index("outer"), lax.axis_index("inner")
    return o, i // 4, (i // 2) % 2, i % 2


def device(o, z, x, c):
    return (o, z * 4 + x * 2 + c)


def greet(o, z, x, c):
    barrier = pltpu.get_barrier_semaphore()
    signal = functools.partial(pl.semaphore_signal, barrier, inc=1, device_id_type=MESH)
    signal(device_id=device(1 - o, z, x, c))
    signal(device_id=device(o, z, 1 - x, c))
    signal(device_id=device(o, z, x, 1 - c))

    @pl.when(z > 0)
    def _():
        signal(device_id=device(o, z - 1, x, c))

    @pl.when(z < 3)
    def _():
        signal(device_id=device(o, z + 1, x, c))

    pl.semaphore_wait(barrier, 3 + jnp.where(z > 0, 1, 0) + jnp.where(z < 3, 1, 0))


GATHER_PARTS = (
        (0, 0, 16, 0, 128, False, False), (1, 0, 48, 0, 384, True, False), (1, 0, 48, 768, 384, False, False), (1, 0,
    48, 384, 384, True, False), (2, 0, 48, 0, 384, False, False), (3, 0, 48, 768, 768, True, True), (3, 0, 48, 0, 768,
    False, False), (5, 0, 48, 768, 384, True, True), (4, 0, 96, 0, 384, False, False), (4, 96, 96, 0, 384, True, False),
    (6, 0, 48, 0, 384, False, True), (5, 0, 48, 384, 384, True, False), (5, 0, 48, 0, 384, False, False), (7, 0, 48,
    768, 768, True, False), (7, 0, 48, 0, 768, False, False), (8, 96, 96, 0, 384, True, True), (8, 0, 96, 0, 384, True,
    False))
GATHER_PLAN = (
        (0, 0, 0), (0, 0, 1), (0, 0, 2), (0, 0, 3), (0, 0, 4), (0, 1, 0), (0, 1, 1), (0, 1, 2), (0, 1, 3), (0, 1, 4),
    (0, 2, 0), (0, 2, 1), (0, 2, 2), (0, 2, 3), (0, 2, 4), (0, 3, 0), (0, 0, 5), (0, 3, 1), (0, 0, 6), (0, 3, 2), (0, 0,
    7), (0, 3, 3), (0, 4, 0), (0, 0, 8), (0, 3, 4), (0, 0, 9), (0, 1, 5), (0, 1, 6), (0, 1, 8), (0, 4, 1), (0, 1, 9),
    (0, 2, 6), (0, 4, 2), (0, 2, 8), (0, 1, 7), (0, 2, 9), (0, 3, 6), (0, 4, 3), (0, 0, 10), (0, 5, 0), (0, 3, 8), (0,
    0, 11), (0, 3, 9), (0, 4, 4), (0, 6, 0), (0, 0, 12), (0, 1, 11), (0, 2, 5), (1, 5, 1), (1, 5, 2), (1, 2, 7), (1, 2,
    11), (1, 1, 12), (1, 6, 1), (1, 6, 2), (1, 3, 5), (1, 0, 13), (1, 4, 6), (1, 3, 7), (1, 0, 14), (1, 3, 11), (1, 0,
    15), (1, 5, 3), (1, 2, 12), (1, 1, 10), (1, 6, 3), (3, 4, 5), (3, 4, 8), (5, 4, 9), (5, 1, 13), (7, 5, 4), (7, 4,
    7), (8, 1, 14), (9, 3, 12), (9, 6, 4), (9, 0, 16), (10, 5, 6), (11, 5, 5), (11, 4, 11), (11, 6, 6), (11, 2, 13),
    (11, 1, 15), (11, 6, 5), (11, 2, 10), (11, 5, 9), (11, 5, 7), (12, 2, 14), (13, 6, 7), (13, 6, 9), (13, 4, 12), (13,
    1, 16), (14, 5, 8), (14, 3, 13), (14, 5, 11), (15, 2, 15), (15, 3, 10), (15, 3, 14), (15, 6, 8), (15, 2, 16), (15,
    6, 11), (15, 5, 12), (16, 6, 12), (18, 4, 13), (18, 3, 15), (20, 4, 10), (20, 4, 14), (21, 3, 16), (23, 5, 13), (23,
    4, 15), (24, 5, 14), (25, 5, 10), (25, 6, 13), (26, 6, 10), (26, 6, 14), (26, 4, 16), (27, 5, 15), (29, 6, 15), (29,
    5, 16), (31, 6, 16))


class Gather:
    @staticmethod
    def semaphores(n):
        return [pltpu.SemaphoreType.DMA(k) for k in ((n,), (n, 23), (n, 19))]

    def __init__(self, parts, shards, outs, local_sem, send_sem, recv_sem):
        o, z, x, c = place()
        n = len(parts)

        def shard(p):
            a, r0, r, c0, w, _, _ = parts[p]
            return shards[a].at[pl.ds(r0, r), pl.ds(c0, w)]

        def blocks(p, oo):
            a, r0, r, c0, w, _, _ = parts[p]
            rows, each = shards[a].shape
            view = outs[a].reshape(4, 2, 2, rows, 2 * each)
            return view, pl.ds(r0, r), pl.ds(pl.multiple_of(oo * each + c0, 128), w)

        def chunk(p, k):
            view, rows, columns = blocks(p, o)
            return view.at[k, x, c, rows, columns]

        def group(p, second, first):
            first_x = parts[p][5]
            px, po = (first, second) if first_x else (second, first)
            view, rows, columns = blocks(p, o if po else 1 - o)
            return view.at[:, x if px else 1 - x, c, rows, columns]

        def send(p, src, dst, slot, target):
            return pltpu.make_async_remote_copy(
                src_ref=src, dst_ref=dst, send_sem=send_sem.at[p, slot[0]], recv_sem=recv_sem.at[p, slot[1]],
                device_id=target, device_id_type=MESH)

        def wait(ref, sem):
            pltpu.make_async_copy(ref, ref, sem).wait()

        def up(p, k, hop, src=None):
            b = chunk(p, k)
            return send(p, b if src is None else src, b, (hop, k), device(o, z + 1, x, c))

        def down(p, k, hop, src=None):
            b = chunk(p, k)
            return send(p, b if src is None else src, b, (3 + hop, k), device(o, z - 1, x, c))

        def near(p, second):
            return device(o, z, 1 - x, c) if parts[p][5] != second else device(1 - o, z, x, c)

        def to_core(p, second, first):
            b = group(p, second, first)
            send(p, b, b, (9 + 2 * second + first, 7 + 2 * second + first), device(o, z, x, 1 - c)).start()

        def to_second(p, first):
            b = group(p, 1, first)
            send(p, b, b, (7 + first, 5 + first), near(p, True)).start()

        def local(p):
            return pltpu.make_async_copy(shard(p), chunk(p, z), local_sem.at[p])

        def own(p):
            @pl.when(z < 3)
            def _():
                up(p, z, 0, shard(p)).start()

            @pl.when(z > 0)
            def _():
                down(p, z, 0, shard(p)).start()

            local(p).start()

        def hop(d):
            def go(p):
                @pl.when(z >= d)
                def _():
                    wait(chunk(p, z - d), recv_sem.at[p, z - d])
                    if d < 3:
                        @pl.when(z < 3)
                        def _():
                            up(p, z - d, d).start()

                @pl.when(z + d <= 3)
                def _():
                    wait(chunk(p, z + d), recv_sem.at[p, z + d])
                    if d < 3:
                        @pl.when(z > 0)
                        def _():
                            down(p, z + d, d).start()
            return go

        third = hop(3)

        def first(p):
            third(p)
            local(p).wait()
            b = group(p, 1, 1)
            send(p, b, b, (6, 4), near(p, False)).start()
            to_second(p, 1)
            to_core(p, 1, 1)

        def second(p):
            wait(group(p, 1, 0), recv_sem.at[p, 4])
            to_second(p, 0)
            to_core(p, 1, 0)

        def cores(p):
            for f in (1, 0):
                wait(group(p, 0, f), recv_sem.at[p, 5 + f])
                to_core(p, 0, f)

        def arrived(p):
            for slot in range(4):
                wait(group(p, 1, 1), recv_sem.at[p, 7 + slot])

        def plane(p, second, first):
            first_x = parts[p][5]
            px, po = (first, second) if first_x else (second, first)
            view, rows, columns = blocks(p, o if po else 1 - o)
            return view.at[z, x if px else 1 - x, c, rows, columns]

        def layer(p, k, oo):
            view, rows, columns = blocks(p, oo)
            return view.at[k, :, c, rows, columns]

        def late_own(p):
            s, b = shard(p), plane(p, 1, 1)
            send(p, s, b, (12, 8), near(p, False)).start()
            send(p, s, b, (13, 9), near(p, True)).start()
            local(p).start()

        def late_first(p):
            b = plane(p, 1, 0)
            wait(b, recv_sem.at[p, 8])
            send(p, b, b, (14, 10), near(p, True)).start()

        def spread(p, k, hop, rise, fall):
            for oo in (0, 1):
                b = layer(p, k, oo)
                if rise:
                    @pl.when(z < 3)
                    def _():
                        send(p, b, b, (2 * hop + oo, 2 * k + oo), device(o, z + 1, x, c)).start()
                if fall:
                    @pl.when(z > 0)
                    def _():
                        send(p, b, b, (6 + 2 * hop + oo, 2 * k + oo), device(o, z - 1, x, c)).start()
                send(p, b, b, (15 + 2 * k + oo, 11 + 2 * k + oo), device(o, z, x, 1 - c)).start()

        def late_second(p):
            wait(plane(p, 0, 1), recv_sem.at[p, 9])
            wait(plane(p, 0, 0), recv_sem.at[p, 10])
            local(p).wait()
            spread(p, z, 0, True, True)

        def late_hop(d):
            def go(p):
                for k, there, rise in ((z - d, z >= d, True), (z + d, z + d <= 3, False)):
                    @pl.when(there)
                    def _():
                        for oo in (0, 1):
                            wait(layer(p, k, oo), recv_sem.at[p, 2 * k + oo])
                        spread(p, k, d, rise and d < 3, not rise and d < 3)
            return go

        def late_arrived(p):
            for slot in range(8):
                wait(layer(p, 0, 0), recv_sem.at[p, 11 + slot])

        def late_finish(p):
            for oo in (0, 1):
                for d in range(3):
                    @pl.when(jnp.logical_and(z < 3, z >= d))
                    def _():
                        wait(layer(p, 0, 0), send_sem.at[p, 2 * d + oo])

                    @pl.when(jnp.logical_and(z > 0, z + d <= 3))
                    def _():
                        wait(layer(p, 0, 0), send_sem.at[p, 6 + 2 * d + oo])
            for slot in (12, 13, 14):
                wait(plane(p, 1, 1), send_sem.at[p, slot])
            for slot in range(15, 23):
                wait(layer(p, 0, 0), send_sem.at[p, slot])

        def early_finish(p):
            for d in range(3):
                @pl.when(jnp.logical_and(z < 3, z >= d))
                def _():
                    wait(chunk(p, z), send_sem.at[p, d])

                @pl.when(jnp.logical_and(z > 0, z + d <= 3))
                def _():
                    wait(chunk(p, z), send_sem.at[p, 3 + d])
            for slot in range(6, 13):
                wait(group(p, 1, 1), send_sem.at[p, slot])

        early = (own, hop(1), hop(2), first, second, cores, arrived)
        late = (late_own, late_first, late_second, late_hop(1), late_hop(2), late_hop(3), late_arrived)

        def finish():
            for p in range(n):
                (late_finish if parts[p][6] else early_finish)(p)

        self.finish = finish
        self.take = lambda step, p: (late if parts[p][6] else early)[step](p)

    def begin(self):
        greet(*place())


PARTS = (
        (3, 96, 96, 0, 384, False, 2, False), (2, 0, 48, 0, 768, True, 1, False), (2, 0, 48, 768, 768, True, 3, True),
    (3, 0, 96, 0, 384, True, 0, False), (1, 0, 48, 0, 384, True, 4, False), (0, 0, 48, 640, 512, False, 6, False), (7,
    96, 96, 0, 384, False, 2, False), (0, 0, 48, 0, 640, True, 5, False), (6, 0, 48, 768, 768, True, 3, True), (6, 0,
    48, 0, 768, True, 1, False), (4, 0, 48, 640, 512, False, 6, False), (4, 0, 48, 0, 640, True, 5, False), (5, 0, 48,
    0, 384, False, 4, False), (7, 0, 96, 0, 384, True, 0, False), (8, 0, 16, 0, 128, True, 7, False))
BACK_PLAN = (
        (0, 0, 3), (0, 0, 2), (0, 0, 0), (0, 0, 1), (0, 0, 4), (1, 1, 3), (2, 2, 3), (2, 1, 2), (2, 1, 0), (3, 2, 2),
    (3, 2, 0), (3, 1, 1), (4, 2, 1), (4, 1, 4), (5, 3, 3), (5, 2, 4), (6, 4, 3), (6, 3, 2), (6, 3, 0), (7, 4, 0), (10,
    5, 3), (10, 0, 7), (10, 0, 5), (10, 4, 2), (10, 6, 3), (10, 3, 1), (11, 4, 1), (11, 1, 7), (12, 7, 3), (12, 2, 7),
    (12, 1, 5), (12, 5, 0), (13, 8, 3), (13, 2, 5), (13, 5, 2), (13, 6, 0), (13, 5, 1), (13, 3, 4), (14, 9, 3), (14, 6,
    1), (14, 4, 4), (15, 3, 7), (15, 7, 0), (16, 0, 13), (16, 4, 7), (16, 3, 5), (16, 6, 2), (16, 8, 0), (16, 7, 1),
    (16, 5, 4), (17, 4, 5), (17, 6, 4), (18, 1, 13), (18, 9, 0), (18, 0, 6), (18, 8, 1), (19, 2, 13), (19, 5, 7), (19,
    7, 4), (20, 1, 6), (20, 6, 7), (20, 5, 5), (20, 7, 2), (20, 0, 8), (20, 9, 1), (20, 0, 9), (20, 8, 4), (20, 6, 5),
    (20, 2, 6), (21, 9, 4), (22, 1, 8), (22, 7, 7), (23, 2, 8), (23, 1, 9), (23, 7, 5), (24, 8, 7), (24, 0, 12), (24, 2,
    9), (26, 3, 13), (26, 8, 5), (27, 4, 13), (27, 9, 7), (27, 9, 5), (27, 0, 10), (27, 0, 11), (27, 3, 6), (29, 1, 10),
    (29, 4, 6), (29, 0, 14), (29, 2, 10), (29, 3, 8), (29, 5, 13), (29, 1, 11), (29, 6, 13), (29, 2, 11), (29, 3, 9),
    (29, 4, 9), (29, 1, 12), (29, 5, 6), (29, 2, 12), (29, 3, 10), (29, 6, 6), (29, 7, 13), (29, 4, 10), (29, 4, 8),
    (29, 7, 6), (29, 5, 9), (29, 6, 9), (29, 1, 14), (29, 8, 13), (29, 2, 14), (29, 3, 11), (29, 4, 11), (29, 5, 8),
    (29, 9, 13), (29, 7, 9), (29, 8, 6), (29, 3, 12), (29, 4, 12), (29, 5, 10), (29, 3, 14), (29, 6, 10), (29, 4, 14),
    (29, 9, 6), (29, 8, 9), (29, 5, 11), (29, 6, 8), (29, 7, 10), (29, 6, 11), (29, 5, 14), (29, 9, 9), (29, 6, 14),
    (29, 5, 12), (29, 7, 8), (29, 8, 10), (29, 6, 12), (29, 7, 11), (29, 9, 10), (29, 7, 14), (29, 7, 12), (29, 8, 11),
    (29, 8, 14), (29, 8, 12), (29, 9, 11), (29, 9, 14), (29, 9, 12))


class Scatter:
    def __init__(self, parts, grads, outs, core_in, second_in, first_in, buffers, sems):
        o, z, x, c = place()
        acc, z_in, stage_own, stage_got, stage_second, stage_first, stage_out = buffers
        send_sem, recv_sem, own_sem, stage_sem, out_sem = sems
        n = len(parts)

        def kind(p):
            return 1 if parts[p][2] == 96 else 0

        def of(p):
            return parts[p][2], parts[p][4]

        def part(ref, p):
            r, w = of(p)
            return ref.at[:, pl.ds(0, r), pl.ds(0, w)]

        def group(p, second, first, core):
            g, r0, r, c0, w, first_x, _, _ = parts[p]
            px, po = (first, second) if first_x else (second, first)
            xx = x if px else 1 - x
            oo = o if po else 1 - o
            height, width = grads[g].shape
            each = width // 2
            return grads[g].reshape(4, 2, 2, height // 16, width).at[:, xx, core, pl.ds(r0, r), pl.ds(pl.multiple_of(oo * each + c0, 128), w)]

        def far(p, second):
            return device(o, z, 1 - x, c) if parts[p][5] != second else device(1 - o, z, x, c)

        def send(p, src, dst, kind_, slot, target):
            return pltpu.make_async_remote_copy(
                src_ref=src, dst_ref=dst, send_sem=send_sem.at[p, kind_], recv_sem=recv_sem.at[p, slot],
                device_id=target, device_id_type=MESH)

        def wait(ref, sem):
            pltpu.make_async_copy(ref, ref, sem).wait()

        slots, last_user = {}, {}
        turn = [0, 0]
        for p in range(n):
            k = kind(p)
            if parts[p][7]:
                slots[p], last_user[p] = None, None
                continue
            slots[p] = turn[k] % 2
            last_user[p] = next((q for q in range(p - 1, -1, -1) if kind(q) == k and slots[q] == slots[p]), None)
            turn[k] += 1

        def own_of(p):
            return part(stage_own[kind(p)].at[slots[p]], p)

        def total(p):
            return acc[parts[p][6]]

        def begin(p):
            for second in (0, 1):
                for first in (0, 1):
                    send(p, group(p, second, first, 1 - c), core_in[p].at[pl.ds(second * 8 + first * 4, 4)], 0, 0,
                         device(o, z, x, 1 - c)).start()
            for second in (0, 1) if parts[p][7] else (1,):
                for first in (0, 1):
                    at = second * 8 + first * 4 if parts[p][7] else first * 4
                    pltpu.make_async_copy(group(p, second, first, c), total(p).at[pl.ds(at, 4)], own_sem.at[p]).start()

        def core_fetch(p):
            k = kind(p)
            if last_user[p] is not None:
                q = last_user[p]
                wait(own_of(q), send_sem.at[q, 1])
            for first in () if parts[p][7] else (0, 1):
                pltpu.make_async_copy(group(p, 0, first, c), own_of(p).at[pl.ds(first * 4, 4)], stage_sem.at[kind(p), 0]).start()
            wait(core_in[p], recv_sem.at[p, 0])
            pltpu.make_async_copy(core_in[p].at[pl.ds(0, 8)], part(stage_got[k], p), stage_sem.at[kind(p), 1]).start()
            pltpu.make_async_copy(core_in[p].at[pl.ds(8, 8)], part(stage_second[k], p), stage_sem.at[kind(p), 2]).start()

        def core_add(p):
            own, got = own_of(p), part(stage_got[kind(p)], p)
            wait(own, stage_sem.at[kind(p), 0])
            wait(got, stage_sem.at[kind(p), 1])
            for first in (0, 1):
                s = pl.ds(first * 4, 4)
                own[s] = own[s] + got[s]
                send(p, own.at[s], second_in[p].at[s], 1, 1 + first, far(p, True)).start()
            mine = part(stage_second[kind(p)], p)
            wait(total(p), own_sem.at[p])
            wait(mine, stage_sem.at[kind(p), 2])
            total(p)[...] = total(p)[...] + mine[...]

        def second_fetch(p):
            got = part(stage_second[kind(p)], p)
            for first in (0, 1):
                s = pl.ds(first * 4, 4)
                wait(second_in[p].at[s], recv_sem.at[p, 1 + first])
            pltpu.make_async_copy(second_in[p], got, stage_sem.at[kind(p), 2]).start()

        def second_add(p):
            got = part(stage_second[kind(p)], p)
            wait(got, stage_sem.at[kind(p), 2])
            t = total(p)
            t[0:4] = t[0:4] + got[0:4]
            send(p, t.at[pl.ds(0, 4)], first_in[p], 2, 3, far(p, False)).start()
            t[4:8] = t[4:8] + got[4:8]

        def send_z(p, k, step):
            to = z + step
            slot = jnp.where(k == to, jnp.where(step > 0, k, 4), k)
            send(p, total(p).at[4 + k], z_in[p].at[slot], 3, 4 + slot, device(o, to, x, c)).start()

        def first_fetch(p):
            wait(first_in[p], recv_sem.at[p, 3])
            pltpu.make_async_copy(first_in[p], part(stage_first[kind(p)], p), stage_sem.at[kind(p), 3]).start()

        def first_add(p):
            got = part(stage_first[kind(p)], p)
            wait(got, stage_sem.at[kind(p), 3])
            t = total(p)
            t[4:8] = t[4:8] + got[...]

            @pl.when(z == 0)
            def _():
                for k in (3, 2, 1):
                    send_z(p, k, 1)

            @pl.when(z == 3)
            def _():
                for k in (0, 1, 2):
                    send_z(p, k, -1)

        def pass_on(p, k, step):
            wait(z_in[p].at[k], recv_sem.at[p, 4 + k])
            total(p)[4 + k] = total(p)[4 + k] + z_in[p][k]
            send_z(p, k, step)

        def along(level):
            def go(p):
                @pl.when(z == level)
                def _():
                    for k in range(3, level, -1):
                        pass_on(p, k, 1)

                @pl.when(z == 3 - level)
                def _():
                    for k in range(0, 3 - level):
                        pass_on(p, k, -1)
            return go

        out_user = [None, None]

        def copy_out(p):
            g, r0, r, c0, w, _, _, _ = parts[p]
            return pltpu.make_async_copy(stage_out[kind(p)].at[pl.ds(0, r), pl.ds(0, w)],
                                         outs[g].at[pl.ds(r0, r), pl.ds(c0, w)], out_sem.at[kind(p)])

        def finish():
            for p in out_user:
                copy_out(p).wait()

        def last(p):
            g, r0, r, c0, w, _, _, _ = parts[p]
            out = stage_out[kind(p)].at[pl.ds(0, r), pl.ds(0, w)]
            if out_user[kind(p)] is not None:
                copy_out(out_user[kind(p)]).wait()
            out_user[kind(p)] = p
            out[...] = total(p)[4 + z].astype(jnp.float32)

            @pl.when(z > 0)
            def _():
                wait(z_in[p].at[z], recv_sem.at[p, 4 + z])
                out[...] += z_in[p][z].astype(jnp.float32)

            @pl.when(z < 3)
            def _():
                wait(z_in[p].at[4], recv_sem.at[p, 8])
                out[...] += z_in[p][4].astype(jnp.float32)

            copy_out(p).start()
            wait(core_in[p], send_sem.at[p, 0])
            if all(last_user[q] != p for q in range(n)):
                wait(own_of(p), send_sem.at[p, 1])
            wait(first_in[p], send_sem.at[p, 2])
            wait(first_in[p].at[pl.ds(0, 3)], send_sem.at[p, 3])

        def planes(p):
            r, w = of(p)
            return total(p).reshape(4, 4, r, w)

        def send_plane(p, k, step):
            to = z + step
            slot = jnp.where(k == to, jnp.where(step > 0, k, 4), k)
            send(p, planes(p).at[:, k], second_in[p].at[pl.ds(slot * 4, 4)], 3, 4 + slot, device(o, to, x, c)).start()

        def early_add(p):
            k = kind(p)
            got, more = part(stage_got[k], p), part(stage_second[k], p)
            t = total(p)
            wait(t, own_sem.at[p])
            wait(got, stage_sem.at[k, 1])
            wait(more, stage_sem.at[k, 2])
            t[0:8] = t[0:8] + got[...]
            t[8:16] = t[8:16] + more[...]

            @pl.when(z == 0)
            def _():
                for j in (3, 2, 1):
                    send_plane(p, j, 1)

            @pl.when(z == 3)
            def _():
                for j in (0, 1, 2):
                    send_plane(p, j, -1)

        def take_planes(p, taken):
            stage = part(stage_second[kind(p)], p)
            copies = []
            for j, (slot, _) in enumerate(taken):
                wait(second_in[p].at[pl.ds(0, 4)], recv_sem.at[p, 4 + slot])
                copies.append(pltpu.make_async_copy(second_in[p].at[pl.ds(slot * 4, 4)], stage.at[pl.ds(j * 4, 4)],
                                                    stage_sem.at[kind(p), 2]))
                copies[-1].start()
            wait(stage.at[pl.ds(0, 4 * len(taken))], stage_sem.at[kind(p), 2])
            for j, (_, k) in enumerate(taken):
                v = planes(p).at[:, k]
                v[...] = v[...] + stage[j * 4 : j * 4 + 4]

        def early_along(level):
            def go(p):
                @pl.when(z == level)
                def _():
                    ks = range(3, level, -1)
                    take_planes(p, [(k, k) for k in ks])
                    for k in ks:
                        send_plane(p, k, 1)

                @pl.when(z == 3 - level)
                def _():
                    ks = range(0, 3 - level)
                    take_planes(p, [(k, k) for k in ks])
                    for k in ks:
                        send_plane(p, k, -1)
            return go

        def early_end(p):
            @pl.when(z == 0)
            def _():
                take_planes(p, [(4, 0)])

            @pl.when(z == 3)
            def _():
                take_planes(p, [(3, 3)])

            for k in (1, 2):
                @pl.when(z == k)
                def _():
                    take_planes(p, [(k, k), (4, k)])
            send(p, planes(p).at[pl.ds(0, 2), z], z_in[p].at[pl.ds(0, 2)], 1, 1, far(p, True)).start()

        def early_second(p):
            wait(z_in[p].at[pl.ds(0, 2)], recv_sem.at[p, 1])
            for f in (0, 1):
                v = planes(p).at[2 + f, z]
                v[...] = v[...] + z_in[p][f]
            send(p, planes(p).at[2, z], z_in[p].at[2], 2, 3, far(p, False)).start()

        def early_last(p):
            g, r0, r, c0, w, _, _, _ = parts[p]
            out = stage_out[kind(p)].at[pl.ds(0, r), pl.ds(0, w)]
            if out_user[kind(p)] is not None:
                copy_out(out_user[kind(p)]).wait()
            out_user[kind(p)] = p
            wait(z_in[p].at[2], recv_sem.at[p, 3])
            out[...] = planes(p)[3, z].astype(jnp.float32) + z_in[p][2].astype(jnp.float32)
            copy_out(p).start()
            wait(core_in[p], send_sem.at[p, 0])
            wait(total(p).at[pl.ds(0, 12)], send_sem.at[p, 3])
            wait(z_in[p].at[pl.ds(0, 2)], send_sem.at[p, 1])
            wait(z_in[p].at[2], send_sem.at[p, 2])

        self.finish = finish
        late = (begin, core_fetch, core_add, second_fetch, second_add, first_fetch, first_add, along(1), along(2), last)
        early = (begin, core_fetch, early_add, early_along(1), early_along(2), early_end, early_second, early_last)
        self.take = lambda step, p: (early if parts[p][7] else late)[step](p)

    @staticmethod
    def shapes(parts):
        return [shape(20 if m == 8 and s[7] else m, s[2], s[4]) for m in (16, 8, 4) for s in parts]

    @staticmethod
    def scratch(parts):
        b16 = jnp.bfloat16
        sizes = {s[6]: (16 if s[7] else 8, s[2], s[4]) for s in parts}
        acc = [(sizes[k], b16) for k in sorted(sizes)]
        lands = [((3 if s[7] else 5, s[2], s[4]), b16) for s in parts]
        stages = [((m, 48, 768), b16) if k == 0 else ((m, 96, 384), b16) for m in (8, 8, 4) for k in (0, 1)]
        stages = [((2, 8, 48, 768), b16), ((2, 8, 96, 384), b16)] + stages
        stages += [((48, 768), jnp.float32), ((96, 384), jnp.float32)]
        n = len(parts)
        return buffers(*acc, *lands, *stages) + [pltpu.SemaphoreType.DMA(k) for k in ((n, 4), (n, 9), (n,), (2, 4), (2,))]

    @staticmethod
    def unpack(parts, refs):
        n, m = len(parts), len({s[6] for s in parts})
        acc, refs = refs[:m], refs[m:]
        z_in, refs = refs[:n], refs[n:]
        return (acc, z_in, refs[0:2], refs[2:4], refs[4:6], refs[6:8], refs[8:10]), refs[10:15]


D = 768
SCALE = 0.125 * 1.4426950408889634
ROWS = 256
VMEM_BYTES = 127 * 2**19


def mul(a, b, ca=1, cb=0):
    return lax.dot_general(a, b, (((ca,), (cb,)), ((), ())), preferred_element_type=jnp.float32)


def low(v):
    return v.astype(jnp.bfloat16)


def cols(j):
    return pl.ds(pl.multiple_of(j * D, D), D)


def rms_scale(v):
    return lax.rsqrt(jnp.mean(v * v, axis=-1, keepdims=True) + 1e-06)


def rms_back(v, gain, grad):
    r = rms_scale(v)
    unit = v * r
    scaled = grad * gain
    back = r * (scaled - unit * jnp.mean(scaled * unit, axis=-1, keepdims=True))
    return back, jnp.sum((grad * unit).reshape(-1, 8, v.shape[-1]), axis=0)


def gelu_and_slope(u):
    k = 0.7978845608028654
    inner = u * (k + k * 0.044715 * (u * u))
    half = 0.5 + 0.5 * jnp.tanh(inner)
    return u * half, half * (1.0 + (1.0 - half) * (6.0 * inner - 4.0 * k * u))


def halves(v):
    lane = lax.broadcasted_iota(jnp.int32, v.shape, 1)
    zero = jnp.zeros_like(v)
    return jnp.where(lane < 64, v, zero), jnp.where(lane < 64, zero, v)


def two(v):
    first = low(v)
    return first, low(v - first.astype(jnp.float32))


def staggered(tiles, product, finish):
    held = product(tiles[0])
    for t, later in zip(tiles, tiles[1:] + [None]):
        coming = product(later) if later is not None else None
        finish(t, held)
        held = coming


class Block:
    def __init__(self, rows, refs):
        self.rows = rows
        self.__dict__.update(refs)

    @staticmethod
    def scratch(rows):
        f32, b16 = jnp.float32, jnp.bfloat16
        return dict(
            branch=((rows, D), f32), projected=((rows, 3 * D), b16), merged=((rows, D), b16), lse=((6, 8, rows), f32),
            active=((rows, 4 * D), b16), slope=((rows, 4 * D), b16), normed=((rows, D), b16), normed_mlp=((rows, D), b16))

    def rows_of(self, t):
        return self.x[t].astype(jnp.float32)

    def tiles(self):
        return [slice(i, i + ROWS) for i in range(0, self.rows, ROWS)]

    def norm(self):
        for t in self.tiles():
            x = self.rows_of(t)
            self.normed[t] = low(x * rms_scale(x) * self.gain_attn[...])

    def project(self, j):
        c = cols(j)
        self.projected[:, c] = low(mul(self.normed[...], self.qkv[:, c]))

    def pair(self, ref, part, pair, rows=slice(None)):
        return ref[rows, pl.ds(pl.multiple_of(part * D + pair * 128, 128), 128)]

    def attend(self, pair):
        v = self.pair(self.projected, 2, pair)
        lane = lax.broadcasted_iota(jnp.int32, v.shape, 1)
        one = jnp.ones_like(v)
        vs = jnp.where(lane < 64, v, one), jnp.where(lane < 64, one, v)
        causal = lax.broadcasted_iota(jnp.int32, (ROWS, ROWS), 0) >= lax.broadcasted_iota(jnp.int32, (ROWS, ROWS), 1)
        for t in self.tiles():
            n = t.stop
            qs = halves(self.pair(self.projected, 0, pair, t))
            k = self.pair(self.projected, 1, pair, slice(0, n))
            scores = [mul(qs[h], k, 1, 1) for h in range(2)]
            heads = []
            for h in range(2):
                s = scores[h]
                last = jnp.where(causal, s[:, t.start:], -1e30)
                s = last if t.start == 0 else jnp.concatenate([s[:, : t.start], last], axis=1)
                m = jnp.max(s, axis=1, keepdims=True) * SCALE
                o = mul(low(jnp.exp2(s * SCALE - m)), vs[h][:n])
                l = jnp.concatenate([o[:, 64:], o[:, :64]], axis=1)
                self.lse[pair, h : h + 1, t] = (m + jnp.log2(l)).T[64 * h : 64 * h + 1]
                heads.append(o / l)
            self.merged[t, pl.ds(pl.multiple_of(pair * 128, 128), 128)] = low(jnp.where(lane[:ROWS] < 64, *heads))

    def join(self):
        for t in self.tiles():
            branch = mul(self.merged[t], self.out[...])
            self.branch[t] = branch
            middle = self.rows_of(t) + branch
            self.normed_mlp[t] = low(middle * rms_scale(middle) * self.gain_mlp[...])

    def widen(self, j):
        c = cols(j)

        def finish(t, pre):
            active, slope = gelu_and_slope(pre)
            self.active[t, c] = low(active)
            self.slope[t, c] = low(slope)

        staggered(self.tiles(), lambda t: mul(self.normed_mlp[t], self.up[:, c]), finish)

    def narrow(self, t):
        return mul(self.active[t], self.down[...])

    def back_wide(self, j):
        c = cols(j)

        def finish(t, grad):
            self.slope[t, c] = low(grad * self.slope[t, c].astype(jnp.float32))

        staggered(self.tiles(), lambda t: mul(self.grad_low[t], self.down[c, :], 1, 1), finish)

    def grad_down(self, j):
        return low(mul(self.active[:, cols(j)], self.grad_low[...], 0, 0))

    def grad_up(self, j):
        return low(mul(self.normed_mlp[...], self.slope[:, cols(j)], 0, 0))

    def back_mlp(self, grad_of):
        total = jnp.zeros((8, D), jnp.float32)
        for t in self.tiles():
            grad = mul(self.slope[t], self.up[...], 1, 1)
            back, gain = rms_back(self.rows_of(t) + self.branch[t], self.gain_mlp[...], grad)
            total = total + gain
            self.branch[t] = back
            self.normed_mlp[t] = low(grad_of(t) + back)
        return jnp.sum(total, axis=0, keepdims=True)

    def grad_out(self):
        return low(mul(self.merged[...], self.normed_mlp[...], 0, 0))

    def back_merged(self):
        self.active[:, :D] = low(mul(self.normed_mlp[...], self.out[...], 1, 1))

    def attend_back(self, pair, turned):
        rows = self.rows
        q, do = self.pair(self.projected, 0, pair), self.pair(self.active, 0, pair)
        qs, dos = halves(q), halves(do)
        dd = do.astype(jnp.float32) * self.pair(self.merged, 0, pair).astype(jnp.float32)
        pick = lax.broadcasted_iota(jnp.int32, (8, 128), 0) == lax.broadcasted_iota(jnp.int32, (8, 128), 1) // 64
        delta = lax.dot_general(pick.astype(jnp.float32), dd, (((1,), (1,)), ((), ())), precision=lax.Precision.HIGHEST,
                                preferred_element_type=jnp.float32)
        causal = lax.broadcasted_iota(jnp.int32, (ROWS, ROWS), 1) >= lax.broadcasted_iota(jnp.int32, (ROWS, ROWS), 0)
        for t in self.tiles():
            a = t.start
            ks, vs = halves(self.pair(self.projected, 1, pair, t)), halves(self.pair(self.projected, 2, pair, t))
            dk = dv = dq = 0.0
            scores = [mul(ks[h], q[a:], 1, 1) for h in range(2)]
            dps = [mul(vs[h], do[a:], 1, 1) for h in range(2)]
            for h in range(2):
                s, dp = scores[h], dps[h]
                p = jnp.exp2(s * SCALE - self.lse[pair, h : h + 1, a:])
                first = jnp.where(causal, p[:, :ROWS], 0.0)
                p = first if t.stop == rows else jnp.concatenate([first, p[:, ROWS:]], axis=1)
                ds = low(p * (dp - delta[h : h + 1, a:]))
                dv = dv + mul(low(p), dos[h][a:])
                dk = dk + mul(ds, qs[h][a:])
                dq = dq + mul(ks[h], ds, 0, 0)
            lanes = pl.multiple_of(pair * 128, 128)
            self.projected[t, pl.ds(D + lanes, 128)] = low(0.125 * dk)
            self.projected[t, pl.ds(2 * D + lanes, 128)] = low(dv)
            if a == 0:
                turned[:, :rows] = dq
            else:
                turned[:, a:rows] += dq
        self.projected[:, pl.ds(lanes, 128)] = low(0.125 * turned[:, :rows].T)

    def grad_qkv(self, j):
        return low(mul(self.normed[...], self.projected[:, cols(j)], 0, 0))

    def back_norm(self, finish):
        total = jnp.zeros((8, D), jnp.float32)
        for t in self.tiles():
            grad = mul(self.projected[t], self.qkv[...], 1, 1)
            back, gain = rms_back(self.rows_of(t), self.gain_attn[...], grad)
            total = total + gain
            finish(t, back + self.branch[t])
        return jnp.sum(total, axis=0, keepdims=True)


SAVED = ("branch", "projected", "merged", "lse", "active", "slope", "normed", "normed_mlp")


def run(steps, hooks=None):
    at = 0
    waits = []
    for count, body in steps:
        if count == 0:
            waits.append(body)
            continue
        before = [list(hooks[at + k]) if hooks else [] for k in range(count)]
        at += count
        for f in before[0]:
            f()
        for f in waits:
            f(0)
        waits = []
        if count == 1:
            body(0)
            continue

        @pl.loop(0, count)
        def _(j):
            for k in range(1, count):
                if before[k]:
                    @pl.when(j == k)
                    def _():
                        for f in before[k]:
                            f()
            body(j)


class Loads:
    def __init__(self, pairs, sems):
        self.copies = {k: pltpu.make_async_copy(a, b, sems.at[j]) for j, (k, a, b) in enumerate(pairs)}
        for c in self.copies.values():
            c.start()

    def need(self, *names):
        for n in names:
            self.copies[n].wait()


class Ship:
    def __init__(self, stages, sems):
        self.stages, self.sems, self.single = stages, sems, len(stages) == 1

    def wait(self, slot):
        slot = min(slot, len(self.stages) - 1)
        pltpu.make_async_copy(self.stages[slot], self.stages[slot], self.sems.at[slot]).wait()

    def send(self, slot, value, target, busy):
        slot = min(slot, len(self.stages) - 1)
        if busy is True:
            self.wait(slot)
        elif busy is not False:
            pl.when(busy)(lambda: self.wait(slot))
        self.stages[slot][...] = value()
        pltpu.make_async_copy(self.stages[slot], target, self.sems.at[slot]).start()


def wide_steps(b, grad_of, ship, targets, vec):
    gout, gup, gdown = targets

    def wide(j):
        b.back_wide(j)
        ship.send(0, lambda: b.grad_down(j), gdown.at[cols(j), :], j > 0)
        ship.send(1, lambda: b.grad_up(j), gup.at[:, cols(j)], ship.single or j > 0)

    def mlp(_):
        ship.wait(0)
        if not ship.single:
            ship.wait(1)
        vec(b.back_mlp(grad_of))

    def out(_):
        ship.send(1, b.grad_out, gout, False)
        b.back_merged()

    return [(4, wide), (1, mlp), (1, out)]


def attend_steps(b, ship, gqkv, vec, finish, turned, busy):
    def qkv(j):
        ship.send(1, lambda: b.grad_qkv(j), gqkv.at[:, cols(j)], True if busy else j > 0)

    def norm(_):
        vec(b.back_norm(finish))
        ship.wait(1)

    return [(6, lambda j: b.attend_back(j, turned)), (3, qkv), (1, norm)]


def shape(*dims, dtype=jnp.bfloat16):
    return jax.ShapeDtypeStruct(dims, dtype)


def any_specs(n):
    return [pl.BlockSpec(memory_space=pl.ANY)] * n


def vmem_specs(n):
    return [pl.BlockSpec(memory_space=pltpu.VMEM)] * n


WEIGHTS = [((D, 3 * D), jnp.bfloat16), ((D, D), jnp.bfloat16), ((D, 4 * D), jnp.bfloat16), ((4 * D, D), jnp.bfloat16)]


def buffers(*pairs):
    return [pltpu.VMEM(dims, dtype) for dims, dtype in pairs]


def kept_buffers(rows):
    s = Block.scratch(rows)
    return [s[k] for k in SAVED]


def spots(start, count, spot):
    at = lax.broadcasted_iota(jnp.int32, (count, spot.shape[1]), 0) + start
    return low(jnp.where(at == spot, 1.0, 0.0))


def spots_of(index_ref, class_ref, length):
    slot = lax.broadcasted_iota(jnp.int32, index_ref.shape, 1)
    return jnp.where(slot < lax.shift_left(length // 8, class_ref[...]), index_ref[...], -1)


def lane_map(outer, inner):
    each = D // (outer * inner)
    d = np.arange(D, dtype=np.int32)
    return np.stack([d // each % inner, d // (each * inner) * 128 + d % each])


def spread_map(tiles_columns, map_ref):
    at = lax.broadcasted_iota(jnp.int32, (tiles_columns, D), 0)
    return low(jnp.where(at == map_ref[1:2], 1.0, 0.0))


def read_vectors(tiles, map_ref):
    rows, columns = tiles.shape
    every = mul(tiles[...], spread_map(columns, map_ref))
    inner = lax.broadcasted_iota(jnp.int32, (rows, D), 0) // 16
    return jnp.sum(jnp.where(inner == map_ref[0:1], every, 0.0).reshape(rows // 16, 16, D), axis=0)


def write_vectors(vectors, rows, columns, map_ref):
    every = jnp.broadcast_to(vectors[None], (rows // 16, 16, D)).reshape(rows, D)
    inner = lax.broadcasted_iota(jnp.int32, (rows, D), 0) // 16
    return low(mul(low(jnp.where(inner == map_ref[0:1], every, 0.0)), spread_map(columns, map_ref), 1, 1))


def gate_of(x, router):
    return jax.nn.sigmoid(jnp.sum(x * router, axis=-1, keepdims=True))


def routed_forward_steps(b, need, hidden, spot_ref, chosen, vec_ref, extra, keep):
    length = hidden.shape[0]

    def pick(_):
        chosen[...] = spots(0, length, spot_ref[...])
        need("hidden")
        for t in b.tiles():
            b.x[t] = low(mul(chosen[:, t], hidden[...], 0, 0))
        need("vectors")
        b.norm()
        keep("x", "normed")

    def join(_):
        keep("projected", "merged", "lse")
        need("out")
        b.join()
        keep("branch", "normed_mlp")

    def narrow(_):
        keep("active", "slope")
        need("down")
        for t in b.tiles():
            extra[t] = b.branch[t] + b.narrow(t)
        keep("change")

    def put(_):
        rows = [gate_of(b.rows_of(t), vec_ref[2:3]) * extra[t] for t in b.tiles()]
        pieces = [two(r) for r in rows]
        for i in range(0, length, ROWS):
            t = slice(i, i + ROWS)
            total = hidden[t].astype(jnp.float32)
            for piece, s in zip(pieces, b.tiles()):
                for p in piece:
                    total = total + mul(chosen[t, s], p)
            b.middle[t] = total

    return [(1, pick), (0, lambda _: need("qkv")), (3, b.project), (6, b.attend), (1, join), (0, lambda _: need("up")), (4, b.widen),
            (1, narrow), (1, put)]


KEPT = ("x", "change") + SAVED


def kept_shapes(rows):
    return [((rows, D), jnp.bfloat16), ((rows, D), jnp.float32)] + kept_buffers(rows)


def routed_backward_steps(b, need, grad, spot_ref, vec_ref, change, grad_rows, gate, ship, targets, vec, turned,
                          grad_hbm, grad_sem):
    length = grad.shape[0]
    router = vec_ref.at[2:3]
    gqkv, *others = targets

    def take(_):
        pieces = two(grad[...])
        need("x", "change")
        for t in b.tiles():
            chosen = spots(0, length, spot_ref[:, t])
            rows = mul(chosen, pieces[0], 0, 0) + mul(chosen, pieces[1], 0, 0)
            g = gate_of(b.rows_of(t), router[...])
            b.grad_low[t], grad_rows[t] = two(g * rows)
            logits = jnp.sum(rows * change[t], axis=-1, keepdims=True) * g * (1.0 - g)
            gate[t] = jnp.broadcast_to(logits, (ROWS, 128))
        need("down", "active", "slope", "normed_mlp")

    def finish(t, g):
        change[t] = g + gate[t, 0:1] * router[...]

    def put(_):
        pieces = [two(change[t]) for t in b.tiles()]
        for i in range(0, length, ROWS):
            t = slice(i, i + ROWS)
            total = grad[t]
            for piece, s in zip(pieces, b.tiles()):
                chosen = spots(i, ROWS, spot_ref[:, s])
                for p in piece:
                    total = total + mul(chosen, p)
            grad[t] = total
            pltpu.make_async_copy(grad.at[t], grad_hbm.at[t], grad_sem).start()

    def route(_):
        total = jnp.zeros((8, D), jnp.float32)
        for t in b.tiles():
            total = total + jnp.sum((gate[t, 0:1] * b.rows_of(t)).reshape(-1, 8, D), axis=0)
        vec(2, jnp.sum(total, axis=0, keepdims=True))

    wide, mlp, out = wide_steps(b, lambda t: b.grad_low[t].astype(jnp.float32) + grad_rows[t].astype(jnp.float32), ship, others, lambda v: vec(1, v))
    attend, qkv, norm = attend_steps(b, ship, gqkv, lambda v: vec(0, v), finish, turned, True)

    def wants(*names):
        return (0, lambda _: need(*names))

    return [(1, take), wide, wants("up", "branch"), mlp, wants("out", "merged"), out, wants("projected", "lse"), attend,
            wants("normed"), qkv, wants("qkv"), norm, (1, route), (1, put)]


KEPT_DENSE = ("x", "projected", "merged", "lse")


def forward_kernel(remote, *refs):
    hidden_hbm, cot_hbm, index_ref, class_ref, map_ref, first_ref, *refs = refs
    given, refs = refs[:8], refs[8:]
    if remote:
        whole, refs = refs[:9], refs[9:]
    else:
        whole = [first_ref, *given]
    vec_ref, gvec_ref, y_hbm, plus_hbm, gmerged_hbm, gout_hbm, gup_hbm, gdown_hbm, *refs = refs
    n, m = len(KEPT), len(KEPT_DENSE)
    kept_hbm, refs = dict(zip(KEPT, refs[:n])), refs[n:]
    dense_hbm, refs = dict(zip(KEPT_DENSE, refs[:m])), refs[m:]
    hidden, cot, chosen, tiles, qkv, out, up, down, qkv_b, out_b, *refs = refs
    change, branch_a, lse_a, active, slope, x, branch, projected, merged, lse, normed, normed_mlp, stage, *refs = refs
    load_sem, keep_sem, dense_sem, stage_sem, row_sem, *refs = refs
    length, half = hidden.shape[0], index_ref.shape[1]
    spot_ref = spots_of(index_ref, class_ref, length)
    top, rest = pl.ds(0, half), pl.ds(half, half)
    kept = dict(x=active.at[rest, cols(0)], change=change, branch=branch_a, projected=active.at[top, pl.ds(0, 3 * D)],
                merged=active.at[rest, cols(1)], lse=lse_a, active=slope.at[top], slope=slope.at[rest],
                normed=active.at[rest, cols(2)], normed_mlp=active.at[rest, cols(3)])
    into = (tiles, qkv, out, up, down, qkv_b, out_b, up, down)
    loads = [pltpu.make_async_copy(src, dst, load_sem.at[j]) for j, (src, dst) in enumerate(zip(whole, into))]
    loads += [pltpu.make_async_copy(src, dst, load_sem.at[9 + j]) for j, (src, dst) in enumerate(((hidden_hbm, hidden), (cot_hbm, cot)))]
    where = dict(vectors=0, qkv=1, out=2, up=3, down=4, hidden=9)
    loads[9].start()
    loads[10].start()

    def need(name):
        loads[where[name]].wait()
        if name == "vectors":
            vec_ref[...] = read_vectors(tiles, map_ref)

    saves = {k: pltpu.make_async_copy(kept[k], kept_hbm[k], keep_sem.at[j]) for j, k in enumerate(KEPT)}
    dense = dict(x=x, projected=projected, merged=merged, lse=lse)
    dense_saves = {k: pltpu.make_async_copy(dense[k], dense_hbm[k], dense_sem.at[j]) for j, k in enumerate(KEPT_DENSE)}

    def keep(*wanted):
        for k in wanted:
            saves[k].start()

    b = Block(half, dict(kept, middle=x, qkv=qkv, out=out, up=up, down=down,
                         gain_attn=vec_ref.at[0:1], gain_mlp=vec_ref.at[1:2]))
    d = Block(length, dict(dense, branch=branch, normed=normed, normed_mlp=normed_mlp, active=active, slope=slope, grad_low=cot,
                           qkv=qkv_b, out=out_b, up=up, down=down, gain_attn=vec_ref.at[3:4], gain_mlp=vec_ref.at[4:5]))

    def norm(_):
        dense_saves["x"].start()
        d.norm()

    def join(_):
        for k in KEPT_DENSE[1:]:
            dense_saves[k].start()
        loads[6].wait()
        d.join()

    def before_widen(_):
        for c in saves.values():
            c.wait()
        loads[7].wait()

    def narrow(_):
        loads[8].wait()
        for t in d.tiles():
            hidden[t] = low(x[t] + branch[t] + d.narrow(t))
        pltpu.make_async_copy(hidden, y_hbm, row_sem.at[0]).start()
        loads[10].wait()

    def cot_of(t):
        return cot[t].astype(jnp.float32)

    def vec(value):
        gvec_ref[...] = value

    def grad(_):
        for t in d.tiles():
            branch[t] += cot_of(t)
        pltpu.make_async_copy(branch, plus_hbm, row_sem.at[1]).start()

    ship = Ship((stage.at[0], stage.at[1]), stage_sem)
    wide, mlp, last = wide_steps(d, cot_of, ship, (gout_hbm, gup_hbm, gdown_hbm), vec)
    steps = routed_forward_steps(b, need, hidden, spot_ref, chosen, vec_ref, change, keep)
    steps += [(1, norm), (0, lambda _: loads[5].wait()), (3, d.project), (6, d.attend), (1, join), (0, before_widen), (4, d.widen),
              (1, narrow), wide, mlp, (0, grad), last]
    late = 17
    if remote:
        tile, *refs = refs
        tile[...] = jnp.zeros_like(tile)
        tile[: first_ref.shape[0], : first_ref.shape[1]] = first_ref[...]
        flow = Gather(GATHER_PARTS, [tile, *given], whole, *refs)
        ends = {}
        for _, step, p in GATHER_PLAN:
            if step == 6:
                ends[GATHER_PARTS[p][0]] = p
        units = [[] for _ in range(sum(c for c, _ in steps) + 1)]
        for unit, step, p in GATHER_PLAN:
            units[unit].append(functools.partial(flow.take, step, p))
            a = GATHER_PARTS[p][0]
            if step == 6 and p == ends[a]:
                units[max(unit, late) if a > 6 else unit].append(loads[a].start)
        flow.begin()
    else:
        for c in loads[:7]:
            c.start()
        units = [[] for _ in range(sum(c for c, _ in steps) + 1)]
        units[late] = [loads[7].start, loads[8].start]
    run(steps, units)
    for f in units[-1]:
        f()
    gmerged = pltpu.make_async_copy(active.at[:, pl.ds(0, D)], gmerged_hbm, row_sem.at[2])
    gmerged.start()
    ship.wait(1)
    if remote:
        flow.finish()
    for c in dense_saves.values():
        c.wait()
    gmerged.wait()
    pltpu.make_async_copy(hidden, y_hbm, row_sem.at[0]).wait()
    pltpu.make_async_copy(branch, plus_hbm, row_sem.at[1]).wait()


def forward(remote, hidden, cot, index, capacity_class, place_map, vectors, weights, outer, inner):
    length, rows = hidden.shape[0], index.shape[1]
    f32, b16 = jnp.float32, jnp.bfloat16
    kept, short, every = kept_shapes(rows), Block.scratch(rows), Block.scratch(length)
    every["x"] = every["branch"]
    dense = [every[k] for k in KEPT_DENSE]
    whole = [shape(16 * inner, 128 * outer)] + [shape(w.shape[0] * inner, w.shape[1] * outer) for w in weights] if remote else []
    scratch = buffers(((length, D), b16), ((length, D), b16), ((length, rows), b16), ((16 * inner, 128 * outer), b16), *WEIGHTS,
                      *WEIGHTS[:2], ((rows, D), f32), short["branch"], short["lse"],
                      *[every[k] for k in ("active", "slope", "x", "branch", "projected", "merged", "lse", "normed", "normed_mlp")],
                      ((2, D, D), b16))
    scratch += [pltpu.SemaphoreType.DMA((k,)) for k in (11, len(kept), len(dense), 2, 3)]
    if remote:
        scratch += buffers(((16, 128), b16)) + Gather.semaphores(len(GATHER_PARTS))
    results = pl.pallas_call(
        functools.partial(forward_kernel, remote),
        in_specs=any_specs(2) + vmem_specs(3 + remote) + any_specs(9 - remote),
        out_specs=any_specs(len(whole)) + vmem_specs(2) + any_specs(6 + len(kept) + len(dense)),
        out_shape=whole + [shape(16, D, dtype=f32), shape(1, D, dtype=f32), shape(length, D), shape(length, D, dtype=f32),
                           shape(length, D)] + [shape(*s) for s, _ in WEIGHTS[1:]] + [shape(*s, dtype=t) for s, t in kept + dense],
        scratch_shapes=scratch,
        compiler_params=pltpu.CompilerParams(vmem_limit_bytes=VMEM_BYTES, **(dict(collective_id=0, has_side_effects=True) if remote else {})),
        name="forward",
    )(hidden, cot, index, capacity_class, place_map, vectors, *weights)
    if remote:
        weights, results = results[1:9], results[9:]
    return weights, results[:8], results[8 : 8 + len(kept)], results[8 + len(kept) :]


DENSE_IN = ("x", "projected", "merged", "lse", "grad_merged", "plus")


def backward_kernel(remote, *refs):
    index_ref, class_ref, map_ref, vec_ref, gmlp_ref, *refs = refs
    weights_hbm, refs = refs[:5], refs[5:]
    n, m = len(KEPT), len(DENSE_IN)
    dense_hbm, refs = dict(zip(DENSE_IN, refs[:m])), refs[m:]
    kept_hbm, refs = dict(zip(KEPT, refs[:n])), refs[n:]
    given, refs = refs[:3], refs[3:]
    input_hbm, *refs = refs
    if remote:
        outs, refs = refs[:9], refs[9:]
    else:
        gvec_ref, *refs = refs
    made, refs = refs[:5], refs[5:]
    if remote:
        k = len(PARTS)
        core_in, second_in, first_in, refs = refs[:k], refs[k : 2 * k], refs[2 * k : 3 * k], refs[3 * k :]
    (x, plus, projected, merged, grad_merged, lse, normed, qkv, turned, grad_rows, gate, out, up, down, x_a, active, slope,
     stage, load_sem, stage_sem, row_sem, *refs) = refs
    half = index_ref.shape[1]
    spot_ref = spots_of(index_ref, class_ref, dense_hbm["x"].shape[0])
    top, rest = pl.ds(0, half), pl.ds(half, half)
    a_refs = dict(x=x_a, change=plus.at[rest], branch=plus.at[top], projected=projected.at[top], merged=merged.at[top],
                  lse=lse.at[:, :, top], active=active, slope=slope, normed=normed.at[top], normed_mlp=normed.at[rest])
    copies = dict(zip(("d_qkv", "qkv", "out", "up", "down"), zip(weights_hbm, (qkv, qkv, out, up, down))))
    copies.update({"d_" + k: (dense_hbm[k], r) for k, r in zip(DENSE_IN, (x, projected, merged, lse, grad_merged, plus))})
    copies.update({k: (kept_hbm[k], a_refs[k]) for k in KEPT})
    copies = {k: pltpu.make_async_copy(*v, load_sem.at[j]) for j, (k, v) in enumerate(copies.items())}
    late = ("change", "normed_mlp", "branch", "merged", "projected", "lse", "normed", "qkv")
    for k in ("d_projected", "d_merged", "d_grad_merged", "d_lse"):
        copies[k].start()

    def need(*names):
        for k in names:
            copies[k].wait()

    d = Block(x.shape[0], dict(x=x, branch=plus, projected=projected, merged=merged, lse=lse, active=grad_merged, normed=normed,
                               qkv=qkv, gain_attn=vec_ref.at[3:4]))
    b = Block(half, dict(a_refs, grad_low=grad_merged.at[rest], qkv=qkv, out=out, up=up, down=down,
                         gain_attn=vec_ref.at[0:1], gain_mlp=vec_ref.at[1:2]))
    if remote:
        gvec_ref, tile, *refs = refs
    gvec_ref[...] = jnp.zeros_like(gvec_ref)
    gvec_ref[4:5] = gmlp_ref[...]

    def vec(j, value):
        gvec_ref[j : j + 1] = value

    ship = Ship((stage,), stage_sem)
    gqkv_b, gqkv_a, gout_a, gup_a, gdown_a = made

    def finish(t, g):
        x[t] = g

    attend, qkv_step, norm_step = attend_steps(d, ship, gqkv_b, lambda v: vec(3, v), finish, turned, False)

    def norm(_):
        norm_step[1](0)
        for k in late:
            copies[k].start()

    def enter(_):
        need("d_projected", "d_merged", "d_grad_merged", "d_lse")
        for k in ("d_x", "d_qkv", "d_plus", "x", "down", "active", "slope", "up", "out"):
            copies[k].start()

    steps = [(0, enter), attend,
             (0, lambda _: need("d_x")), (0, lambda _: d.norm()), qkv_step, (0, lambda _: need("d_qkv", "d_plus")), (1, norm)]
    steps += routed_backward_steps(b, need, x, spot_ref, vec_ref, a_refs["change"], grad_rows, gate, ship,
                                   (gqkv_a, gout_a, gup_a, gdown_a), vec, turned, input_hbm, row_sem.at[0])
    if not remote:
        run(steps)
    else:
        grads = (gqkv_b, *given, gqkv_a, gout_a, gup_a, gdown_a, tile)
        sums = Scatter(PARTS, grads, outs, core_in, second_in, first_in, *Scatter.unpack(PARTS, refs))

        hooks = [[] for _ in range(sum(c for c, _ in steps) + 1)]
        for unit, step, p in BACK_PLAN:
            hooks[unit].append(functools.partial(sums.take, step, p))
        greet(*place())
        run(steps, hooks)
        tile[...] = write_vectors(gvec_ref[...], *tile.shape, map_ref)
        for g in hooks[-1]:
            g()
        sums.finish()
    pltpu.make_async_copy(x, input_hbm, row_sem.at[0]).wait()


def backward(remote, index, capacity_class, place_map, vec, gmlp, weights, dense, kept, given, outer, inner):
    length, rows = dense[0].shape[0], index.shape[1]
    f32, b16 = jnp.float32, jnp.bfloat16
    made = [shape(*WEIGHTS[j][0]) for j in (0, 0, 1, 2, 3)]
    results = [shape(length, D, dtype=f32)]
    specs = any_specs(1)
    if remote:
        shards = [shape(s[0] // inner, s[1] // outer, dtype=f32) for s, _ in WEIGHTS]
        results += shards + shards + [shape(16, 128, dtype=f32)]
        specs += any_specs(9)
        lands = Scatter.shapes(PARTS)
    else:
        results += [shape(16, D, dtype=f32)]
        specs += vmem_specs(1)
        lands = []
    every = dict(Block.scratch(length), x=((length, D), f32))
    short = Block.scratch(rows)
    scratch = buffers(*[every[k] for k in ("x", "x", "projected", "merged", "merged", "lse", "normed")], WEIGHTS[0],
                      ((128, length), f32), ((rows, D), b16), ((rows, 128), f32), *WEIGHTS[1:],
                      ((rows, D), b16), short["active"], short["slope"], ((D, D), b16))
    scratch += [pltpu.SemaphoreType.DMA((k,)) for k in (5 + len(DENSE_IN) + len(kept), 2, 1)]
    if remote:
        scratch += buffers(((16, D), f32), ((16 * inner, 128 * outer), b16)) + Scatter.scratch(PARTS)
    return pl.pallas_call(
        functools.partial(backward_kernel, remote),
        in_specs=vmem_specs(5) + any_specs(5 + len(dense) + len(kept) + len(given)),
        out_specs=specs + any_specs(len(made) + len(lands)),
        out_shape=results + made + lands,
        scratch_shapes=scratch,
        compiler_params=pltpu.CompilerParams(vmem_limit_bytes=VMEM_BYTES, **(dict(collective_id=1, has_side_effects=True) if remote else {})),
        name="backward",
    )(index, capacity_class, place_map, vec, gmlp, *weights, *dense, *kept, *given)


def spread_vectors(vectors, outer, inner):
    rows = vectors.reshape(vectors.shape[0], outer, inner, -1).transpose(2, 0, 1, 3).astype(jnp.bfloat16)
    tiles = jnp.pad(rows, ((0, 0), (0, 16 - rows.shape[1]), (0, 0), (0, 128 - rows.shape[3])))
    return tiles.reshape(inner * 16, outer * 128)


def deliver_kernel(n, *refs):
    tile, sums, outs, vectors = refs[0], refs[1 : n + 1], refs[n + 1 : 2 * n + 1], refs[2 * n + 1 :]
    for a, b in zip(sums, outs):
        b[...] = a[...]
    for j, v in enumerate(vectors):
        v[...] = tile[j : j + 1, : v.shape[1]]


def deliver(tile, sums, each, count):
    n = len(sums)
    return pl.pallas_call(
        functools.partial(deliver_kernel, n),
        in_specs=vmem_specs(1 + n),
        out_specs=vmem_specs(n + count),
        out_shape=[shape(*s.shape, dtype=s.dtype) for s in sums] + [shape(1, each, dtype=jnp.float32)] * count,
        name="deliver",
    )(tile, *sums)


def fits(shards, outer, inner):
    return outer == 2 and inner == 16 and all(s.shape[0] % 16 == 0 and s.shape[1] % 128 == 0 for s in shards)


def per_device(outer, inner, *args):
    hidden, cotangent, capacity_class, token_index = args[:4]
    (gain_attn_a, qkv_a, out_a, gain_mlp_a, up_a, down_a, router_shard,
     gain_attn_b, qkv_b, out_b, gain_mlp_b, up_b, down_b) = args[4:]
    hidden, cotangent = hidden[0], cotangent[0]
    length = hidden.shape[0]
    vectors = jnp.stack((gain_attn_a, gain_mlp_a, router_shard, gain_attn_b, gain_mlp_b))
    shards = [qkv_a, out_a, up_a, down_a, qkv_b, out_b, up_b, down_b]
    remote = fits(shards, outer, inner)
    if not remote:
        tile = jnp.pad(vectors, ((0, 16 - vectors.shape[0]), (0, 128 - vectors.shape[1])))
        vectors, *shards = [
            lax.all_gather(lax.all_gather(s, "inner", axis=0, tiled=True), "outer", axis=1, tiled=True) for s in (tile, *shards)
        ]
    spot = (token_index, capacity_class.reshape(1, 1), lane_map(outer, inner))
    whole, made, kept, dense = forward(remote, hidden, cotangent, *spot, vectors, shards, outer, inner)
    vec, gmlp, output, plus, grad_merged, *given = made
    input_grad, *res = backward(
        remote, *spot, vec, gmlp, (whole[4], *whole[:4]), [*dense, grad_merged, plus], kept, given, outer, inner)
    if remote:
        done, gtile = res[:8], res[8]
    else:
        gvec, gqkv_b, *grads_a = res
        done = [
            lax.psum_scatter(
                lax.psum_scatter(s, "outer", scatter_dimension=1, tiled=True), "inner", scatter_dimension=0, tiled=True
            ).astype(jnp.float32)
            for s in [gqkv_b, *given, *grads_a, spread_vectors(gvec[:5], outer, inner)]
        ]
        done, gtile = done[:8], done[8]
    each = gain_attn_a.shape[0]
    res = deliver(gtile, done, each, 5)
    gb, ga, v = res[:4], res[4:8], [r[0] for r in res[8:]]
    return (output[None], input_grad[None], v[0], ga[0], ga[1], v[1], ga[2], ga[3], v[2], v[3], gb[0], gb[1], v[4], gb[2], gb[3])


def solution(mesh):
    outer, inner = mesh.shape["outer"], mesh.shape["inner"]
    both = ("outer", "inner")
    rows, vector, matrix = P(both, None, None), P(both), P("inner", "outer")
    block = (vector, matrix, matrix, vector, matrix, matrix)
    return jax.shard_map(
        functools.partial(per_device, outer, inner),
        mesh=mesh,
        in_specs=(rows, rows, vector, P(both, None)) + block + (vector,) + block,
        out_specs=(rows, rows) + block + (vector,) + block,
        check_vma=False,
    )
```
